32 devices in a mesh: seq: 8 (over z, x), head: 4 (over y, core).
Axes of the slice: x: 2, y: 2, z: 4, core: 2. Of those that a mesh axis runs over, the one named last changes fastest.
Arguments:
- ssm_input: float32 [4096, 4096], P('seq', 'head'), may hold values from -50 to 50
- gate_input: bfloat16 [4096, 4096], P('seq', 'head'), may hold values from -6 to 6
- step_raw: float32 [4096, 64], P('seq', 'head'), may hold values from -6 to 8192
- decay_log: float32 [64], P('head')
- state_in: float32 [4096, 4, 128], P('seq', 'head'), may hold values from -0.5 to 0.5
- state_out: float32 [4096, 4, 128], P('seq', 'head'), may hold values from -6 to 6
- skip_gain: float32 [64], P('head'), may hold values from 0.5 to 2
- norm_gain: float32 [4096], P('head'), may hold values from 0.25 to 1.75
- out_weight: bfloat16 [4096, 4096], P('head'), may hold values from -0.09375 to 0.09375
Outputs:
- layer_out: bfloat16 [4096, 4096], P(('seq', 'head'))
The draws below stay inside these ranges and needn't reach their ends.
All inputs are finite; a program needn't handle non-finite values.
Results may differ from the reference program's by a relative error of at most 0.015.
Values may be sent and summed in bfloat16 or wider, within the bound.
No kernel may reach another device: no remote copies, remote signals or barrier semaphores. Data moves between devices by JAX's collectives and lax.ppermute only.
A program may use at most 192 MiB of HBM per device.

```python
import math
import jax
import jax.numpy as jnp
from jax import lax

HEAD_COUNT = 64
P_SIZE = 64
N = 128
GROUPS = 4
DOUT = 4096
SPAN = 256
TOKENS = 4096


def spike_layout(key):
    base_offset = jax.random.fold_in(key, 9173)
    random_key_list = jax.random.split(base_offset, 5)
    pick = jax.random.uniform(random_key_list[0], (HEAD_COUNT,))
    fast_share = 0.4
    slow_rate = jnp.exp(jax.random.uniform(random_key_list[1], (HEAD_COUNT,), minval=math.log(0.5), maxval=math.log(5.0))) / TOKENS
    fast_rate = jnp.exp(jax.random.uniform(random_key_list[2], (HEAD_COUNT,), minval=math.log(1.0 / 3.0), maxval=0.0))
    rate_values = jnp.where(pick < fast_share, fast_rate, slow_rate)
    spots = jax.random.randint(random_key_list[3], (3,), 0, TOKENS)
    flagged_rows = jnp.any(jnp.arange(TOKENS)[:, None] == spots[None, :], axis=1)
    spike_increment = jax.random.uniform(random_key_list[4], (HEAD_COUNT,), minval=0.22, maxval=0.6) / rate_values
    return (rate_values, flagged_rows, spike_increment)


def draw_decay_log(key, part):
    rate_values, flagged_rows, spike_increment = spike_layout(key)
    return jnp.log(rate_values).astype(jnp.float32)


def draw_step_raw(key, part):
    rate_values, flagged_rows, spike_increment = spike_layout(key)
    noise_key = jax.random.fold_in(key, 31)
    base_offset = -3.0 + 0.7 * jnp.clip(jax.random.normal(noise_key, (TOKENS, HEAD_COUNT)), -4.0, 4.0)
    spike_unscaled = spike_increment + jnp.log(-jnp.expm1(-spike_increment))
    return jnp.where(flagged_rows[:, None], spike_unscaled[None, :], base_offset).astype(jnp.float32)


def draw_ssm_input(key, part):
    rate_values, flagged_rows, spike_increment = spike_layout(key)
    random_key_list = jax.random.split(jax.random.fold_in(key, 57), 3)
    values = jnp.clip(jax.random.normal(random_key_list[0], (TOKENS, HEAD_COUNT * P_SIZE)), -4.0, 4.0)
    half_range = 0.5 * math.log(10.0)
    row_scale = jnp.exp(jax.random.uniform(random_key_list[1], (TOKENS, 1), minval=-half_range, maxval=half_range))
    col_scale = jnp.exp(jax.random.uniform(random_key_list[2], (1, HEAD_COUNT * P_SIZE), minval=-half_range, maxval=half_range))
    attenuation = jnp.where(flagged_rows[:, None], 1.0 / spike_increment[None, :], 1.0)
    return (values * row_scale * col_scale * jnp.repeat(attenuation, P_SIZE, axis=1)).astype(jnp.float32)


def levels(key, shape, cuts, least, largest):
    def one(position, blocks):
        draws = jax.random.uniform(jax.random.fold_in(jax.random.fold_in(key, 6), position), (blocks,), jnp.float32, least / len(cuts), largest / len(cuts))
        return jnp.repeat(jnp.exp(draws), shape[position] // blocks).reshape((-1,) + (1,) * (len(shape) - position - 1))

    loudness = one(*cuts[0])
    for cut in cuts[1:]:
        loudness = loudness * one(*cut)
    return loudness


def bell_draw(key, dims, scale, bound, cuts=(), dtype=jnp.bfloat16):
    loudness = levels(key, dims, cuts, -0.22, 0.18) if cuts else 1.0
    values = jax.random.normal(key, dims, jnp.float32) * scale * loudness
    return jnp.minimum(jnp.maximum(values, -bound), bound).astype(dtype)


def setup_inputs(seed: int = 0) -> dict:
    key_of = jax.random.split(jax.random.key(seed), 10)
    return {
        "ssm_input": draw_ssm_input(jax.random.fold_in(key_of[9], 71), 0),
        "gate_input": bell_draw(key_of[1], (TOKENS, HEAD_COUNT * P_SIZE), 1.0, 6.0, ((0, 8), (1, 4))),
        "step_raw": draw_step_raw(jax.random.fold_in(key_of[9], 71), 0),
        "decay_log": draw_decay_log(jax.random.fold_in(key_of[9], 71), 0),
        "state_in": bell_draw(key_of[4], (TOKENS, GROUPS, N), N ** -0.5, 0.5, ((0, 8), (1, 4)), jnp.float32),
        "state_out": bell_draw(key_of[5], (TOKENS, GROUPS, N), 1.0, 6.0, ((0, 8), (1, 4)), jnp.float32),
        "skip_gain": jnp.clip(0.5 + 1.5 * jax.random.uniform(key_of[6], (HEAD_COUNT,), jnp.float32) ** levels(key_of[6], (HEAD_COUNT,), ((0, 4),), -0.2, 0.2), 0.5, 2.0),
        "norm_gain": jnp.clip(1.0 + 0.15 * jax.random.normal(key_of[7], (HEAD_COUNT * P_SIZE,), jnp.float32), 0.25, 1.75),
        "out_weight": bell_draw(key_of[8], (HEAD_COUNT * P_SIZE, DOUT), (HEAD_COUNT * P_SIZE) ** -0.5, 0.09375, ((0, 4),)),
    }


def span_pass(carry, blocks_in):
    exact = lax.Precision.HIGHEST
    inputs, steps_in, logs_in, in_rows, out_rows = blocks_in
    per_group = HEAD_COUNT // GROUPS
    cumulative = jnp.cumsum(logs_in, axis=0)
    across = jnp.transpose(cumulative, (1, 0))
    causal = jnp.arange(SPAN)[:, None] >= jnp.arange(SPAN)[None, :]
    decays_in = jnp.exp(jnp.where(causal[None], across[:, :, None] - across[:, None, :], -jnp.inf))
    scores = jnp.einsum('ign,jgn->gij', out_rows, in_rows, precision=exact)
    mixing = jnp.repeat(scores, per_group, axis=0) * decays_in
    weighted = inputs * steps_in[:, :, None]
    within = jnp.einsum('hij,jhp->ihp', mixing, weighted, precision=exact)
    in_heads = jnp.repeat(in_rows, per_group, axis=1)
    out_heads = jnp.repeat(out_rows, per_group, axis=1)
    carried = jnp.einsum('ihn,hpn->ihp', out_heads, carry, precision=exact) * jnp.exp(cumulative)[:, :, None]
    to_end = jnp.exp(cumulative[-1][None, :] - cumulative)
    added = jnp.einsum('jhp,jhn->hpn', weighted * to_end[:, :, None], in_heads, precision=exact)
    new_state = carry * jnp.exp(cumulative[-1])[:, None, None] + added
    return (new_state, within + carried)

def reference(ssm_input, gate_input, step_raw, decay_log, state_in, state_out, skip_gain, norm_gain, out_weight):
    span_count = TOKENS // SPAN
    step = jax.nn.softplus(step_raw)
    logdecay = -step * jnp.exp(decay_log)[None, :]
    blocks_all = (ssm_input.reshape(span_count, SPAN, HEAD_COUNT, P_SIZE), step.reshape(span_count, SPAN, HEAD_COUNT), logdecay.reshape(span_count, SPAN, HEAD_COUNT), state_in.reshape(span_count, SPAN, GROUPS, N), state_out.reshape(span_count, SPAN, GROUPS, N))
    start_state = jnp.zeros((HEAD_COUNT, P_SIZE, N), jnp.float32)
    _, outputs = lax.scan(span_pass, start_state, blocks_all)
    ssd = outputs.reshape(TOKENS, HEAD_COUNT, P_SIZE) + skip_gain[None, :, None] * ssm_input.reshape(TOKENS, HEAD_COUNT, P_SIZE)
    gated = ssd.reshape(TOKENS, HEAD_COUNT * P_SIZE) * jax.nn.silu(gate_input.astype(jnp.float32))
    grouped = gated.reshape(TOKENS, GROUPS, HEAD_COUNT * P_SIZE // GROUPS)
    scaled = grouped * lax.rsqrt(lax.optimization_barrier(jnp.mean(grouped * grouped, axis=2, keepdims=True)) + 1e-05)
    normed = (scaled.reshape(TOKENS, HEAD_COUNT * P_SIZE) * norm_gain[None, :]).astype(jnp.bfloat16)
    return jnp.dot(normed, out_weight, preferred_element_type=jnp.float32).astype(jnp.bfloat16)
```

```python
import functools

import jax
import jax.numpy as jnp
from jax import lax
from jax.experimental import pallas as pl
from jax.experimental.pallas import tpu as pltpu
from jax.sharding import PartitionSpec as P

P_SIZE = 64
N = 128
CHUNK = 128
LANES = 128
BF = jnp.bfloat16
F32 = jnp.float32
VMEM_LIMIT = 24 * 1024 * 1024


def dot(a, b, contract=((1,), (0,)), precision=None):
    return lax.dot_general(a, b, (contract, ((), ())), precision=precision, preferred_element_type=F32)


def split2(v):
    hi = v.astype(BF)
    return hi, (v - hi.astype(F32)).astype(BF)


def split3(v):
    hi, rest = v.astype(BF), v
    rest = v - hi.astype(F32)
    mid = rest.astype(BF)
    return hi, mid, (rest - mid.astype(F32)).astype(BF)


def pick(rows, lanes, heads, per_head, first):
    r = lax.broadcasted_iota(jnp.int32, (rows, lanes), 0) % heads
    l = lax.broadcasted_iota(jnp.int32, (rows, lanes), 1) // per_head + first
    return jnp.where(r == l, 1.0, 0.0).astype(BF)


def state_kernel(raw_ref, rate_ref, x_ref, b_ref, msg_ref, aux_ref, wk):
    g = pl.program_id(0)
    heads, tok = raw_ref.shape
    width = x_ref.shape[1]
    chunks = tok // CHUNK

    @pl.when(g == 0)
    def _():
        raw = raw_ref[...]
        step = jnp.maximum(raw, 0.0) + jnp.log1p(jnp.exp(-jnp.abs(raw)))
        logs = -step * jnp.exp(rate_ref[...])
        parts = split3(logs)
        stacked = jnp.concatenate(
            [p[:, c * CHUNK:(c + 1) * CHUNK] for c in range(chunks) for p in parts], axis=0
        )
        s = lax.broadcasted_iota(jnp.int32, (CHUNK, 2 * CHUNK), 0)
        t = lax.broadcasted_iota(jnp.int32, (CHUNK, 2 * CHUNK), 1)
        tri = jnp.where(jnp.where(t < CHUNK, t - s, s - t + (CHUNK - 1)) >= 0, 1.0, 0.0).astype(BF)
        sums = dot(stacked, tri)
        pre, suf = [], []
        for c in range(chunks):
            base = 3 * heads * c
            total = (
                sums[base:base + heads] + sums[base + heads:base + 2 * heads]
            ) + sums[base + 2 * heads:base + 3 * heads]
            pre.append(total[:, :CHUNK])
            suf.append(total[:, CHUNK:])
        after = jnp.zeros((heads, 1), F32)
        for c in reversed(range(chunks)):
            w = step[:, c * CHUNK:(c + 1) * CHUNK] * jnp.exp(suf[c] + after)
            hi, lo = split2(w)
            wk[:heads, c * CHUNK:(c + 1) * CHUNK] = hi
            wk[heads:, c * CHUNK:(c + 1) * CHUNK] = lo
            after = after + pre[c][:, CHUNK - 1:]
        hi, lo = split2(jnp.broadcast_to(jnp.exp(after), (heads, CHUNK)))
        wk[:heads, tok:] = hi
        wk[heads:, tok:] = lo
        aux_ref[:heads] = step
        aux_ref[heads:2 * heads] = jnp.concatenate(pre, axis=1)
        aux_ref[2 * heads:] = jnp.concatenate(suf, axis=1)

    spread = dot(
        wk[...], pick(2 * heads, width, heads, P_SIZE, g * (width // P_SIZE)), ((0,), (0,))
    )
    weighted = (x_ref[...] * spread[:tok]).astype(BF)
    state = dot(b_ref[...].astype(BF), weighted, ((0,), (0,)))
    hi, lo = split2(spread[tok:tok + 8])
    decay = jnp.concatenate([hi.astype(F32), lo.astype(F32)], axis=0).astype(BF)
    for i in range(width // LANES):
        cut = slice(i * LANES, (i + 1) * LANES)
        msg_ref[i, :N] = state[:, cut].astype(BF)
        msg_ref[i, N:] = decay[:, cut]


def local_states(raw, rate, x, b):
    heads, tok = raw.shape
    width = 256
    blocks = x.shape[1] // LANES
    return pl.pallas_call(
        state_kernel,
        grid=(x.shape[1] // width,),
        in_specs=[
            pl.BlockSpec((heads, tok), lambda g: (0, 0)),
            pl.BlockSpec((heads, 1), lambda g: (0, 0)),
            pl.BlockSpec((tok, width), lambda g: (0, g)),
            pl.BlockSpec((tok, N), lambda g: (0, 0)),
        ],
        out_specs=[
            pl.BlockSpec((width // LANES, N + 16, LANES), lambda g: (g, 0, 0)),
            pl.BlockSpec((3 * heads, tok), lambda g: (0, 0)),
        ],
        out_shape=[
            jax.ShapeDtypeStruct((blocks, N + 16, LANES), BF),
            jax.ShapeDtypeStruct((3 * heads, tok), F32),
        ],
        scratch_shapes=[pltpu.VMEM((2 * heads, tok + CHUNK), BF)],
        compiler_params=pltpu.CompilerParams(vmem_limit_bytes=VMEM_LIMIT),
        cost_estimate=pl.CostEstimate(flops=400_000_000, bytes_accessed=2_800_000, transcendentals=0),
        name="local_states",
    )(raw, rate, x, b)


def prefix_kernel(msg_ref, out_ref):
    total = jnp.zeros((N, LANES), F32)
    for j in range(msg_ref.shape[0]):
        out_ref[j] = total.astype(BF)
        tail = msg_ref[j, N:].astype(F32)
        decay = tail[:1] + tail[8:9]
        total = total * decay + msg_ref[j, :N].astype(F32)


def prefix(msg):
    count = msg.shape[0]
    return pl.pallas_call(
        prefix_kernel,
        out_shape=jax.ShapeDtypeStruct((count, N, LANES), BF),
        compiler_params=pltpu.CompilerParams(vmem_limit_bytes=VMEM_LIMIT),
        cost_estimate=pl.CostEstimate(flops=1_000_000, bytes_accessed=600_000, transcendentals=0),
        name="prefix",
    )(msg)


def within_kernel(aux_ref, x_ref, b_ref, c_ref, skip_ref, y_ref, ec_ref, scores, trip, duo, lines):
    g = pl.program_id(0)
    tok, width = x_ref.shape
    heads = aux_ref.shape[0] // 3
    chunks = tok // CHUNK
    here = width // P_SIZE

    @pl.when(g == 0)
    def _():
        before = jnp.zeros((heads, 1), F32)
        i = lax.broadcasted_iota(jnp.int32, (CHUNK, CHUNK), 0)
        j = lax.broadcasted_iota(jnp.int32, (CHUNK, CHUNK), 1)
        for c in range(chunks):
            cut = slice(c * CHUNK, (c + 1) * CHUNK)
            step, pre, suf = (aux_ref[k * heads:(k + 1) * heads, cut] for k in range(3))
            trip[c] = jnp.concatenate([v for v in split3(pre)], axis=0)
            for k, value in enumerate((step, step * jnp.exp(suf), jnp.exp(pre))):
                hi, lo = split2(value)
                duo[c, :heads, k * CHUNK:(k + 1) * CHUNK] = hi
                duo[c, heads:, k * CHUNK:(k + 1) * CHUNK] = lo
            hi, lo = split2(jnp.exp(pre + before))
            ec_ref[:heads, cut] = hi
            ec_ref[heads:, cut] = lo
            before = before + pre[:, CHUNK - 1:]
            for k in range(heads // here):
                lines[k, :here, cut] = pre[k * here:(k + 1) * here]
            raw = dot(c_ref[cut], b_ref[cut], ((1,), (1,)), lax.Precision.HIGHEST)
            scores[c] = jnp.where(i >= j, raw, 0.0)

    spread = pick(2 * heads, width, heads, P_SIZE, g * here)
    columns = pick(3 * heads, here * CHUNK, heads, CHUNK, g * here)
    lane = lax.broadcasted_iota(jnp.int32, (CHUNK, LANES), 1)
    state = jnp.zeros((N, width), F32)
    mine = lines[g]
    for c in range(chunks):
        cut = slice(c * CHUNK, (c + 1) * CHUNK)
        wide = dot(duo[c], spread, ((0,), (0,)))
        x = x_ref[cut]
        stepped = x * wide[:CHUNK]
        lead = wide[2 * CHUNK:]
        tall = dot(trip[c], columns, ((0,), (0,)))
        outs = []
        for pair in range(here // 2):
            mixes = []
            for h in (2 * pair, 2 * pair + 1):
                gap = tall[:, h * CHUNK:(h + 1) * CHUNK] - mine[h:h + 1, cut]
                mixes.append((scores[c] * jnp.exp(jnp.minimum(gap, 0.0))).astype(BF))
            both = stepped[:, pair * LANES:(pair + 1) * LANES]
            stacked = jnp.concatenate(
                [
                    jnp.where(lane < P_SIZE, both, 0.0).astype(BF),
                    jnp.where(lane < P_SIZE, 0.0, both).astype(BF),
                ],
                axis=0,
            )
            outs.append(dot(jnp.concatenate(mixes, axis=1), stacked))
        y = jnp.concatenate(outs, axis=1) + skip_ref[...] * x
        if c:
            y = y + lead * dot(c_ref[cut].astype(BF), state.astype(BF))
        y_ref[cut] = y
        if c < chunks - 1:
            weighted = (x * wide[CHUNK:2 * CHUNK]).astype(BF)
            added = dot(b_ref[cut].astype(BF), weighted, ((0,), (0,)))
            state = state * lead[CHUNK - 1:] + added


def within(aux, x, b, c, skip):
    tok, channels = x.shape
    heads = aux.shape[0] // 3
    width = 256
    chunks = tok // CHUNK
    return pl.pallas_call(
        within_kernel,
        grid=(channels // width,),
        in_specs=[
            pl.BlockSpec((3 * heads, tok), lambda g: (0, 0)),
            pl.BlockSpec((tok, width), lambda g: (0, g)),
            pl.BlockSpec((tok, N), lambda g: (0, 0)),
            pl.BlockSpec((tok, N), lambda g: (0, 0)),
            pl.BlockSpec((1, width), lambda g: (0, g)),
        ],
        out_specs=[
            pl.BlockSpec((tok, width), lambda g: (0, g)),
            pl.BlockSpec((2 * heads, tok), lambda g: (0, 0)),
        ],
        out_shape=[
            jax.ShapeDtypeStruct((tok, channels), F32),
            jax.ShapeDtypeStruct((2 * heads, tok), BF),
        ],
        scratch_shapes=[
            pltpu.VMEM((chunks, CHUNK, CHUNK), F32),
            pltpu.VMEM((chunks, 3 * heads, CHUNK), BF),
            pltpu.VMEM((chunks, 2 * heads, 3 * CHUNK), BF),
            pltpu.VMEM((channels // width, 8, tok), F32),
        ],
        compiler_params=pltpu.CompilerParams(vmem_limit_bytes=VMEM_LIMIT),
        cost_estimate=pl.CostEstimate(
            flops=2_000_000_000, bytes_accessed=5_000_000, transcendentals=1_000_000
        ),
        name="within",
    )(aux, x, b, c, skip)


def finish_rows(y, c, incoming_ref, ec, gate, gain):
    channels = y.shape[1]
    heads = ec.shape[0] // 2
    c = c.astype(BF)
    carried = jnp.concatenate([dot(c, incoming_ref[k]) for k in range(incoming_ref.shape[0])], axis=1)
    lead = dot(ec, pick(2 * heads, channels, heads, P_SIZE, 0), ((0,), (0,)))
    ssd = y + lead * carried
    v = gate.astype(F32)
    gated = ssd * (v / (1.0 + jnp.exp(-v)))
    mean = jnp.mean(gated * gated, axis=1, keepdims=True)
    return (gated * lax.rsqrt(mean + 1e-05) * gain).astype(BF)


def project_kernel(
    order, y0, y1, c0, c1, e0, e1, g0, g1, incoming, gain, w, theirs, mine, normed_out, normed
):
    @pl.when(pl.program_id(0) == 0)
    def _():
        rows = y0.shape[0]
        normed[:rows] = finish_rows(y0[...], c0[...], incoming, e0[...], g0[...], gain[...])
        normed[rows:] = finish_rows(y1[...], c1[...], incoming, e1[...], g1[...], gain[...])
        normed_out[...] = normed[...]

    rows = y0.shape[0]
    out = dot(normed[...], w[...])
    theirs[...] = out[:rows].astype(BF)
    mine[...] = out[rows:]


def finish_project(order, first, y, c, ec, gate, incoming, gain, w, columns):
    tok, channels = y.shape
    rows = CHUNK
    wide = 1024
    heads2 = ec.shape[0]

    def row(k):
        return lambda j, order: (order[first + k], 0)

    return pl.pallas_call(
        project_kernel,
        grid_spec=pltpu.PrefetchScalarGridSpec(
            num_scalar_prefetch=1,
            grid=(columns // wide,),
            in_specs=[
                pl.BlockSpec((rows, channels), row(0)),
                pl.BlockSpec((rows, channels), row(1)),
                pl.BlockSpec((rows, N), row(0)),
                pl.BlockSpec((rows, N), row(1)),
                pl.BlockSpec((heads2, rows), lambda j, order: (0, order[first])),
                pl.BlockSpec((heads2, rows), lambda j, order: (0, order[first + 1])),
                pl.BlockSpec((rows, channels), row(0)),
                pl.BlockSpec((rows, channels), row(1)),
                pl.BlockSpec(incoming.shape, lambda j, order: (0, 0, 0)),
                pl.BlockSpec((1, channels), lambda j, order: (0, 0)),
                pl.BlockSpec((channels, wide), lambda j, order: (0, j)),
            ],
            out_specs=[
                pl.BlockSpec((rows, wide), lambda j, order: (0, j)),
                pl.BlockSpec((rows, wide), lambda j, order: (0, j)),
                pl.BlockSpec((2 * rows, channels), lambda j, order: (0, 0)),
            ],
            scratch_shapes=[pltpu.VMEM((2 * rows, channels), BF)],
        ),
        out_shape=[
            jax.ShapeDtypeStruct((rows, columns), BF),
            jax.ShapeDtypeStruct((rows, columns), F32),
            jax.ShapeDtypeStruct((2 * rows, channels), BF),
        ],
        compiler_params=pltpu.CompilerParams(vmem_limit_bytes=VMEM_LIMIT),
        cost_estimate=pl.CostEstimate(
            flops=2 * 2 * rows * channels * columns,
            bytes_accessed=2 * channels * columns,
            transcendentals=0,
        ),
        name="finish_project",
    )(order, y, y, c, c, ec, ec, gate, gate, incoming, gain, w)


def more_kernel(normed, w, theirs, mine):
    rows = theirs.shape[0]
    out = dot(normed[...], w[...])
    theirs[...] = out[:rows].astype(BF)
    mine[...] = out[rows:]


def project_more(normed, w, start):
    rows2, channels = normed.shape
    rows = rows2 // 2
    wide = 1024
    columns = w.shape[1] - start
    return pl.pallas_call(
        more_kernel,
        grid=(columns // wide,),
        in_specs=[
            pl.BlockSpec((rows2, channels), lambda j: (0, 0)),
            pl.BlockSpec((channels, wide), lambda j: (0, j + start // wide)),
        ],
        out_specs=[pl.BlockSpec((rows, wide), lambda j: (0, j))] * 2,
        out_shape=[
            jax.ShapeDtypeStruct((rows, columns), BF),
            jax.ShapeDtypeStruct((rows, columns), F32),
        ],
        compiler_params=pltpu.CompilerParams(vmem_limit_bytes=VMEM_LIMIT),
        cost_estimate=pl.CostEstimate(
            flops=2 * rows2 * channels * columns,
            bytes_accessed=2 * channels * columns,
            transcendentals=0,
        ),
        name="project_more",
    )(normed, w)


def incoming_states(msg, count):
    if count == msg.shape[0]:
        arrived = lax.all_to_all(msg, "seq", 0, 0, tiled=True)
        return lax.all_to_all(prefix(arrived), "seq", 0, 0, tiled=True)
    everyone = lax.all_gather(msg, "seq")
    mine = lax.axis_index("seq")

    def turn(j, total):
        part = everyone[j].astype(F32)
        decay = part[:, N:N + 1] + part[:, N + 8:N + 9]
        return jnp.where(j < mine, total * decay + part[:, :N], total)

    zero = jnp.zeros((msg.shape[0], N, LANES), F32)
    return lax.fori_loop(0, count - 1, turn, zero).astype(BF)


def per_device(
    seq_count,
    ssm_input,
    gate_input,
    step_raw,
    decay_log,
    state_in,
    state_out,
    skip_gain,
    norm_gain,
    out_weight,
):
    tok = ssm_input.shape[0]
    heads = decay_log.shape[0]
    b = state_in.reshape(tok, N)
    c = state_out.reshape(tok, N)
    msg, aux = local_states(step_raw.T, decay_log.reshape(heads, 1), ssm_input, b)
    incoming = incoming_states(msg, seq_count)
    skip = jnp.repeat(skip_gain, P_SIZE).reshape(1, -1)
    y, ec = within(aux, ssm_input, b, c, skip)

    me = lax.axis_index("head")
    order = jnp.stack([me ^ 3, me ^ 2, me ^ 1, me]).astype(jnp.int32)
    near = [(h, h ^ 1) for h in range(4)]
    far = [(h, h ^ 2) for h in range(4)]
    gain = norm_gain.reshape(1, -1)
    dout = out_weight.shape[1]
    half = dout // 2
    theirs, mine, normed = finish_project(
        order, 0, y, c, ec, gate_input, incoming, gain, out_weight, half
    )
    come = lax.ppermute(theirs, "head", near)
    first = lax.ppermute((mine + come.astype(F32)).astype(BF), "head", far)
    theirs, mine = project_more(normed, out_weight, half)
    come = lax.ppermute(theirs, "head", near)
    second = lax.ppermute((mine + come.astype(F32)).astype(BF), "head", far)
    theirs, mine, _ = finish_project(
        order, 2, y, c, ec, gate_input, incoming, gain, out_weight, dout
    )
    come = lax.ppermute(theirs, "head", near)
    kept = mine + come.astype(F32)
    return jnp.concatenate(
        [
            (kept[:, :half] + first.astype(F32)).astype(BF),
            (kept[:, half:] + second.astype(F32)).astype(BF),
        ],
        axis=1,
    )


def solution(mesh):
    in_specs = (
        P("seq", "head"),
        P("seq", "head"),
        P("seq", "head"),
        P("head"),
        P("seq", "head", None),
        P("seq", "head", None),
        P("head"),
        P("head"),
        P("head", None),
    )
    out_specs = P(("seq", "head"), None)
    return jax.shard_map(
        functools.partial(per_device, mesh.shape["seq"]),
        mesh=mesh,
        in_specs=in_specs,
        out_specs=out_specs,
        check_vma=False,
    )
```

```python
import functools

import jax
import jax.numpy as jnp
from jax import lax
from jax.experimental import pallas as pl
from jax.experimental.pallas import tpu as pltpu
from jax.sharding import PartitionSpec as P

P_SIZE = 64
N = 128
CHUNK = 128
LANES = 128
BF = jnp.bfloat16
F32 = jnp.float32
VMEM_LIMIT = 24 * 1024 * 1024
WHOLE_VMEM = 60 * 1024 * 1024
PIECES = ((0, 1024), (1024, 1024), (2048, 2048))


def dot(a, b, contract=((1,), (0,)), precision=None):
    return lax.dot_general(a, b, (contract, ((), ())), precision=precision, preferred_element_type=F32)


def split2(v):
    hi = v.astype(BF)
    return hi, (v - hi.astype(F32)).astype(BF)


def split3(v):
    hi, rest = v.astype(BF), v
    rest = v - hi.astype(F32)
    mid = rest.astype(BF)
    return hi, mid, (rest - mid.astype(F32)).astype(BF)


def pick(rows, lanes, heads, per_head, first):
    r = lax.broadcasted_iota(jnp.int32, (rows, lanes), 0) % heads
    l = lax.broadcasted_iota(jnp.int32, (rows, lanes), 1) // per_head + first
    return jnp.where(r == l, 1.0, 0.0).astype(BF)


def state_kernel(raw_ref, rate_ref, x_ref, b_ref, msg_ref, aux_ref, wk):
    g = pl.program_id(0)
    heads, tok = raw_ref.shape
    width = x_ref.shape[1]
    chunks = tok // CHUNK

    @pl.when(g == 0)
    def _():
        raw = raw_ref[...]
        step = jnp.maximum(raw, 0.0) + jnp.log1p(jnp.exp(-jnp.abs(raw)))
        r = lax.broadcasted_iota(jnp.int32, (heads, heads), 0)
        l = lax.broadcasted_iota(jnp.int32, (heads, heads), 1)
        rate = jnp.sum(jnp.where(r == l, rate_ref[...], 0.0), axis=1, keepdims=True)
        logs = -step * jnp.exp(rate)
        parts = split3(logs)
        stacked = jnp.concatenate(
            [p[:, c * CHUNK:(c + 1) * CHUNK] for c in range(chunks) for p in parts], axis=0
        )
        s = lax.broadcasted_iota(jnp.int32, (CHUNK, 2 * CHUNK), 0)
        t = lax.broadcasted_iota(jnp.int32, (CHUNK, 2 * CHUNK), 1)
        tri = jnp.where(jnp.where(t < CHUNK, t - s, s - t + (CHUNK - 1)) >= 0, 1.0, 0.0).astype(BF)
        sums = dot(stacked, tri)
        pre, suf = [], []
        for c in range(chunks):
            base = 3 * heads * c
            total = (
                sums[base:base + heads] + sums[base + heads:base + 2 * heads]
            ) + sums[base + 2 * heads:base + 3 * heads]
            pre.append(total[:, :CHUNK])
            suf.append(total[:, CHUNK:])
        after = jnp.zeros((heads, 1), F32)
        for c in reversed(range(chunks)):
            w = step[:, c * CHUNK:(c + 1) * CHUNK] * jnp.exp(suf[c] + after)
            hi, lo = split2(w)
            wk[:heads, c * CHUNK:(c + 1) * CHUNK] = hi
            wk[heads:, c * CHUNK:(c + 1) * CHUNK] = lo
            after = after + pre[c][:, CHUNK - 1:]
        hi, lo = split2(jnp.broadcast_to(jnp.exp(after), (heads, CHUNK)))
        wk[:heads, tok:] = hi
        wk[heads:, tok:] = lo
        aux_ref[:heads] = step
        aux_ref[heads:2 * heads] = jnp.concatenate(pre, axis=1)
        aux_ref[2 * heads:] = jnp.concatenate(suf, axis=1)

    spread = dot(
        wk[...], pick(2 * heads, width, heads, P_SIZE, g * (width // P_SIZE)), ((0,), (0,))
    )
    weighted = (x_ref[...] * spread[:tok]).astype(BF)
    state = dot(b_ref[...].astype(BF), weighted, ((0,), (0,)))
    hi, lo = split2(spread[tok:tok + 8])
    decay = jnp.concatenate([hi.astype(F32), lo.astype(F32)], axis=0).astype(BF)
    for i in range(width // LANES):
        cut = slice(i * LANES, (i + 1) * LANES)
        msg_ref[i, :N] = state[:, cut].astype(BF)
        msg_ref[i, N:] = decay[:, cut]


def local_states(raw, rate, x, b):
    heads, tok = raw.shape
    width = 256
    blocks = x.shape[1] // LANES
    return pl.pallas_call(
        state_kernel,
        grid=(x.shape[1] // width,),
        in_specs=[
            pl.BlockSpec((heads, tok), lambda g: (0, 0)),
            pl.BlockSpec((1, heads), lambda g: (0, 0)),
            pl.BlockSpec((tok, width), lambda g: (0, g)),
            pl.BlockSpec((tok, N), lambda g: (0, 0)),
        ],
        out_specs=[
            pl.BlockSpec((width // LANES, N + 16, LANES), lambda g: (g, 0, 0)),
            pl.BlockSpec((3 * heads, tok), lambda g: (0, 0)),
        ],
        out_shape=[
            jax.ShapeDtypeStruct((blocks, N + 16, LANES), BF),
            jax.ShapeDtypeStruct((3 * heads, tok), F32),
        ],
        scratch_shapes=[pltpu.VMEM((2 * heads, tok + CHUNK), BF)],
        compiler_params=pltpu.CompilerParams(vmem_limit_bytes=WHOLE_VMEM),
        cost_estimate=pl.CostEstimate(flops=400_000_000, bytes_accessed=2_800_000, transcendentals=0),
        name="local_states",
    )(raw, rate, x, b)


def prefix_kernel(msg_ref, out_ref):
    total = jnp.zeros((N, LANES), F32)
    for j in range(msg_ref.shape[0]):
        out_ref[j] = total.astype(BF)
        tail = msg_ref[j, N:].astype(F32)
        decay = tail[:1] + tail[8:9]
        total = total * decay + msg_ref[j, :N].astype(F32)


def prefix(msg):
    count = msg.shape[0]
    return pl.pallas_call(
        prefix_kernel,
        out_shape=jax.ShapeDtypeStruct((count, N, LANES), BF),
        compiler_params=pltpu.CompilerParams(vmem_limit_bytes=VMEM_LIMIT),
        cost_estimate=pl.CostEstimate(flops=1_000_000, bytes_accessed=600_000, transcendentals=0),
        name="prefix",
    )(msg)


def within_kernel(aux_ref, x_ref, b_ref, c_ref, gate_ref, skip_ref, own_ref, lead_ref, scores, trip, duo, lines):
    g = pl.program_id(0)
    tok, width = x_ref.shape
    heads = aux_ref.shape[0] // 3
    chunks = tok // CHUNK
    here = width // P_SIZE

    @pl.when(g == 0)
    def _():
        before = jnp.zeros((heads, 1), F32)
        i = lax.broadcasted_iota(jnp.int32, (CHUNK, CHUNK), 0)
        j = lax.broadcasted_iota(jnp.int32, (CHUNK, CHUNK), 1)
        for c in range(chunks):
            cut = slice(c * CHUNK, (c + 1) * CHUNK)
            step, pre, suf = (aux_ref[k * heads:(k + 1) * heads, cut] for k in range(3))
            trip[c] = jnp.concatenate([v for v in split3(pre)], axis=0)
            for k, value in enumerate(
                (step, step * jnp.exp(suf), jnp.exp(pre), jnp.exp(pre + before))
            ):
                hi, lo = split2(value)
                duo[c, :heads, k * CHUNK:(k + 1) * CHUNK] = hi
                duo[c, heads:, k * CHUNK:(k + 1) * CHUNK] = lo
            before = before + pre[:, CHUNK - 1:]
            for k in range(heads // here):
                lines[k, :here, cut] = pre[k * here:(k + 1) * here]
            raw = dot(c_ref[cut], b_ref[cut], ((1,), (1,)), lax.Precision.HIGHEST)
            scores[c] = jnp.where(i >= j, raw, 0.0)

    spread = pick(2 * heads, width, heads, P_SIZE, g * here)
    columns = pick(3 * heads, here * CHUNK, heads, CHUNK, g * here)
    lane = lax.broadcasted_iota(jnp.int32, (CHUNK, LANES), 1)
    state = jnp.zeros((N, width), F32)
    mine = lines[g]
    for c in range(chunks):
        cut = slice(c * CHUNK, (c + 1) * CHUNK)
        wide = dot(duo[c], spread, ((0,), (0,)))
        x = x_ref[cut]
        stepped = x * wide[:CHUNK]
        lead = wide[2 * CHUNK:3 * CHUNK]
        tall = dot(trip[c], columns, ((0,), (0,)))
        outs = []
        for pair in range(here // 2):
            mixes = []
            for h in (2 * pair, 2 * pair + 1):
                gap = tall[:, h * CHUNK:(h + 1) * CHUNK] - mine[h:h + 1, cut]
                mixes.append((scores[c] * jnp.exp(jnp.minimum(gap, 0.0))).astype(BF))
            both = stepped[:, pair * LANES:(pair + 1) * LANES]
            stacked = jnp.concatenate(
                [
                    jnp.where(lane < P_SIZE, both, 0.0).astype(BF),
                    jnp.where(lane < P_SIZE, 0.0, both).astype(BF),
                ],
                axis=0,
            )
            outs.append(dot(jnp.concatenate(mixes, axis=1), stacked))
        y = jnp.concatenate(outs, axis=1) + skip_ref[...] * x
        if c:
            y = y + lead * dot(c_ref[cut].astype(BF), state.astype(BF))
        v = gate_ref[cut].astype(F32)
        silu = v / (1.0 + jnp.exp(-v))
        own_ref[cut] = y * silu
        lead_ref[cut] = wide[3 * CHUNK:] * silu
        if c < chunks - 1:
            weighted = (x * wide[CHUNK:2 * CHUNK]).astype(BF)
            added = dot(b_ref[cut].astype(BF), weighted, ((0,), (0,)))
            state = state * lead[CHUNK - 1:] + added


def within(aux, x, b, c, gate, skip):
    tok, channels = x.shape
    heads = aux.shape[0] // 3
    width = 256
    chunks = tok // CHUNK
    return pl.pallas_call(
        within_kernel,
        grid=(channels // width,),
        in_specs=[
            pl.BlockSpec((3 * heads, tok), lambda g: (0, 0)),
            pl.BlockSpec((tok, width), lambda g: (0, g)),
            pl.BlockSpec((tok, N), lambda g: (0, 0)),
            pl.BlockSpec((tok, N), lambda g: (0, 0)),
            pl.BlockSpec((tok, width), lambda g: (0, g)),
            pl.BlockSpec((1, width), lambda g: (0, g)),
        ],
        out_specs=[pl.BlockSpec((tok, width), lambda g: (0, g))] * 2,
        out_shape=[jax.ShapeDtypeStruct((tok, channels), F32)] * 2,
        scratch_shapes=[
            pltpu.VMEM((chunks, CHUNK, CHUNK), F32),
            pltpu.VMEM((chunks, 3 * heads, CHUNK), BF),
            pltpu.VMEM((chunks, 2 * heads, 4 * CHUNK), BF),
            pltpu.VMEM((channels // width, 8, tok), F32),
        ],
        compiler_params=pltpu.CompilerParams(vmem_limit_bytes=VMEM_LIMIT),
        cost_estimate=pl.CostEstimate(
            flops=2_000_000_000, bytes_accessed=5_000_000, transcendentals=1_000_000
        ),
        name="within",
    )(aux, x, b, c, gate, skip)


def finish_rows(own, lead, c, incoming_ref, gain):
    c = c.astype(BF)
    carried = jnp.concatenate([dot(c, incoming_ref[k]) for k in range(incoming_ref.shape[0])], axis=1)
    gated = own + lead * carried
    mean = jnp.mean(gated * gated, axis=1, keepdims=True)
    return (gated * lax.rsqrt(mean + 1e-05) * gain).astype(BF)


def far_kernel(
    order, o0, o1, l0, l1, c0, c1, incoming, gain, w, theirs, mine, normed, weights, sem
):
    columns = theirs.shape[1]
    rows = o0.shape[0]
    load = pltpu.make_async_copy(w.at[:, :columns], weights, sem)
    load.start()
    normed[:rows] = finish_rows(o0[...], l0[...], c0[...], incoming, gain[...])
    normed[rows:] = finish_rows(o1[...], l1[...], c1[...], incoming, gain[...])
    load.wait()
    out = dot(normed[...], weights[...])
    theirs[...] = out[:rows].astype(BF)
    mine[...] = out[rows:]


def near_kernel(order, o0, o1, l0, l1, c0, c1, incoming, gain, w, theirs, mine, normed):
    rows = o0.shape[0]

    @pl.when(pl.program_id(0) == 0)
    def _():
        normed[:rows] = finish_rows(o0[...], l0[...], c0[...], incoming, gain[...])
        normed[rows:] = finish_rows(o1[...], l1[...], c1[...], incoming, gain[...])

    out = dot(normed[...], w[...])
    theirs[...] = out[:rows].astype(BF)
    mine[...] = out[rows:]


def finish_project(order, far, own, lead, c, incoming, gain, w, columns):
    channels = own.shape[1]
    rows = CHUNK
    first = 0 if far else 2
    wide = columns if far else 1024

    def row(k):
        return lambda j, order: (order[first + k], 0)

    normed = pltpu.VMEM((2 * rows, channels), BF)
    return pl.pallas_call(
        far_kernel if far else near_kernel,
        grid_spec=pltpu.PrefetchScalarGridSpec(
            num_scalar_prefetch=1,
            grid=(columns // wide,),
            in_specs=[
                pl.BlockSpec((rows, channels), row(0)),
                pl.BlockSpec((rows, channels), row(1)),
                pl.BlockSpec((rows, channels), row(0)),
                pl.BlockSpec((rows, channels), row(1)),
                pl.BlockSpec((rows, N), row(0)),
                pl.BlockSpec((rows, N), row(1)),
                pl.BlockSpec(incoming.shape, lambda j, order: (0, 0, 0)),
                pl.BlockSpec((1, channels), lambda j, order: (0, 0)),
                pl.BlockSpec(memory_space=pl.ANY)
                if far
                else pl.BlockSpec((channels, wide), lambda j, order: (0, j)),
            ],
            out_specs=[
                pl.BlockSpec((rows, wide), lambda j, order: (0, j)),
                pl.BlockSpec((rows, wide), lambda j, order: (0, j)),
            ]
            + ([pl.BlockSpec((2 * rows, channels), lambda j, order: (0, 0))] if far else []),
            scratch_shapes=[pltpu.VMEM((channels, wide), BF), pltpu.SemaphoreType.DMA]
            if far
            else [normed],
        ),
        out_shape=[
            jax.ShapeDtypeStruct((rows, columns), BF),
            jax.ShapeDtypeStruct((rows, columns), F32),
        ]
        + ([jax.ShapeDtypeStruct((2 * rows, channels), BF)] if far else []),
        compiler_params=pltpu.CompilerParams(vmem_limit_bytes=WHOLE_VMEM),
        cost_estimate=pl.CostEstimate(
            flops=2 * 2 * rows * channels * columns,
            bytes_accessed=2 * channels * columns,
            transcendentals=0,
        ),
        name="finish_far" if far else "finish_near",
    )(order, own, own, lead, lead, c, c, incoming, gain, w)


def more_kernel(normed, w, theirs, mine):
    rows = theirs.shape[0]
    out = dot(normed[...], w[...])
    theirs[...] = out[:rows].astype(BF)
    mine[...] = out[rows:]


def project_more(normed, w, start, columns):
    rows2, channels = normed.shape
    rows = rows2 // 2
    wide = 512
    return pl.pallas_call(
        more_kernel,
        grid=(columns // wide,),
        in_specs=[
            pl.BlockSpec((rows2, channels), lambda j: (0, 0)),
            pl.BlockSpec((channels, wide), lambda j: (0, j + start // wide)),
        ],
        out_specs=[pl.BlockSpec((rows, wide), lambda j: (0, j))] * 2,
        out_shape=[
            jax.ShapeDtypeStruct((rows, columns), BF),
            jax.ShapeDtypeStruct((rows, columns), F32),
        ],
        compiler_params=pltpu.CompilerParams(vmem_limit_bytes=WHOLE_VMEM),
        cost_estimate=pl.CostEstimate(
            flops=2 * rows2 * channels * columns,
            bytes_accessed=2 * channels * columns,
            transcendentals=0,
        ),
        name="project_more",
    )(normed, w)


def early_kernel(kept, first, second, out):
    j = pl.program_id(0)

    @pl.when(j == 0)
    def _():
        out[...] = (kept[...] + first[...].astype(F32)).astype(BF)

    @pl.when(j == 1)
    def _():
        out[...] = (kept[...] + second[...].astype(F32)).astype(BF)


def early_sums(kept, first, second):
    rows, wide = first.shape
    return pl.pallas_call(
        early_kernel,
        grid=(2,),
        in_specs=[
            pl.BlockSpec((rows, wide), lambda j: (0, j)),
            pl.BlockSpec((rows, wide), lambda j: (0, 0)),
            pl.BlockSpec((rows, wide), lambda j: (0, 0)),
        ],
        out_specs=pl.BlockSpec((rows, wide), lambda j: (0, j)),
        out_shape=jax.ShapeDtypeStruct(kept.shape, BF),
        compiler_params=pltpu.CompilerParams(vmem_limit_bytes=VMEM_LIMIT),
        name="early_sums",
    )(kept, first, second)


def last_kernel(kept, third, filled, out):
    out[...] = (kept[...] + third[...].astype(F32)).astype(BF)


def last_sums(kept, third, filled):
    rows, wide = third.shape
    return pl.pallas_call(
        last_kernel,
        grid=(1,),
        in_specs=[
            pl.BlockSpec((rows, wide), lambda j: (0, 1)),
            pl.BlockSpec((rows, wide), lambda j: (0, 0)),
            pl.BlockSpec(memory_space=pl.ANY),
        ],
        out_specs=pl.BlockSpec((rows, wide), lambda j: (0, 1)),
        out_shape=jax.ShapeDtypeStruct(kept.shape, BF),
        input_output_aliases={2: 0},
        compiler_params=pltpu.CompilerParams(vmem_limit_bytes=VMEM_LIMIT),
        name="last_sums",
    )(kept, third, filled)


def incoming_states(msg, count):
    if count == msg.shape[0]:
        arrived = lax.all_to_all(msg, "seq", 0, 0, tiled=True)
        return lax.all_to_all(prefix(arrived), "seq", 0, 0, tiled=True)
    everyone = lax.all_gather(msg, "seq")
    mine = lax.axis_index("seq")

    def turn(j, total):
        part = everyone[j].astype(F32)
        decay = part[:, N:N + 1] + part[:, N + 8:N + 9]
        return jnp.where(j < mine, total * decay + part[:, :N], total)

    zero = jnp.zeros((msg.shape[0], N, LANES), F32)
    return lax.fori_loop(0, count - 1, turn, zero).astype(BF)


def per_device(
    seq_count,
    ssm_input,
    gate_input,
    step_raw,
    decay_log,
    state_in,
    state_out,
    skip_gain,
    norm_gain,
    out_weight,
):
    tok = ssm_input.shape[0]
    heads = decay_log.shape[0]
    b = state_in.reshape(tok, N)
    c = state_out.reshape(tok, N)
    msg, aux = local_states(step_raw.T, decay_log.reshape(1, heads), ssm_input, b)
    incoming = incoming_states(msg, seq_count)
    skip = jnp.repeat(skip_gain, P_SIZE).reshape(1, -1)
    own, lead = within(aux, ssm_input, b, c, gate_input, skip)

    me = lax.axis_index("head")
    order = jnp.stack([me ^ 3, me ^ 2, me ^ 1, me]).astype(jnp.int32)
    near = [(h, h ^ 1) for h in range(4)]
    far = [(h, h ^ 2) for h in range(4)]
    gain = norm_gain.reshape(1, -1)

    def paired(theirs, mine):
        return mine + lax.ppermute(theirs, "head", near).astype(F32)

    theirs, mine, normed = finish_project(
        order, True, own, lead, c, incoming, gain, out_weight, PIECES[0][1]
    )
    sent = [paired(theirs, mine).astype(BF)]
    sent.append(paired(*project_more(normed, out_weight, *PIECES[1])).astype(BF))
    normed, sent[0] = lax.optimization_barrier((normed, sent[0]))
    sent.append(paired(*project_more(normed, out_weight, *PIECES[2])).astype(BF))
    arrived = [lax.ppermute(part, "head", far) for part in sent[:2]]
    order, sent[2] = lax.optimization_barrier((order, sent[2]))
    arrived.append(lax.ppermute(sent[2], "head", far))
    kept = paired(
        *finish_project(
            order, False, own, lead, c, incoming, gain, out_weight, out_weight.shape[1]
        )
    )
    return last_sums(kept, arrived[2], early_sums(kept, arrived[0], arrived[1]))


def solution(mesh):
    in_specs = (
        P("seq", "head"),
        P("seq", "head"),
        P("seq", "head"),
        P("head"),
        P("seq", "head", None),
        P("seq", "head", None),
        P("head"),
        P("head"),
        P("head", None),
    )
    out_specs = P(("seq", "head"), None)
    return jax.shard_map(
        functools.partial(per_device, mesh.shape["seq"]),
        mesh=mesh,
        in_specs=in_specs,
        out_specs=out_specs,
        check_vma=False,
    )
```

```python
import functools

import jax
import jax.numpy as jnp
from jax import lax
from jax.experimental import pallas as pl
from jax.experimental.pallas import tpu as pltpu
from jax.sharding import PartitionSpec as P

P_SIZE = 64
N = 128
CHUNK = 128
LANES = 128
BF = jnp.bfloat16
F32 = jnp.float32
VMEM_LIMIT = 24 * 1024 * 1024
WHOLE_VMEM = 60 * 1024 * 1024
PIECES = ((0, 1024), (1024, 1024), (2048, 2048))


def dot(a, b, contract=((1,), (0,)), precision=None):
    return lax.dot_general(a, b, (contract, ((), ())), precision=precision, preferred_element_type=F32)


def split2(v):
    hi = v.astype(BF)
    return hi, (v - hi.astype(F32)).astype(BF)


def split3(v):
    hi, rest = v.astype(BF), v
    rest = v - hi.astype(F32)
    mid = rest.astype(BF)
    return hi, mid, (rest - mid.astype(F32)).astype(BF)


def pick(rows, lanes, heads, per_head, first):
    r = lax.broadcasted_iota(jnp.int32, (rows, lanes), 0) % heads
    l = lax.broadcasted_iota(jnp.int32, (rows, lanes), 1) // per_head + first
    return jnp.where(r == l, 1.0, 0.0).astype(BF)


def step_vectors(raw, rate_row, wk, aux_ref):
    heads, tok = raw.shape
    chunks = tok // CHUNK
    step = jnp.maximum(raw, 0.0) + jnp.log1p(jnp.exp(-jnp.abs(raw)))
    r = lax.broadcasted_iota(jnp.int32, (heads, heads), 0)
    l = lax.broadcasted_iota(jnp.int32, (heads, heads), 1)
    rate = jnp.sum(jnp.where(r == l, rate_row, 0.0), axis=1, keepdims=True)
    logs = -step * jnp.exp(rate)
    parts = split3(logs)
    stacked = jnp.concatenate(
        [p[:, c * CHUNK:(c + 1) * CHUNK] for c in range(chunks) for p in parts], axis=0
    )
    s = lax.broadcasted_iota(jnp.int32, (CHUNK, 2 * CHUNK), 0)
    t = lax.broadcasted_iota(jnp.int32, (CHUNK, 2 * CHUNK), 1)
    tri = jnp.where(jnp.where(t < CHUNK, t - s, s - t + (CHUNK - 1)) >= 0, 1.0, 0.0).astype(BF)
    sums = dot(stacked, tri)
    pre, suf = [], []
    for c in range(chunks):
        base = 3 * heads * c
        total = (
            sums[base:base + heads] + sums[base + heads:base + 2 * heads]
        ) + sums[base + 2 * heads:base + 3 * heads]
        pre.append(total[:, :CHUNK])
        suf.append(total[:, CHUNK:])
    after = jnp.zeros((heads, 1), F32)
    for c in reversed(range(chunks)):
        w = step[:, c * CHUNK:(c + 1) * CHUNK] * jnp.exp(suf[c] + after)
        hi, lo = split2(w)
        wk[:heads, c * CHUNK:(c + 1) * CHUNK] = hi
        wk[heads:, c * CHUNK:(c + 1) * CHUNK] = lo
        after = after + pre[c][:, CHUNK - 1:]
    hi, lo = split2(jnp.broadcast_to(jnp.exp(after), (heads, CHUNK)))
    wk[:heads, tok:] = hi
    wk[heads:, tok:] = lo
    aux_ref[:heads] = step
    aux_ref[heads:2 * heads] = jnp.concatenate(pre, axis=1)
    aux_ref[2 * heads:] = jnp.concatenate(suf, axis=1)


def tail_rows(decays):
    r = lax.broadcasted_iota(jnp.int32, (16, LANES), 0)
    tail = jnp.zeros((16, LANES), F32)
    for k, decay in enumerate(decays):
        hi, lo = split2(decay)
        tail = jnp.where(r == 2 * k, hi.astype(F32), tail)
        tail = jnp.where(r == 2 * k + 1, lo.astype(F32), tail)
    return tail.astype(BF)


def decays_of(msg):
    blocks = (msg.shape[0] - 16) // N
    tail = msg[blocks * N:].astype(F32)
    return [tail[2 * k:2 * k + 1] + tail[2 * k + 1:2 * k + 2] for k in range(blocks)]


def half_message(x_ref, b, wk, first_head, msg):
    tok, lanes = x_ref.shape
    heads2 = wk.shape[0]
    width = 256
    decays = []
    for g in range(lanes // width):
        chosen = pick(heads2, width, heads2 // 2, P_SIZE, first_head + g * (width // P_SIZE))
        spread = dot(wk[...], chosen, ((0,), (0,)))
        weighted = (x_ref[:, g * width:(g + 1) * width] * spread[:tok]).astype(BF)
        state = dot(b, weighted, ((0,), (0,)))
        for i in range(width // LANES):
            k = g * (width // LANES) + i
            msg[k * N:(k + 1) * N] = state[:, i * LANES:(i + 1) * LANES].astype(BF)
            decays.append(spread[tok:tok + 1, i * LANES:(i + 1) * LANES])
    msg[msg.shape[0] - 16:] = tail_rows(decays)


def half_kernel(give, raw, rate, x, b, msg, wk, aux, raw_v, rate_v, x_v, b_v, sems):
    lanes = x_v.shape[1]
    mine = lax.axis_index("seq") % 2
    half = 1 - mine if give else mine
    loads = [
        pltpu.make_async_copy(b, b_v, sems.at[0]),
        pltpu.make_async_copy(
            x.at[:, pl.ds(pl.multiple_of(half * lanes, lanes), lanes)], x_v, sems.at[1]
        ),
    ]
    if give:
        loads += [
            pltpu.make_async_copy(raw, raw_v, sems.at[2]),
            pltpu.make_async_copy(rate, rate_v, sems.at[3]),
        ]
    for load in reversed(loads):
        load.start()
    if give:
        loads[2].wait()
        loads[3].wait()
        step_vectors(raw_v[...], rate_v[...], wk, aux)
    loads[0].wait()
    loads[1].wait()
    half_message(x_v, b_v[...].astype(BF), wk, half * (lanes // P_SIZE), msg)


def give_kernel(raw, rate, x, b, msg, wk, aux, raw_v, rate_v, x_v, b_v, sems):
    half_kernel(True, raw, rate, x, b, msg, wk, aux, raw_v, rate_v, x_v, b_v, sems)


def keep_kernel(wk, x, b, msg, x_v, b_v, sems):
    half_kernel(False, None, None, x, b, msg, wk, None, None, None, x_v, b_v, sems)


HBM = pl.BlockSpec(memory_space=pltpu.HBM)


def give_states(raw, rate, x, b):
    heads, tok = raw.shape
    lanes = x.shape[1] // 2
    return pl.pallas_call(
        give_kernel,
        in_specs=[HBM] * 4,
        out_shape=[
            jax.ShapeDtypeStruct((lanes + 16, LANES), BF),
            jax.ShapeDtypeStruct((2 * heads, tok + CHUNK), BF),
            jax.ShapeDtypeStruct((3 * heads, tok), F32),
        ],
        scratch_shapes=[
            pltpu.VMEM((heads, tok), F32),
            pltpu.VMEM((1, heads), F32),
            pltpu.VMEM((tok, lanes), F32),
            pltpu.VMEM((tok, N), F32),
            pltpu.SemaphoreType.DMA((4,)),
        ],
        compiler_params=pltpu.CompilerParams(vmem_limit_bytes=WHOLE_VMEM),
        cost_estimate=pl.CostEstimate(flops=200_000_000, bytes_accessed=1_500_000, transcendentals=0),
        name="give_states",
    )(raw, rate, x, b)


def keep_states(wk, x, b):
    tok = x.shape[0]
    lanes = x.shape[1] // 2
    return pl.pallas_call(
        keep_kernel,
        in_specs=[pl.BlockSpec(memory_space=pltpu.VMEM), HBM, HBM],
        out_shape=jax.ShapeDtypeStruct((lanes + 16, LANES), BF),
        scratch_shapes=[
            pltpu.VMEM((tok, lanes), F32),
            pltpu.VMEM((tok, N), F32),
            pltpu.SemaphoreType.DMA((2,)),
        ],
        compiler_params=pltpu.CompilerParams(vmem_limit_bytes=VMEM_LIMIT),
        cost_estimate=pl.CostEstimate(flops=200_000_000, bytes_accessed=1_500_000, transcendentals=0),
        name="keep_states",
    )(wk, x, b)


def link(later, earlier, out):
    ahead, behind = decays_of(later), decays_of(earlier)
    for k, decay in enumerate(ahead):
        rows = slice(k * N, (k + 1) * N)
        out[rows] = (later[rows].astype(F32) + decay * earlier[rows].astype(F32)).astype(BF)
    out[len(ahead) * N:] = tail_rows([p * q for p, q in zip(ahead, behind)])


def pair_kernel(own, come, out):
    odd = lax.axis_index("seq") % 2

    @pl.when(odd == 0)
    def _():
        link(come, own, out)

    @pl.when(odd == 1)
    def _():
        link(own, come, out)


def end_kernel(last, before, own, come, mine, theirs):
    blocks = mine.shape[0] // N
    odd = lax.axis_index("seq") % 2

    def fill(even_section, ahead_ref, behind_ref):
        step, span = decays_of(last), decays_of(even_section)
        for k in range(blocks):
            rows = slice(k * N, (k + 1) * N)
            start = last[rows].astype(F32)
            if before is not None:
                start = start + step[k] * before[rows].astype(F32)
            ahead_ref[rows] = start.astype(BF)
            behind_ref[rows] = (even_section[rows].astype(F32) + span[k] * start).astype(BF)

    @pl.when(odd == 0)
    def _():
        fill(own, mine, theirs)

    @pl.when(odd == 1)
    def _():
        fill(come, theirs, mine)


def scan_call(kernel, operands, shapes, name):
    return pl.pallas_call(
        kernel,
        out_shape=[jax.ShapeDtypeStruct(shape, BF) for shape in shapes],
        compiler_params=pltpu.CompilerParams(vmem_limit_bytes=VMEM_LIMIT),
        cost_estimate=pl.CostEstimate(flops=500_000, bytes_accessed=400_000, transcendentals=0),
        name=name,
    )(*operands)


def incoming_states(give, keep, count, hold):
    pair = [(s, s ^ 1) for s in range(count)]
    come = lax.ppermute(give, "seq", pair)
    run = scan_call(pair_kernel, (keep, come), [keep.shape], "join_pair")[0]
    start, distance = None, 2
    while distance < count:
        got = lax.ppermute(run, "seq", [(s, s + distance) for s in range(count - distance)])
        if distance * 2 >= count:
            break
        run = scan_call(link, (run, got), [keep.shape], "join_run")[0]
        start = got if start is None else scan_call(link, (start, got), [keep.shape], "join_start")[0]
        distance *= 2
    hold, got = hold(got)
    half = (keep.shape[0] - 16, LANES)
    mine, theirs = scan_call(end_kernel, (start, got, keep, come), [half, half], "join_end")
    return hold, mine, lax.ppermute(theirs, "seq", pair)


def within_kernel(aux_ref, x_ref, b_ref, c_ref, gate_ref, skip_ref, own_ref, lead_ref, scores, trip, duo, lines):
    g = pl.program_id(0)
    tok, width = x_ref.shape
    heads = aux_ref.shape[0] // 3
    chunks = tok // CHUNK
    here = width // P_SIZE

    @pl.when(g == 0)
    def _():
        before = jnp.zeros((heads, 1), F32)
        i = lax.broadcasted_iota(jnp.int32, (CHUNK, CHUNK), 0)
        j = lax.broadcasted_iota(jnp.int32, (CHUNK, CHUNK), 1)
        for c in range(chunks):
            cut = slice(c * CHUNK, (c + 1) * CHUNK)
            step, pre, suf = (aux_ref[k * heads:(k + 1) * heads, cut] for k in range(3))
            trip[c] = jnp.concatenate([v for v in split3(pre)], axis=0)
            for k, value in enumerate(
                (step, step * jnp.exp(suf), jnp.exp(pre), jnp.exp(pre + before))
            ):
                hi, lo = split2(value)
                duo[c, :heads, k * CHUNK:(k + 1) * CHUNK] = hi
                duo[c, heads:, k * CHUNK:(k + 1) * CHUNK] = lo
            before = before + pre[:, CHUNK - 1:]
            for k in range(heads // here):
                lines[k, :here, cut] = pre[k * here:(k + 1) * here]
            raw = dot(c_ref[cut], b_ref[cut], ((1,), (1,)), lax.Precision.HIGHEST)
            scores[c] = jnp.where(i >= j, raw, 0.0)

    spread = pick(2 * heads, width, heads, P_SIZE, g * here)
    columns = pick(3 * heads, here * CHUNK, heads, CHUNK, g * here)
    lane = lax.broadcasted_iota(jnp.int32, (CHUNK, LANES), 1)
    state = jnp.zeros((N, width), F32)
    mine = lines[g]
    for c in range(chunks):
        cut = slice(c * CHUNK, (c + 1) * CHUNK)
        wide = dot(duo[c], spread, ((0,), (0,)))
        x = x_ref[cut]
        stepped = x * wide[:CHUNK]
        lead = wide[2 * CHUNK:3 * CHUNK]
        tall = dot(trip[c], columns, ((0,), (0,)))
        outs = []
        for pair in range(here // 2):
            mixes = []
            for h in (2 * pair, 2 * pair + 1):
                gap = tall[:, h * CHUNK:(h + 1) * CHUNK] - mine[h:h + 1, cut]
                mixes.append((scores[c] * jnp.exp(jnp.minimum(gap, 0.0))).astype(BF))
            both = stepped[:, pair * LANES:(pair + 1) * LANES]
            stacked = jnp.concatenate(
                [
                    jnp.where(lane < P_SIZE, both, 0.0).astype(BF),
                    jnp.where(lane < P_SIZE, 0.0, both).astype(BF),
                ],
                axis=0,
            )
            outs.append(dot(jnp.concatenate(mixes, axis=1), stacked))
        y = jnp.concatenate(outs, axis=1) + skip_ref[...] * x
        if c:
            y = y + lead * dot(c_ref[cut].astype(BF), state.astype(BF))
        v = gate_ref[cut].astype(F32)
        silu = v / (1.0 + jnp.exp(-v))
        own_ref[cut] = y * silu
        lead_ref[cut] = wide[3 * CHUNK:] * silu
        if c < chunks - 1:
            weighted = (x * wide[CHUNK:2 * CHUNK]).astype(BF)
            added = dot(b_ref[cut].astype(BF), weighted, ((0,), (0,)))
            state = state * lead[CHUNK - 1:] + added


def within(aux, x, b, c, gate, skip):
    tok, channels = x.shape
    heads = aux.shape[0] // 3
    width = 256
    chunks = tok // CHUNK
    return pl.pallas_call(
        within_kernel,
        grid=(channels // width,),
        in_specs=[
            pl.BlockSpec((3 * heads, tok), lambda g: (0, 0)),
            pl.BlockSpec((tok, width), lambda g: (0, g)),
            pl.BlockSpec((tok, N), lambda g: (0, 0)),
            pl.BlockSpec((tok, N), lambda g: (0, 0)),
            pl.BlockSpec((tok, width), lambda g: (0, g)),
            pl.BlockSpec((1, width), lambda g: (0, g)),
        ],
        out_specs=[pl.BlockSpec((tok, width), lambda g: (0, g))] * 2,
        out_shape=[jax.ShapeDtypeStruct((tok, channels), F32)] * 2,
        scratch_shapes=[
            pltpu.VMEM((chunks, CHUNK, CHUNK), F32),
            pltpu.VMEM((chunks, 3 * heads, CHUNK), BF),
            pltpu.VMEM((chunks, 2 * heads, 4 * CHUNK), BF),
            pltpu.VMEM((channels // width, 8, tok), F32),
        ],
        compiler_params=pltpu.CompilerParams(vmem_limit_bytes=VMEM_LIMIT),
        cost_estimate=pl.CostEstimate(
            flops=2_000_000_000, bytes_accessed=5_000_000, transcendentals=1_000_000
        ),
        name="within",
    )(aux, x, b, c, gate, skip)


def finish_rows(own, lead, c, incoming, gain):
    c = c.astype(BF)
    blocks = incoming.shape[1] // N
    carried = jnp.concatenate(
        [dot(c, incoming[h, k * N:(k + 1) * N]) for h in range(2) for k in range(blocks)], axis=1
    )
    gated = own + lead * carried
    mean = jnp.mean(gated * gated, axis=1, keepdims=True)
    return (gated * lax.rsqrt(mean + 1e-05) * gain).astype(BF)


def start_weights(w, start, weights, sems):
    count, _, wide = weights.shape
    loads = [
        pltpu.make_async_copy(w.at[:, start + k * wide:start + (k + 1) * wide], weights.at[k], sems.at[k])
        for k in range(count)
    ]
    for load in loads:
        load.start()
    return loads


def project_rows(normed, loads, weights, theirs, mine):
    rows = theirs.shape[0]
    wide = weights.shape[2]
    for k, load in enumerate(loads):
        load.wait()
        out = dot(normed[...], weights[k])
        theirs[:, k * wide:(k + 1) * wide] = out[:rows].astype(BF)
        mine[:, k * wide:(k + 1) * wide] = out[rows:]


def finish_kernel(
    order, o0, o1, l0, l1, c0, c1, here, there, gain, w, theirs, mine, normed, incoming, weights, sems
):
    rows = o0.shape[0]
    loads = start_weights(w, 0, weights, sems)
    odd = lax.axis_index("seq") % 2
    incoming[odd] = here[...]
    incoming[1 - odd] = there[...]
    normed[:rows] = finish_rows(o0[...], l0[...], c0[...], incoming, gain[...])
    normed[rows:] = finish_rows(o1[...], l1[...], c1[...], incoming, gain[...])
    project_rows(normed, loads, weights, theirs, mine)


def finish_project(order, first, own, lead, c, here, there, gain, w, columns, name):
    channels = own.shape[1]
    rows = CHUNK
    wide = 512

    def row(k):
        return lambda j, order: (order[first + k], 0)

    def whole(j, order):
        return (0, 0)

    return pl.pallas_call(
        finish_kernel,
        grid_spec=pltpu.PrefetchScalarGridSpec(
            num_scalar_prefetch=1,
            grid=(1,),
            in_specs=[
                pl.BlockSpec((rows, channels), row(0)),
                pl.BlockSpec((rows, channels), row(1)),
                pl.BlockSpec((rows, channels), row(0)),
                pl.BlockSpec((rows, channels), row(1)),
                pl.BlockSpec((rows, N), row(0)),
                pl.BlockSpec((rows, N), row(1)),
                pl.BlockSpec(here.shape, whole),
                pl.BlockSpec(there.shape, whole),
                pl.BlockSpec((1, channels), whole),
                HBM,
            ],
            out_specs=[
                pl.BlockSpec((rows, columns), whole),
                pl.BlockSpec((rows, columns), whole),
                pl.BlockSpec((2 * rows, channels), whole),
            ],
            scratch_shapes=[
                pltpu.VMEM((2,) + here.shape, BF),
                pltpu.VMEM((columns // wide, channels, wide), BF),
                pltpu.SemaphoreType.DMA((columns // wide,)),
            ],
        ),
        out_shape=[
            jax.ShapeDtypeStruct((rows, columns), BF),
            jax.ShapeDtypeStruct((rows, columns), F32),
            jax.ShapeDtypeStruct((2 * rows, channels), BF),
        ],
        compiler_params=pltpu.CompilerParams(vmem_limit_bytes=VMEM_LIMIT),
        cost_estimate=pl.CostEstimate(
            flops=2 * 2 * rows * channels * columns,
            bytes_accessed=2 * channels * columns,
            transcendentals=0,
        ),
        name=name,
    )(order, own, own, lead, lead, c, c, here, there, gain, w)


def more_kernel(start, normed, w, theirs, mine, weights, sems):
    project_rows(normed, start_weights(w, start, weights, sems), weights, theirs, mine)


def project_more(normed, w, start, columns):
    rows2, channels = normed.shape
    rows = rows2 // 2
    wide = 512
    return pl.pallas_call(
        functools.partial(more_kernel, start),
        in_specs=[pl.BlockSpec(memory_space=pltpu.VMEM), HBM],
        out_shape=[
            jax.ShapeDtypeStruct((rows, columns), BF),
            jax.ShapeDtypeStruct((rows, columns), F32),
        ],
        scratch_shapes=[
            pltpu.VMEM((columns // wide, channels, wide), BF),
            pltpu.SemaphoreType.DMA((columns // wide,)),
        ],
        compiler_params=pltpu.CompilerParams(vmem_limit_bytes=VMEM_LIMIT),
        cost_estimate=pl.CostEstimate(
            flops=2 * rows2 * channels * columns,
            bytes_accessed=2 * channels * columns,
            transcendentals=0,
        ),
        name="project_more",
    )(normed, w)


def pass_kernel(*refs):
    pass


def await_piece(piece, earlier):
    arrays = [piece, *earlier]
    return pl.pallas_call(
        pass_kernel,
        in_specs=[pl.BlockSpec(memory_space=pl.ANY)] * len(arrays),
        out_specs=[pl.BlockSpec(memory_space=pl.ANY)] * len(arrays),
        out_shape=[jax.ShapeDtypeStruct(v.shape, v.dtype) for v in arrays],
        input_output_aliases={k: k for k in range(len(arrays))},
        cost_estimate=pl.CostEstimate(
            flops=20_000_000_000, bytes_accessed=100_000_000, transcendentals=0
        ),
        name="await_piece",
    )(*arrays)


def last_kernel(kept, third, second, first, out):
    @pl.when(pl.program_id(0) == 0)
    def _():
        wide = first.shape[1]
        out[:, :wide] = (kept[:, :wide] + first[...].astype(F32)).astype(BF)
        out[:, wide:] = (kept[:, wide:] + second[...].astype(F32)).astype(BF)

    @pl.when(pl.program_id(0) == 1)
    def _():
        out[...] = (kept[...] + third[...].astype(F32)).astype(BF)


def last_sums(kept, third, second, first):
    rows, wide = third.shape
    return pl.pallas_call(
        last_kernel,
        grid=(2,),
        in_specs=[
            pl.BlockSpec((rows, wide), lambda j: (0, j)),
            pl.BlockSpec((rows, wide), lambda j: (0, 0)),
            pl.BlockSpec(second.shape, lambda j: (0, 0)),
            pl.BlockSpec(first.shape, lambda j: (0, 0)),
        ],
        out_specs=pl.BlockSpec((rows, wide), lambda j: (0, j)),
        out_shape=jax.ShapeDtypeStruct(kept.shape, BF),
        compiler_params=pltpu.CompilerParams(vmem_limit_bytes=VMEM_LIMIT),
        name="last_sums",
    )(kept, third, second, first)


def per_device(
    seq_count,
    ssm_input,
    gate_input,
    step_raw,
    decay_log,
    state_in,
    state_out,
    skip_gain,
    norm_gain,
    out_weight,
):
    tok = ssm_input.shape[0]
    heads = decay_log.shape[0]
    b = state_in.reshape(tok, N)
    c = state_out.reshape(tok, N)
    give, wk, aux = give_states(step_raw.T, decay_log.reshape(1, heads), ssm_input, b)
    keep = keep_states(wk, ssm_input, b)
    skip = jnp.repeat(skip_gain, P_SIZE).reshape(1, -1)
    local = within(aux, ssm_input, b, c, gate_input, skip)
    (own, lead), here, there = incoming_states(
        give, keep, seq_count, lambda got: lax.optimization_barrier((local, got))
    )

    me = lax.axis_index("head")
    order = jnp.stack([me ^ 3, me ^ 2, me ^ 1, me]).astype(jnp.int32)
    near = [(h, h ^ 1) for h in range(4)]
    far = [(h, h ^ 2) for h in range(4)]
    gain = norm_gain.reshape(1, -1)

    def paired(theirs, mine):
        return mine + lax.ppermute(theirs, "head", near).astype(F32)

    theirs, mine, normed = finish_project(
        order, 0, own, lead, c, here, there, gain, out_weight, PIECES[0][1], "finish_far"
    )
    sent = [paired(theirs, mine).astype(BF)]
    for piece in PIECES[1:]:
        sent.append(paired(*project_more(normed, out_weight, *piece)).astype(BF))
        normed, sent[0] = lax.optimization_barrier((normed, sent[0]))
    order, sent[0] = lax.optimization_barrier((order, sent[0]))
    theirs, mine, _ = finish_project(
        order, 2, own, lead, c, here, there, gain, out_weight, out_weight.shape[1], "finish_near"
    )
    kept = paired(theirs, mine)
    arrived = []
    for part in sent:
        arrived = await_piece(lax.ppermute(part, "head", far), arrived)
    return last_sums(kept, *arrived)


def solution(mesh):
    in_specs = (
        P("seq", "head"),
        P("seq", "head"),
        P("seq", "head"),
        P("head"),
        P("seq", "head", None),
        P("seq", "head", None),
        P("head"),
        P("head"),
        P("head", None),
    )
    out_specs = P(("seq", "head"), None)
    return jax.shard_map(
        functools.partial(per_device, mesh.shape["seq"]),
        mesh=mesh,
        in_specs=in_specs,
        out_specs=out_specs,
        check_vma=False,
    )
```

```python
import functools

import jax
import jax.numpy as jnp
from jax import lax
from jax.experimental import pallas as pl
from jax.experimental.pallas import tpu as pltpu
from jax.sharding import PartitionSpec as P

P_SIZE = 64
N = 128
CHUNK = 128
LANES = 128
BF = jnp.bfloat16
F32 = jnp.float32
VMEM_LIMIT = 16 * 1024 * 1024
WHOLE_VMEM = 61 * 1024 * 1024 + 512 * 1024
PIECES = ((0, 1024), (1024, 1536), (2560, 1536))


def dot(a, b, contract=((1,), (0,)), precision=None):
    return lax.dot_general(a, b, (contract, ((), ())), precision=precision, preferred_element_type=F32)


def split2(v):
    hi = v.astype(BF)
    return hi, (v - hi.astype(F32)).astype(BF)


def split3(v):
    hi, rest = v.astype(BF), v
    rest = v - hi.astype(F32)
    mid = rest.astype(BF)
    return hi, mid, (rest - mid.astype(F32)).astype(BF)


def pick(rows, lanes, heads, per_head, first):
    r = lax.broadcasted_iota(jnp.int32, (rows, lanes), 0) % heads
    l = lax.broadcasted_iota(jnp.int32, (rows, lanes), 1) // per_head + first
    return jnp.where(r == l, 1.0, 0.0).astype(BF)


def step_vectors(raw, rate_row, wk, aux_ref):
    heads, tok = raw.shape
    chunks = tok // CHUNK
    step = jnp.maximum(raw, 0.0) + jnp.log1p(jnp.exp(-jnp.abs(raw)))
    r = lax.broadcasted_iota(jnp.int32, (heads, heads), 0)
    l = lax.broadcasted_iota(jnp.int32, (heads, heads), 1)
    rate = jnp.sum(jnp.where(r == l, rate_row, 0.0), axis=1, keepdims=True)
    logs = -step * jnp.exp(rate)
    parts = split3(logs)
    stacked = jnp.concatenate(
        [p[:, c * CHUNK:(c + 1) * CHUNK] for c in range(chunks) for p in parts], axis=0
    )
    s = lax.broadcasted_iota(jnp.int32, (CHUNK, 2 * CHUNK), 0)
    t = lax.broadcasted_iota(jnp.int32, (CHUNK, 2 * CHUNK), 1)
    tri = jnp.where(jnp.where(t < CHUNK, t - s, s - t + (CHUNK - 1)) >= 0, 1.0, 0.0).astype(BF)
    sums = dot(stacked, tri)
    pre, suf = [], []
    for c in range(chunks):
        base = 3 * heads * c
        total = (
            sums[base:base + heads] + sums[base + heads:base + 2 * heads]
        ) + sums[base + 2 * heads:base + 3 * heads]
        pre.append(total[:, :CHUNK])
        suf.append(total[:, CHUNK:])
    after = jnp.zeros((heads, 1), F32)
    for c in reversed(range(chunks)):
        w = step[:, c * CHUNK:(c + 1) * CHUNK] * jnp.exp(suf[c] + after)
        hi, lo = split2(w)
        wk[:heads, c * CHUNK:(c + 1) * CHUNK] = hi
        wk[heads:, c * CHUNK:(c + 1) * CHUNK] = lo
        after = after + pre[c][:, CHUNK - 1:]
    hi, lo = split2(jnp.broadcast_to(jnp.exp(after), (heads, CHUNK)))
    wk[:heads, tok:] = hi
    wk[heads:, tok:] = lo
    aux_ref[:heads] = step
    aux_ref[heads:2 * heads] = jnp.concatenate(pre, axis=1)
    aux_ref[2 * heads:] = jnp.concatenate(suf, axis=1)


def tail_rows(decays):
    r = lax.broadcasted_iota(jnp.int32, (16, LANES), 0)
    tail = jnp.zeros((16, LANES), F32)
    for k, decay in enumerate(decays):
        hi, lo = split2(decay)
        tail = jnp.where(r == 2 * k, hi.astype(F32), tail)
        tail = jnp.where(r == 2 * k + 1, lo.astype(F32), tail)
    return tail.astype(BF)


def decays_of(msg):
    blocks = (msg.shape[0] - 16) // N
    tail = msg[blocks * N:].astype(F32)
    return [tail[2 * k:2 * k + 1] + tail[2 * k + 1:2 * k + 2] for k in range(blocks)]


def half_message(x_ref, b, wk, first_head, msg):
    tok, lanes = x_ref.shape
    heads2 = wk.shape[0]
    width = 256
    decays = []
    for g in range(lanes // width):
        chosen = pick(heads2, width, heads2 // 2, P_SIZE, first_head + g * (width // P_SIZE))
        spread = dot(wk[...], chosen, ((0,), (0,)))
        weighted = (x_ref[:, g * width:(g + 1) * width] * spread[:tok]).astype(BF)
        state = dot(b, weighted, ((0,), (0,)))
        for i in range(width // LANES):
            k = g * (width // LANES) + i
            msg[k * N:(k + 1) * N] = state[:, i * LANES:(i + 1) * LANES].astype(BF)
            decays.append(spread[tok:tok + 1, i * LANES:(i + 1) * LANES])
    msg[msg.shape[0] - 16:] = tail_rows(decays)


def half_kernel(give, raw, rate, x, b, msg, wk, aux, raw_v, rate_v, x_v, b_v, sems):
    lanes = x_v.shape[1]
    mine = lax.axis_index("seq") % 2
    half = 1 - mine if give else mine
    loads = [
        pltpu.make_async_copy(b, b_v, sems.at[0]),
        pltpu.make_async_copy(
            x.at[:, pl.ds(pl.multiple_of(half * lanes, lanes), lanes)], x_v, sems.at[1]
        ),
    ]
    if give:
        loads += [
            pltpu.make_async_copy(raw, raw_v, sems.at[2]),
            pltpu.make_async_copy(rate, rate_v, sems.at[3]),
        ]
    for load in reversed(loads):
        load.start()
    if give:
        loads[2].wait()
        loads[3].wait()
        step_vectors(raw_v[...], rate_v[...], wk, aux)
    loads[0].wait()
    loads[1].wait()
    half_message(x_v, b_v[...].astype(BF), wk, half * (lanes // P_SIZE), msg)


def give_kernel(raw, rate, x, b, msg, wk, aux, raw_v, rate_v, x_v, b_v, sems):
    half_kernel(True, raw, rate, x, b, msg, wk, aux, raw_v, rate_v, x_v, b_v, sems)


def keep_kernel(wk, x, b, msg, x_v, b_v, sems):
    half_kernel(False, None, None, x, b, msg, wk, None, None, None, x_v, b_v, sems)


HBM = pl.BlockSpec(memory_space=pltpu.HBM)


def give_states(raw, rate, x, b):
    heads, tok = raw.shape
    lanes = x.shape[1] // 2
    return pl.pallas_call(
        give_kernel,
        in_specs=[HBM] * 4,
        out_shape=[
            jax.ShapeDtypeStruct((lanes + 16, LANES), BF),
            jax.ShapeDtypeStruct((2 * heads, tok + CHUNK), BF),
            jax.ShapeDtypeStruct((3 * heads, tok), F32),
        ],
        scratch_shapes=[
            pltpu.VMEM((heads, tok), F32),
            pltpu.VMEM((1, heads), F32),
            pltpu.VMEM((tok, lanes), F32),
            pltpu.VMEM((tok, N), F32),
            pltpu.SemaphoreType.DMA((4,)),
        ],
        compiler_params=pltpu.CompilerParams(vmem_limit_bytes=WHOLE_VMEM),
        cost_estimate=pl.CostEstimate(flops=200_000_000, bytes_accessed=1_500_000, transcendentals=0),
        name="give_states",
    )(raw, rate, x, b)


def keep_states(wk, x, b):
    tok = x.shape[0]
    lanes = x.shape[1] // 2
    return pl.pallas_call(
        keep_kernel,
        in_specs=[pl.BlockSpec(memory_space=pltpu.VMEM), HBM, HBM],
        out_shape=jax.ShapeDtypeStruct((lanes + 16, LANES), BF),
        scratch_shapes=[
            pltpu.VMEM((tok, lanes), F32),
            pltpu.VMEM((tok, N), F32),
            pltpu.SemaphoreType.DMA((2,)),
        ],
        compiler_params=pltpu.CompilerParams(vmem_limit_bytes=VMEM_LIMIT),
        cost_estimate=pl.CostEstimate(flops=200_000_000, bytes_accessed=1_500_000, transcendentals=0),
        name="keep_states",
    )(wk, x, b)


def link(later, earlier, out):
    ahead, behind = decays_of(later), decays_of(earlier)
    for k, decay in enumerate(ahead):
        rows = slice(k * N, (k + 1) * N)
        out[rows] = (later[rows].astype(F32) + decay * earlier[rows].astype(F32)).astype(BF)
    out[len(ahead) * N:] = tail_rows([p * q for p, q in zip(ahead, behind)])


def pair_kernel(own, come, out):
    odd = lax.axis_index("seq") % 2

    @pl.when(odd == 0)
    def _():
        link(come, own, out)

    @pl.when(odd == 1)
    def _():
        link(own, come, out)


def end_kernel(last, before, own, come, mine, theirs):
    blocks = mine.shape[0] // N
    odd = lax.axis_index("seq") % 2

    def fill(even_section, ahead_ref, behind_ref):
        step, span = decays_of(last), decays_of(even_section)
        for k in range(blocks):
            rows = slice(k * N, (k + 1) * N)
            start = last[rows].astype(F32)
            if before is not None:
                start = start + step[k] * before[rows].astype(F32)
            ahead_ref[rows] = start.astype(BF)
            behind_ref[rows] = (even_section[rows].astype(F32) + span[k] * start).astype(BF)

    @pl.when(odd == 0)
    def _():
        fill(own, mine, theirs)

    @pl.when(odd == 1)
    def _():
        fill(come, theirs, mine)


def scan_call(kernel, operands, shapes, name):
    return pl.pallas_call(
        kernel,
        out_shape=[jax.ShapeDtypeStruct(shape, BF) for shape in shapes],
        compiler_params=pltpu.CompilerParams(vmem_limit_bytes=VMEM_LIMIT),
        cost_estimate=pl.CostEstimate(flops=500_000, bytes_accessed=400_000, transcendentals=0),
        name=name,
    )(*operands)


def incoming_states(give, keep, count, hold):
    pair = [(s, s ^ 1) for s in range(count)]
    come = lax.ppermute(give, "seq", pair)
    run = scan_call(pair_kernel, (keep, come), [keep.shape], "join_pair")[0]
    start, distance = None, 2
    while distance < count:
        got = lax.ppermute(run, "seq", [(s, s + distance) for s in range(count - distance)])
        if distance * 2 >= count:
            break
        run = scan_call(link, (run, got), [keep.shape], "join_run")[0]
        start = got if start is None else scan_call(link, (start, got), [keep.shape], "join_start")[0]
        distance *= 2
    hold, got = hold(got)
    half = (keep.shape[0] - 16, LANES)
    mine, theirs = scan_call(end_kernel, (start, got, keep, come), [half, half], "join_end")
    return hold, mine, lax.ppermute(theirs, "seq", pair)


def within_kernel(aux_ref, x_ref, b_ref, c_ref, gate_ref, skip_ref, own_ref, lead_ref, scores, trip, duo, lines):
    g = pl.program_id(0)
    tok, width = x_ref.shape
    heads = aux_ref.shape[0] // 3
    chunks = tok // CHUNK
    here = width // P_SIZE

    @pl.when(g == 0)
    def _():
        before = jnp.zeros((heads, 1), F32)
        i = lax.broadcasted_iota(jnp.int32, (CHUNK, CHUNK), 0)
        j = lax.broadcasted_iota(jnp.int32, (CHUNK, CHUNK), 1)
        for c in range(chunks):
            cut = slice(c * CHUNK, (c + 1) * CHUNK)
            step, pre, suf = (aux_ref[k * heads:(k + 1) * heads, cut] for k in range(3))
            trip[c] = jnp.concatenate([v for v in split3(pre)], axis=0)
            for k, value in enumerate(
                (step, step * jnp.exp(suf), jnp.exp(pre), jnp.exp(pre + before))
            ):
                hi, lo = split2(value)
                duo[c, :heads, k * CHUNK:(k + 1) * CHUNK] = hi
                duo[c, heads:, k * CHUNK:(k + 1) * CHUNK] = lo
            before = before + pre[:, CHUNK - 1:]
            for k in range(heads // here):
                lines[k, :here, cut] = pre[k * here:(k + 1) * here]
            raw = dot(c_ref[cut], b_ref[cut], ((1,), (1,)), lax.Precision.HIGHEST)
            scores[c] = jnp.where(i >= j, raw, 0.0)

    spread = pick(2 * heads, width, heads, P_SIZE, g * here)
    columns = pick(3 * heads, here * CHUNK, heads, CHUNK, g * here)
    gains = jnp.broadcast_to(jnp.concatenate(split3(skip_ref[...]), axis=1), (8, 3 * heads))
    skip = dot(gains, pick(3 * heads, width, heads, P_SIZE, g * here))[:1]
    lane = lax.broadcasted_iota(jnp.int32, (CHUNK, LANES), 1)
    state = jnp.zeros((N, width), F32)
    mine = lines[g]
    for c in range(chunks):
        cut = slice(c * CHUNK, (c + 1) * CHUNK)
        wide = dot(duo[c], spread, ((0,), (0,)))
        x = x_ref[cut]
        stepped = x * wide[:CHUNK]
        lead = wide[2 * CHUNK:3 * CHUNK]
        tall = dot(trip[c], columns, ((0,), (0,)))
        outs = []
        for pair in range(here // 2):
            mixes = []
            for h in (2 * pair, 2 * pair + 1):
                gap = tall[:, h * CHUNK:(h + 1) * CHUNK] - mine[h:h + 1, cut]
                mixes.append((scores[c] * jnp.exp(jnp.minimum(gap, 0.0))).astype(BF))
            both = stepped[:, pair * LANES:(pair + 1) * LANES]
            stacked = jnp.concatenate(
                [
                    jnp.where(lane < P_SIZE, both, 0.0).astype(BF),
                    jnp.where(lane < P_SIZE, 0.0, both).astype(BF),
                ],
                axis=0,
            )
            outs.append(dot(jnp.concatenate(mixes, axis=1), stacked))
        y = jnp.concatenate(outs, axis=1) + skip * x
        if c:
            y = y + lead * dot(c_ref[cut].astype(BF), state.astype(BF))
        v = gate_ref[cut].astype(F32)
        silu = v / (1.0 + jnp.exp(-v))
        own_ref[cut] = y * silu
        lead_ref[cut] = wide[3 * CHUNK:] * silu
        if c < chunks - 1:
            weighted = (x * wide[CHUNK:2 * CHUNK]).astype(BF)
            added = dot(b_ref[cut].astype(BF), weighted, ((0,), (0,)))
            state = state * lead[CHUNK - 1:] + added


def within(aux, x, b, c, gate, skip):
    tok, channels = x.shape
    heads = aux.shape[0] // 3
    width = 256
    chunks = tok // CHUNK
    return pl.pallas_call(
        within_kernel,
        grid=(channels // width,),
        in_specs=[
            pl.BlockSpec((3 * heads, tok), lambda g: (0, 0)),
            pl.BlockSpec((tok, width), lambda g: (0, g)),
            pl.BlockSpec((tok, N), lambda g: (0, 0)),
            pl.BlockSpec((tok, N), lambda g: (0, 0)),
            pl.BlockSpec((tok, width), lambda g: (0, g)),
            pl.BlockSpec((1, heads), lambda g: (0, 0)),
        ],
        out_specs=[pl.BlockSpec((tok, width), lambda g: (0, g))] * 2,
        out_shape=[jax.ShapeDtypeStruct((tok, channels), F32)] * 2,
        scratch_shapes=[
            pltpu.VMEM((chunks, CHUNK, CHUNK), F32),
            pltpu.VMEM((chunks, 3 * heads, CHUNK), BF),
            pltpu.VMEM((chunks, 2 * heads, 4 * CHUNK), BF),
            pltpu.VMEM((channels // width, 8, tok), F32),
        ],
        compiler_params=pltpu.CompilerParams(vmem_limit_bytes=VMEM_LIMIT),
        cost_estimate=pl.CostEstimate(
            flops=2_000_000_000, bytes_accessed=5_000_000, transcendentals=1_000_000
        ),
        name="within",
    )(aux, x, b, c, gate, skip)


def finish_rows(own, lead, c, incoming, gain):
    c = c.astype(BF)
    blocks = incoming.shape[1] // N
    carried = jnp.concatenate(
        [dot(c, incoming[h, k * N:(k + 1) * N]) for h in range(2) for k in range(blocks)], axis=1
    )
    gated = own + lead * carried
    mean = jnp.mean(gated * gated, axis=1, keepdims=True)
    return (gated * lax.rsqrt(mean + 1e-05) * gain).astype(BF)


VMEM = pl.BlockSpec(memory_space=pltpu.VMEM)


def rows_of(ref, block):
    return ref[pl.ds(pl.multiple_of(block * CHUNK, CHUNK), CHUNK), :]


def finish_block(block, own, lead, c, incoming, gain):
    return finish_rows(
        rows_of(own, block), rows_of(lead, block), rows_of(c, block), incoming, gain[...]
    )


def fill_incoming(here, there, incoming):
    odd = lax.axis_index("seq") % 2
    incoming[odd] = here[...]
    incoming[1 - odd] = there[...]


def project_both(normed, w, start, columns, theirs, mine, at=0):
    wide = 512
    for k in range(0, columns, wide):
        out = dot(normed[...], w[:, start + k:start + k + wide])
        theirs[:, at + k:at + k + wide] = out[:CHUNK].astype(BF)
        mine[:, k:k + wide] = out[CHUNK:]


def far_kernel(columns, own, lead, c, here, there, gain, w, theirs, mine, normed, incoming):
    me = lax.axis_index("head")
    fill_incoming(here, there, incoming)
    normed[:CHUNK] = finish_block(me ^ 3, own, lead, c, incoming, gain)
    normed[CHUNK:] = finish_block(me ^ 2, own, lead, c, incoming, gain)
    project_both(normed, w, 0, columns, theirs, mine)


def more_kernel(start, columns, normed, w, theirs, mine):
    project_both(normed, w, start, columns, theirs, mine)


def mixed_kernel(
    start, columns, normed, own, lead, c, here, there, gain, w, theirs, mine, kept, incoming, given
):
    me = lax.axis_index("head")
    project_both(normed, w, start, columns, theirs, mine)
    fill_incoming(here, there, incoming)
    given[...] = finish_block(me ^ 1, own, lead, c, incoming, gain)
    kept[...] = finish_block(me, own, lead, c, incoming, gain)
    wide = 512
    for k in range(0, w.shape[1], wide):
        theirs[:, columns + k:columns + k + wide] = dot(given[...], w[:, k:k + wide]).astype(BF)


def kept_kernel(columns, kept, come, w, out):
    wide = 512
    for k in range(0, w.shape[1], wide):
        out[:, k:k + wide] = dot(kept[...], w[:, k:k + wide]) + come[
            :, columns + k:columns + k + wide
        ].astype(F32)


def add_kernel(mine, come, out):
    out[...] = (mine[...] + come[:, :out.shape[1]].astype(F32)).astype(BF)


def local_call(kernel, operands, outs, name, scratch=(), flops=0, limit=VMEM_LIMIT):
    return pl.pallas_call(
        kernel,
        in_specs=[VMEM] * len(operands),
        out_specs=[VMEM] * len(outs),
        out_shape=[jax.ShapeDtypeStruct(shape, dtype) for shape, dtype in outs],
        scratch_shapes=list(scratch),
        compiler_params=pltpu.CompilerParams(vmem_limit_bytes=limit),
        cost_estimate=pl.CostEstimate(flops=flops, bytes_accessed=0, transcendentals=0),
        name=name,
    )(*operands)


def pass_kernel(*refs):
    pass


def await_piece(piece, earlier):
    arrays = [piece, *earlier]
    return pl.pallas_call(
        pass_kernel,
        in_specs=[pl.BlockSpec(memory_space=pl.ANY)] * len(arrays),
        out_specs=[pl.BlockSpec(memory_space=pl.ANY)] * len(arrays),
        out_shape=[jax.ShapeDtypeStruct(v.shape, v.dtype) for v in arrays],
        input_output_aliases={k: k for k in range(len(arrays))},
        compiler_params=pltpu.CompilerParams(vmem_limit_bytes=1024 * 1024),
        cost_estimate=pl.CostEstimate(
            flops=20_000_000_000, bytes_accessed=100_000_000, transcendentals=0
        ),
        name="await_piece",
    )(*arrays)


def last_kernel(kept, third, second, first, out):
    at = 0
    for piece in (first, second, third):
        cut = slice(at, at + piece.shape[1])
        out[:, cut] = (kept[:, cut] + piece[...].astype(F32)).astype(BF)
        at += piece.shape[1]


def per_device(
    seq_count,
    ssm_input,
    gate_input,
    step_raw,
    decay_log,
    state_in,
    state_out,
    skip_gain,
    norm_gain,
    out_weight,
):
    tok = ssm_input.shape[0]
    heads = decay_log.shape[0]
    b = state_in.reshape(tok, N)
    c = state_out.reshape(tok, N)
    give, wk, aux = give_states(step_raw.T, decay_log.reshape(1, heads), ssm_input, b)
    keep = keep_states(wk, ssm_input, b)
    local = within(aux, ssm_input, b, c, gate_input, skip_gain.reshape(1, heads))
    (own, lead), here, there = incoming_states(
        give, keep, seq_count, lambda got: lax.optimization_barrier((local, got))
    )

    near = [(h, h ^ 1) for h in range(4)]
    far = [(h, h ^ 2) for h in range(4)]
    gain = norm_gain.reshape(1, -1)
    channels, dout = out_weight.shape
    rows = CHUNK
    states = pltpu.VMEM((2,) + here.shape, BF)
    finish = (own, lead, c, here, there, gain, out_weight)
    (_, one), (start2, two), (start3, three) = PIECES

    def piece_outs(columns, extra=0):
        return [((rows, columns + extra), BF), ((rows, columns), F32)]

    def add(mine, theirs):
        come = lax.ppermute(theirs, "head", near)
        return local_call(add_kernel, (mine, come), [(mine.shape, BF)], "add_pair", limit=1 << 22)[0], come

    theirs, mine, normed = local_call(
        functools.partial(far_kernel, one),
        finish,
        piece_outs(one) + [((2 * rows, channels), BF)],
        "finish_far",
        [states],
        4 * rows * channels * one,
    )
    first, _ = add(mine, theirs)
    theirs, mine = local_call(
        functools.partial(more_kernel, start2, two),
        (normed, out_weight),
        piece_outs(two),
        "project_more",
        flops=4 * rows * channels * two,
    )
    second, _ = add(mine, theirs)
    normed, first, second = lax.optimization_barrier((normed, first, second))
    theirs, mine, kept = local_call(
        functools.partial(mixed_kernel, start3, three),
        (normed,) + finish,
        piece_outs(three, dout) + [((rows, channels), BF)],
        "finish_near",
        [states, pltpu.VMEM((rows, channels), BF)],
        2 * rows * channels * (2 * three + dout),
    )
    third, come = add(mine, theirs)
    kept = local_call(
        functools.partial(kept_kernel, three),
        (kept, come, out_weight),
        [((rows, dout), F32)],
        "project_kept",
        flops=2 * rows * channels * dout,
    )[0]
    arrived = []
    for part in (first, second, third):
        arrived = await_piece(lax.ppermute(part, "head", far), arrived)
    return local_call(
        last_kernel, (kept, *arrived), [((rows, dout), BF)], "last_sums", limit=1 << 23
    )[0]


def solution(mesh):
    in_specs = (
        P("seq", "head"),
        P("seq", "head"),
        P("seq", "head"),
        P("head"),
        P("seq", "head", None),
        P("seq", "head", None),
        P("head"),
        P("head"),
        P("head", None),
    )
    out_specs = P(("seq", "head"), None)
    return jax.shard_map(
        functools.partial(per_device, mesh.shape["seq"]),
        mesh=mesh,
        in_specs=in_specs,
        out_specs=out_specs,
        check_vma=False,
    )
```

```python
import functools

import jax
import jax.numpy as jnp
from jax import lax
from jax.experimental import pallas as pl
from jax.experimental.pallas import tpu as pltpu
from jax.sharding import PartitionSpec as P

P_SIZE = 64
N = 128
CHUNK = 128
LANES = 128
BF = jnp.bfloat16
F32 = jnp.float32
VMEM_LIMIT = 16 * 1024 * 1024
WHOLE_VMEM = 61 * 1024 * 1024 + 512 * 1024
PIECES = ((0, 1024), (1024, 512), (1536, 1536), (3072, 1024))


def dot(a, b, contract=((1,), (0,)), precision=None):
    return lax.dot_general(a, b, (contract, ((), ())), precision=precision, preferred_element_type=F32)


def split2(v):
    hi = v.astype(BF)
    return hi, (v - hi.astype(F32)).astype(BF)


def split3(v):
    hi, rest = v.astype(BF), v
    rest = v - hi.astype(F32)
    mid = rest.astype(BF)
    return hi, mid, (rest - mid.astype(F32)).astype(BF)


def pick(rows, lanes, heads, per_head, first):
    r = lax.broadcasted_iota(jnp.int32, (rows, lanes), 0) % heads
    l = lax.broadcasted_iota(jnp.int32, (rows, lanes), 1) // per_head + first
    return jnp.where(r == l, 1.0, 0.0).astype(BF)


def step_vectors(raw, rate_row, wk, aux_ref):
    heads, tok = raw.shape
    chunks = tok // CHUNK
    step = jnp.maximum(raw, 0.0) + jnp.log1p(jnp.exp(-jnp.abs(raw)))
    r = lax.broadcasted_iota(jnp.int32, (heads, heads), 0)
    l = lax.broadcasted_iota(jnp.int32, (heads, heads), 1)
    rate = jnp.sum(jnp.where(r == l, rate_row, 0.0), axis=1, keepdims=True)
    logs = -step * jnp.exp(rate)
    parts = split3(logs)
    stacked = jnp.concatenate(
        [p[:, c * CHUNK:(c + 1) * CHUNK] for c in range(chunks) for p in parts], axis=0
    )
    s = lax.broadcasted_iota(jnp.int32, (CHUNK, 2 * CHUNK), 0)
    t = lax.broadcasted_iota(jnp.int32, (CHUNK, 2 * CHUNK), 1)
    tri = jnp.where(jnp.where(t < CHUNK, t - s, s - t + (CHUNK - 1)) >= 0, 1.0, 0.0).astype(BF)
    sums = dot(stacked, tri)
    pre, suf = [], []
    for c in range(chunks):
        base = 3 * heads * c
        total = (
            sums[base:base + heads] + sums[base + heads:base + 2 * heads]
        ) + sums[base + 2 * heads:base + 3 * heads]
        pre.append(total[:, :CHUNK])
        suf.append(total[:, CHUNK:])
    after = jnp.zeros((heads, 1), F32)
    for c in reversed(range(chunks)):
        w = step[:, c * CHUNK:(c + 1) * CHUNK] * jnp.exp(suf[c] + after)
        hi, lo = split2(w)
        wk[:heads, c * CHUNK:(c + 1) * CHUNK] = hi
        wk[heads:, c * CHUNK:(c + 1) * CHUNK] = lo
        after = after + pre[c][:, CHUNK - 1:]
    hi, lo = split2(jnp.broadcast_to(jnp.exp(after), (heads, CHUNK)))
    wk[:heads, tok:] = hi
    wk[heads:, tok:] = lo
    for c in range(chunks):
        aux_ref[c, :heads] = step[:, c * CHUNK:(c + 1) * CHUNK]
        aux_ref[c, heads:2 * heads] = pre[c]
        aux_ref[c, 2 * heads:] = suf[c]


def tail_rows(decays):
    r = lax.broadcasted_iota(jnp.int32, (16, LANES), 0)
    tail = jnp.zeros((16, LANES), F32)
    for k, decay in enumerate(decays):
        hi, lo = split2(decay)
        tail = jnp.where(r == 2 * k, hi.astype(F32), tail)
        tail = jnp.where(r == 2 * k + 1, lo.astype(F32), tail)
    return tail.astype(BF)


def decays_of(msg):
    blocks = (msg.shape[0] - 16) // N
    tail = msg[blocks * N:].astype(F32)
    return [tail[2 * k:2 * k + 1] + tail[2 * k + 1:2 * k + 2] for k in range(blocks)]


def half_message(x_ref, b, wk, first_head, msg):
    tok, lanes = x_ref.shape
    heads2 = wk.shape[0]
    width = 256
    decays = []
    for g in range(lanes // width):
        chosen = pick(heads2, width, heads2 // 2, P_SIZE, first_head + g * (width // P_SIZE))
        spread = dot(wk[...], chosen, ((0,), (0,)))
        weighted = (x_ref[:, g * width:(g + 1) * width] * spread[:tok]).astype(BF)
        state = dot(b, weighted, ((0,), (0,)))
        for i in range(width // LANES):
            k = g * (width // LANES) + i
            msg[k * N:(k + 1) * N] = state[:, i * LANES:(i + 1) * LANES].astype(BF)
            decays.append(spread[tok:tok + 1, i * LANES:(i + 1) * LANES])
    msg[msg.shape[0] - 16:] = tail_rows(decays)


def half_kernel(give, raw, rate, x, b, msg, wk, aux, raw_v, rate_v, x_v, b_v, sems):
    lanes = x_v.shape[1]
    mine = lax.axis_index("seq") % 2
    half = 1 - mine if give else mine
    loads = [
        pltpu.make_async_copy(b, b_v, sems.at[0]),
        pltpu.make_async_copy(
            x.at[:, pl.ds(pl.multiple_of(half * lanes, lanes), lanes)], x_v, sems.at[1]
        ),
    ]
    if give:
        loads += [
            pltpu.make_async_copy(raw, raw_v, sems.at[2]),
            pltpu.make_async_copy(rate, rate_v, sems.at[3]),
        ]
    for load in reversed(loads):
        load.start()
    if give:
        loads[2].wait()
        loads[3].wait()
        step_vectors(raw_v[...], rate_v[...], wk, aux)
    loads[0].wait()
    loads[1].wait()
    half_message(x_v, b_v[...].astype(BF), wk, half * (lanes // P_SIZE), msg)


def give_kernel(raw, rate, x, b, msg, wk, aux, raw_v, rate_v, x_v, b_v, sems):
    half_kernel(True, raw, rate, x, b, msg, wk, aux, raw_v, rate_v, x_v, b_v, sems)


def keep_kernel(wk, x, b, msg, x_v, b_v, sems):
    half_kernel(False, None, None, x, b, msg, wk, None, None, None, x_v, b_v, sems)


HBM = pl.BlockSpec(memory_space=pltpu.HBM)


def give_states(raw, rate, x, b):
    heads, tok = raw.shape
    lanes = x.shape[1] // 2
    return pl.pallas_call(
        give_kernel,
        in_specs=[HBM] * 4,
        out_shape=[
            jax.ShapeDtypeStruct((lanes + 16, LANES), BF),
            jax.ShapeDtypeStruct((2 * heads, tok + CHUNK), BF),
            jax.ShapeDtypeStruct((tok // CHUNK, 3 * heads, CHUNK), F32),
        ],
        scratch_shapes=[
            pltpu.VMEM((heads, tok), F32),
            pltpu.VMEM((1, heads), F32),
            pltpu.VMEM((tok, lanes), F32),
            pltpu.VMEM((tok, N), F32),
            pltpu.SemaphoreType.DMA((4,)),
        ],
        compiler_params=pltpu.CompilerParams(vmem_limit_bytes=WHOLE_VMEM),
        cost_estimate=pl.CostEstimate(flops=200_000_000, bytes_accessed=1_500_000, transcendentals=0),
        name="give_states",
    )(raw, rate, x, b)


def keep_states(wk, x, b):
    tok = x.shape[0]
    lanes = x.shape[1] // 2
    return pl.pallas_call(
        keep_kernel,
        in_specs=[pl.BlockSpec(memory_space=pltpu.VMEM), HBM, HBM],
        out_shape=jax.ShapeDtypeStruct((lanes + 16, LANES), BF),
        scratch_shapes=[
            pltpu.VMEM((tok, lanes), F32),
            pltpu.VMEM((tok, N), F32),
            pltpu.SemaphoreType.DMA((2,)),
        ],
        compiler_params=pltpu.CompilerParams(vmem_limit_bytes=VMEM_LIMIT),
        cost_estimate=pl.CostEstimate(flops=200_000_000, bytes_accessed=1_500_000, transcendentals=0),
        name="keep_states",
    )(wk, x, b)


def link(later, earlier, out):
    ahead, behind = decays_of(later), decays_of(earlier)
    for k, decay in enumerate(ahead):
        rows = slice(k * N, (k + 1) * N)
        out[rows] = (later[rows].astype(F32) + decay * earlier[rows].astype(F32)).astype(BF)
    out[len(ahead) * N:] = tail_rows([p * q for p, q in zip(ahead, behind)])


def pair_kernel(own, come, out):
    odd = lax.axis_index("seq") % 2

    @pl.when(odd == 0)
    def _():
        link(come, own, out)

    @pl.when(odd == 1)
    def _():
        link(own, come, out)


def end_kernel(last, before, own, come, mine, theirs):
    blocks = mine.shape[0] // N
    odd = lax.axis_index("seq") % 2

    def fill(even_section, ahead_ref, behind_ref):
        step, span = decays_of(last), decays_of(even_section)
        for k in range(blocks):
            rows = slice(k * N, (k + 1) * N)
            start = last[rows].astype(F32)
            if before is not None:
                start = start + step[k] * before[rows].astype(F32)
            ahead_ref[rows] = start.astype(BF)
            behind_ref[rows] = (even_section[rows].astype(F32) + span[k] * start).astype(BF)

    @pl.when(odd == 0)
    def _():
        fill(own, mine, theirs)

    @pl.when(odd == 1)
    def _():
        fill(come, theirs, mine)


def scan_call(kernel, operands, shapes, name):
    return pl.pallas_call(
        kernel,
        out_shape=[jax.ShapeDtypeStruct(shape, BF) for shape in shapes],
        compiler_params=pltpu.CompilerParams(vmem_limit_bytes=VMEM_LIMIT),
        cost_estimate=pl.CostEstimate(flops=500_000, bytes_accessed=400_000, transcendentals=0),
        name=name,
    )(*operands)


def incoming_states(give, keep, count, hold):
    pair = [(s, s ^ 1) for s in range(count)]
    come = lax.ppermute(give, "seq", pair)
    run = scan_call(pair_kernel, (keep, come), [keep.shape], "join_pair")[0]
    start, distance = None, 2
    while distance < count:
        got = lax.ppermute(run, "seq", [(s, s + distance) for s in range(count - distance)])
        if distance * 2 >= count:
            break
        run = scan_call(link, (run, got), [keep.shape], "join_run")[0]
        start = got if start is None else scan_call(link, (start, got), [keep.shape], "join_start")[0]
        distance *= 2
    hold, got = hold(got)
    half = (keep.shape[0] - 16, LANES)
    mine, theirs = scan_call(end_kernel, (start, got, keep, come), [half, half], "join_end")
    return hold, mine, lax.ppermute(theirs, "seq", pair)


def rows_of(ref, block):
    return ref[pl.ds(pl.multiple_of(block * CHUNK, CHUNK), CHUNK), :]


def within_kernel(
    far, aux, x_ref, b_ref, c_ref, gate_ref, skip_ref, own_ref, lead_ref,
    scores, trip, duo, early, lines, state,
):
    g = pl.program_id(0)
    width = x_ref.shape[1]
    heads = aux.shape[1] // 3
    here = width // P_SIZE
    half = lax.axis_index("head") // 2
    half = 1 - half if far else half

    @pl.when(g == 0)
    def _():
        def vectors(c):
            return [aux[c, k * heads:(k + 1) * heads] for k in range(3)]

        def put(ref, i, values):
            for k, value in enumerate(values):
                hi, lo = split2(value)
                ref[i, :heads, k * CHUNK:(k + 1) * CHUNK] = hi
                ref[i, heads:, k * CHUNK:(k + 1) * CHUNK] = lo

        before = jnp.zeros((heads, 1), F32)
        for i in range(2):
            step, pre, suf = vectors(i)
            put(early, i, (step * jnp.exp(suf), jnp.exp(pre)))
            before = before + jnp.where(half == 1, pre[:, CHUNK - 1:], 0.0)
        r = lax.broadcasted_iota(jnp.int32, (CHUNK, CHUNK), 0)
        l = lax.broadcasted_iota(jnp.int32, (CHUNK, CHUNK), 1)
        for i in range(2):
            step, pre, suf = vectors(2 * half + i)
            trip[i] = jnp.concatenate(split3(pre), axis=0)
            put(duo, i, (step, step * jnp.exp(suf), jnp.exp(pre), jnp.exp(pre + before)))
            before = before + pre[:, CHUNK - 1:]
            for k in range(heads // here):
                lines[k, :here, i * CHUNK:(i + 1) * CHUNK] = pre[k * here:(k + 1) * here]
            raw = dot(
                rows_of(c_ref, 2 * half + i),
                rows_of(b_ref, 2 * half + i),
                ((1,), (1,)),
                lax.Precision.HIGHEST,
            )
            scores[i] = jnp.where(r >= l, raw, 0.0)

    spread = pick(2 * heads, width, heads, P_SIZE, g * here)
    columns = pick(3 * heads, here * CHUNK, heads, CHUNK, g * here)
    gains = jnp.broadcast_to(jnp.concatenate(split3(skip_ref[...]), axis=1), (8, 3 * heads))
    skip = dot(gains, pick(3 * heads, width, heads, P_SIZE, g * here))[:1]
    lane = lax.broadcasted_iota(jnp.int32, (CHUNK, LANES), 1)
    mine = lines[g]

    def follow(c, last, weights):
        weighted = (rows_of(x_ref, c) * weights).astype(BF)
        added = dot(rows_of(b_ref, c).astype(BF), weighted, ((0,), (0,)))
        state[...] = state[...] * last + added

    state[...] = jnp.zeros_like(state)

    @pl.when(half == 1)
    def _():
        for i in range(2):
            wide = dot(early[i], spread, ((0,), (0,)))
            follow(i, wide[2 * CHUNK - 1:], wide[:CHUNK])

    for i in range(2):
        cut = slice(i * CHUNK, (i + 1) * CHUNK)
        block = 2 * half + i
        wide = dot(duo[i], spread, ((0,), (0,)))
        x = rows_of(x_ref, block)
        stepped = x * wide[:CHUNK]
        lead = wide[2 * CHUNK:3 * CHUNK]
        tall = dot(trip[i], columns, ((0,), (0,)))
        outs = []
        for pair in range(here // 2):
            mixes = []
            for h in (2 * pair, 2 * pair + 1):
                gap = tall[:, h * CHUNK:(h + 1) * CHUNK] - mine[h:h + 1, cut]
                mixes.append((scores[i] * jnp.exp(jnp.minimum(gap, 0.0))).astype(BF))
            both = stepped[:, pair * LANES:(pair + 1) * LANES]
            stacked = jnp.concatenate(
                [
                    jnp.where(lane < P_SIZE, both, 0.0).astype(BF),
                    jnp.where(lane < P_SIZE, 0.0, both).astype(BF),
                ],
                axis=0,
            )
            outs.append(dot(jnp.concatenate(mixes, axis=1), stacked))
        y = jnp.concatenate(outs, axis=1) + skip * x
        y = y + lead * dot(rows_of(c_ref, block).astype(BF), state[...].astype(BF))
        v = rows_of(gate_ref, block).astype(F32)
        silu = v / (1.0 + jnp.exp(-v))
        own_ref[cut] = y * silu
        lead_ref[cut] = wide[3 * CHUNK:] * silu
        if i == 0:
            follow(block, lead[CHUNK - 1:], wide[CHUNK:2 * CHUNK])


def within(far, aux, x, b, c, gate, skip):
    tok, channels = x.shape
    chunks, heads3, _ = aux.shape
    heads = heads3 // 3
    width = 256
    return pl.pallas_call(
        functools.partial(within_kernel, far),
        grid=(channels // width,),
        in_specs=[
            pl.BlockSpec(aux.shape, lambda g: (0, 0, 0)),
            pl.BlockSpec((tok, width), lambda g: (0, g)),
            pl.BlockSpec((tok, N), lambda g: (0, 0)),
            pl.BlockSpec((tok, N), lambda g: (0, 0)),
            pl.BlockSpec((tok, width), lambda g: (0, g)),
            pl.BlockSpec((1, heads), lambda g: (0, 0)),
        ],
        out_specs=[pl.BlockSpec((2 * CHUNK, width), lambda g: (0, g))] * 2,
        out_shape=[jax.ShapeDtypeStruct((2 * CHUNK, channels), F32)] * 2,
        scratch_shapes=[
            pltpu.VMEM((2, CHUNK, CHUNK), F32),
            pltpu.VMEM((2, 3 * heads, CHUNK), BF),
            pltpu.VMEM((2, 2 * heads, 4 * CHUNK), BF),
            pltpu.VMEM((2, 2 * heads, 2 * CHUNK), BF),
            pltpu.VMEM((channels // width, 8, 2 * CHUNK), F32),
            pltpu.VMEM((N, width), F32),
        ],
        compiler_params=pltpu.CompilerParams(vmem_limit_bytes=VMEM_LIMIT),
        cost_estimate=pl.CostEstimate(
            flops=4_000_000_000, bytes_accessed=3_000_000, transcendentals=500_000
        ),
        name="within_far" if far else "within_near",
    )(aux, x, b, c, gate, skip)


def finish_rows(own, lead, c, incoming, gain):
    c = c.astype(BF)
    blocks = incoming.shape[1] // N
    carried = jnp.concatenate(
        [dot(c, incoming[h, k * N:(k + 1) * N]) for h in range(2) for k in range(blocks)], axis=1
    )
    gated = own + lead * carried
    mean = jnp.mean(gated * gated, axis=1, keepdims=True)
    return (gated * lax.rsqrt(mean + 1e-05) * gain).astype(BF)


VMEM = pl.BlockSpec(memory_space=pltpu.VMEM)


def finish_block(block, own, lead, c, incoming, gain):
    return finish_rows(
        rows_of(own, block % 2), rows_of(lead, block % 2), rows_of(c, block), incoming, gain[...]
    )


def fill_incoming(here, there, incoming):
    odd = lax.axis_index("seq") % 2
    incoming[odd] = here[...]
    incoming[1 - odd] = there[...]


def project_both(normed, w, start, columns, theirs, mine, at=0):
    wide = 512
    for k in range(0, columns, wide):
        out = dot(normed[...], w[:, start + k:start + k + wide])
        theirs[:, at + k:at + k + wide] = out[:CHUNK].astype(BF)
        mine[:, k:k + wide] = out[CHUNK:]


def far_kernel(columns, own, lead, c, here, there, gain, w, theirs, mine, normed, incoming):
    me = lax.axis_index("head")
    fill_incoming(here, there, incoming)
    normed[:CHUNK] = finish_block(me ^ 3, own, lead, c, incoming, gain)
    normed[CHUNK:] = finish_block(me ^ 2, own, lead, c, incoming, gain)
    project_both(normed, w, 0, columns, theirs, mine)


def more_kernel(start, columns, normed, w, theirs, mine):
    project_both(normed, w, start, columns, theirs, mine)


def mixed_kernel(
    start, columns, normed, own, lead, c, here, there, gain, w, theirs, mine, kept, incoming, given
):
    me = lax.axis_index("head")
    project_both(normed, w, start, columns, theirs, mine)
    fill_incoming(here, there, incoming)
    given[...] = finish_block(me ^ 1, own, lead, c, incoming, gain)
    kept[...] = finish_block(me, own, lead, c, incoming, gain)
    wide = 512
    for k in range(0, w.shape[1], wide):
        theirs[:, columns + k:columns + k + wide] = dot(given[...], w[:, k:k + wide]).astype(BF)


def kept_kernel(columns, kept, come, w, out):
    wide = 512
    for k in range(0, w.shape[1], wide):
        out[:, k:k + wide] = dot(kept[...], w[:, k:k + wide]) + come[
            :, columns + k:columns + k + wide
        ].astype(F32)


def add_kernel(mine, come, out):
    out[...] = (mine[...] + come[:, :out.shape[1]].astype(F32)).astype(BF)


def local_call(kernel, operands, outs, name, scratch=(), flops=0, limit=VMEM_LIMIT):
    return pl.pallas_call(
        kernel,
        in_specs=[VMEM] * len(operands),
        out_specs=[VMEM] * len(outs),
        out_shape=[jax.ShapeDtypeStruct(shape, dtype) for shape, dtype in outs],
        scratch_shapes=list(scratch),
        compiler_params=pltpu.CompilerParams(vmem_limit_bytes=limit),
        cost_estimate=pl.CostEstimate(flops=flops, bytes_accessed=0, transcendentals=0),
        name=name,
    )(*operands)


def pass_kernel(*refs):
    pass


def await_piece(piece, *earlier):
    arrays = [piece, *earlier]
    return pl.pallas_call(
        pass_kernel,
        in_specs=[pl.BlockSpec(memory_space=pl.ANY)] * len(arrays),
        out_specs=[pl.BlockSpec(memory_space=pl.ANY)] * len(arrays),
        out_shape=[jax.ShapeDtypeStruct(v.shape, v.dtype) for v in arrays],
        input_output_aliases={k: k for k in range(len(arrays))},
        compiler_params=pltpu.CompilerParams(vmem_limit_bytes=1024 * 1024),
        cost_estimate=pl.CostEstimate(
            flops=20_000_000_000, bytes_accessed=100_000_000, transcendentals=0
        ),
        name="await_piece",
    )(*arrays)


def early_kernel(kept, first, second, third, out):
    at = 0
    for piece in (first, second, third):
        cut = slice(at, at + piece.shape[1])
        out[:, cut] = (kept[:, cut] + piece[...].astype(F32)).astype(BF)
        at += piece.shape[1]


def early_sums(kept, first, second, third):
    rows = first.shape[0]
    wide = first.shape[1] + second.shape[1] + third.shape[1]
    return pl.pallas_call(
        early_kernel,
        grid=(1,),
        in_specs=[VMEM] * 4,
        out_specs=pl.BlockSpec((rows, wide), lambda j: (0, 0)),
        out_shape=jax.ShapeDtypeStruct(kept.shape, BF),
        compiler_params=pltpu.CompilerParams(vmem_limit_bytes=VMEM_LIMIT),
        name="early_sums",
    )(kept, first, second, third)


def last_kernel(kept, third, filled, out):
    out[...] = (kept[...] + third[...].astype(F32)).astype(BF)


def last_sums(kept, third, filled):
    rows, wide = third.shape
    last = kept.shape[1] // wide - 1
    return pl.pallas_call(
        last_kernel,
        grid=(1,),
        in_specs=[
            pl.BlockSpec((rows, wide), lambda j: (0, last)),
            pl.BlockSpec((rows, wide), lambda j: (0, 0)),
            pl.BlockSpec(memory_space=pl.ANY),
        ],
        out_specs=pl.BlockSpec((rows, wide), lambda j: (0, last)),
        out_shape=jax.ShapeDtypeStruct(kept.shape, BF),
        input_output_aliases={2: 0},
        compiler_params=pltpu.CompilerParams(vmem_limit_bytes=VMEM_LIMIT),
        name="last_sums",
    )(kept, third, filled)


def per_device(
    seq_count,
    ssm_input,
    gate_input,
    step_raw,
    decay_log,
    state_in,
    state_out,
    skip_gain,
    norm_gain,
    out_weight,
):
    tok = ssm_input.shape[0]
    heads = decay_log.shape[0]
    b = state_in.reshape(tok, N)
    c = state_out.reshape(tok, N)
    give, wk, aux = give_states(step_raw.T, decay_log.reshape(1, heads), ssm_input, b)
    keep = keep_states(wk, ssm_input, b)
    inputs = (ssm_input, b, c, gate_input, skip_gain.reshape(1, heads))
    local = within(True, aux, *inputs)
    (own, lead), here, there = incoming_states(
        give, keep, seq_count, lambda got: lax.optimization_barrier((local, got))
    )

    near = [(h, h ^ 1) for h in range(4)]
    far = [(h, h ^ 2) for h in range(4)]
    gain = norm_gain.reshape(1, -1)
    channels, dout = out_weight.shape
    rows = CHUNK
    states = pltpu.VMEM((2,) + here.shape, BF)
    finish = (own, lead, c, here, there, gain, out_weight)
    (_, one), (start2, two), (start3, three), (start4, four) = PIECES

    def piece_outs(columns, extra=0):
        return [((rows, columns + extra), BF), ((rows, columns), F32)]

    def add(mine, theirs):
        come = lax.ppermute(theirs, "head", near)
        return local_call(add_kernel, (mine, come), [(mine.shape, BF)], "add_pair", limit=1 << 22)[0], come

    theirs, mine, normed = local_call(
        functools.partial(far_kernel, one),
        finish,
        piece_outs(one) + [((2 * rows, channels), BF)],
        "finish_far",
        [states],
        4 * rows * channels * one,
    )
    first, _ = add(mine, theirs)
    normed, first = lax.optimization_barrier((normed, first))

    def more(start, columns):
        theirs, mine = local_call(
            functools.partial(more_kernel, start, columns),
            (normed, out_weight),
            piece_outs(columns),
            "project_more",
            flops=4 * rows * channels * columns,
        )
        return add(mine, theirs)[0]

    second = more(start2, two)
    normed, aux, second = lax.optimization_barrier((normed, aux, second))
    near_own, near_lead = within(False, aux, *inputs)
    third = more(start3, three)
    normed, third = lax.optimization_barrier((normed, third))
    theirs, mine, kept = local_call(
        functools.partial(mixed_kernel, start4, four),
        (normed, near_own, near_lead) + finish[2:],
        piece_outs(four, dout) + [((rows, channels), BF)],
        "finish_near",
        [states, pltpu.VMEM((rows, channels), BF)],
        2 * rows * channels * (2 * four + dout),
    )
    fourth, come = add(mine, theirs)
    kept = local_call(
        functools.partial(kept_kernel, four),
        (kept, come, out_weight),
        [((rows, dout), F32)],
        "project_kept",
        flops=2 * rows * channels * dout,
    )[0]
    arrived = []
    for part in (first, second, third):
        arrived = await_piece(lax.ppermute(part, "head", far), *arrived)
    filled = early_sums(kept, *reversed(arrived))
    fourth, filled = await_piece(lax.ppermute(fourth, "head", far), filled)
    return last_sums(kept, fourth, filled)


def solution(mesh):
    in_specs = (
        P("seq", "head"),
        P("seq", "head"),
        P("seq", "head"),
        P("head"),
        P("seq", "head", None),
        P("seq", "head", None),
        P("head"),
        P("head"),
        P("head", None),
    )
    out_specs = P(("seq", "head"), None)
    return jax.shard_map(
        functools.partial(per_device, mesh.shape["seq"]),
        mesh=mesh,
        in_specs=in_specs,
        out_specs=out_specs,
        check_vma=False,
    )
```

```python
import functools

import jax
import jax.numpy as jnp
from jax import lax
from jax.experimental import pallas as pl
from jax.experimental.pallas import tpu as pltpu
from jax.sharding import PartitionSpec as P

P_SIZE = 64
N = 128
CHUNK = 128
LANES = 128
BF = jnp.bfloat16
F32 = jnp.float32
VMEM_LIMIT = 16 * 1024 * 1024
WHOLE_VMEM = 61 * 1024 * 1024 + 512 * 1024
PIECES = ((0, 1024), (1024, 1536), (2560, 1536))


def dot(a, b, contract=((1,), (0,)), precision=None):
    return lax.dot_general(a, b, (contract, ((), ())), precision=precision, preferred_element_type=F32)


def split2(v):
    hi = v.astype(BF)
    return hi, (v - hi.astype(F32)).astype(BF)


def split3(v):
    hi, rest = v.astype(BF), v
    rest = v - hi.astype(F32)
    mid = rest.astype(BF)
    return hi, mid, (rest - mid.astype(F32)).astype(BF)


def pick(rows, lanes, heads, per_head, first):
    r = lax.broadcasted_iota(jnp.int32, (rows, lanes), 0) % heads
    l = lax.broadcasted_iota(jnp.int32, (rows, lanes), 1) // per_head + first
    return jnp.where(r == l, 1.0, 0.0).astype(BF)


def step_vectors(raw, rate_row, wk, aux_ref):
    heads, tok = raw.shape
    chunks = tok // CHUNK
    step = jnp.maximum(raw, 0.0) + jnp.log1p(jnp.exp(-jnp.abs(raw)))
    r = lax.broadcasted_iota(jnp.int32, (heads, heads), 0)
    l = lax.broadcasted_iota(jnp.int32, (heads, heads), 1)
    rate = jnp.sum(jnp.where(r == l, rate_row, 0.0), axis=1, keepdims=True)
    logs = -step * jnp.exp(rate)
    parts = split3(logs)
    stacked = jnp.concatenate(
        [p[:, c * CHUNK:(c + 1) * CHUNK] for c in range(chunks) for p in parts], axis=0
    )
    s = lax.broadcasted_iota(jnp.int32, (CHUNK, 2 * CHUNK), 0)
    t = lax.broadcasted_iota(jnp.int32, (CHUNK, 2 * CHUNK), 1)
    tri = jnp.where(jnp.where(t < CHUNK, t - s, s - t + (CHUNK - 1)) >= 0, 1.0, 0.0).astype(BF)
    sums = dot(stacked, tri)
    pre, suf = [], []
    for c in range(chunks):
        base = 3 * heads * c
        total = (
            sums[base:base + heads] + sums[base + heads:base + 2 * heads]
        ) + sums[base + 2 * heads:base + 3 * heads]
        pre.append(total[:, :CHUNK])
        suf.append(total[:, CHUNK:])
    after = jnp.zeros((heads, 1), F32)
    for c in reversed(range(chunks)):
        w = step[:, c * CHUNK:(c + 1) * CHUNK] * jnp.exp(suf[c] + after)
        hi, lo = split2(w)
        wk[:heads, c * CHUNK:(c + 1) * CHUNK] = hi
        wk[heads:, c * CHUNK:(c + 1) * CHUNK] = lo
        after = after + pre[c][:, CHUNK - 1:]
    hi, lo = split2(jnp.broadcast_to(jnp.exp(after), (heads, CHUNK)))
    wk[:heads, tok:] = hi
    wk[heads:, tok:] = lo
    for c in range(chunks):
        aux_ref[c, :heads] = step[:, c * CHUNK:(c + 1) * CHUNK]
        aux_ref[c, heads:2 * heads] = pre[c]
        aux_ref[c, 2 * heads:] = suf[c]


def tail_rows(decays):
    r = lax.broadcasted_iota(jnp.int32, (16, LANES), 0)
    tail = jnp.zeros((16, LANES), F32)
    for k, decay in enumerate(decays):
        hi, lo = split2(decay)
        tail = jnp.where(r == 2 * k, hi.astype(F32), tail)
        tail = jnp.where(r == 2 * k + 1, lo.astype(F32), tail)
    return tail.astype(BF)


def decays_of(msg):
    blocks = (msg.shape[0] - 16) // N
    tail = msg[blocks * N:].astype(F32)
    return [tail[2 * k:2 * k + 1] + tail[2 * k + 1:2 * k + 2] for k in range(blocks)]


def half_message(x_ref, b, wk, first_head, msg):
    tok, lanes = x_ref.shape
    heads2 = wk.shape[0]
    width = 256
    decays = []
    for g in range(lanes // width):
        chosen = pick(heads2, width, heads2 // 2, P_SIZE, first_head + g * (width // P_SIZE))
        spread = dot(wk[...], chosen, ((0,), (0,)))
        weighted = (x_ref[:, g * width:(g + 1) * width] * spread[:tok]).astype(BF)
        state = dot(b, weighted, ((0,), (0,)))
        for i in range(width // LANES):
            k = g * (width // LANES) + i
            msg[k * N:(k + 1) * N] = state[:, i * LANES:(i + 1) * LANES].astype(BF)
            decays.append(spread[tok:tok + 1, i * LANES:(i + 1) * LANES])
    msg[msg.shape[0] - 16:] = tail_rows(decays)


def half_kernel(give, raw, rate, x, b, msg, wk, aux, raw_v, rate_v, x_v, b_v, sems):
    lanes = x_v.shape[1]
    mine = lax.axis_index("seq") % 2
    half = 1 - mine if give else mine
    loads = [
        pltpu.make_async_copy(b, b_v, sems.at[0]),
        pltpu.make_async_copy(
            x.at[:, pl.ds(pl.multiple_of(half * lanes, lanes), lanes)], x_v, sems.at[1]
        ),
    ]
    if give:
        loads += [
            pltpu.make_async_copy(raw, raw_v, sems.at[2]),
            pltpu.make_async_copy(rate, rate_v, sems.at[3]),
        ]
    for load in reversed(loads):
        load.start()
    if give:
        loads[2].wait()
        loads[3].wait()
        step_vectors(raw_v[...], rate_v[...], wk, aux)
    loads[0].wait()
    loads[1].wait()
    half_message(x_v, b_v[...].astype(BF), wk, half * (lanes // P_SIZE), msg)


def give_kernel(raw, rate, x, b, msg, wk, aux, raw_v, rate_v, x_v, b_v, sems):
    half_kernel(True, raw, rate, x, b, msg, wk, aux, raw_v, rate_v, x_v, b_v, sems)


def keep_kernel(wk, x, b, msg, x_v, b_v, sems):
    half_kernel(False, None, None, x, b, msg, wk, None, None, None, x_v, b_v, sems)


HBM = pl.BlockSpec(memory_space=pltpu.HBM)
VMEM = pl.BlockSpec(memory_space=pltpu.VMEM)


def give_states(raw, rate, x, b):
    heads, tok = raw.shape
    lanes = x.shape[1] // 2
    return pl.pallas_call(
        give_kernel,
        in_specs=[HBM] * 4,
        out_shape=[
            jax.ShapeDtypeStruct((lanes + 16, LANES), BF),
            jax.ShapeDtypeStruct((2 * heads, tok + CHUNK), BF),
            jax.ShapeDtypeStruct((tok // CHUNK, 3 * heads, CHUNK), F32),
        ],
        scratch_shapes=[
            pltpu.VMEM((heads, tok), F32),
            pltpu.VMEM((1, heads), F32),
            pltpu.VMEM((tok, lanes), F32),
            pltpu.VMEM((tok, N), F32),
            pltpu.SemaphoreType.DMA((4,)),
        ],
        compiler_params=pltpu.CompilerParams(vmem_limit_bytes=WHOLE_VMEM),
        cost_estimate=pl.CostEstimate(flops=200_000_000, bytes_accessed=1_500_000, transcendentals=0),
        name="give_states",
    )(raw, rate, x, b)


def keep_states(wk, x, b):
    tok = x.shape[0]
    lanes = x.shape[1] // 2
    return pl.pallas_call(
        keep_kernel,
        in_specs=[pl.BlockSpec(memory_space=pltpu.VMEM), HBM, HBM],
        out_shape=jax.ShapeDtypeStruct((lanes + 16, LANES), BF),
        scratch_shapes=[
            pltpu.VMEM((tok, lanes), F32),
            pltpu.VMEM((tok, N), F32),
            pltpu.SemaphoreType.DMA((2,)),
        ],
        compiler_params=pltpu.CompilerParams(vmem_limit_bytes=VMEM_LIMIT),
        cost_estimate=pl.CostEstimate(flops=200_000_000, bytes_accessed=1_500_000, transcendentals=0),
        name="keep_states",
    )(wk, x, b)


def link(later, earlier, out):
    ahead, behind = decays_of(later), decays_of(earlier)
    for k, decay in enumerate(ahead):
        rows = slice(k * N, (k + 1) * N)
        out[rows] = (later[rows].astype(F32) + decay * earlier[rows].astype(F32)).astype(BF)
    out[len(ahead) * N:] = tail_rows([p * q for p, q in zip(ahead, behind)])


def pair_kernel(own, come, out):
    odd = lax.axis_index("seq") % 2

    @pl.when(odd == 0)
    def _():
        link(come, own, out)

    @pl.when(odd == 1)
    def _():
        link(own, come, out)


def end_kernel(last, before, own, come, mine, theirs):
    blocks = mine.shape[0] // N
    odd = lax.axis_index("seq") % 2

    def fill(even_section, ahead_ref, behind_ref):
        step, span = decays_of(last), decays_of(even_section)
        for k in range(blocks):
            rows = slice(k * N, (k + 1) * N)
            start = last[rows].astype(F32)
            if before is not None:
                start = start + step[k] * before[rows].astype(F32)
            ahead_ref[rows] = start.astype(BF)
            behind_ref[rows] = (even_section[rows].astype(F32) + span[k] * start).astype(BF)

    @pl.when(odd == 0)
    def _():
        fill(own, mine, theirs)

    @pl.when(odd == 1)
    def _():
        fill(come, theirs, mine)


def scan_call(kernel, operands, shapes, name):
    return pl.pallas_call(
        kernel,
        out_shape=[jax.ShapeDtypeStruct(shape, BF) for shape in shapes],
        compiler_params=pltpu.CompilerParams(vmem_limit_bytes=VMEM_LIMIT),
        cost_estimate=pl.CostEstimate(flops=500_000, bytes_accessed=400_000, transcendentals=0),
        name=name,
    )(*operands)


def incoming_states(give, keep, count, hold):
    pair = [(s, s ^ 1) for s in range(count)]
    come = lax.ppermute(give, "seq", pair)
    run = scan_call(pair_kernel, (keep, come), [keep.shape], "join_pair")[0]
    start, distance = None, 2
    while distance < count:
        got = lax.ppermute(run, "seq", [(s, s + distance) for s in range(count - distance)])
        if distance * 2 >= count:
            break
        run = scan_call(link, (run, got), [keep.shape], "join_run")[0]
        start = got if start is None else scan_call(link, (start, got), [keep.shape], "join_start")[0]
        distance *= 2
    hold, got = hold(got)
    half = (keep.shape[0] - 16, LANES)
    mine, theirs = scan_call(end_kernel, (start, got, keep, come), [half, half], "join_end")
    return hold, mine, lax.ppermute(theirs, "seq", pair)


def rows_of(ref, block):
    return ref[pl.ds(pl.multiple_of(block * CHUNK, CHUNK), CHUNK), :]


def within_kernel(far, aux, x_ref, b_ref, c_ref, gate_ref, skip_ref, own_ref, lead_ref):
    channels = x_ref.shape[1]
    heads = aux.shape[1] // 3
    width = 256
    here = width // P_SIZE
    half = lax.axis_index("head") // 2
    half = 1 - half if far else half
    second = half == 1

    def vectors(c):
        return [aux[c, k * heads:(k + 1) * heads] for k in range(3)]

    def put(values):
        return jnp.concatenate([jnp.concatenate(split2(v), axis=0) for v in values], axis=1)

    first, then = vectors(0), vectors(1)
    ends = [v[1][:, CHUNK - 1:] for v in (first, then)]
    early = put(
        [
            jnp.where(second, first[0] * jnp.exp(first[2] + ends[1]), 0.0),
            jnp.where(second, then[0] * jnp.exp(then[2]), 0.0),
        ]
    )
    before = jnp.where(second, ends[0] + ends[1], 0.0)
    r = lax.broadcasted_iota(jnp.int32, (CHUNK, CHUNK), 0)
    l = lax.broadcasted_iota(jnp.int32, (CHUNK, CHUNK), 1)
    duo, trip, lines, scores, rows_b, rows_c, rows_x, rows_g = ([] for _ in range(8))
    for i in range(2):
        block = 2 * half + i
        step, pre, suf = vectors(block)
        duo.append(put((step, step * jnp.exp(suf), jnp.exp(pre), jnp.exp(pre + before))))
        trip.append(jnp.concatenate(split3(pre), axis=0))
        lines.append(pre)
        before = before + pre[:, CHUNK - 1:]
        b, c = rows_of(b_ref, block), rows_of(c_ref, block)
        raw = dot(c, b, ((1,), (1,)), lax.Precision.HIGHEST)
        scores.append(jnp.where(r >= l, raw, 0.0))
        rows_b.append(b.astype(BF))
        rows_c.append(c.astype(BF))
        rows_x.append(rows_of(x_ref, block))
        rows_g.append(rows_of(gate_ref, block))
    early_b = b_ref[:2 * CHUNK].astype(BF)
    gains = jnp.broadcast_to(jnp.concatenate(split3(skip_ref[...]), axis=1), (8, 3 * heads))
    lane = lax.broadcasted_iota(jnp.int32, (CHUNK, LANES), 1)
    for g in range(channels // width):
        at = slice(g * width, (g + 1) * width)
        spread = pick(2 * heads, width, heads, P_SIZE, g * here)
        columns = pick(3 * heads, here * CHUNK, heads, CHUNK, g * here)
        skip = dot(gains, pick(3 * heads, width, heads, P_SIZE, g * here))[:1]
        weights = dot(early, spread, ((0,), (0,)))
        state = dot(early_b, (x_ref[:2 * CHUNK, at] * weights).astype(BF), ((0,), (0,)))
        for i in range(2):
            cut = slice(i * CHUNK, (i + 1) * CHUNK)
            wide = dot(duo[i], spread, ((0,), (0,)))
            x = rows_x[i][:, at]
            stepped = x * wide[:CHUNK]
            lead = wide[2 * CHUNK:3 * CHUNK]
            tall = dot(trip[i], columns, ((0,), (0,)))
            outs = []
            for pair in range(here // 2):
                mixes = []
                for h in (2 * pair, 2 * pair + 1):
                    line = lines[i][g * here + h:g * here + h + 1]
                    gap = tall[:, h * CHUNK:(h + 1) * CHUNK] - line
                    mixes.append((scores[i] * jnp.exp(jnp.minimum(gap, 0.0))).astype(BF))
                both = stepped[:, pair * LANES:(pair + 1) * LANES]
                stacked = jnp.concatenate(
                    [
                        jnp.where(lane < P_SIZE, both, 0.0).astype(BF),
                        jnp.where(lane < P_SIZE, 0.0, both).astype(BF),
                    ],
                    axis=0,
                )
                outs.append(dot(jnp.concatenate(mixes, axis=1), stacked))
            y = jnp.concatenate(outs, axis=1) + skip * x
            y = y + lead * dot(rows_c[i], state.astype(BF))
            v = rows_g[i][:, at].astype(F32)
            silu = v / (1.0 + jnp.exp(-v))
            own_ref[cut, at] = y * silu
            lead_ref[cut, at] = wide[3 * CHUNK:] * silu
            if i == 0:
                weighted = (x * wide[CHUNK:2 * CHUNK]).astype(BF)
                state = state * lead[CHUNK - 1:] + dot(rows_b[i], weighted, ((0,), (0,)))


def within(far, aux, x, b, c, gate, skip):
    channels = x.shape[1]
    return pl.pallas_call(
        functools.partial(within_kernel, far),
        in_specs=[VMEM] * 6,
        out_specs=[VMEM] * 2,
        out_shape=[jax.ShapeDtypeStruct((2 * CHUNK, channels), F32)] * 2,
        compiler_params=pltpu.CompilerParams(vmem_limit_bytes=VMEM_LIMIT),
        cost_estimate=pl.CostEstimate(
            flops=4_000_000_000, bytes_accessed=3_000_000, transcendentals=500_000
        ),
        name="within_far" if far else "within_near",
    )(aux, x, b, c, gate, skip)


def finish_rows(own, lead, c, incoming, gain):
    c = c.astype(BF)
    blocks = incoming.shape[1] // N
    carried = jnp.concatenate(
        [dot(c, incoming[h, k * N:(k + 1) * N]) for h in range(2) for k in range(blocks)], axis=1
    )
    gated = own + lead * carried
    mean = jnp.mean(gated * gated, axis=1, keepdims=True)
    return (gated * lax.rsqrt(mean + 1e-05) * gain).astype(BF)


def finish_block(block, own, lead, c, incoming, gain):
    return finish_rows(
        rows_of(own, block % 2), rows_of(lead, block % 2), rows_of(c, block), incoming, gain[...]
    )


def fill_incoming(here, there, incoming):
    odd = lax.axis_index("seq") % 2
    incoming[odd] = here[...]
    incoming[1 - odd] = there[...]


def project_both(normed, w, start, columns, theirs, mine, at=0):
    wide = 512
    for k in range(0, columns, wide):
        out = dot(normed[...], w[:, start + k:start + k + wide])
        theirs[:, at + k:at + k + wide] = out[:CHUNK].astype(BF)
        mine[:, k:k + wide] = out[CHUNK:]


def far_kernel(columns, own, lead, c, here, there, gain, w, theirs, mine, normed, incoming):
    me = lax.axis_index("head")
    fill_incoming(here, there, incoming)
    normed[:CHUNK] = finish_block(me ^ 3, own, lead, c, incoming, gain)
    normed[CHUNK:] = finish_block(me ^ 2, own, lead, c, incoming, gain)
    project_both(normed, w, 0, columns, theirs, mine)


def more_kernel(start, columns, normed, w, theirs, mine):
    project_both(normed, w, start, columns, theirs, mine)


def mixed_kernel(
    start, columns, normed, own, lead, c, here, there, gain, w, theirs, mine, kept, incoming, given
):
    me = lax.axis_index("head")
    project_both(normed, w, start, columns, theirs, mine)
    fill_incoming(here, there, incoming)
    given[...] = finish_block(me ^ 1, own, lead, c, incoming, gain)
    kept[...] = finish_block(me, own, lead, c, incoming, gain)
    wide = 512
    for k in range(0, w.shape[1], wide):
        theirs[:, columns + k:columns + k + wide] = dot(given[...], w[:, k:k + wide]).astype(BF)


def kept_kernel(columns, kept, come, w, out):
    wide = 512
    for k in range(0, w.shape[1], wide):
        out[:, k:k + wide] = dot(kept[...], w[:, k:k + wide]) + come[
            :, columns + k:columns + k + wide
        ].astype(F32)


def add_kernel(mine, come, out):
    out[...] = (mine[...] + come[:, :out.shape[1]].astype(F32)).astype(BF)


def local_call(kernel, operands, outs, name, scratch=(), flops=0, limit=VMEM_LIMIT):
    return pl.pallas_call(
        kernel,
        in_specs=[VMEM] * len(operands),
        out_specs=[VMEM] * len(outs),
        out_shape=[jax.ShapeDtypeStruct(shape, dtype) for shape, dtype in outs],
        scratch_shapes=list(scratch),
        compiler_params=pltpu.CompilerParams(vmem_limit_bytes=limit),
        cost_estimate=pl.CostEstimate(flops=flops, bytes_accessed=0, transcendentals=0),
        name=name,
    )(*operands)


def pass_kernel(*refs):
    pass


def await_piece(piece, *earlier):
    arrays = [piece, *earlier]
    return pl.pallas_call(
        pass_kernel,
        in_specs=[pl.BlockSpec(memory_space=pl.ANY)] * len(arrays),
        out_specs=[pl.BlockSpec(memory_space=pl.ANY)] * len(arrays),
        out_shape=[jax.ShapeDtypeStruct(v.shape, v.dtype) for v in arrays],
        input_output_aliases={k: k for k in range(len(arrays))},
        compiler_params=pltpu.CompilerParams(vmem_limit_bytes=1024 * 1024),
        cost_estimate=pl.CostEstimate(
            flops=20_000_000_000, bytes_accessed=100_000_000, transcendentals=0
        ),
        name="await_piece",
    )(*arrays)


def early_kernel(kept, first, second, out):
    at = 0
    for piece in (first, second):
        cut = slice(at, at + piece.shape[1])
        out[:, cut] = (kept[:, cut] + piece[...].astype(F32)).astype(BF)
        at += piece.shape[1]


def early_sums(kept, first, second):
    rows = first.shape[0]
    wide = first.shape[1] + second.shape[1]
    return pl.pallas_call(
        early_kernel,
        grid=(1,),
        in_specs=[VMEM] * 3,
        out_specs=pl.BlockSpec((rows, wide), lambda j: (0, 0)),
        out_shape=jax.ShapeDtypeStruct(kept.shape, BF),
        compiler_params=pltpu.CompilerParams(vmem_limit_bytes=VMEM_LIMIT),
        name="early_sums",
    )(kept, first, second)


def last_kernel(kept, third, filled, out):
    out[...] = (kept[...] + third[...].astype(F32)).astype(BF)


def last_sums(kept, third, filled):
    rows, wide = third.shape
    block = 512
    start = (kept.shape[1] - wide) // block
    return pl.pallas_call(
        last_kernel,
        grid=(wide // block,),
        in_specs=[
            pl.BlockSpec((rows, block), lambda j: (0, j + start)),
            pl.BlockSpec((rows, block), lambda j: (0, j)),
            pl.BlockSpec(memory_space=pl.ANY),
        ],
        out_specs=pl.BlockSpec((rows, block), lambda j: (0, j + start)),
        out_shape=jax.ShapeDtypeStruct(kept.shape, BF),
        input_output_aliases={2: 0},
        compiler_params=pltpu.CompilerParams(vmem_limit_bytes=VMEM_LIMIT),
        name="last_sums",
    )(kept, third, filled)


def per_device(
    seq_count,
    ssm_input,
    gate_input,
    step_raw,
    decay_log,
    state_in,
    state_out,
    skip_gain,
    norm_gain,
    out_weight,
):
    tok = ssm_input.shape[0]
    heads = decay_log.shape[0]
    b = state_in.reshape(tok, N)
    c = state_out.reshape(tok, N)
    give, wk, aux = give_states(step_raw.T, decay_log.reshape(1, heads), ssm_input, b)
    keep = keep_states(wk, ssm_input, b)
    inputs = (ssm_input, b, c, gate_input, skip_gain.reshape(1, heads))
    local = within(True, aux, *inputs)
    (own, lead), here, there = incoming_states(
        give, keep, seq_count, lambda got: lax.optimization_barrier((local, got))
    )

    near = [(h, h ^ 1) for h in range(4)]
    far = [(h, h ^ 2) for h in range(4)]
    gain = norm_gain.reshape(1, -1)
    channels, dout = out_weight.shape
    rows = CHUNK
    states = pltpu.VMEM((2,) + here.shape, BF)
    finish = (own, lead, c, here, there, gain, out_weight)
    (_, one), (start2, two), (start3, three) = PIECES

    def piece_outs(columns, extra=0):
        return [((rows, columns + extra), BF), ((rows, columns), F32)]

    def add(mine, theirs):
        come = lax.ppermute(theirs, "head", near)
        return local_call(add_kernel, (mine, come), [(mine.shape, BF)], "add_pair", limit=1 << 22)[0], come

    theirs, mine, normed = local_call(
        functools.partial(far_kernel, one),
        finish,
        piece_outs(one) + [((2 * rows, channels), BF)],
        "finish_far",
        [states],
        4 * rows * channels * one,
    )
    first, _ = add(mine, theirs)
    normed, aux, first = lax.optimization_barrier((normed, aux, first))
    theirs, mine = local_call(
        functools.partial(more_kernel, start2, two),
        (normed, out_weight),
        piece_outs(two),
        "project_more",
        flops=4 * rows * channels * two,
    )
    second, _ = add(mine, theirs)
    near_own, near_lead = within(False, aux, *inputs)
    normed, second = lax.optimization_barrier((normed, second))
    theirs, mine, kept = local_call(
        functools.partial(mixed_kernel, start3, three),
        (normed, near_own, near_lead) + finish[2:],
        piece_outs(three, dout) + [((rows, channels), BF)],
        "finish_near",
        [states, pltpu.VMEM((rows, channels), BF)],
        2 * rows * channels * (2 * three + dout),
    )
    third, come = add(mine, theirs)
    kept = local_call(
        functools.partial(kept_kernel, three),
        (kept, come, out_weight),
        [((rows, dout), F32)],
        "project_kept",
        flops=2 * rows * channels * dout,
    )[0]
    first = await_piece(lax.ppermute(first, "head", far))[0]
    second, first = await_piece(lax.ppermute(second, "head", far), first)
    filled = early_sums(kept, first, second)
    third, filled = await_piece(lax.ppermute(third, "head", far), filled)
    return last_sums(kept, third, filled)


def solution(mesh):
    in_specs = (
        P("seq", "head"),
        P("seq", "head"),
        P("seq", "head"),
        P("head"),
        P("seq", "head", None),
        P("seq", "head", None),
        P("head"),
        P("head"),
        P("head", None),
    )
    out_specs = P(("seq", "head"), None)
    return jax.shard_map(
        functools.partial(per_device, mesh.shape["seq"]),
        mesh=mesh,
        in_specs=in_specs,
        out_specs=out_specs,
        check_vma=False,
    )
```

```python
import functools

import jax
import jax.numpy as jnp
from jax import lax
from jax.experimental import pallas as pl
from jax.experimental.pallas import tpu as pltpu
from jax.sharding import PartitionSpec as P

P_SIZE = 64
N = 128
CHUNK = 128
LANES = 128
BF = jnp.bfloat16
F32 = jnp.float32
VMEM_LIMIT = 16 * 1024 * 1024
WHOLE_VMEM = 61 * 1024 * 1024 + 512 * 1024
PIECES = ((0, 1024), (1024, 1536), (2560, 1536))


def dot(a, b, contract=((1,), (0,)), precision=None):
    return lax.dot_general(a, b, (contract, ((), ())), precision=precision, preferred_element_type=F32)


def split2(v):
    hi = v.astype(BF)
    return hi, (v - hi.astype(F32)).astype(BF)


def split3(v):
    hi, rest = v.astype(BF), v
    rest = v - hi.astype(F32)
    mid = rest.astype(BF)
    return hi, mid, (rest - mid.astype(F32)).astype(BF)


def pick(rows, lanes, heads, per_head, first):
    r = lax.broadcasted_iota(jnp.int32, (rows, lanes), 0) % heads
    l = lax.broadcasted_iota(jnp.int32, (rows, lanes), 1) // per_head + first
    return jnp.where(r == l, 1.0, 0.0).astype(BF)


def step_vectors(raw, rate_row, wk, aux_ref):
    heads, tok = raw.shape
    chunks = tok // CHUNK
    step = jnp.maximum(raw, 0.0) + jnp.log1p(jnp.exp(-jnp.abs(raw)))
    r = lax.broadcasted_iota(jnp.int32, (heads, heads), 0)
    l = lax.broadcasted_iota(jnp.int32, (heads, heads), 1)
    rate = jnp.sum(jnp.where(r == l, rate_row, 0.0), axis=1, keepdims=True)
    logs = -step * jnp.exp(rate)
    parts = split3(logs)
    stacked = jnp.concatenate(
        [p[:, c * CHUNK:(c + 1) * CHUNK] for c in range(chunks) for p in parts], axis=0
    )
    s = lax.broadcasted_iota(jnp.int32, (CHUNK, 2 * CHUNK), 0)
    t = lax.broadcasted_iota(jnp.int32, (CHUNK, 2 * CHUNK), 1)
    tri = jnp.where(jnp.where(t < CHUNK, t - s, s - t + (CHUNK - 1)) >= 0, 1.0, 0.0).astype(BF)
    sums = dot(stacked, tri)
    pre, suf = [], []
    for c in range(chunks):
        base = 3 * heads * c
        total = (
            sums[base:base + heads] + sums[base + heads:base + 2 * heads]
        ) + sums[base + 2 * heads:base + 3 * heads]
        pre.append(total[:, :CHUNK])
        suf.append(total[:, CHUNK:])
    after = jnp.zeros((heads, 1), F32)
    for c in reversed(range(chunks)):
        w = step[:, c * CHUNK:(c + 1) * CHUNK] * jnp.exp(suf[c] + after)
        hi, lo = split2(w)
        wk[:heads, c * CHUNK:(c + 1) * CHUNK] = hi
        wk[heads:, c * CHUNK:(c + 1) * CHUNK] = lo
        after = after + pre[c][:, CHUNK - 1:]
    hi, lo = split2(jnp.broadcast_to(jnp.exp(after), (heads, CHUNK)))
    wk[:heads, tok:] = hi
    wk[heads:, tok:] = lo
    for c in range(chunks):
        aux_ref[c, :heads] = step[:, c * CHUNK:(c + 1) * CHUNK]
        aux_ref[c, heads:2 * heads] = pre[c]
        aux_ref[c, 2 * heads:] = suf[c]


def tail_rows(decays):
    r = lax.broadcasted_iota(jnp.int32, (16, LANES), 0)
    tail = jnp.zeros((16, LANES), F32)
    for k, decay in enumerate(decays):
        hi, lo = split2(decay)
        tail = jnp.where(r == 2 * k, hi.astype(F32), tail)
        tail = jnp.where(r == 2 * k + 1, lo.astype(F32), tail)
    return tail.astype(BF)


def decays_of(msg):
    blocks = (msg.shape[0] - 16) // N
    tail = msg[blocks * N:].astype(F32)
    return [tail[2 * k:2 * k + 1] + tail[2 * k + 1:2 * k + 2] for k in range(blocks)]


def half_message(x_ref, b, wk, first_head, msg):
    tok, lanes = x_ref.shape
    heads2 = wk.shape[0]
    width = 256
    decays = []
    for g in range(lanes // width):
        chosen = pick(heads2, width, heads2 // 2, P_SIZE, first_head + g * (width // P_SIZE))
        spread = dot(wk[...], chosen, ((0,), (0,)))
        weighted = (x_ref[:, g * width:(g + 1) * width] * spread[:tok]).astype(BF)
        state = dot(b, weighted, ((0,), (0,)))
        for i in range(width // LANES):
            k = g * (width // LANES) + i
            msg[k * N:(k + 1) * N] = state[:, i * LANES:(i + 1) * LANES].astype(BF)
            decays.append(spread[tok:tok + 1, i * LANES:(i + 1) * LANES])
    msg[msg.shape[0] - 16:] = tail_rows(decays)


def half_kernel(give, raw, rate, x, b, msg, wk, aux, raw_v, rate_v, x_v, b_v, sems):
    lanes = x_v.shape[1]
    mine = lax.axis_index("seq") % 2
    half = 1 - mine if give else mine
    loads = [
        pltpu.make_async_copy(b, b_v, sems.at[0]),
        pltpu.make_async_copy(
            x.at[:, pl.ds(pl.multiple_of(half * lanes, lanes), lanes)], x_v, sems.at[1]
        ),
    ]
    if give:
        loads += [
            pltpu.make_async_copy(raw, raw_v, sems.at[2]),
            pltpu.make_async_copy(rate, rate_v, sems.at[3]),
        ]
    for load in reversed(loads):
        load.start()
    if give:
        loads[2].wait()
        loads[3].wait()
        step_vectors(raw_v[...], rate_v[...], wk, aux)
    loads[0].wait()
    loads[1].wait()
    half_message(x_v, b_v[...].astype(BF), wk, half * (lanes // P_SIZE), msg)


def give_kernel(raw, rate, x, b, msg, wk, aux, raw_v, rate_v, x_v, b_v, sems):
    half_kernel(True, raw, rate, x, b, msg, wk, aux, raw_v, rate_v, x_v, b_v, sems)


def keep_kernel(wk, x, b, msg, x_v, b_v, sems):
    half_kernel(False, None, None, x, b, msg, wk, None, None, None, x_v, b_v, sems)


HBM = pl.BlockSpec(memory_space=pltpu.HBM)
VMEM = pl.BlockSpec(memory_space=pltpu.VMEM)


def give_states(raw, rate, x, b):
    heads, tok = raw.shape
    lanes = x.shape[1] // 2
    return pl.pallas_call(
        give_kernel,
        in_specs=[HBM] * 4,
        out_shape=[
            jax.ShapeDtypeStruct((lanes + 16, LANES), BF),
            jax.ShapeDtypeStruct((2 * heads, tok + CHUNK), BF),
            jax.ShapeDtypeStruct((tok // CHUNK, 3 * heads, CHUNK), F32),
        ],
        scratch_shapes=[
            pltpu.VMEM((heads, tok), F32),
            pltpu.VMEM((1, heads), F32),
            pltpu.VMEM((tok, lanes), F32),
            pltpu.VMEM((tok, N), F32),
            pltpu.SemaphoreType.DMA((4,)),
        ],
        compiler_params=pltpu.CompilerParams(vmem_limit_bytes=WHOLE_VMEM),
        cost_estimate=pl.CostEstimate(flops=200_000_000, bytes_accessed=1_500_000, transcendentals=0),
        name="give_states",
    )(raw, rate, x, b)


def keep_states(wk, x, b):
    tok = x.shape[0]
    lanes = x.shape[1] // 2
    return pl.pallas_call(
        keep_kernel,
        in_specs=[pl.BlockSpec(memory_space=pltpu.VMEM), HBM, HBM],
        out_shape=jax.ShapeDtypeStruct((lanes + 16, LANES), BF),
        scratch_shapes=[
            pltpu.VMEM((tok, lanes), F32),
            pltpu.VMEM((tok, N), F32),
            pltpu.SemaphoreType.DMA((2,)),
        ],
        compiler_params=pltpu.CompilerParams(vmem_limit_bytes=VMEM_LIMIT),
        cost_estimate=pl.CostEstimate(flops=200_000_000, bytes_accessed=1_500_000, transcendentals=0),
        name="keep_states",
    )(wk, x, b)


def link(later, earlier, out):
    ahead, behind = decays_of(later), decays_of(earlier)
    for k, decay in enumerate(ahead):
        rows = slice(k * N, (k + 1) * N)
        out[rows] = (later[rows].astype(F32) + decay * earlier[rows].astype(F32)).astype(BF)
    out[len(ahead) * N:] = tail_rows([p * q for p, q in zip(ahead, behind)])


def pair_kernel(own, come, out):
    odd = lax.axis_index("seq") % 2

    @pl.when(odd == 0)
    def _():
        link(come, own, out)

    @pl.when(odd == 1)
    def _():
        link(own, come, out)


def end_kernel(last, before, own, come, mine, theirs):
    blocks = mine.shape[0] // N
    odd = lax.axis_index("seq") % 2

    def fill(even_section, ahead_ref, behind_ref):
        step, span = decays_of(last), decays_of(even_section)
        for k in range(blocks):
            rows = slice(k * N, (k + 1) * N)
            start = last[rows].astype(F32)
            if before is not None:
                start = start + step[k] * before[rows].astype(F32)
            ahead_ref[rows] = start.astype(BF)
            behind_ref[rows] = (even_section[rows].astype(F32) + span[k] * start).astype(BF)

    @pl.when(odd == 0)
    def _():
        fill(own, mine, theirs)

    @pl.when(odd == 1)
    def _():
        fill(come, theirs, mine)


def scan_call(kernel, operands, shapes, name):
    return pl.pallas_call(
        kernel,
        out_shape=[jax.ShapeDtypeStruct(shape, BF) for shape in shapes],
        compiler_params=pltpu.CompilerParams(vmem_limit_bytes=VMEM_LIMIT),
        cost_estimate=pl.CostEstimate(flops=500_000, bytes_accessed=400_000, transcendentals=0),
        name=name,
    )(*operands)


def incoming_states(give, keep, count, hold):
    pair = [(s, s ^ 1) for s in range(count)]
    come = lax.ppermute(give, "seq", pair)
    run = scan_call(pair_kernel, (keep, come), [keep.shape], "join_pair")[0]
    start, distance = None, 2
    while distance < count:
        got = lax.ppermute(run, "seq", [(s, s + distance) for s in range(count - distance)])
        if distance * 2 >= count:
            break
        run = scan_call(link, (run, got), [keep.shape], "join_run")[0]
        start = got if start is None else scan_call(link, (start, got), [keep.shape], "join_start")[0]
        distance *= 2
    hold, got = hold(got)
    half = (keep.shape[0] - 16, LANES)
    mine, theirs = scan_call(end_kernel, (start, got, keep, come), [half, half], "join_end")
    return hold, mine, lax.ppermute(theirs, "seq", pair)


def rows_of(ref, block):
    return ref[pl.ds(pl.multiple_of(block * CHUNK, CHUNK), CHUNK), :]


def within_kernel(far, aux, x_ref, b_ref, c_ref, gate_ref, skip_ref, own_ref, lead_ref):
    channels = x_ref.shape[1]
    heads = aux.shape[1] // 3
    width = 256
    here = width // P_SIZE
    half = lax.axis_index("head") // 2
    half = 1 - half if far else half
    second = half == 1

    def vectors(c):
        return [aux[c, k * heads:(k + 1) * heads] for k in range(3)]

    def put(values):
        return jnp.concatenate([jnp.concatenate(split2(v), axis=0) for v in values], axis=1)

    first, then = vectors(0), vectors(1)
    ends = [v[1][:, CHUNK - 1:] for v in (first, then)]
    early = put(
        [
            jnp.where(second, first[0] * jnp.exp(first[2] + ends[1]), 0.0),
            jnp.where(second, then[0] * jnp.exp(then[2]), 0.0),
        ]
    )
    before = jnp.where(second, ends[0] + ends[1], 0.0)
    r = lax.broadcasted_iota(jnp.int32, (CHUNK, CHUNK), 0)
    l = lax.broadcasted_iota(jnp.int32, (CHUNK, CHUNK), 1)
    duo, trip, lines, scores, rows_b, rows_c, rows_x, rows_g = ([] for _ in range(8))
    for i in range(2):
        block = 2 * half + i
        step, pre, suf = vectors(block)
        duo.append(put((step, step * jnp.exp(suf), jnp.exp(pre), jnp.exp(pre + before))))
        trip.append(jnp.concatenate(split3(pre), axis=0))
        lines.append(pre)
        before = before + pre[:, CHUNK - 1:]
        b, c = rows_of(b_ref, block), rows_of(c_ref, block)
        raw = dot(c, b, ((1,), (1,)), lax.Precision.HIGHEST)
        scores.append(jnp.where(r >= l, raw, 0.0))
        rows_b.append(b.astype(BF))
        rows_c.append(c.astype(BF))
        rows_x.append(rows_of(x_ref, block))
        rows_g.append(rows_of(gate_ref, block))
    early_b = b_ref[:2 * CHUNK].astype(BF)
    gains = jnp.broadcast_to(jnp.concatenate(split3(skip_ref[...]), axis=1), (8, 3 * heads))
    lane = lax.broadcasted_iota(jnp.int32, (CHUNK, LANES), 1)
    for g in range(channels // width):
        at = slice(g * width, (g + 1) * width)
        spread = pick(2 * heads, width, heads, P_SIZE, g * here)
        columns = pick(3 * heads, here * CHUNK, heads, CHUNK, g * here)
        skip = dot(gains, pick(3 * heads, width, heads, P_SIZE, g * here))[:1]
        weights = dot(early, spread, ((0,), (0,)))
        state = dot(early_b, (x_ref[:2 * CHUNK, at] * weights).astype(BF), ((0,), (0,)))
        for i in range(2):
            cut = slice(i * CHUNK, (i + 1) * CHUNK)
            wide = dot(duo[i], spread, ((0,), (0,)))
            x = rows_x[i][:, at]
            stepped = x * wide[:CHUNK]
            lead = wide[2 * CHUNK:3 * CHUNK]
            tall = dot(trip[i], columns, ((0,), (0,)))
            outs = []
            for pair in range(here // 2):
                mixes = []
                for h in (2 * pair, 2 * pair + 1):
                    line = lines[i][g * here + h:g * here + h + 1]
                    gap = tall[:, h * CHUNK:(h + 1) * CHUNK] - line
                    mixes.append((scores[i] * jnp.exp(jnp.minimum(gap, 0.0))).astype(BF))
                both = stepped[:, pair * LANES:(pair + 1) * LANES]
                stacked = jnp.concatenate(
                    [
                        jnp.where(lane < P_SIZE, both, 0.0).astype(BF),
                        jnp.where(lane < P_SIZE, 0.0, both).astype(BF),
                    ],
                    axis=0,
                )
                outs.append(dot(jnp.concatenate(mixes, axis=1), stacked))
            y = jnp.concatenate(outs, axis=1) + skip * x
            y = y + lead * dot(rows_c[i], state.astype(BF))
            v = rows_g[i][:, at].astype(F32)
            silu = v / (1.0 + jnp.exp(-v))
            own_ref[cut, at] = y * silu
            lead_ref[cut, at] = wide[3 * CHUNK:] * silu
            if i == 0:
                weighted = (x * wide[CHUNK:2 * CHUNK]).astype(BF)
                state = state * lead[CHUNK - 1:] + dot(rows_b[i], weighted, ((0,), (0,)))


def within(far, aux, x, b, c, gate, skip):
    channels = x.shape[1]
    return pl.pallas_call(
        functools.partial(within_kernel, far),
        in_specs=[VMEM] * 6,
        out_specs=[VMEM] * 2,
        out_shape=[jax.ShapeDtypeStruct((2 * CHUNK, channels), F32)] * 2,
        compiler_params=pltpu.CompilerParams(vmem_limit_bytes=VMEM_LIMIT),
        cost_estimate=pl.CostEstimate(
            flops=4_000_000_000, bytes_accessed=3_000_000, transcendentals=500_000
        ),
        name="within_far" if far else "within_near",
    )(aux, x, b, c, gate, skip)


def finish_rows(own, lead, c, incoming, gain):
    c = c.astype(BF)
    blocks = incoming.shape[1] // N
    carried = jnp.concatenate(
        [dot(c, incoming[h, k * N:(k + 1) * N]) for h in range(2) for k in range(blocks)], axis=1
    )
    gated = own + lead * carried
    mean = jnp.mean(gated * gated, axis=1, keepdims=True)
    return (gated * lax.rsqrt(mean + 1e-05) * gain).astype(BF)


def finish_block(block, own, lead, c, incoming, gain):
    return finish_rows(
        rows_of(own, block % 2), rows_of(lead, block % 2), rows_of(c, block), incoming, gain[...]
    )


def fill_incoming(here, there, incoming):
    odd = lax.axis_index("seq") % 2
    incoming[odd] = here[...]
    incoming[1 - odd] = there[...]


def project_both(normed, w, start, columns, theirs, mine, at=0):
    wide = 512
    for k in range(0, columns, wide):
        out = dot(normed[...], w[:, start + k:start + k + wide])
        theirs[:, at + k:at + k + wide] = out[:CHUNK].astype(BF)
        mine[:, k:k + wide] = out[CHUNK:]


def far_kernel(columns, own, lead, c, here, there, gain, w, theirs, mine, normed, incoming):
    me = lax.axis_index("head")
    fill_incoming(here, there, incoming)
    normed[:CHUNK] = finish_block(me ^ 3, own, lead, c, incoming, gain)
    normed[CHUNK:] = finish_block(me ^ 2, own, lead, c, incoming, gain)
    project_both(normed, w, 0, columns, theirs, mine)


def more_kernel(start, columns, normed, w, theirs, mine):
    project_both(normed, w, start, columns, theirs, mine)


def mixed_kernel(
    start, columns, normed, own, lead, c, here, there, gain, w, theirs, mine, kept, incoming, given
):
    me = lax.axis_index("head")
    project_both(normed, w, start, columns, theirs, mine)
    fill_incoming(here, there, incoming)
    given[...] = finish_block(me ^ 1, own, lead, c, incoming, gain)
    kept[...] = finish_block(me, own, lead, c, incoming, gain)
    wide = 512
    for k in range(0, w.shape[1], wide):
        theirs[:, columns + k:columns + k + wide] = dot(given[...], w[:, k:k + wide]).astype(BF)


def kept_kernel(columns, kept, come, w, out):
    wide = 512
    for k in range(0, w.shape[1], wide):
        out[:, k:k + wide] = dot(kept[...], w[:, k:k + wide]) + come[
            :, columns + k:columns + k + wide
        ].astype(F32)


def add_kernel(mine, come, out):
    out[...] = (mine[...] + come[:, :out.shape[1]].astype(F32)).astype(BF)


def local_call(kernel, operands, outs, name, scratch=(), flops=0, limit=VMEM_LIMIT):
    return pl.pallas_call(
        kernel,
        in_specs=[VMEM] * len(operands),
        out_specs=[VMEM] * len(outs),
        out_shape=[jax.ShapeDtypeStruct(shape, dtype) for shape, dtype in outs],
        scratch_shapes=list(scratch),
        compiler_params=pltpu.CompilerParams(vmem_limit_bytes=limit),
        cost_estimate=pl.CostEstimate(flops=flops, bytes_accessed=0, transcendentals=0),
        name=name,
    )(*operands)


def pass_kernel(*refs):
    pass


def await_piece(piece, *earlier):
    arrays = [piece, *earlier]
    return pl.pallas_call(
        pass_kernel,
        in_specs=[pl.BlockSpec(memory_space=pl.ANY)] * len(arrays),
        out_specs=[pl.BlockSpec(memory_space=pl.ANY)] * len(arrays),
        out_shape=[jax.ShapeDtypeStruct(v.shape, v.dtype) for v in arrays],
        input_output_aliases={k: k for k in range(len(arrays))},
        compiler_params=pltpu.CompilerParams(vmem_limit_bytes=1024 * 1024),
        cost_estimate=pl.CostEstimate(
            flops=20_000_000_000, bytes_accessed=100_000_000, transcendentals=0
        ),
        name="await_piece",
    )(*arrays)


def early_kernel(kept, first, second, out):
    at = 0
    for piece in (first, second):
        cut = slice(at, at + piece.shape[1])
        out[:, cut] = (kept[:, cut] + piece[...].astype(F32)).astype(BF)
        at += piece.shape[1]


def early_sums(kept, first, second):
    rows = first.shape[0]
    wide = first.shape[1] + second.shape[1]
    return pl.pallas_call(
        early_kernel,
        grid=(1,),
        in_specs=[VMEM] * 3,
        out_specs=pl.BlockSpec((rows, wide), lambda j: (0, 0)),
        out_shape=jax.ShapeDtypeStruct(kept.shape, BF),
        compiler_params=pltpu.CompilerParams(vmem_limit_bytes=VMEM_LIMIT),
        name="early_sums",
    )(kept, first, second)


def last_kernel(kept, third, filled, out, part, sems):
    wide = third.shape[1]
    start = kept.shape[1] - wide
    block = wide // 2
    stores = []
    for k in range(2):
        cut = slice(k * block, (k + 1) * block)
        part[:, cut] = (
            kept[:, start + k * block:start + (k + 1) * block] + third[:, cut].astype(F32)
        ).astype(BF)
        stores.append(
            pltpu.make_async_copy(
                part.at[:, cut], out.at[:, start + k * block:start + (k + 1) * block], sems.at[k]
            )
        )
        stores[k].start()
    for store in stores:
        store.wait()


def last_sums(kept, third, filled):
    return pl.pallas_call(
        last_kernel,
        in_specs=[VMEM, VMEM, pl.BlockSpec(memory_space=pl.ANY)],
        out_specs=pl.BlockSpec(memory_space=pl.ANY),
        out_shape=jax.ShapeDtypeStruct(kept.shape, BF),
        input_output_aliases={2: 0},
        scratch_shapes=[pltpu.VMEM(third.shape, BF), pltpu.SemaphoreType.DMA((2,))],
        compiler_params=pltpu.CompilerParams(vmem_limit_bytes=VMEM_LIMIT),
        name="last_sums",
    )(kept, third, filled)


def per_device(
    seq_count,
    ssm_input,
    gate_input,
    step_raw,
    decay_log,
    state_in,
    state_out,
    skip_gain,
    norm_gain,
    out_weight,
):
    tok = ssm_input.shape[0]
    heads = decay_log.shape[0]
    b = state_in.reshape(tok, N)
    c = state_out.reshape(tok, N)
    give, wk, aux = give_states(step_raw.T, decay_log.reshape(1, heads), ssm_input, b)
    keep = keep_states(wk, ssm_input, b)
    inputs = (ssm_input, b, c, gate_input, skip_gain.reshape(1, heads))
    local = within(True, aux, *inputs)
    (own, lead), here, there = incoming_states(
        give, keep, seq_count, lambda got: lax.optimization_barrier((local, got))
    )

    near = [(h, h ^ 1) for h in range(4)]
    far = [(h, h ^ 2) for h in range(4)]
    gain = norm_gain.reshape(1, -1)
    channels, dout = out_weight.shape
    rows = CHUNK
    states = pltpu.VMEM((2,) + here.shape, BF)
    finish = (own, lead, c, here, there, gain, out_weight)
    (_, one), (start2, two), (start3, three) = PIECES

    def piece_outs(columns, extra=0):
        return [((rows, columns + extra), BF), ((rows, columns), F32)]

    def add(mine, theirs):
        come = lax.ppermute(theirs, "head", near)
        return local_call(add_kernel, (mine, come), [(mine.shape, BF)], "add_pair", limit=1 << 22)[0], come

    theirs, mine, normed = local_call(
        functools.partial(far_kernel, one),
        finish,
        piece_outs(one) + [((2 * rows, channels), BF)],
        "finish_far",
        [states],
        4 * rows * channels * one,
    )
    first, _ = add(mine, theirs)
    aux, first = lax.optimization_barrier((aux, first))
    theirs, mine = local_call(
        functools.partial(more_kernel, start2, two),
        (normed, out_weight),
        piece_outs(two),
        "project_more",
        flops=4 * rows * channels * two,
    )
    second, _ = add(mine, theirs)
    near_own, near_lead = within(False, aux, *inputs)
    normed, second = lax.optimization_barrier((normed, second))
    theirs, mine, kept = local_call(
        functools.partial(mixed_kernel, start3, three),
        (normed, near_own, near_lead) + finish[2:],
        piece_outs(three, dout) + [((rows, channels), BF)],
        "finish_near",
        [states, pltpu.VMEM((rows, channels), BF)],
        2 * rows * channels * (2 * three + dout),
    )
    third, come = add(mine, theirs)
    kept = local_call(
        functools.partial(kept_kernel, three),
        (kept, come, out_weight),
        [((rows, dout), F32)],
        "project_kept",
        flops=2 * rows * channels * dout,
    )[0]
    first = await_piece(lax.ppermute(first, "head", far))[0]
    second, first = await_piece(lax.ppermute(second, "head", far), first)
    filled = early_sums(kept, first, second)
    third, filled = await_piece(lax.ppermute(third, "head", far), filled)
    return last_sums(kept, third, filled)


def solution(mesh):
    in_specs = (
        P("seq", "head"),
        P("seq", "head"),
        P("seq", "head"),
        P("head"),
        P("seq", "head", None),
        P("seq", "head", None),
        P("head"),
        P("head"),
        P("head", None),
    )
    out_specs = P(("seq", "head"), None)
    return jax.shard_map(
        functools.partial(per_device, mesh.shape["seq"]),
        mesh=mesh,
        in_specs=in_specs,
        out_specs=out_specs,
        check_vma=False,
    )
```

```python
import functools

import jax
import jax.numpy as jnp
from jax import lax
from jax.experimental import pallas as pl
from jax.experimental.pallas import tpu as pltpu
from jax.sharding import PartitionSpec as P

P_SIZE = 64
N = 128
CHUNK = 128
LANES = 128
BF = jnp.bfloat16
F32 = jnp.float32
VMEM_LIMIT = 16 * 1024 * 1024
WHOLE_VMEM = 61 * 1024 * 1024 + 512 * 1024
PIECES = ((0, 1024), (1024, 1536), (2560, 1536))


def dot(a, b, contract=((1,), (0,)), precision=None):
    return lax.dot_general(a, b, (contract, ((), ())), precision=precision, preferred_element_type=F32)


def split2(v):
    hi = v.astype(BF)
    return hi, (v - hi.astype(F32)).astype(BF)


def split3(v):
    hi, rest = v.astype(BF), v
    rest = v - hi.astype(F32)
    mid = rest.astype(BF)
    return hi, mid, (rest - mid.astype(F32)).astype(BF)


def pick(rows, lanes, heads, per_head, first):
    r = lax.broadcasted_iota(jnp.int32, (rows, lanes), 0) % heads
    l = lax.broadcasted_iota(jnp.int32, (rows, lanes), 1) // per_head + first
    return jnp.where(r == l, 1.0, 0.0).astype(BF)


def step_vectors(raw, rate_row, wk, aux_ref):
    heads, tok = raw.shape
    chunks = tok // CHUNK
    step = jnp.maximum(raw, 0.0) + jnp.log1p(jnp.exp(-jnp.abs(raw)))
    r = lax.broadcasted_iota(jnp.int32, (heads, heads), 0)
    l = lax.broadcasted_iota(jnp.int32, (heads, heads), 1)
    rate = jnp.sum(jnp.where(r == l, rate_row, 0.0), axis=1, keepdims=True)
    logs = -step * jnp.exp(rate)
    parts = split3(logs)
    stacked = jnp.concatenate(
        [p[:, c * CHUNK:(c + 1) * CHUNK] for c in range(chunks) for p in parts], axis=0
    )
    s = lax.broadcasted_iota(jnp.int32, (CHUNK, 2 * CHUNK), 0)
    t = lax.broadcasted_iota(jnp.int32, (CHUNK, 2 * CHUNK), 1)
    tri = jnp.where(jnp.where(t < CHUNK, t - s, s - t + (CHUNK - 1)) >= 0, 1.0, 0.0).astype(BF)
    sums = dot(stacked, tri)
    pre, suf = [], []
    for c in range(chunks):
        base = 3 * heads * c
        total = (
            sums[base:base + heads] + sums[base + heads:base + 2 * heads]
        ) + sums[base + 2 * heads:base + 3 * heads]
        pre.append(total[:, :CHUNK])
        suf.append(total[:, CHUNK:])
    after = jnp.zeros((heads, 1), F32)
    for c in reversed(range(chunks)):
        w = step[:, c * CHUNK:(c + 1) * CHUNK] * jnp.exp(suf[c] + after)
        hi, lo = split2(w)
        wk[:heads, c * CHUNK:(c + 1) * CHUNK] = hi
        wk[heads:, c * CHUNK:(c + 1) * CHUNK] = lo
        after = after + pre[c][:, CHUNK - 1:]
    hi, lo = split2(jnp.broadcast_to(jnp.exp(after), (heads, CHUNK)))
    wk[:heads, tok:] = hi
    wk[heads:, tok:] = lo
    for c in range(chunks):
        aux_ref[c, :heads] = step[:, c * CHUNK:(c + 1) * CHUNK]
        aux_ref[c, heads:2 * heads] = pre[c]
        aux_ref[c, 2 * heads:] = suf[c]


def tail_rows(decays):
    r = lax.broadcasted_iota(jnp.int32, (16, LANES), 0)
    tail = jnp.zeros((16, LANES), F32)
    for k, decay in enumerate(decays):
        hi, lo = split2(decay)
        tail = jnp.where(r == 2 * k, hi.astype(F32), tail)
        tail = jnp.where(r == 2 * k + 1, lo.astype(F32), tail)
    return tail.astype(BF)


def decays_of(msg):
    blocks = (msg.shape[0] - 16) // N
    tail = msg[blocks * N:].astype(F32)
    return [tail[2 * k:2 * k + 1] + tail[2 * k + 1:2 * k + 2] for k in range(blocks)]


def half_message(x_ref, b, wk, first_head, msg):
    tok, lanes = x_ref.shape
    heads2 = wk.shape[0]
    width = 256
    decays = []
    for g in range(lanes // width):
        chosen = pick(heads2, width, heads2 // 2, P_SIZE, first_head + g * (width // P_SIZE))
        spread = dot(wk[...], chosen, ((0,), (0,)))
        weighted = (x_ref[:, g * width:(g + 1) * width] * spread[:tok]).astype(BF)
        state = dot(b, weighted, ((0,), (0,)))
        for i in range(width // LANES):
            k = g * (width // LANES) + i
            msg[k * N:(k + 1) * N] = state[:, i * LANES:(i + 1) * LANES].astype(BF)
            decays.append(spread[tok:tok + 1, i * LANES:(i + 1) * LANES])
    msg[msg.shape[0] - 16:] = tail_rows(decays)


def half_kernel(give, raw, rate, x, b, msg, wk, aux, raw_v, rate_v, x_v, b_v, sems):
    lanes = x_v.shape[1]
    mine = lax.axis_index("seq") % 2
    half = 1 - mine if give else mine
    loads = [
        pltpu.make_async_copy(b, b_v, sems.at[0]),
        pltpu.make_async_copy(
            x.at[:, pl.ds(pl.multiple_of(half * lanes, lanes), lanes)], x_v, sems.at[1]
        ),
    ]
    if give:
        loads += [
            pltpu.make_async_copy(raw, raw_v, sems.at[2]),
            pltpu.make_async_copy(rate, rate_v, sems.at[3]),
        ]
    for load in reversed(loads):
        load.start()
    if give:
        loads[2].wait()
        loads[3].wait()
        step_vectors(raw_v[...], rate_v[...], wk, aux)
    loads[0].wait()
    loads[1].wait()
    half_message(x_v, b_v[...].astype(BF), wk, half * (lanes // P_SIZE), msg)


def give_kernel(raw, rate, x, b, msg, wk, aux, raw_v, rate_v, x_v, b_v, sems):
    half_kernel(True, raw, rate, x, b, msg, wk, aux, raw_v, rate_v, x_v, b_v, sems)


def keep_kernel(wk, x, b, msg, x_v, b_v, sems):
    half_kernel(False, None, None, x, b, msg, wk, None, None, None, x_v, b_v, sems)


HBM = pl.BlockSpec(memory_space=pltpu.HBM)
VMEM = pl.BlockSpec(memory_space=pltpu.VMEM)


def give_states(raw, rate, x, b):
    heads, tok = raw.shape
    lanes = x.shape[1] // 2
    return pl.pallas_call(
        give_kernel,
        in_specs=[HBM] * 4,
        out_shape=[
            jax.ShapeDtypeStruct((lanes + 16, LANES), BF),
            jax.ShapeDtypeStruct((2 * heads, tok + CHUNK), BF),
            jax.ShapeDtypeStruct((tok // CHUNK, 3 * heads, CHUNK), F32),
        ],
        scratch_shapes=[
            pltpu.VMEM((heads, tok), F32),
            pltpu.VMEM((1, heads), F32),
            pltpu.VMEM((tok, lanes), F32),
            pltpu.VMEM((tok, N), F32),
            pltpu.SemaphoreType.DMA((4,)),
        ],
        compiler_params=pltpu.CompilerParams(vmem_limit_bytes=WHOLE_VMEM),
        cost_estimate=pl.CostEstimate(flops=200_000_000, bytes_accessed=1_500_000, transcendentals=0),
        name="give_states",
    )(raw, rate, x, b)


def keep_states(wk, x, b):
    tok = x.shape[0]
    lanes = x.shape[1] // 2
    return pl.pallas_call(
        keep_kernel,
        in_specs=[pl.BlockSpec(memory_space=pltpu.VMEM), HBM, HBM],
        out_shape=jax.ShapeDtypeStruct((lanes + 16, LANES), BF),
        scratch_shapes=[
            pltpu.VMEM((tok, lanes), F32),
            pltpu.VMEM((tok, N), F32),
            pltpu.SemaphoreType.DMA((2,)),
        ],
        compiler_params=pltpu.CompilerParams(vmem_limit_bytes=VMEM_LIMIT),
        cost_estimate=pl.CostEstimate(flops=200_000_000, bytes_accessed=1_500_000, transcendentals=0),
        name="keep_states",
    )(wk, x, b)


def link(later, earlier, out):
    ahead, behind = decays_of(later), decays_of(earlier)
    for k, decay in enumerate(ahead):
        rows = slice(k * N, (k + 1) * N)
        out[rows] = (later[rows].astype(F32) + decay * earlier[rows].astype(F32)).astype(BF)
    out[len(ahead) * N:] = tail_rows([p * q for p, q in zip(ahead, behind)])


def is_later(distance):
    return (lax.axis_index("seq") // distance) % 2


def run_kernel(distance, own, come, out):
    later = is_later(distance)

    @pl.when(later == 0)
    def _():
        link(come, own, out)

    @pl.when(later == 1)
    def _():
        link(own, come, out)


def first_ahead_kernel(distance, come, out):
    later = is_later(distance)
    rows = out.shape[0] - 16

    @pl.when(later == 0)
    def _():
        out[:rows] = jnp.zeros((rows, LANES), BF)
        out[rows:] = tail_rows([jnp.ones((1, LANES), F32)] * (rows // N))

    @pl.when(later == 1)
    def _():
        out[...] = come[...]


def ahead_kernel(distance, ahead, come, out):
    later = is_later(distance)

    @pl.when(later == 0)
    def _():
        out[...] = ahead[...]

    @pl.when(later == 1)
    def _():
        link(ahead, come, out)


def end_kernel(distance, ahead, last, own, come, mine, theirs):
    blocks = mine.shape[0] // N
    weight = is_later(distance).astype(F32)
    odd = is_later(1)

    def fill(even_section, ahead_ref, behind_ref):
        step, span = decays_of(ahead), decays_of(even_section)
        for k in range(blocks):
            rows = slice(k * N, (k + 1) * N)
            start = ahead[rows].astype(F32) + (weight * step[k]) * last[rows].astype(F32)
            ahead_ref[rows] = start.astype(BF)
            behind_ref[rows] = (even_section[rows].astype(F32) + span[k] * start).astype(BF)

    @pl.when(odd == 0)
    def _():
        fill(own, mine, theirs)

    @pl.when(odd == 1)
    def _():
        fill(come, theirs, mine)


def scan_call(kernel, operands, shapes, name):
    return pl.pallas_call(
        kernel,
        out_shape=[jax.ShapeDtypeStruct(shape, BF) for shape in shapes],
        compiler_params=pltpu.CompilerParams(vmem_limit_bytes=VMEM_LIMIT),
        cost_estimate=pl.CostEstimate(flops=500_000, bytes_accessed=400_000, transcendentals=0),
        name=name,
    )(*operands)


def incoming_states(give, keep, count, hold):
    def exchange(value, distance):
        return lax.ppermute(value, "seq", [(s, s ^ distance) for s in range(count)])

    def joined(kernel, distance, *operands):
        name = kernel.__name__[:-len("_kernel")]
        return scan_call(functools.partial(kernel, distance), operands, [keep.shape], name)[0]

    come = exchange(give, 1)
    run, distance = joined(run_kernel, 1, keep, come), 2
    got = exchange(run, distance)
    ahead = joined(first_ahead_kernel, distance, got)
    while distance * 2 < count:
        run, distance = joined(run_kernel, distance, run, got), distance * 2
        got = exchange(run, distance)
        if distance * 2 < count:
            ahead = joined(ahead_kernel, distance, ahead, got)
    hold, got = hold(got)
    half = (keep.shape[0] - 16, LANES)
    mine, theirs = scan_call(
        functools.partial(end_kernel, distance), (ahead, got, keep, come), [half, half], "join_end"
    )
    return hold, mine, exchange(theirs, 1)


def rows_of(ref, block):
    return ref[pl.ds(pl.multiple_of(block * CHUNK, CHUNK), CHUNK), :]


def within_kernel(far, aux, x_ref, b_ref, c_ref, gate_ref, skip_ref, own_ref, lead_ref):
    channels = x_ref.shape[1]
    heads = aux.shape[1] // 3
    width = 256
    here = width // P_SIZE
    half = lax.axis_index("head") // 2
    half = 1 - half if far else half
    second = half == 1

    def vectors(c):
        return [aux[c, k * heads:(k + 1) * heads] for k in range(3)]

    def put(values):
        return jnp.concatenate([jnp.concatenate(split2(v), axis=0) for v in values], axis=1)

    first, then = vectors(0), vectors(1)
    ends = [v[1][:, CHUNK - 1:] for v in (first, then)]
    early = put(
        [
            jnp.where(second, first[0] * jnp.exp(first[2] + ends[1]), 0.0),
            jnp.where(second, then[0] * jnp.exp(then[2]), 0.0),
        ]
    )
    before = jnp.where(second, ends[0] + ends[1], 0.0)
    r = lax.broadcasted_iota(jnp.int32, (CHUNK, CHUNK), 0)
    l = lax.broadcasted_iota(jnp.int32, (CHUNK, CHUNK), 1)
    duo, trip, lines, scores, rows_b, rows_c, rows_x, rows_g = ([] for _ in range(8))
    for i in range(2):
        block = 2 * half + i
        step, pre, suf = vectors(block)
        duo.append(put((step, step * jnp.exp(suf), jnp.exp(pre), jnp.exp(pre + before))))
        trip.append(jnp.concatenate(split3(pre), axis=0))
        lines.append(pre)
        before = before + pre[:, CHUNK - 1:]
        b, c = rows_of(b_ref, block), rows_of(c_ref, block)
        raw = dot(c, b, ((1,), (1,)), lax.Precision.HIGHEST)
        scores.append(jnp.where(r >= l, raw, 0.0))
        rows_b.append(b.astype(BF))
        rows_c.append(c.astype(BF))
        rows_x.append(rows_of(x_ref, block))
        rows_g.append(rows_of(gate_ref, block))
    early_b = b_ref[:2 * CHUNK].astype(BF)
    gains = jnp.broadcast_to(jnp.concatenate(split3(skip_ref[...]), axis=1), (8, 3 * heads))
    lane = lax.broadcasted_iota(jnp.int32, (CHUNK, LANES), 1)
    for g in range(channels // width):
        at = slice(g * width, (g + 1) * width)
        spread = pick(2 * heads, width, heads, P_SIZE, g * here)
        columns = pick(3 * heads, here * CHUNK, heads, CHUNK, g * here)
        skip = dot(gains, pick(3 * heads, width, heads, P_SIZE, g * here))[:1]
        weights = dot(early, spread, ((0,), (0,)))
        state = dot(early_b, (x_ref[:2 * CHUNK, at] * weights).astype(BF), ((0,), (0,)))
        for i in range(2):
            cut = slice(i * CHUNK, (i + 1) * CHUNK)
            wide = dot(duo[i], spread, ((0,), (0,)))
            x = rows_x[i][:, at]
            stepped = x * wide[:CHUNK]
            lead = wide[2 * CHUNK:3 * CHUNK]
            tall = dot(trip[i], columns, ((0,), (0,)))
            outs = []
            for pair in range(here // 2):
                mixes = []
                for h in (2 * pair, 2 * pair + 1):
                    line = lines[i][g * here + h:g * here + h + 1]
                    gap = tall[:, h * CHUNK:(h + 1) * CHUNK] - line
                    mixes.append((scores[i] * jnp.exp(jnp.minimum(gap, 0.0))).astype(BF))
                both = stepped[:, pair * LANES:(pair + 1) * LANES]
                stacked = jnp.concatenate(
                    [
                        jnp.where(lane < P_SIZE, both, 0.0).astype(BF),
                        jnp.where(lane < P_SIZE, 0.0, both).astype(BF),
                    ],
                    axis=0,
                )
                outs.append(dot(jnp.concatenate(mixes, axis=1), stacked))
            y = jnp.concatenate(outs, axis=1) + skip * x
            y = y + lead * dot(rows_c[i], state.astype(BF))
            v = rows_g[i][:, at].astype(F32)
            silu = v / (1.0 + jnp.exp(-v))
            own_ref[cut, at] = y * silu
            lead_ref[cut, at] = wide[3 * CHUNK:] * silu
            if i == 0:
                weighted = (x * wide[CHUNK:2 * CHUNK]).astype(BF)
                state = state * lead[CHUNK - 1:] + dot(rows_b[i], weighted, ((0,), (0,)))


def within(far, aux, x, b, c, gate, skip):
    channels = x.shape[1]
    return pl.pallas_call(
        functools.partial(within_kernel, far),
        in_specs=[VMEM] * 6,
        out_specs=[VMEM] * 2,
        out_shape=[jax.ShapeDtypeStruct((2 * CHUNK, channels), F32)] * 2,
        compiler_params=pltpu.CompilerParams(vmem_limit_bytes=VMEM_LIMIT),
        cost_estimate=pl.CostEstimate(
            flops=4_000_000_000, bytes_accessed=3_000_000, transcendentals=500_000
        ),
        name="within_far" if far else "within_near",
    )(aux, x, b, c, gate, skip)


def finish_rows(own, lead, c, incoming, gain):
    c = c.astype(BF)
    blocks = incoming.shape[1] // N
    carried = jnp.concatenate(
        [dot(c, incoming[h, k * N:(k + 1) * N]) for h in range(2) for k in range(blocks)], axis=1
    )
    gated = own + lead * carried
    mean = jnp.mean(gated * gated, axis=1, keepdims=True)
    return (gated * lax.rsqrt(mean + 1e-05) * gain).astype(BF)


def finish_block(block, own, lead, c, incoming, gain):
    return finish_rows(
        rows_of(own, block % 2), rows_of(lead, block % 2), rows_of(c, block), incoming, gain[...]
    )


def fill_incoming(here, there, incoming):
    odd = lax.axis_index("seq") % 2
    incoming[odd] = here[...]
    incoming[1 - odd] = there[...]


def project_both(normed, w, start, columns, theirs, mine, at=0):
    wide = 512
    for k in range(0, columns, wide):
        out = dot(normed[...], w[:, start + k:start + k + wide])
        theirs[:, at + k:at + k + wide] = out[:CHUNK].astype(BF)
        mine[:, k:k + wide] = out[CHUNK:]


def far_kernel(columns, own, lead, c, here, there, gain, w, theirs, mine, normed, incoming):
    me = lax.axis_index("head")
    fill_incoming(here, there, incoming)
    normed[:CHUNK] = finish_block(me ^ 3, own, lead, c, incoming, gain)
    normed[CHUNK:] = finish_block(me ^ 2, own, lead, c, incoming, gain)
    project_both(normed, w, 0, columns, theirs, mine)


def more_kernel(start, columns, normed, w, theirs, mine):
    project_both(normed, w, start, columns, theirs, mine)


def mixed_kernel(
    start, columns, normed, own, lead, c, here, there, gain, w, theirs, mine, kept, incoming, given
):
    me = lax.axis_index("head")
    project_both(normed, w, start, columns, theirs, mine)
    fill_incoming(here, there, incoming)
    given[...] = finish_block(me ^ 1, own, lead, c, incoming, gain)
    kept[...] = finish_block(me, own, lead, c, incoming, gain)
    wide = 512
    for k in range(0, w.shape[1], wide):
        theirs[:, columns + k:columns + k + wide] = dot(given[...], w[:, k:k + wide]).astype(BF)


def kept_kernel(columns, kept, come, w, out):
    wide = 512
    for k in range(0, w.shape[1], wide):
        out[:, k:k + wide] = dot(kept[...], w[:, k:k + wide]) + come[
            :, columns + k:columns + k + wide
        ].astype(F32)


def add_kernel(mine, come, out):
    out[...] = (mine[...] + come[:, :out.shape[1]].astype(F32)).astype(BF)


def local_call(kernel, operands, outs, name, scratch=(), flops=0, limit=VMEM_LIMIT):
    return pl.pallas_call(
        kernel,
        in_specs=[VMEM] * len(operands),
        out_specs=[VMEM] * len(outs),
        out_shape=[jax.ShapeDtypeStruct(shape, dtype) for shape, dtype in outs],
        scratch_shapes=list(scratch),
        compiler_params=pltpu.CompilerParams(vmem_limit_bytes=limit),
        cost_estimate=pl.CostEstimate(flops=flops, bytes_accessed=0, transcendentals=0),
        name=name,
    )(*operands)


def pass_kernel(*refs):
    pass


def await_piece(piece, *earlier):
    arrays = [piece, *earlier]
    return pl.pallas_call(
        pass_kernel,
        in_specs=[pl.BlockSpec(memory_space=pl.ANY)] * len(arrays),
        out_specs=[pl.BlockSpec(memory_space=pl.ANY)] * len(arrays),
        out_shape=[jax.ShapeDtypeStruct(v.shape, v.dtype) for v in arrays],
        input_output_aliases={k: k for k in range(len(arrays))},
        compiler_params=pltpu.CompilerParams(vmem_limit_bytes=1024 * 1024),
        cost_estimate=pl.CostEstimate(
            flops=20_000_000_000, bytes_accessed=100_000_000, transcendentals=0
        ),
        name="await_piece",
    )(*arrays)


def early_kernel(kept, first, second, out):
    at = 0
    for piece in (first, second):
        cut = slice(at, at + piece.shape[1])
        out[:, cut] = (kept[:, cut] + piece[...].astype(F32)).astype(BF)
        at += piece.shape[1]


def early_sums(kept, first, second):
    rows = first.shape[0]
    wide = first.shape[1] + second.shape[1]
    return pl.pallas_call(
        early_kernel,
        grid=(1,),
        in_specs=[VMEM] * 3,
        out_specs=pl.BlockSpec((rows, wide), lambda j: (0, 0)),
        out_shape=jax.ShapeDtypeStruct(kept.shape, BF),
        compiler_params=pltpu.CompilerParams(vmem_limit_bytes=VMEM_LIMIT),
        name="early_sums",
    )(kept, first, second)


def last_kernel(kept, third, filled, out, part, sems):
    wide = third.shape[1]
    start = kept.shape[1] - wide
    block = wide // 2
    stores = []
    for k in range(2):
        cut = slice(k * block, (k + 1) * block)
        part[:, cut] = (
            kept[:, start + k * block:start + (k + 1) * block] + third[:, cut].astype(F32)
        ).astype(BF)
        stores.append(
            pltpu.make_async_copy(
                part.at[:, cut], out.at[:, start + k * block:start + (k + 1) * block], sems.at[k]
            )
        )
        stores[k].start()
    for store in stores:
        store.wait()


def last_sums(kept, third, filled):
    return pl.pallas_call(
        last_kernel,
        in_specs=[VMEM, VMEM, pl.BlockSpec(memory_space=pl.ANY)],
        out_specs=pl.BlockSpec(memory_space=pl.ANY),
        out_shape=jax.ShapeDtypeStruct(kept.shape, BF),
        input_output_aliases={2: 0},
        scratch_shapes=[pltpu.VMEM(third.shape, BF), pltpu.SemaphoreType.DMA((2,))],
        compiler_params=pltpu.CompilerParams(vmem_limit_bytes=VMEM_LIMIT),
        name="last_sums",
    )(kept, third, filled)


def per_device(
    seq_count,
    ssm_input,
    gate_input,
    step_raw,
    decay_log,
    state_in,
    state_out,
    skip_gain,
    norm_gain,
    out_weight,
):
    tok = ssm_input.shape[0]
    heads = decay_log.shape[0]
    b = state_in.reshape(tok, N)
    c = state_out.reshape(tok, N)
    give, wk, aux = give_states(step_raw.T, decay_log.reshape(1, heads), ssm_input, b)
    keep = keep_states(wk, ssm_input, b)
    inputs = (ssm_input, b, c, gate_input, skip_gain.reshape(1, heads))
    local = within(True, aux, *inputs)
    (own, lead), here, there = incoming_states(
        give, keep, seq_count, lambda got: lax.optimization_barrier((local, got))
    )

    near = [(h, h ^ 1) for h in range(4)]
    far = [(h, h ^ 2) for h in range(4)]
    gain = norm_gain.reshape(1, -1)
    channels, dout = out_weight.shape
    rows = CHUNK
    states = pltpu.VMEM((2,) + here.shape, BF)
    finish = (own, lead, c, here, there, gain, out_weight)
    (_, one), (start2, two), (start3, three) = PIECES

    def piece_outs(columns, extra=0):
        return [((rows, columns + extra), BF), ((rows, columns), F32)]

    def add(mine, theirs):
        come = lax.ppermute(theirs, "head", near)
        return local_call(add_kernel, (mine, come), [(mine.shape, BF)], "add_pair", limit=1 << 22)[0], come

    theirs, mine, normed = local_call(
        functools.partial(far_kernel, one),
        finish,
        piece_outs(one) + [((2 * rows, channels), BF)],
        "finish_far",
        [states],
        4 * rows * channels * one,
    )
    first, _ = add(mine, theirs)
    aux, first = lax.optimization_barrier((aux, first))
    theirs, mine = local_call(
        functools.partial(more_kernel, start2, two),
        (normed, out_weight),
        piece_outs(two),
        "project_more",
        flops=4 * rows * channels * two,
    )
    second, _ = add(mine, theirs)
    near_own, near_lead = within(False, aux, *inputs)
    normed, second = lax.optimization_barrier((normed, second))
    theirs, mine, kept = local_call(
        functools.partial(mixed_kernel, start3, three),
        (normed, near_own, near_lead) + finish[2:],
        piece_outs(three, dout) + [((rows, channels), BF)],
        "finish_near",
        [states, pltpu.VMEM((rows, channels), BF)],
        2 * rows * channels * (2 * three + dout),
    )
    third, come = add(mine, theirs)
    kept = local_call(
        functools.partial(kept_kernel, three),
        (kept, come, out_weight),
        [((rows, dout), F32)],
        "project_kept",
        flops=2 * rows * channels * dout,
    )[0]
    first = await_piece(lax.ppermute(first, "head", far))[0]
    second, first = await_piece(lax.ppermute(second, "head", far), first)
    filled = early_sums(kept, first, second)
    third, filled = await_piece(lax.ppermute(third, "head", far), filled)
    return last_sums(kept, third, filled)


def solution(mesh):
    in_specs = (
        P("seq", "head"),
        P("seq", "head"),
        P("seq", "head"),
        P("head"),
        P("seq", "head", None),
        P("seq", "head", None),
        P("head"),
        P("head"),
        P("head", None),
    )
    out_specs = P(("seq", "head"), None)
    return jax.shard_map(
        functools.partial(per_device, mesh.shape["seq"]),
        mesh=mesh,
        in_specs=in_specs,
        out_specs=out_specs,
        check_vma=False,
    )
```

```python
import functools

import jax
import jax.numpy as jnp
from jax import lax
from jax.experimental import pallas as pl
from jax.experimental.pallas import tpu as pltpu
from jax.sharding import PartitionSpec as P

P_SIZE = 64
N = 128
CHUNK = 128
LANES = 128
BF = jnp.bfloat16
F32 = jnp.float32
VMEM_LIMIT = 16 * 1024 * 1024
WHOLE_VMEM = 61 * 1024 * 1024 + 512 * 1024
PIECES = ((0, 1024), (1024, 1536), (2560, 1536))


def dot(a, b, contract=((1,), (0,)), precision=None):
    return lax.dot_general(a, b, (contract, ((), ())), precision=precision, preferred_element_type=F32)


def split2(v):
    hi = v.astype(BF)
    return hi, (v - hi.astype(F32)).astype(BF)


def split3(v):
    hi, rest = v.astype(BF), v
    rest = v - hi.astype(F32)
    mid = rest.astype(BF)
    return hi, mid, (rest - mid.astype(F32)).astype(BF)


def pick(rows, lanes, heads, per_head, first):
    r = lax.broadcasted_iota(jnp.int32, (rows, lanes), 0) % heads
    l = lax.broadcasted_iota(jnp.int32, (rows, lanes), 1) // per_head + first
    return jnp.where(r == l, 1.0, 0.0).astype(BF)


def step_vectors(raw, rate_row, wk, aux_ref):
    heads, tok = raw.shape
    chunks = tok // CHUNK
    step = jnp.maximum(raw, 0.0) + jnp.log1p(jnp.exp(-jnp.abs(raw)))
    r = lax.broadcasted_iota(jnp.int32, (heads, heads), 0)
    l = lax.broadcasted_iota(jnp.int32, (heads, heads), 1)
    rate = jnp.sum(jnp.where(r == l, rate_row, 0.0), axis=1, keepdims=True)
    logs = -step * jnp.exp(rate)
    parts = split3(logs)
    stacked = jnp.concatenate(
        [p[:, c * CHUNK:(c + 1) * CHUNK] for c in range(chunks) for p in parts], axis=0
    )
    s = lax.broadcasted_iota(jnp.int32, (CHUNK, 2 * CHUNK), 0)
    t = lax.broadcasted_iota(jnp.int32, (CHUNK, 2 * CHUNK), 1)
    tri = jnp.where(jnp.where(t < CHUNK, t - s, s - t + (CHUNK - 1)) >= 0, 1.0, 0.0).astype(BF)
    sums = dot(stacked, tri)
    pre, suf = [], []
    for c in range(chunks):
        base = 3 * heads * c
        total = (
            sums[base:base + heads] + sums[base + heads:base + 2 * heads]
        ) + sums[base + 2 * heads:base + 3 * heads]
        pre.append(total[:, :CHUNK])
        suf.append(total[:, CHUNK:])
    after = jnp.zeros((heads, 1), F32)
    for c in reversed(range(chunks)):
        w = step[:, c * CHUNK:(c + 1) * CHUNK] * jnp.exp(suf[c] + after)
        hi, lo = split2(w)
        wk[:heads, c * CHUNK:(c + 1) * CHUNK] = hi
        wk[heads:, c * CHUNK:(c + 1) * CHUNK] = lo
        after = after + pre[c][:, CHUNK - 1:]
    hi, lo = split2(jnp.broadcast_to(jnp.exp(after), (heads, CHUNK)))
    wk[:heads, tok:] = hi
    wk[heads:, tok:] = lo
    for c in range(chunks):
        aux_ref[c, :heads] = step[:, c * CHUNK:(c + 1) * CHUNK]
        aux_ref[c, heads:2 * heads] = pre[c]
        aux_ref[c, 2 * heads:] = suf[c]


def tail_rows(decays):
    r = lax.broadcasted_iota(jnp.int32, (16, LANES), 0)
    tail = jnp.zeros((16, LANES), F32)
    for k, decay in enumerate(decays):
        hi, lo = split2(decay)
        tail = jnp.where(r == 2 * k, hi.astype(F32), tail)
        tail = jnp.where(r == 2 * k + 1, lo.astype(F32), tail)
    return tail.astype(BF)


def decays_of(msg):
    blocks = (msg.shape[0] - 16) // N
    tail = msg[blocks * N:].astype(F32)
    return [tail[2 * k:2 * k + 1] + tail[2 * k + 1:2 * k + 2] for k in range(blocks)]


def half_messages(x_ref, b, wk, first_head, msgs):
    tok, lanes = x_ref.shape
    heads2 = wk.shape[0]
    width = lanes // len(msgs)
    for g, msg in enumerate(msgs):
        chosen = pick(heads2, width, heads2 // 2, P_SIZE, first_head + g * (width // P_SIZE))
        spread = dot(wk[...], chosen, ((0,), (0,)))
        weighted = (x_ref[:, g * width:(g + 1) * width] * spread[:tok]).astype(BF)
        state = dot(b, weighted, ((0,), (0,)))
        decays = []
        for k in range(width // LANES):
            msg[k * N:(k + 1) * N] = state[:, k * LANES:(k + 1) * LANES].astype(BF)
            decays.append(spread[tok:tok + 1, k * LANES:(k + 1) * LANES])
        msg[msg.shape[0] - 16:] = tail_rows(decays)


def half_kernel(give, raw, rate, x, b, msgs, wk, aux, raw_v, rate_v, x_v, b_v, sems):
    lanes = x_v.shape[1]
    mine = lax.axis_index("seq") % 2
    half = 1 - mine if give else mine
    loads = [
        pltpu.make_async_copy(b, b_v, sems.at[0]),
        pltpu.make_async_copy(
            x.at[:, pl.ds(pl.multiple_of(half * lanes, lanes), lanes)], x_v, sems.at[1]
        ),
    ]
    if give:
        loads += [
            pltpu.make_async_copy(raw, raw_v, sems.at[2]),
            pltpu.make_async_copy(rate, rate_v, sems.at[3]),
        ]
    for load in reversed(loads):
        load.start()
    if give:
        loads[2].wait()
        loads[3].wait()
        step_vectors(raw_v[...], rate_v[...], wk, aux)
    loads[0].wait()
    loads[1].wait()
    half_messages(x_v, b_v[...].astype(BF), wk, half * (lanes // P_SIZE), msgs)


def give_kernel(raw, rate, x, b, msg0, msg1, wk, aux, raw_v, rate_v, x_v, b_v, sems):
    half_kernel(True, raw, rate, x, b, (msg0, msg1), wk, aux, raw_v, rate_v, x_v, b_v, sems)


def keep_kernel(wk, x, b, msg0, msg1, x_v, b_v, sems):
    half_kernel(False, None, None, x, b, (msg0, msg1), wk, None, None, None, x_v, b_v, sems)


HBM = pl.BlockSpec(memory_space=pltpu.HBM)
VMEM = pl.BlockSpec(memory_space=pltpu.VMEM)


def give_states(raw, rate, x, b):
    heads, tok = raw.shape
    lanes = x.shape[1] // 2
    return pl.pallas_call(
        give_kernel,
        in_specs=[HBM] * 4,
        out_shape=[
            jax.ShapeDtypeStruct((lanes // 2 + 16, LANES), BF),
            jax.ShapeDtypeStruct((lanes // 2 + 16, LANES), BF),
            jax.ShapeDtypeStruct((2 * heads, tok + CHUNK), BF),
            jax.ShapeDtypeStruct((tok // CHUNK, 3 * heads, CHUNK), F32),
        ],
        scratch_shapes=[
            pltpu.VMEM((heads, tok), F32),
            pltpu.VMEM((1, heads), F32),
            pltpu.VMEM((tok, lanes), F32),
            pltpu.VMEM((tok, N), F32),
            pltpu.SemaphoreType.DMA((4,)),
        ],
        compiler_params=pltpu.CompilerParams(vmem_limit_bytes=WHOLE_VMEM),
        cost_estimate=pl.CostEstimate(flops=200_000_000, bytes_accessed=1_500_000, transcendentals=0),
        name="give_states",
    )(raw, rate, x, b)


def keep_states(wk, x, b):
    tok = x.shape[0]
    lanes = x.shape[1] // 2
    return pl.pallas_call(
        keep_kernel,
        in_specs=[pl.BlockSpec(memory_space=pltpu.VMEM), HBM, HBM],
        out_shape=[jax.ShapeDtypeStruct((lanes // 2 + 16, LANES), BF)] * 2,
        scratch_shapes=[
            pltpu.VMEM((tok, lanes), F32),
            pltpu.VMEM((tok, N), F32),
            pltpu.SemaphoreType.DMA((2,)),
        ],
        compiler_params=pltpu.CompilerParams(vmem_limit_bytes=VMEM_LIMIT),
        cost_estimate=pl.CostEstimate(flops=200_000_000, bytes_accessed=1_500_000, transcendentals=0),
        name="keep_states",
    )(wk, x, b)


def link(later, earlier, out):
    ahead, behind = decays_of(later), decays_of(earlier)
    for k, decay in enumerate(ahead):
        rows = slice(k * N, (k + 1) * N)
        out[rows] = (later[rows].astype(F32) + decay * earlier[rows].astype(F32)).astype(BF)
    out[len(ahead) * N:] = tail_rows([p * q for p, q in zip(ahead, behind)])


def is_later(distance):
    return (lax.axis_index("seq") // distance) % 2


def run_kernel(distance, own, come, out):
    later = is_later(distance)

    @pl.when(later == 0)
    def _():
        link(come, own, out)

    @pl.when(later == 1)
    def _():
        link(own, come, out)


def first_ahead_kernel(distance, come, out):
    later = is_later(distance)
    rows = out.shape[0] - 16

    @pl.when(later == 0)
    def _():
        out[:rows] = jnp.zeros((rows, LANES), BF)
        out[rows:] = tail_rows([jnp.ones((1, LANES), F32)] * (rows // N))

    @pl.when(later == 1)
    def _():
        out[...] = come[...]


def ahead_kernel(distance, ahead, come, out):
    later = is_later(distance)

    @pl.when(later == 0)
    def _():
        out[...] = ahead[...]

    @pl.when(later == 1)
    def _():
        link(ahead, come, out)


def end_kernel(distance, ahead, last, own, come, mine, theirs):
    blocks = mine.shape[0] // N
    weight = is_later(distance).astype(F32)
    odd = is_later(1)

    def fill(even_section, ahead_ref, behind_ref):
        step, span = decays_of(ahead), decays_of(even_section)
        for k in range(blocks):
            rows = slice(k * N, (k + 1) * N)
            start = ahead[rows].astype(F32) + (weight * step[k]) * last[rows].astype(F32)
            ahead_ref[rows] = start.astype(BF)
            behind_ref[rows] = (even_section[rows].astype(F32) + span[k] * start).astype(BF)

    @pl.when(odd == 0)
    def _():
        fill(own, mine, theirs)

    @pl.when(odd == 1)
    def _():
        fill(come, theirs, mine)


def scan_call(kernel, operands, shapes, name):
    return pl.pallas_call(
        kernel,
        out_shape=[jax.ShapeDtypeStruct(shape, BF) for shape in shapes],
        compiler_params=pltpu.CompilerParams(vmem_limit_bytes=VMEM_LIMIT),
        cost_estimate=pl.CostEstimate(flops=500_000, bytes_accessed=400_000, transcendentals=0),
        name=name,
    )(*operands)


def incoming_states(give, keep, count, hold):
    def exchange(value, distance):
        return lax.ppermute(value, "seq", [(s, s ^ distance) for s in range(count)])

    def joined(kernel, distance, *operands):
        name = kernel.__name__[:-len("_kernel")]
        return scan_call(functools.partial(kernel, distance), operands, [keep.shape], name)[0]

    come = exchange(give, 1)
    run, distance = joined(run_kernel, 1, keep, come), 2
    got = exchange(run, distance)
    ahead = joined(first_ahead_kernel, distance, got)
    while distance * 2 < count:
        run, distance = joined(run_kernel, distance, run, got), distance * 2
        got = exchange(run, distance)
        if distance * 2 < count:
            ahead = joined(ahead_kernel, distance, ahead, got)
    if hold is not None:
        hold, got = lax.optimization_barrier((hold, got))
    half = (keep.shape[0] - 16, LANES)
    mine, theirs = scan_call(
        functools.partial(end_kernel, distance), (ahead, got, keep, come), [half, half], "join_end"
    )
    return hold, mine, exchange(theirs, 1)


def rows_of(ref, block):
    return ref[pl.ds(pl.multiple_of(block * CHUNK, CHUNK), CHUNK), :]


def within_kernel(far, aux, x_ref, b_ref, c_ref, gate_ref, skip_ref, own_ref, lead_ref):
    channels = x_ref.shape[1]
    heads = aux.shape[1] // 3
    width = 256
    here = width // P_SIZE
    half = lax.axis_index("head") // 2
    half = 1 - half if far else half
    second = half == 1

    def vectors(c):
        return [aux[c, k * heads:(k + 1) * heads] for k in range(3)]

    def put(values):
        return jnp.concatenate([jnp.concatenate(split2(v), axis=0) for v in values], axis=1)

    first, then = vectors(0), vectors(1)
    ends = [v[1][:, CHUNK - 1:] for v in (first, then)]
    early = put(
        [
            jnp.where(second, first[0] * jnp.exp(first[2] + ends[1]), 0.0),
            jnp.where(second, then[0] * jnp.exp(then[2]), 0.0),
        ]
    )
    before = jnp.where(second, ends[0] + ends[1], 0.0)
    r = lax.broadcasted_iota(jnp.int32, (CHUNK, CHUNK), 0)
    l = lax.broadcasted_iota(jnp.int32, (CHUNK, CHUNK), 1)
    duo, trip, lines, scores, rows_b, rows_c, rows_x, rows_g = ([] for _ in range(8))
    for i in range(2):
        block = 2 * half + i
        step, pre, suf = vectors(block)
        duo.append(put((step, step * jnp.exp(suf), jnp.exp(pre), jnp.exp(pre + before))))
        trip.append(jnp.concatenate(split3(pre), axis=0))
        lines.append(pre)
        before = before + pre[:, CHUNK - 1:]
        b, c = rows_of(b_ref, block), rows_of(c_ref, block)
        raw = dot(c, b, ((1,), (1,)), lax.Precision.HIGHEST)
        scores.append(jnp.where(r >= l, raw, 0.0))
        rows_b.append(b.astype(BF))
        rows_c.append(c.astype(BF))
        rows_x.append(rows_of(x_ref, block))
        rows_g.append(rows_of(gate_ref, block))
    early_b = b_ref[:2 * CHUNK].astype(BF)
    gains = jnp.broadcast_to(jnp.concatenate(split3(skip_ref[...]), axis=1), (8, 3 * heads))
    lane = lax.broadcasted_iota(jnp.int32, (CHUNK, LANES), 1)
    for g in range(channels // width):
        at = slice(g * width, (g + 1) * width)
        spread = pick(2 * heads, width, heads, P_SIZE, g * here)
        columns = pick(3 * heads, here * CHUNK, heads, CHUNK, g * here)
        skip = dot(gains, pick(3 * heads, width, heads, P_SIZE, g * here))[:1]
        weights = dot(early, spread, ((0,), (0,)))
        state = dot(early_b, (x_ref[:2 * CHUNK, at] * weights).astype(BF), ((0,), (0,)))
        for i in range(2):
            cut = slice(i * CHUNK, (i + 1) * CHUNK)
            wide = dot(duo[i], spread, ((0,), (0,)))
            x = rows_x[i][:, at]
            stepped = x * wide[:CHUNK]
            lead = wide[2 * CHUNK:3 * CHUNK]
            tall = dot(trip[i], columns, ((0,), (0,)))
            outs = []
            for pair in range(here // 2):
                mixes = []
                for h in (2 * pair, 2 * pair + 1):
                    line = lines[i][g * here + h:g * here + h + 1]
                    gap = tall[:, h * CHUNK:(h + 1) * CHUNK] - line
                    mixes.append((scores[i] * jnp.exp(jnp.minimum(gap, 0.0))).astype(BF))
                both = stepped[:, pair * LANES:(pair + 1) * LANES]
                stacked = jnp.concatenate(
                    [
                        jnp.where(lane < P_SIZE, both, 0.0).astype(BF),
                        jnp.where(lane < P_SIZE, 0.0, both).astype(BF),
                    ],
                    axis=0,
                )
                outs.append(dot(jnp.concatenate(mixes, axis=1), stacked))
            y = jnp.concatenate(outs, axis=1) + skip * x
            y = y + lead * dot(rows_c[i], state.astype(BF))
            v = rows_g[i][:, at].astype(F32)
            silu = v / (1.0 + jnp.exp(-v))
            own_ref[cut, at] = y * silu
            lead_ref[cut, at] = wide[3 * CHUNK:] * silu
            if i == 0:
                weighted = (x * wide[CHUNK:2 * CHUNK]).astype(BF)
                state = state * lead[CHUNK - 1:] + dot(rows_b[i], weighted, ((0,), (0,)))


def within(far, aux, x, b, c, gate, skip):
    channels = x.shape[1]
    return pl.pallas_call(
        functools.partial(within_kernel, far),
        in_specs=[VMEM] * 6,
        out_specs=[VMEM] * 2,
        out_shape=[jax.ShapeDtypeStruct((2 * CHUNK, channels), F32)] * 2,
        compiler_params=pltpu.CompilerParams(vmem_limit_bytes=VMEM_LIMIT),
        cost_estimate=pl.CostEstimate(
            flops=4_000_000_000, bytes_accessed=3_000_000, transcendentals=500_000
        ),
        name="within_far" if far else "within_near",
    )(aux, x, b, c, gate, skip)


def finish_rows(own, lead, c, incoming, gain):
    c = c.astype(BF)
    blocks = incoming.shape[1] // N
    carried = jnp.concatenate(
        [dot(c, incoming[h, k * N:(k + 1) * N]) for h in range(2) for k in range(blocks)], axis=1
    )
    gated = own + lead * carried
    mean = jnp.mean(gated * gated, axis=1, keepdims=True)
    return (gated * lax.rsqrt(mean + 1e-05) * gain).astype(BF)


def finish_block(block, own, lead, c, incoming, gain):
    return finish_rows(
        rows_of(own, block % 2), rows_of(lead, block % 2), rows_of(c, block), incoming, gain[...]
    )


def fill_incoming(here0, here1, there0, there1, incoming):
    odd = lax.axis_index("seq") % 2
    rows = here0.shape[0]
    incoming[odd, :rows] = here0[...]
    incoming[odd, rows:] = here1[...]
    incoming[1 - odd, :rows] = there0[...]
    incoming[1 - odd, rows:] = there1[...]


def project_both(normed, w, start, columns, theirs, mine, at=0):
    wide = 512
    for k in range(0, columns, wide):
        out = dot(normed[...], w[:, start + k:start + k + wide])
        theirs[:, at + k:at + k + wide] = out[:CHUNK].astype(BF)
        mine[:, k:k + wide] = out[CHUNK:]


def far_kernel(
    columns, own, lead, c, here0, here1, there0, there1, gain, w, theirs, mine, normed, incoming
):
    me = lax.axis_index("head")
    fill_incoming(here0, here1, there0, there1, incoming)
    normed[:CHUNK] = finish_block(me ^ 3, own, lead, c, incoming, gain)
    normed[CHUNK:] = finish_block(me ^ 2, own, lead, c, incoming, gain)
    project_both(normed, w, 0, columns, theirs, mine)


def more_kernel(start, columns, normed, w, theirs, mine):
    project_both(normed, w, start, columns, theirs, mine)


def mixed_kernel(
    start, columns, normed, own, lead, c, here0, here1, there0, there1, gain, w,
    theirs, mine, kept, incoming, given,
):
    me = lax.axis_index("head")
    project_both(normed, w, start, columns, theirs, mine)
    fill_incoming(here0, here1, there0, there1, incoming)
    given[...] = finish_block(me ^ 1, own, lead, c, incoming, gain)
    kept[...] = finish_block(me, own, lead, c, incoming, gain)
    wide = 512
    for k in range(0, w.shape[1], wide):
        theirs[:, columns + k:columns + k + wide] = dot(given[...], w[:, k:k + wide]).astype(BF)


def kept_kernel(columns, kept, come, w, out):
    wide = 512
    for k in range(0, w.shape[1], wide):
        out[:, k:k + wide] = dot(kept[...], w[:, k:k + wide]) + come[
            :, columns + k:columns + k + wide
        ].astype(F32)


def add_kernel(mine, come, out):
    out[...] = (mine[...] + come[:, :out.shape[1]].astype(F32)).astype(BF)


def local_call(kernel, operands, outs, name, scratch=(), flops=0, limit=VMEM_LIMIT):
    return pl.pallas_call(
        kernel,
        in_specs=[VMEM] * len(operands),
        out_specs=[VMEM] * len(outs),
        out_shape=[jax.ShapeDtypeStruct(shape, dtype) for shape, dtype in outs],
        scratch_shapes=list(scratch),
        compiler_params=pltpu.CompilerParams(vmem_limit_bytes=limit),
        cost_estimate=pl.CostEstimate(flops=flops, bytes_accessed=0, transcendentals=0),
        name=name,
    )(*operands)


def pass_kernel(*refs):
    pass


def await_piece(piece, *earlier):
    arrays = [piece, *earlier]
    return pl.pallas_call(
        pass_kernel,
        in_specs=[pl.BlockSpec(memory_space=pl.ANY)] * len(arrays),
        out_specs=[pl.BlockSpec(memory_space=pl.ANY)] * len(arrays),
        out_shape=[jax.ShapeDtypeStruct(v.shape, v.dtype) for v in arrays],
        input_output_aliases={k: k for k in range(len(arrays))},
        compiler_params=pltpu.CompilerParams(vmem_limit_bytes=1024 * 1024),
        cost_estimate=pl.CostEstimate(
            flops=20_000_000_000, bytes_accessed=100_000_000, transcendentals=0
        ),
        name="await_piece",
    )(*arrays)


def early_kernel(kept, first, second, out):
    at = 0
    for piece in (first, second):
        cut = slice(at, at + piece.shape[1])
        out[:, cut] = (kept[:, cut] + piece[...].astype(F32)).astype(BF)
        at += piece.shape[1]


def early_sums(kept, first, second):
    rows = first.shape[0]
    wide = first.shape[1] + second.shape[1]
    return pl.pallas_call(
        early_kernel,
        grid=(1,),
        in_specs=[VMEM] * 3,
        out_specs=pl.BlockSpec((rows, wide), lambda j: (0, 0)),
        out_shape=jax.ShapeDtypeStruct(kept.shape, BF),
        compiler_params=pltpu.CompilerParams(vmem_limit_bytes=VMEM_LIMIT),
        name="early_sums",
    )(kept, first, second)


def last_kernel(kept, third, filled, out, part, sems):
    wide = third.shape[1]
    start = kept.shape[1] - wide
    block = wide // 2
    stores = []
    for k in range(2):
        cut = slice(k * block, (k + 1) * block)
        part[:, cut] = (
            kept[:, start + k * block:start + (k + 1) * block] + third[:, cut].astype(F32)
        ).astype(BF)
        stores.append(
            pltpu.make_async_copy(
                part.at[:, cut], out.at[:, start + k * block:start + (k + 1) * block], sems.at[k]
            )
        )
        stores[k].start()
    for store in stores:
        store.wait()


def last_sums(kept, third, filled):
    return pl.pallas_call(
        last_kernel,
        in_specs=[VMEM, VMEM, pl.BlockSpec(memory_space=pl.ANY)],
        out_specs=pl.BlockSpec(memory_space=pl.ANY),
        out_shape=jax.ShapeDtypeStruct(kept.shape, BF),
        input_output_aliases={2: 0},
        scratch_shapes=[pltpu.VMEM(third.shape, BF), pltpu.SemaphoreType.DMA((2,))],
        compiler_params=pltpu.CompilerParams(vmem_limit_bytes=VMEM_LIMIT),
        name="last_sums",
    )(kept, third, filled)


def per_device(
    seq_count,
    ssm_input,
    gate_input,
    step_raw,
    decay_log,
    state_in,
    state_out,
    skip_gain,
    norm_gain,
    out_weight,
):
    tok = ssm_input.shape[0]
    heads = decay_log.shape[0]
    b = state_in.reshape(tok, N)
    c = state_out.reshape(tok, N)
    give0, give1, wk, aux = give_states(step_raw.T, decay_log.reshape(1, heads), ssm_input, b)
    keep0, keep1 = keep_states(wk, ssm_input, b)
    inputs = (ssm_input, b, c, gate_input, skip_gain.reshape(1, heads))
    local = within(True, aux, *inputs)
    (own, lead), here0, there0 = incoming_states(give0, keep0, seq_count, local)
    _, here1, there1 = incoming_states(give1, keep1, seq_count, None)

    near = [(h, h ^ 1) for h in range(4)]
    far = [(h, h ^ 2) for h in range(4)]
    gain = norm_gain.reshape(1, -1)
    channels, dout = out_weight.shape
    rows = CHUNK
    states = pltpu.VMEM((2, 2 * here0.shape[0], LANES), BF)
    finish = (own, lead, c, here0, here1, there0, there1, gain, out_weight)
    (_, one), (start2, two), (start3, three) = PIECES

    def piece_outs(columns, extra=0):
        return [((rows, columns + extra), BF), ((rows, columns), F32)]

    def add(mine, theirs):
        come = lax.ppermute(theirs, "head", near)
        return local_call(add_kernel, (mine, come), [(mine.shape, BF)], "add_pair", limit=1 << 22)[0], come

    theirs, mine, normed = local_call(
        functools.partial(far_kernel, one),
        finish,
        piece_outs(one) + [((2 * rows, channels), BF)],
        "finish_far",
        [states],
        4 * rows * channels * one,
    )
    first, _ = add(mine, theirs)
    aux, first = lax.optimization_barrier((aux, first))
    theirs, mine = local_call(
        functools.partial(more_kernel, start2, two),
        (normed, out_weight),
        piece_outs(two),
        "project_more",
        flops=4 * rows * channels * two,
    )
    second, _ = add(mine, theirs)
    near_own, near_lead = within(False, aux, *inputs)
    normed, second = lax.optimization_barrier((normed, second))
    theirs, mine, kept = local_call(
        functools.partial(mixed_kernel, start3, three),
        (normed, near_own, near_lead) + finish[2:],
        piece_outs(three, dout) + [((rows, channels), BF)],
        "finish_near",
        [states, pltpu.VMEM((rows, channels), BF)],
        2 * rows * channels * (2 * three + dout),
    )
    third, come = add(mine, theirs)
    kept = local_call(
        functools.partial(kept_kernel, three),
        (kept, come, out_weight),
        [((rows, dout), F32)],
        "project_kept",
        flops=2 * rows * channels * dout,
    )[0]
    first = await_piece(lax.ppermute(first, "head", far))[0]
    second, first = await_piece(lax.ppermute(second, "head", far), first)
    filled = early_sums(kept, first, second)
    third, filled = await_piece(lax.ppermute(third, "head", far), filled)
    return last_sums(kept, third, filled)


def solution(mesh):
    in_specs = (
        P("seq", "head"),
        P("seq", "head"),
        P("seq", "head"),
        P("head"),
        P("seq", "head", None),
        P("seq", "head", None),
        P("head"),
        P("head"),
        P("head", None),
    )
    out_specs = P(("seq", "head"), None)
    return jax.shard_map(
        functools.partial(per_device, mesh.shape["seq"]),
        mesh=mesh,
        in_specs=in_specs,
        out_specs=out_specs,
        check_vma=False,
    )
```

```python
import functools

import jax
import jax.numpy as jnp
from jax import lax
from jax.experimental import pallas as pl
from jax.experimental.pallas import tpu as pltpu
from jax.sharding import PartitionSpec as P

P_SIZE = 64
N = 128
CHUNK = 128
LANES = 128
BF = jnp.bfloat16
F32 = jnp.float32
VMEM_LIMIT = 16 * 1024 * 1024
WHOLE_VMEM = 61 * 1024 * 1024 + 512 * 1024
PIECES = ((0, 1024), (1024, 1536), (2560, 1536))


def dot(a, b, contract=((1,), (0,)), precision=None):
    return lax.dot_general(a, b, (contract, ((), ())), precision=precision, preferred_element_type=F32)


def split2(v):
    hi = v.astype(BF)
    return hi, (v - hi.astype(F32)).astype(BF)


def split3(v):
    hi, rest = v.astype(BF), v
    rest = v - hi.astype(F32)
    mid = rest.astype(BF)
    return hi, mid, (rest - mid.astype(F32)).astype(BF)


def pick(rows, lanes, heads, per_head, first):
    r = lax.broadcasted_iota(jnp.int32, (rows, lanes), 0) % heads
    l = lax.broadcasted_iota(jnp.int32, (rows, lanes), 1) // per_head + first
    return jnp.where(r == l, 1.0, 0.0).astype(BF)


def step_vectors(raw, rate_row, wk, aux_ref):
    heads, tok = raw.shape
    chunks = tok // CHUNK
    step = jnp.maximum(raw, 0.0) + jnp.log1p(jnp.exp(-jnp.abs(raw)))
    r = lax.broadcasted_iota(jnp.int32, (heads, heads), 0)
    l = lax.broadcasted_iota(jnp.int32, (heads, heads), 1)
    rate = jnp.sum(jnp.where(r == l, rate_row, 0.0), axis=1, keepdims=True)
    logs = -step * jnp.exp(rate)
    parts = split3(logs)
    stacked = jnp.concatenate(
        [p[:, c * CHUNK:(c + 1) * CHUNK] for c in range(chunks) for p in parts], axis=0
    )
    s = lax.broadcasted_iota(jnp.int32, (CHUNK, 2 * CHUNK), 0)
    t = lax.broadcasted_iota(jnp.int32, (CHUNK, 2 * CHUNK), 1)
    tri = jnp.where(jnp.where(t < CHUNK, t - s, s - t + (CHUNK - 1)) >= 0, 1.0, 0.0).astype(BF)
    sums = dot(stacked, tri)
    pre, suf = [], []
    for c in range(chunks):
        base = 3 * heads * c
        total = (
            sums[base:base + heads] + sums[base + heads:base + 2 * heads]
        ) + sums[base + 2 * heads:base + 3 * heads]
        pre.append(total[:, :CHUNK])
        suf.append(total[:, CHUNK:])
    after = jnp.zeros((heads, 1), F32)
    for c in reversed(range(chunks)):
        w = step[:, c * CHUNK:(c + 1) * CHUNK] * jnp.exp(suf[c] + after)
        hi, lo = split2(w)
        wk[:heads, c * CHUNK:(c + 1) * CHUNK] = hi
        wk[heads:, c * CHUNK:(c + 1) * CHUNK] = lo
        after = after + pre[c][:, CHUNK - 1:]
    hi, lo = split2(jnp.broadcast_to(jnp.exp(after), (heads, CHUNK)))
    wk[:heads, tok:] = hi
    wk[heads:, tok:] = lo
    for c in range(chunks):
        aux_ref[c, :heads] = step[:, c * CHUNK:(c + 1) * CHUNK]
        aux_ref[c, heads:2 * heads] = pre[c]
        aux_ref[c, 2 * heads:] = suf[c]


def tail_rows(decays):
    r = lax.broadcasted_iota(jnp.int32, (16, LANES), 0)
    tail = jnp.zeros((16, LANES), F32)
    for k, decay in enumerate(decays):
        hi, lo = split2(decay)
        tail = jnp.where(r == 2 * k, hi.astype(F32), tail)
        tail = jnp.where(r == 2 * k + 1, lo.astype(F32), tail)
    return tail.astype(BF)


def decays_of(msg):
    blocks = (msg.shape[0] - 16) // N
    tail = msg[blocks * N:].astype(F32)
    return [tail[2 * k:2 * k + 1] + tail[2 * k + 1:2 * k + 2] for k in range(blocks)]


def quarter_message(x, b, wk, first_head, msg):
    tok, width = x.shape
    heads2 = wk.shape[0]
    spread = dot(wk[...], pick(heads2, width, heads2 // 2, P_SIZE, first_head), ((0,), (0,)))
    state = dot(b, (x * spread[:tok]).astype(BF), ((0,), (0,)))
    decays = []
    for k in range(width // LANES):
        msg[k * N:(k + 1) * N] = state[:, k * LANES:(k + 1) * LANES].astype(BF)
        decays.append(spread[tok:tok + 1, k * LANES:(k + 1) * LANES])
    msg[msg.shape[0] - 16:] = tail_rows(decays)


def load_quarter(x, x_v, quarter, sem):
    width = x_v.shape[1]
    return pltpu.make_async_copy(
        x.at[:, pl.ds(pl.multiple_of(quarter * width, width), width)], x_v, sem
    )


def give_kernel(raw, rate, x, b, msg1, msg2, msg3, wk, aux, raw_v, rate_v, x_v, b_v, sems):
    mine = lax.axis_index("seq") % 4
    loads = [
        pltpu.make_async_copy(raw, raw_v, sems.at[0]),
        pltpu.make_async_copy(rate, rate_v, sems.at[1]),
        pltpu.make_async_copy(b, b_v, sems.at[2]),
    ] + [load_quarter(x, x_v.at[k - 1], mine ^ k, sems.at[2 + k]) for k in (1, 2, 3)]
    for load in loads:
        load.start()
    loads[0].wait()
    loads[1].wait()
    step_vectors(raw_v[...], rate_v[...], wk, aux)
    for load in loads[2:]:
        load.wait()
    b16 = b_v[...].astype(BF)
    heads = x_v.shape[2] // P_SIZE
    for k, msg in ((1, msg1), (2, msg2), (3, msg3)):
        quarter_message(x_v[k - 1], b16, wk, (mine ^ k) * heads, msg)


def keep_kernel(wk, x, b, msg, x_v, b_v, sems):
    mine = lax.axis_index("seq") % 4
    loads = [load_quarter(x, x_v, mine, sems.at[0]), pltpu.make_async_copy(b, b_v, sems.at[1])]
    for load in loads:
        load.start()
    for load in loads:
        load.wait()
    quarter_message(x_v[...], b_v[...].astype(BF), wk, mine * (x_v.shape[1] // P_SIZE), msg)


HBM = pl.BlockSpec(memory_space=pltpu.HBM)
VMEM = pl.BlockSpec(memory_space=pltpu.VMEM)


def give_states(raw, rate, x, b):
    heads, tok = raw.shape
    lanes = x.shape[1] // 4
    return pl.pallas_call(
        give_kernel,
        in_specs=[HBM] * 4,
        out_shape=[jax.ShapeDtypeStruct((lanes // LANES * N + 16, LANES), BF)] * 3
        + [
            jax.ShapeDtypeStruct((2 * heads, tok + CHUNK), BF),
            jax.ShapeDtypeStruct((tok // CHUNK, 3 * heads, CHUNK), F32),
        ],
        scratch_shapes=[
            pltpu.VMEM((heads, tok), F32),
            pltpu.VMEM((1, heads), F32),
            pltpu.VMEM((3, tok, lanes), F32),
            pltpu.VMEM((tok, N), F32),
            pltpu.SemaphoreType.DMA((6,)),
        ],
        compiler_params=pltpu.CompilerParams(vmem_limit_bytes=WHOLE_VMEM),
        cost_estimate=pl.CostEstimate(flops=200_000_000, bytes_accessed=1_500_000, transcendentals=0),
        name="give_states",
    )(raw, rate, x, b)


def keep_states(wk, x, b):
    tok = x.shape[0]
    lanes = x.shape[1] // 4
    return pl.pallas_call(
        keep_kernel,
        in_specs=[VMEM, HBM, HBM],
        out_shape=jax.ShapeDtypeStruct((lanes // LANES * N + 16, LANES), BF),
        scratch_shapes=[
            pltpu.VMEM((tok, lanes), F32),
            pltpu.VMEM((tok, N), F32),
            pltpu.SemaphoreType.DMA((2,)),
        ],
        compiler_params=pltpu.CompilerParams(vmem_limit_bytes=VMEM_LIMIT),
        cost_estimate=pl.CostEstimate(flops=200_000_000, bytes_accessed=1_500_000, transcendentals=0),
        name="keep_states",
    )(wk, x, b)


def link(later, earlier, out):
    ahead, behind = decays_of(later), decays_of(earlier)
    for k, decay in enumerate(ahead):
        rows = slice(k * N, (k + 1) * N)
        out[rows] = (later[rows].astype(F32) + decay * earlier[rows].astype(F32)).astype(BF)
    out[len(ahead) * N:] = tail_rows([p * q for p, q in zip(ahead, behind)])


def is_later(distance):
    return (lax.axis_index("seq") // distance) % 2


def run_kernel(distance, own, come, out):
    later = is_later(distance)

    @pl.when(later == 0)
    def _():
        link(come, own, out)

    @pl.when(later == 1)
    def _():
        link(own, come, out)


def first_ahead_kernel(distance, come, out):
    later = is_later(distance)
    rows = out.shape[0] - 16

    @pl.when(later == 0)
    def _():
        out[:rows] = jnp.zeros((rows, LANES), BF)
        out[rows:] = tail_rows([jnp.ones((1, LANES), F32)] * (rows // N))

    @pl.when(later == 1)
    def _():
        out[...] = come[...]


def ahead_kernel(distance, ahead, come, out):
    later = is_later(distance)

    @pl.when(later == 0)
    def _():
        out[...] = ahead[...]

    @pl.when(later == 1)
    def _():
        link(ahead, come, out)


def by_section(work):
    mine = lax.axis_index("seq") % 4
    for v in range(4):
        pl.when(mine == v)(functools.partial(work, [j ^ v for j in range(4)]))


def join_four_kernel(own, come1, come2, come3, out):
    messages = (own, come1, come2, come3)

    def work(place):
        sections = [messages[p] for p in place]
        decays = [decays_of(section) for section in sections]
        for k in range(len(decays[0])):
            rows = slice(k * N, (k + 1) * N)
            total = sections[0][rows].astype(F32)
            for section, decay in zip(sections[1:], decays[1:]):
                total = section[rows].astype(F32) + decay[k] * total
            out[rows] = total.astype(BF)
        spans = [p * q * r * t for p, q, r, t in zip(*decays)]
        out[len(spans) * N:] = tail_rows(spans)

    by_section(work)


def end_kernel(distance, ahead, last, own, come1, come2, come3, mine, out1, out2, out3):
    messages, outs = (own, come1, come2, come3), (mine, out1, out2, out3)
    weight = is_later(distance).astype(F32)

    def work(place):
        sections, targets = [messages[p] for p in place], [outs[p] for p in place]
        decays = [decays_of(section) for section in sections]
        for k in range(len(decays[0])):
            rows = slice(k * N, (k + 1) * N)
            state = weight * last[rows].astype(F32)
            if ahead is not None:
                state = ahead[rows].astype(F32) + decays_of(ahead)[k] * state
            for j in range(4):
                targets[j][rows] = state.astype(BF)
                if j < 3:
                    state = sections[j][rows].astype(F32) + decays[j][k] * state

    by_section(work)


def scan_call(kernel, operands, shapes, name):
    return pl.pallas_call(
        kernel,
        out_shape=[jax.ShapeDtypeStruct(shape, BF) for shape in shapes],
        compiler_params=pltpu.CompilerParams(vmem_limit_bytes=VMEM_LIMIT),
        cost_estimate=pl.CostEstimate(flops=500_000, bytes_accessed=400_000, transcendentals=0),
        name=name,
    )(*operands)


def incoming_states(gives, keep, count, hold):
    def exchange(value, distance):
        return lax.ppermute(value, "seq", [(s, s ^ distance) for s in range(count)])

    def joined(kernel, *operands):
        return scan_call(kernel, operands, [keep.shape], "join_states")[0]

    parts = [keep] + [exchange(give, k) for k, give in zip((1, 2, 3), gives)]
    run, ahead, distance = joined(join_four_kernel, *parts), None, 4
    got = exchange(run, distance)
    while distance * 2 < count:
        if ahead is None:
            ahead = joined(functools.partial(first_ahead_kernel, distance), got)
        else:
            ahead = joined(functools.partial(ahead_kernel, distance), ahead, got)
        run = joined(functools.partial(run_kernel, distance), run, got)
        distance *= 2
        got = exchange(run, distance)
    hold, got = lax.optimization_barrier((hold, got))
    operands = [got] + parts
    if ahead is None:
        kernel = functools.partial(end_kernel, distance, None)
    else:
        kernel, operands = functools.partial(end_kernel, distance), [ahead] + operands
    shape = (keep.shape[0] - 16, LANES)
    outs = scan_call(kernel, operands, [shape] * 4, "join_end")
    return hold, [outs[0]] + [exchange(out, k) for k, out in zip((1, 2, 3), outs[1:])]


def rows_of(ref, block):
    return ref[pl.ds(pl.multiple_of(block * CHUNK, CHUNK), CHUNK), :]


def within_kernel(far, aux, x_ref, b_ref, c_ref, gate_ref, skip_ref, own_ref, lead_ref):
    channels = x_ref.shape[1]
    heads = aux.shape[1] // 3
    width = 256
    here = width // P_SIZE
    half = lax.axis_index("head") // 2
    half = 1 - half if far else half
    second = half == 1

    def vectors(c):
        return [aux[c, k * heads:(k + 1) * heads] for k in range(3)]

    def put(values):
        return jnp.concatenate([jnp.concatenate(split2(v), axis=0) for v in values], axis=1)

    first, then = vectors(0), vectors(1)
    ends = [v[1][:, CHUNK - 1:] for v in (first, then)]
    early = put(
        [
            jnp.where(second, first[0] * jnp.exp(first[2] + ends[1]), 0.0),
            jnp.where(second, then[0] * jnp.exp(then[2]), 0.0),
        ]
    )
    before = jnp.where(second, ends[0] + ends[1], 0.0)
    r = lax.broadcasted_iota(jnp.int32, (CHUNK, CHUNK), 0)
    l = lax.broadcasted_iota(jnp.int32, (CHUNK, CHUNK), 1)
    duo, trip, lines, scores, rows_b, rows_c, rows_x, rows_g = ([] for _ in range(8))
    for i in range(2):
        block = 2 * half + i
        step, pre, suf = vectors(block)
        duo.append(put((step, step * jnp.exp(suf), jnp.exp(pre), jnp.exp(pre + before))))
        trip.append(jnp.concatenate(split3(pre), axis=0))
        lines.append(pre)
        before = before + pre[:, CHUNK - 1:]
        b, c = rows_of(b_ref, block), rows_of(c_ref, block)
        raw = dot(c, b, ((1,), (1,)), lax.Precision.HIGHEST)
        scores.append(jnp.where(r >= l, raw, 0.0))
        rows_b.append(b.astype(BF))
        rows_c.append(c.astype(BF))
        rows_x.append(rows_of(x_ref, block))
        rows_g.append(rows_of(gate_ref, block))
    early_b = b_ref[:2 * CHUNK].astype(BF)
    gains = jnp.broadcast_to(jnp.concatenate(split3(skip_ref[...]), axis=1), (8, 3 * heads))
    lane = lax.broadcasted_iota(jnp.int32, (CHUNK, LANES), 1)
    for g in range(channels // width):
        at = slice(g * width, (g + 1) * width)
        spread = pick(2 * heads, width, heads, P_SIZE, g * here)
        columns = pick(3 * heads, here * CHUNK, heads, CHUNK, g * here)
        skip = dot(gains, pick(3 * heads, width, heads, P_SIZE, g * here))[:1]
        weights = dot(early, spread, ((0,), (0,)))
        state = dot(early_b, (x_ref[:2 * CHUNK, at] * weights).astype(BF), ((0,), (0,)))
        for i in range(2):
            cut = slice(i * CHUNK, (i + 1) * CHUNK)
            wide = dot(duo[i], spread, ((0,), (0,)))
            x = rows_x[i][:, at]
            stepped = x * wide[:CHUNK]
            lead = wide[2 * CHUNK:3 * CHUNK]
            tall = dot(trip[i], columns, ((0,), (0,)))
            outs = []
            for pair in range(here // 2):
                mixes = []
                for h in (2 * pair, 2 * pair + 1):
                    line = lines[i][g * here + h:g * here + h + 1]
                    gap = tall[:, h * CHUNK:(h + 1) * CHUNK] - line
                    mixes.append((scores[i] * jnp.exp(jnp.minimum(gap, 0.0))).astype(BF))
                both = stepped[:, pair * LANES:(pair + 1) * LANES]
                stacked = jnp.concatenate(
                    [
                        jnp.where(lane < P_SIZE, both, 0.0).astype(BF),
                        jnp.where(lane < P_SIZE, 0.0, both).astype(BF),
                    ],
                    axis=0,
                )
                outs.append(dot(jnp.concatenate(mixes, axis=1), stacked))
            y = jnp.concatenate(outs, axis=1) + skip * x
            y = y + lead * dot(rows_c[i], state.astype(BF))
            v = rows_g[i][:, at].astype(F32)
            silu = v / (1.0 + jnp.exp(-v))
            own_ref[cut, at] = y * silu
            lead_ref[cut, at] = wide[3 * CHUNK:] * silu
            if i == 0:
                weighted = (x * wide[CHUNK:2 * CHUNK]).astype(BF)
                state = state * lead[CHUNK - 1:] + dot(rows_b[i], weighted, ((0,), (0,)))


def within(far, aux, x, b, c, gate, skip):
    channels = x.shape[1]
    return pl.pallas_call(
        functools.partial(within_kernel, far),
        in_specs=[VMEM] * 6,
        out_specs=[VMEM] * 2,
        out_shape=[jax.ShapeDtypeStruct((2 * CHUNK, channels), F32)] * 2,
        compiler_params=pltpu.CompilerParams(vmem_limit_bytes=VMEM_LIMIT),
        cost_estimate=pl.CostEstimate(
            flops=4_000_000_000, bytes_accessed=3_000_000, transcendentals=500_000
        ),
        name="within_far" if far else "within_near",
    )(aux, x, b, c, gate, skip)


def finish_rows(own, lead, c, incoming, gain):
    c = c.astype(BF)
    blocks = incoming.shape[1] // N
    carried = jnp.concatenate(
        [dot(c, incoming[q, k * N:(k + 1) * N]) for q in range(4) for k in range(blocks)], axis=1
    )
    gated = own + lead * carried
    mean = jnp.mean(gated * gated, axis=1, keepdims=True)
    return (gated * lax.rsqrt(mean + 1e-05) * gain).astype(BF)


def finish_block(block, own, lead, c, incoming, gain):
    return finish_rows(
        rows_of(own, block % 2), rows_of(lead, block % 2), rows_of(c, block), incoming, gain[...]
    )


def fill_incoming(quarters, incoming):
    mine = lax.axis_index("seq") % 4
    for k, quarter in enumerate(quarters):
        incoming[mine ^ k] = quarter[...]


def project_both(normed, w, start, columns, theirs, mine, at=0):
    wide = 512
    for k in range(0, columns, wide):
        out = dot(normed[...], w[:, start + k:start + k + wide])
        theirs[:, at + k:at + k + wide] = out[:CHUNK].astype(BF)
        mine[:, k:k + wide] = out[CHUNK:]


def far_kernel(
    columns, own, lead, c, q0, q1, q2, q3, gain, w, theirs, mine, normed, incoming
):
    me = lax.axis_index("head")
    fill_incoming((q0, q1, q2, q3), incoming)
    normed[:CHUNK] = finish_block(me ^ 3, own, lead, c, incoming, gain)
    normed[CHUNK:] = finish_block(me ^ 2, own, lead, c, incoming, gain)
    project_both(normed, w, 0, columns, theirs, mine)


def more_kernel(start, columns, normed, w, theirs, mine):
    project_both(normed, w, start, columns, theirs, mine)


def mixed_kernel(
    start, columns, normed, own, lead, c, q0, q1, q2, q3, gain, w,
    theirs, mine, kept, incoming, given,
):
    me = lax.axis_index("head")
    project_both(normed, w, start, columns, theirs, mine)
    fill_incoming((q0, q1, q2, q3), incoming)
    given[...] = finish_block(me ^ 1, own, lead, c, incoming, gain)
    kept[...] = finish_block(me, own, lead, c, incoming, gain)
    wide = 512
    for k in range(0, w.shape[1], wide):
        theirs[:, columns + k:columns + k + wide] = dot(given[...], w[:, k:k + wide]).astype(BF)


def kept_kernel(columns, kept, come, w, out):
    wide = 512
    for k in range(0, w.shape[1], wide):
        out[:, k:k + wide] = dot(kept[...], w[:, k:k + wide]) + come[
            :, columns + k:columns + k + wide
        ].astype(F32)


def add_kernel(mine, come, out):
    out[...] = (mine[...] + come[:, :out.shape[1]].astype(F32)).astype(BF)


def local_call(kernel, operands, outs, name, scratch=(), flops=0, limit=VMEM_LIMIT):
    return pl.pallas_call(
        kernel,
        in_specs=[VMEM] * len(operands),
        out_specs=[VMEM] * len(outs),
        out_shape=[jax.ShapeDtypeStruct(shape, dtype) for shape, dtype in outs],
        scratch_shapes=list(scratch),
        compiler_params=pltpu.CompilerParams(vmem_limit_bytes=limit),
        cost_estimate=pl.CostEstimate(flops=flops, bytes_accessed=0, transcendentals=0),
        name=name,
    )(*operands)


def pass_kernel(*refs):
    pass


def await_piece(piece, *earlier):
    arrays = [piece, *earlier]
    return pl.pallas_call(
        pass_kernel,
        in_specs=[pl.BlockSpec(memory_space=pl.ANY)] * len(arrays),
        out_specs=[pl.BlockSpec(memory_space=pl.ANY)] * len(arrays),
        out_shape=[jax.ShapeDtypeStruct(v.shape, v.dtype) for v in arrays],
        input_output_aliases={k: k for k in range(len(arrays))},
        compiler_params=pltpu.CompilerParams(vmem_limit_bytes=1024 * 1024),
        cost_estimate=pl.CostEstimate(
            flops=20_000_000_000, bytes_accessed=100_000_000, transcendentals=0
        ),
        name="await_piece",
    )(*arrays)


def early_kernel(kept, first, second, out):
    at = 0
    for piece in (first, second):
        cut = slice(at, at + piece.shape[1])
        out[:, cut] = (kept[:, cut] + piece[...].astype(F32)).astype(BF)
        at += piece.shape[1]


def early_sums(kept, first, second):
    rows = first.shape[0]
    wide = first.shape[1] + second.shape[1]
    return pl.pallas_call(
        early_kernel,
        grid=(1,),
        in_specs=[VMEM] * 3,
        out_specs=pl.BlockSpec((rows, wide), lambda j: (0, 0)),
        out_shape=jax.ShapeDtypeStruct(kept.shape, BF),
        compiler_params=pltpu.CompilerParams(vmem_limit_bytes=VMEM_LIMIT),
        name="early_sums",
    )(kept, first, second)


def last_kernel(kept, third, filled, out, part, sems):
    wide = third.shape[1]
    start = kept.shape[1] - wide
    block = wide // 2
    stores = []
    for k in range(2):
        cut = slice(k * block, (k + 1) * block)
        part[:, cut] = (
            kept[:, start + k * block:start + (k + 1) * block] + third[:, cut].astype(F32)
        ).astype(BF)
        stores.append(
            pltpu.make_async_copy(
                part.at[:, cut], out.at[:, start + k * block:start + (k + 1) * block], sems.at[k]
            )
        )
        stores[k].start()
    for store in stores:
        store.wait()


def last_sums(kept, third, filled):
    return pl.pallas_call(
        last_kernel,
        in_specs=[VMEM, VMEM, pl.BlockSpec(memory_space=pl.ANY)],
        out_specs=pl.BlockSpec(memory_space=pl.ANY),
        out_shape=jax.ShapeDtypeStruct(kept.shape, BF),
        input_output_aliases={2: 0},
        scratch_shapes=[pltpu.VMEM(third.shape, BF), pltpu.SemaphoreType.DMA((2,))],
        compiler_params=pltpu.CompilerParams(vmem_limit_bytes=VMEM_LIMIT),
        name="last_sums",
    )(kept, third, filled)


def per_device(
    seq_count,
    ssm_input,
    gate_input,
    step_raw,
    decay_log,
    state_in,
    state_out,
    skip_gain,
    norm_gain,
    out_weight,
):
    tok = ssm_input.shape[0]
    heads = decay_log.shape[0]
    b = state_in.reshape(tok, N)
    c = state_out.reshape(tok, N)
    *gives, wk, aux = give_states(step_raw.T, decay_log.reshape(1, heads), ssm_input, b)
    keep = keep_states(wk, ssm_input, b)
    inputs = (ssm_input, b, c, gate_input, skip_gain.reshape(1, heads))
    local = within(True, aux, *inputs)
    (own, lead), quarters = incoming_states(gives, keep, seq_count, local)

    near = [(h, h ^ 1) for h in range(4)]
    far = [(h, h ^ 2) for h in range(4)]
    gain = norm_gain.reshape(1, -1)
    channels, dout = out_weight.shape
    rows = CHUNK
    states = pltpu.VMEM((4,) + quarters[0].shape, BF)
    finish = (own, lead, c, *quarters, gain, out_weight)
    (_, one), (start2, two), (start3, three) = PIECES

    def piece_outs(columns, extra=0):
        return [((rows, columns + extra), BF), ((rows, columns), F32)]

    def add(mine, theirs):
        come = lax.ppermute(theirs, "head", near)
        return local_call(add_kernel, (mine, come), [(mine.shape, BF)], "add_pair", limit=1 << 22)[0], come

    theirs, mine, normed = local_call(
        functools.partial(far_kernel, one),
        finish,
        piece_outs(one) + [((2 * rows, channels), BF)],
        "finish_far",
        [states],
        4 * rows * channels * one,
    )
    first, _ = add(mine, theirs)
    aux, first = lax.optimization_barrier((aux, first))
    theirs, mine = local_call(
        functools.partial(more_kernel, start2, two),
        (normed, out_weight),
        piece_outs(two),
        "project_more",
        flops=4 * rows * channels * two,
    )
    second, _ = add(mine, theirs)
    near_own, near_lead = within(False, aux, *inputs)
    normed, second = lax.optimization_barrier((normed, second))
    theirs, mine, kept = local_call(
        functools.partial(mixed_kernel, start3, three),
        (normed, near_own, near_lead) + finish[2:],
        piece_outs(three, dout) + [((rows, channels), BF)],
        "finish_near",
        [states, pltpu.VMEM((rows, channels), BF)],
        2 * rows * channels * (2 * three + dout),
    )
    third, come = add(mine, theirs)
    kept = local_call(
        functools.partial(kept_kernel, three),
        (kept, come, out_weight),
        [((rows, dout), F32)],
        "project_kept",
        flops=2 * rows * channels * dout,
    )[0]
    first = await_piece(lax.ppermute(first, "head", far))[0]
    second, first = await_piece(lax.ppermute(second, "head", far), first)
    filled = early_sums(kept, first, second)
    third, filled = await_piece(lax.ppermute(third, "head", far), filled)
    return last_sums(kept, third, filled)


def solution(mesh):
    in_specs = (
        P("seq", "head"),
        P("seq", "head"),
        P("seq", "head"),
        P("head"),
        P("seq", "head", None),
        P("seq", "head", None),
        P("head"),
        P("head"),
        P("head", None),
    )
    out_specs = P(("seq", "head"), None)
    return jax.shard_map(
        functools.partial(per_device, mesh.shape["seq"]),
        mesh=mesh,
        in_specs=in_specs,
        out_specs=out_specs,
        check_vma=False,
    )
```

```python
import functools

import jax
import jax.numpy as jnp
from jax import lax
from jax.experimental import pallas as pl
from jax.experimental.pallas import tpu as pltpu
from jax.sharding import PartitionSpec as P

P_SIZE = 64
N = 128
CHUNK = 128
LANES = 128
BF = jnp.bfloat16
F32 = jnp.float32
VMEM_LIMIT = 16 * 1024 * 1024
WHOLE_VMEM = 61 * 1024 * 1024 + 512 * 1024
PIECES = ((0, 1024), (1024, 1536), (2560, 1536))


def dot(a, b, contract=((1,), (0,)), precision=None):
    return lax.dot_general(a, b, (contract, ((), ())), precision=precision, preferred_element_type=F32)


def split2(v):
    hi = v.astype(BF)
    return hi, (v - hi.astype(F32)).astype(BF)


def split3(v):
    hi, rest = v.astype(BF), v
    rest = v - hi.astype(F32)
    mid = rest.astype(BF)
    return hi, mid, (rest - mid.astype(F32)).astype(BF)


def pick(rows, lanes, heads, per_head, first):
    r = lax.broadcasted_iota(jnp.int32, (rows, lanes), 0) % heads
    l = lax.broadcasted_iota(jnp.int32, (rows, lanes), 1) // per_head + first
    return jnp.where(r == l, 1.0, 0.0).astype(BF)


def step_vectors(raw, rate_row, wk, aux_ref):
    heads, tok = raw.shape
    chunks = tok // CHUNK
    step = jnp.maximum(raw, 0.0) + jnp.log1p(jnp.exp(-jnp.abs(raw)))
    r = lax.broadcasted_iota(jnp.int32, (heads, heads), 0)
    l = lax.broadcasted_iota(jnp.int32, (heads, heads), 1)
    rate = jnp.sum(jnp.where(r == l, rate_row, 0.0), axis=1, keepdims=True)
    logs = -step * jnp.exp(rate)
    parts = split3(logs)
    stacked = jnp.concatenate(
        [p[:, c * CHUNK:(c + 1) * CHUNK] for c in range(chunks) for p in parts], axis=0
    )
    s = lax.broadcasted_iota(jnp.int32, (CHUNK, 2 * CHUNK), 0)
    t = lax.broadcasted_iota(jnp.int32, (CHUNK, 2 * CHUNK), 1)
    tri = jnp.where(jnp.where(t < CHUNK, t - s, s - t + (CHUNK - 1)) >= 0, 1.0, 0.0).astype(BF)
    sums = dot(stacked, tri)
    pre, suf = [], []
    for c in range(chunks):
        base = 3 * heads * c
        total = (
            sums[base:base + heads] + sums[base + heads:base + 2 * heads]
        ) + sums[base + 2 * heads:base + 3 * heads]
        pre.append(total[:, :CHUNK])
        suf.append(total[:, CHUNK:])
    after = jnp.zeros((heads, 1), F32)
    for c in reversed(range(chunks)):
        w = step[:, c * CHUNK:(c + 1) * CHUNK] * jnp.exp(suf[c] + after)
        hi, lo = split2(w)
        wk[:heads, c * CHUNK:(c + 1) * CHUNK] = hi
        wk[heads:, c * CHUNK:(c + 1) * CHUNK] = lo
        after = after + pre[c][:, CHUNK - 1:]
    hi, lo = split2(jnp.broadcast_to(jnp.exp(after), (heads, CHUNK)))
    wk[:heads, tok:] = hi
    wk[heads:, tok:] = lo
    for c in range(chunks):
        aux_ref[c, :heads] = step[:, c * CHUNK:(c + 1) * CHUNK]
        aux_ref[c, heads:2 * heads] = pre[c]
        aux_ref[c, 2 * heads:] = suf[c]


def tail_rows(decays):
    r = lax.broadcasted_iota(jnp.int32, (16, LANES), 0)
    tail = jnp.zeros((16, LANES), F32)
    for k, decay in enumerate(decays):
        hi, lo = split2(decay)
        tail = jnp.where(r == 2 * k, hi.astype(F32), tail)
        tail = jnp.where(r == 2 * k + 1, lo.astype(F32), tail)
    return tail.astype(BF)


def decays_of(msg):
    blocks = (msg.shape[0] - 16) // N
    tail = msg[blocks * N:].astype(F32)
    return [tail[2 * k:2 * k + 1] + tail[2 * k + 1:2 * k + 2] for k in range(blocks)]


def quarter_message(x, b, wk, first_head, msg):
    tok, width = x.shape
    heads2 = wk.shape[0]
    spread = dot(wk[...], pick(heads2, width, heads2 // 2, P_SIZE, first_head), ((0,), (0,)))
    state = dot(b, (x * spread[:tok]).astype(BF), ((0,), (0,)))
    decays = []
    for k in range(width // LANES):
        msg[k * N:(k + 1) * N] = state[:, k * LANES:(k + 1) * LANES].astype(BF)
        decays.append(spread[tok:tok + 1, k * LANES:(k + 1) * LANES])
    msg[msg.shape[0] - 16:] = tail_rows(decays)


def load_quarter(x, x_v, quarter, sem):
    width = x_v.shape[1]
    return pltpu.make_async_copy(
        x.at[:, pl.ds(pl.multiple_of(quarter * width, width), width)], x_v, sem
    )


def give_kernel(raw, rate, x, b, msg1, msg2, msg3, wk, aux, raw_v, rate_v, x_v, b_v, sems):
    mine = lax.axis_index("seq") % 4
    loads = [
        pltpu.make_async_copy(raw, raw_v, sems.at[0]),
        pltpu.make_async_copy(rate, rate_v, sems.at[1]),
        pltpu.make_async_copy(b, b_v, sems.at[2]),
    ] + [load_quarter(x, x_v.at[k - 1], mine ^ k, sems.at[2 + k]) for k in (1, 2, 3)]
    for load in loads:
        load.start()
    loads[0].wait()
    loads[1].wait()
    step_vectors(raw_v[...], rate_v[...], wk, aux)
    for load in loads[2:]:
        load.wait()
    b16 = b_v[...].astype(BF)
    heads = x_v.shape[2] // P_SIZE
    for k, msg in ((1, msg1), (2, msg2), (3, msg3)):
        quarter_message(x_v[k - 1], b16, wk, (mine ^ k) * heads, msg)


def keep_kernel(wk, x, b, msg, x_v, b_v, sems):
    mine = lax.axis_index("seq") % 4
    loads = [load_quarter(x, x_v, mine, sems.at[0]), pltpu.make_async_copy(b, b_v, sems.at[1])]
    for load in loads:
        load.start()
    for load in loads:
        load.wait()
    quarter_message(x_v[...], b_v[...].astype(BF), wk, mine * (x_v.shape[1] // P_SIZE), msg)


HBM = pl.BlockSpec(memory_space=pltpu.HBM)
VMEM = pl.BlockSpec(memory_space=pltpu.VMEM)


def give_states(raw, rate, x, b):
    heads, tok = raw.shape
    lanes = x.shape[1] // 4
    return pl.pallas_call(
        give_kernel,
        in_specs=[HBM] * 4,
        out_shape=[jax.ShapeDtypeStruct((lanes // LANES * N + 16, LANES), BF)] * 3
        + [
            jax.ShapeDtypeStruct((2 * heads, tok + CHUNK), BF),
            jax.ShapeDtypeStruct((tok // CHUNK, 3 * heads, CHUNK), F32),
        ],
        scratch_shapes=[
            pltpu.VMEM((heads, tok), F32),
            pltpu.VMEM((1, heads), F32),
            pltpu.VMEM((3, tok, lanes), F32),
            pltpu.VMEM((tok, N), F32),
            pltpu.SemaphoreType.DMA((6,)),
        ],
        compiler_params=pltpu.CompilerParams(vmem_limit_bytes=WHOLE_VMEM),
        cost_estimate=pl.CostEstimate(flops=200_000_000, bytes_accessed=1_500_000, transcendentals=0),
        name="give_states",
    )(raw, rate, x, b)


def keep_states(wk, x, b):
    tok = x.shape[0]
    lanes = x.shape[1] // 4
    return pl.pallas_call(
        keep_kernel,
        in_specs=[VMEM, HBM, HBM],
        out_shape=jax.ShapeDtypeStruct((lanes // LANES * N + 16, LANES), BF),
        scratch_shapes=[
            pltpu.VMEM((tok, lanes), F32),
            pltpu.VMEM((tok, N), F32),
            pltpu.SemaphoreType.DMA((2,)),
        ],
        compiler_params=pltpu.CompilerParams(vmem_limit_bytes=VMEM_LIMIT),
        cost_estimate=pl.CostEstimate(flops=200_000_000, bytes_accessed=1_500_000, transcendentals=0),
        name="keep_states",
    )(wk, x, b)


def link(later, earlier, out):
    ahead, behind = decays_of(later), decays_of(earlier)
    for k, decay in enumerate(ahead):
        rows = slice(k * N, (k + 1) * N)
        out[rows] = (later[rows].astype(F32) + decay * earlier[rows].astype(F32)).astype(BF)
    out[len(ahead) * N:] = tail_rows([p * q for p, q in zip(ahead, behind)])


def is_later(distance):
    return (lax.axis_index("seq") // distance) % 2


def run_kernel(distance, own, come, out):
    later = is_later(distance)

    @pl.when(later == 0)
    def _():
        link(come, own, out)

    @pl.when(later == 1)
    def _():
        link(own, come, out)


def first_ahead_kernel(distance, come, out):
    later = is_later(distance)
    rows = out.shape[0] - 16

    @pl.when(later == 0)
    def _():
        out[:rows] = jnp.zeros((rows, LANES), BF)
        out[rows:] = tail_rows([jnp.ones((1, LANES), F32)] * (rows // N))

    @pl.when(later == 1)
    def _():
        out[...] = come[...]


def ahead_kernel(distance, ahead, come, out):
    later = is_later(distance)

    @pl.when(later == 0)
    def _():
        out[...] = ahead[...]

    @pl.when(later == 1)
    def _():
        link(ahead, come, out)


def by_section(work):
    mine = lax.axis_index("seq") % 4
    for v in range(4):
        pl.when(mine == v)(functools.partial(work, [j ^ v for j in range(4)]))


def join_four_kernel(own, come1, come2, come3, out):
    messages = (own, come1, come2, come3)

    def work(place):
        sections = [messages[p] for p in place]
        decays = [decays_of(section) for section in sections]
        for k in range(len(decays[0])):
            rows = slice(k * N, (k + 1) * N)
            total = sections[0][rows].astype(F32)
            for section, decay in zip(sections[1:], decays[1:]):
                total = section[rows].astype(F32) + decay[k] * total
            out[rows] = total.astype(BF)
        spans = [p * q * r * t for p, q, r, t in zip(*decays)]
        out[len(spans) * N:] = tail_rows(spans)

    by_section(work)


def end_kernel(distance, ahead, last, own, come1, come2, come3, mine, out1, out2, out3):
    messages, outs = (own, come1, come2, come3), (mine, out1, out2, out3)
    weight = is_later(distance).astype(F32)

    def work(place):
        sections, targets = [messages[p] for p in place], [outs[p] for p in place]
        decays = [decays_of(section) for section in sections]
        for k in range(len(decays[0])):
            rows = slice(k * N, (k + 1) * N)
            state = weight * last[rows].astype(F32)
            if ahead is not None:
                state = ahead[rows].astype(F32) + decays_of(ahead)[k] * state
            for j in range(4):
                targets[j][rows] = state.astype(BF)
                if j < 3:
                    state = sections[j][rows].astype(F32) + decays[j][k] * state

    by_section(work)


def scan_call(kernel, operands, shapes, name):
    return pl.pallas_call(
        kernel,
        out_shape=[jax.ShapeDtypeStruct(shape, BF) for shape in shapes],
        compiler_params=pltpu.CompilerParams(vmem_limit_bytes=VMEM_LIMIT),
        cost_estimate=pl.CostEstimate(flops=500_000, bytes_accessed=400_000, transcendentals=0),
        name=name,
    )(*operands)


def incoming_states(gives, keep, count, hold):
    def exchange(value, distance):
        return lax.ppermute(value, "seq", [(s, s ^ distance) for s in range(count)])

    def joined(kernel, *operands):
        return scan_call(kernel, operands, [keep.shape], "join_states")[0]

    come = {k: exchange(gives[k - 1], k) for k in (3, 2, 1)}
    parts = [keep] + [come[k] for k in (1, 2, 3)]
    hold, parts = lax.optimization_barrier((hold, parts))
    run, ahead, distance = joined(join_four_kernel, *parts), None, 4
    got = exchange(run, distance)
    while distance * 2 < count:
        if ahead is None:
            ahead = joined(functools.partial(first_ahead_kernel, distance), got)
        else:
            ahead = joined(functools.partial(ahead_kernel, distance), ahead, got)
        run = joined(functools.partial(run_kernel, distance), run, got)
        distance *= 2
        got = exchange(run, distance)
    operands = [got] + parts
    if ahead is None:
        kernel = functools.partial(end_kernel, distance, None)
    else:
        kernel, operands = functools.partial(end_kernel, distance), [ahead] + operands
    shape = (keep.shape[0] - 16, LANES)
    outs = scan_call(kernel, operands, [shape] * 4, "join_end")
    back = {k: exchange(outs[k], k) for k in (3, 2, 1)}
    return hold, [outs[0]] + [back[k] for k in (1, 2, 3)]


def rows_of(ref, block):
    return ref[pl.ds(pl.multiple_of(block * CHUNK, CHUNK), CHUNK), :]


def within_kernel(far, aux, x_ref, b_ref, c_ref, gate_ref, skip_ref, own_ref, lead_ref):
    channels = x_ref.shape[1]
    heads = aux.shape[1] // 3
    width = 256
    here = width // P_SIZE
    half = lax.axis_index("head") // 2
    half = 1 - half if far else half
    second = half == 1

    def vectors(c):
        return [aux[c, k * heads:(k + 1) * heads] for k in range(3)]

    def put(values):
        return jnp.concatenate([jnp.concatenate(split2(v), axis=0) for v in values], axis=1)

    first, then = vectors(0), vectors(1)
    ends = [v[1][:, CHUNK - 1:] for v in (first, then)]
    early = put(
        [
            jnp.where(second, first[0] * jnp.exp(first[2] + ends[1]), 0.0),
            jnp.where(second, then[0] * jnp.exp(then[2]), 0.0),
        ]
    )
    before = jnp.where(second, ends[0] + ends[1], 0.0)
    r = lax.broadcasted_iota(jnp.int32, (CHUNK, CHUNK), 0)
    l = lax.broadcasted_iota(jnp.int32, (CHUNK, CHUNK), 1)
    duo, trip, lines, scores, rows_b, rows_c, rows_x, rows_g = ([] for _ in range(8))
    for i in range(2):
        block = 2 * half + i
        step, pre, suf = vectors(block)
        duo.append(put((step, step * jnp.exp(suf), jnp.exp(pre), jnp.exp(pre + before))))
        trip.append(jnp.concatenate(split3(pre), axis=0))
        lines.append(pre)
        before = before + pre[:, CHUNK - 1:]
        b, c = rows_of(b_ref, block), rows_of(c_ref, block)
        raw = dot(c, b, ((1,), (1,)), lax.Precision.HIGHEST)
        scores.append(jnp.where(r >= l, raw, 0.0))
        rows_b.append(b.astype(BF))
        rows_c.append(c.astype(BF))
        rows_x.append(rows_of(x_ref, block))
        rows_g.append(rows_of(gate_ref, block))
    early_b = b_ref[:2 * CHUNK].astype(BF)
    gains = jnp.broadcast_to(jnp.concatenate(split3(skip_ref[...]), axis=1), (8, 3 * heads))
    lane = lax.broadcasted_iota(jnp.int32, (CHUNK, LANES), 1)
    for g in range(channels // width):
        at = slice(g * width, (g + 1) * width)
        spread = pick(2 * heads, width, heads, P_SIZE, g * here)
        columns = pick(3 * heads, here * CHUNK, heads, CHUNK, g * here)
        skip = dot(gains, pick(3 * heads, width, heads, P_SIZE, g * here))[:1]
        weights = dot(early, spread, ((0,), (0,)))
        state = dot(early_b, (x_ref[:2 * CHUNK, at] * weights).astype(BF), ((0,), (0,)))
        for i in range(2):
            cut = slice(i * CHUNK, (i + 1) * CHUNK)
            wide = dot(duo[i], spread, ((0,), (0,)))
            x = rows_x[i][:, at]
            stepped = x * wide[:CHUNK]
            lead = wide[2 * CHUNK:3 * CHUNK]
            tall = dot(trip[i], columns, ((0,), (0,)))
            outs = []
            for pair in range(here // 2):
                mixes = []
                for h in (2 * pair, 2 * pair + 1):
                    line = lines[i][g * here + h:g * here + h + 1]
                    gap = tall[:, h * CHUNK:(h + 1) * CHUNK] - line
                    mixes.append((scores[i] * jnp.exp(jnp.minimum(gap, 0.0))).astype(BF))
                both = stepped[:, pair * LANES:(pair + 1) * LANES]
                stacked = jnp.concatenate(
                    [
                        jnp.where(lane < P_SIZE, both, 0.0).astype(BF),
                        jnp.where(lane < P_SIZE, 0.0, both).astype(BF),
                    ],
                    axis=0,
                )
                outs.append(dot(jnp.concatenate(mixes, axis=1), stacked))
            y = jnp.concatenate(outs, axis=1) + skip * x
            y = y + lead * dot(rows_c[i], state.astype(BF))
            v = rows_g[i][:, at].astype(F32)
            silu = v / (1.0 + jnp.exp(-v))
            own_ref[cut, at] = y * silu
            lead_ref[cut, at] = wide[3 * CHUNK:] * silu
            if i == 0:
                weighted = (x * wide[CHUNK:2 * CHUNK]).astype(BF)
                state = state * lead[CHUNK - 1:] + dot(rows_b[i], weighted, ((0,), (0,)))


def within(far, aux, x, b, c, gate, skip):
    channels = x.shape[1]
    return pl.pallas_call(
        functools.partial(within_kernel, far),
        in_specs=[VMEM] * 6,
        out_specs=[VMEM] * 2,
        out_shape=[jax.ShapeDtypeStruct((2 * CHUNK, channels), F32)] * 2,
        compiler_params=pltpu.CompilerParams(vmem_limit_bytes=VMEM_LIMIT),
        cost_estimate=pl.CostEstimate(
            flops=4_000_000_000, bytes_accessed=3_000_000, transcendentals=500_000
        ),
        name="within_far" if far else "within_near",
    )(aux, x, b, c, gate, skip)


def finish_rows(own, lead, c, incoming, gain):
    c = c.astype(BF)
    blocks = incoming.shape[1] // N
    carried = jnp.concatenate(
        [dot(c, incoming[q, k * N:(k + 1) * N]) for q in range(4) for k in range(blocks)], axis=1
    )
    gated = own + lead * carried
    mean = jnp.mean(gated * gated, axis=1, keepdims=True)
    return (gated * lax.rsqrt(mean + 1e-05) * gain).astype(BF)


def finish_block(block, own, lead, c, incoming, gain):
    return finish_rows(
        rows_of(own, block % 2), rows_of(lead, block % 2), rows_of(c, block), incoming, gain[...]
    )


def fill_incoming(quarters, incoming):
    mine = lax.axis_index("seq") % 4
    for k, quarter in enumerate(quarters):
        incoming[mine ^ k] = quarter[...]


def project_both(normed, w, start, columns, theirs, mine, at=0):
    wide = 512
    for k in range(0, columns, wide):
        out = dot(normed[...], w[:, start + k:start + k + wide])
        theirs[:, at + k:at + k + wide] = out[:CHUNK].astype(BF)
        mine[:, k:k + wide] = out[CHUNK:]


def far_kernel(
    columns, own, lead, c, q0, q1, q2, q3, gain, w, theirs, mine, normed, incoming
):
    me = lax.axis_index("head")
    fill_incoming((q0, q1, q2, q3), incoming)
    normed[:CHUNK] = finish_block(me ^ 3, own, lead, c, incoming, gain)
    normed[CHUNK:] = finish_block(me ^ 2, own, lead, c, incoming, gain)
    project_both(normed, w, 0, columns, theirs, mine)


def more_kernel(start, columns, normed, w, theirs, mine):
    project_both(normed, w, start, columns, theirs, mine)


def mixed_kernel(
    start, columns, normed, own, lead, c, q0, q1, q2, q3, gain, w,
    theirs, mine, kept, incoming, given,
):
    me = lax.axis_index("head")
    project_both(normed, w, start, columns, theirs, mine)
    fill_incoming((q0, q1, q2, q3), incoming)
    given[...] = finish_block(me ^ 1, own, lead, c, incoming, gain)
    kept[...] = finish_block(me, own, lead, c, incoming, gain)
    wide = 512
    for k in range(0, w.shape[1], wide):
        theirs[:, columns + k:columns + k + wide] = dot(given[...], w[:, k:k + wide]).astype(BF)


def kept_kernel(columns, kept, come, w, out):
    wide = 512
    for k in range(0, w.shape[1], wide):
        out[:, k:k + wide] = dot(kept[...], w[:, k:k + wide]) + come[
            :, columns + k:columns + k + wide
        ].astype(F32)


def add_kernel(mine, come, out):
    out[...] = (mine[...] + come[:, :out.shape[1]].astype(F32)).astype(BF)


def local_call(kernel, operands, outs, name, scratch=(), flops=0, limit=VMEM_LIMIT):
    return pl.pallas_call(
        kernel,
        in_specs=[VMEM] * len(operands),
        out_specs=[VMEM] * len(outs),
        out_shape=[jax.ShapeDtypeStruct(shape, dtype) for shape, dtype in outs],
        scratch_shapes=list(scratch),
        compiler_params=pltpu.CompilerParams(vmem_limit_bytes=limit),
        cost_estimate=pl.CostEstimate(flops=flops, bytes_accessed=0, transcendentals=0),
        name=name,
    )(*operands)


def pass_kernel(*refs):
    pass


def await_piece(piece, *earlier):
    arrays = [piece, *earlier]
    return pl.pallas_call(
        pass_kernel,
        in_specs=[pl.BlockSpec(memory_space=pl.ANY)] * len(arrays),
        out_specs=[pl.BlockSpec(memory_space=pl.ANY)] * len(arrays),
        out_shape=[jax.ShapeDtypeStruct(v.shape, v.dtype) for v in arrays],
        input_output_aliases={k: k for k in range(len(arrays))},
        compiler_params=pltpu.CompilerParams(vmem_limit_bytes=1024 * 1024),
        cost_estimate=pl.CostEstimate(
            flops=20_000_000_000, bytes_accessed=100_000_000, transcendentals=0
        ),
        name="await_piece",
    )(*arrays)


def early_kernel(kept, first, second, out):
    at = 0
    for piece in (first, second):
        cut = slice(at, at + piece.shape[1])
        out[:, cut] = (kept[:, cut] + piece[...].astype(F32)).astype(BF)
        at += piece.shape[1]


def early_sums(kept, first, second):
    rows = first.shape[0]
    wide = first.shape[1] + second.shape[1]
    return pl.pallas_call(
        early_kernel,
        grid=(1,),
        in_specs=[VMEM] * 3,
        out_specs=pl.BlockSpec((rows, wide), lambda j: (0, 0)),
        out_shape=jax.ShapeDtypeStruct(kept.shape, BF),
        compiler_params=pltpu.CompilerParams(vmem_limit_bytes=VMEM_LIMIT),
        name="early_sums",
    )(kept, first, second)


def last_kernel(kept, third, filled, out, part, sems):
    wide = third.shape[1]
    start = kept.shape[1] - wide
    block = wide // 2
    stores = []
    for k in range(2):
        cut = slice(k * block, (k + 1) * block)
        part[:, cut] = (
            kept[:, start + k * block:start + (k + 1) * block] + third[:, cut].astype(F32)
        ).astype(BF)
        stores.append(
            pltpu.make_async_copy(
                part.at[:, cut], out.at[:, start + k * block:start + (k + 1) * block], sems.at[k]
            )
        )
        stores[k].start()
    for store in stores:
        store.wait()


def last_sums(kept, third, filled):
    return pl.pallas_call(
        last_kernel,
        in_specs=[VMEM, VMEM, pl.BlockSpec(memory_space=pl.ANY)],
        out_specs=pl.BlockSpec(memory_space=pl.ANY),
        out_shape=jax.ShapeDtypeStruct(kept.shape, BF),
        input_output_aliases={2: 0},
        scratch_shapes=[pltpu.VMEM(third.shape, BF), pltpu.SemaphoreType.DMA((2,))],
        compiler_params=pltpu.CompilerParams(vmem_limit_bytes=VMEM_LIMIT),
        name="last_sums",
    )(kept, third, filled)


def per_device(
    seq_count,
    ssm_input,
    gate_input,
    step_raw,
    decay_log,
    state_in,
    state_out,
    skip_gain,
    norm_gain,
    out_weight,
):
    tok = ssm_input.shape[0]
    heads = decay_log.shape[0]
    b = state_in.reshape(tok, N)
    c = state_out.reshape(tok, N)
    *gives, wk, aux = give_states(step_raw.T, decay_log.reshape(1, heads), ssm_input, b)
    keep = keep_states(wk, ssm_input, b)
    inputs = (ssm_input, b, c, gate_input, skip_gain.reshape(1, heads))
    local = within(True, aux, *inputs)
    (own, lead), quarters = incoming_states(gives, keep, seq_count, local)

    near = [(h, h ^ 1) for h in range(4)]
    far = [(h, h ^ 2) for h in range(4)]
    gain = norm_gain.reshape(1, -1)
    channels, dout = out_weight.shape
    rows = CHUNK
    states = pltpu.VMEM((4,) + quarters[0].shape, BF)
    finish = (own, lead, c, *quarters, gain, out_weight)
    (_, one), (start2, two), (start3, three) = PIECES

    def piece_outs(columns, extra=0):
        return [((rows, columns + extra), BF), ((rows, columns), F32)]

    def add(mine, theirs):
        come = lax.ppermute(theirs, "head", near)
        return local_call(add_kernel, (mine, come), [(mine.shape, BF)], "add_pair", limit=1 << 22)[0], come

    theirs, mine, normed = local_call(
        functools.partial(far_kernel, one),
        finish,
        piece_outs(one) + [((2 * rows, channels), BF)],
        "finish_far",
        [states],
        4 * rows * channels * one,
    )
    first, _ = add(mine, theirs)
    aux, first = lax.optimization_barrier((aux, first))
    theirs, mine = local_call(
        functools.partial(more_kernel, start2, two),
        (normed, out_weight),
        piece_outs(two),
        "project_more",
        flops=4 * rows * channels * two,
    )
    second, _ = add(mine, theirs)
    near_own, near_lead = within(False, aux, *inputs)
    normed, second = lax.optimization_barrier((normed, second))
    theirs, mine, kept = local_call(
        functools.partial(mixed_kernel, start3, three),
        (normed, near_own, near_lead) + finish[2:],
        piece_outs(three, dout) + [((rows, channels), BF)],
        "finish_near",
        [states, pltpu.VMEM((rows, channels), BF)],
        2 * rows * channels * (2 * three + dout),
    )
    third, come = add(mine, theirs)
    kept = local_call(
        functools.partial(kept_kernel, three),
        (kept, come, out_weight),
        [((rows, dout), F32)],
        "project_kept",
        flops=2 * rows * channels * dout,
    )[0]
    first = await_piece(lax.ppermute(first, "head", far))[0]
    second, first = await_piece(lax.ppermute(second, "head", far), first)
    filled = early_sums(kept, first, second)
    third, filled = await_piece(lax.ppermute(third, "head", far), filled)
    return last_sums(kept, third, filled)


def solution(mesh):
    in_specs = (
        P("seq", "head"),
        P("seq", "head"),
        P("seq", "head"),
        P("head"),
        P("seq", "head", None),
        P("seq", "head", None),
        P("head"),
        P("head"),
        P("head", None),
    )
    out_specs = P(("seq", "head"), None)
    return jax.shard_map(
        functools.partial(per_device, mesh.shape["seq"]),
        mesh=mesh,
        in_specs=in_specs,
        out_specs=out_specs,
        check_vma=False,
    )
```

```python
import functools

import jax
import jax.numpy as jnp
from jax import lax
from jax.experimental import pallas as pl
from jax.experimental.pallas import tpu as pltpu
from jax.sharding import PartitionSpec as P

P_SIZE = 64
N = 128
CHUNK = 128
LANES = 128
BF = jnp.bfloat16
F32 = jnp.float32
VMEM_LIMIT = 16 * 1024 * 1024
WHOLE_VMEM = 58 * 1024 * 1024
PIECES = ((0, 1024), (1024, 1536), (2560, 1536))


def dot(a, b, contract=((1,), (0,)), precision=None):
    return lax.dot_general(a, b, (contract, ((), ())), precision=precision, preferred_element_type=F32)


def split2(v):
    hi = v.astype(BF)
    return hi, (v - hi.astype(F32)).astype(BF)


def split3(v):
    hi, rest = v.astype(BF), v
    rest = v - hi.astype(F32)
    mid = rest.astype(BF)
    return hi, mid, (rest - mid.astype(F32)).astype(BF)


def pick(rows, lanes, heads, per_head, first):
    r = lax.broadcasted_iota(jnp.int32, (rows, lanes), 0) % heads
    l = lax.broadcasted_iota(jnp.int32, (rows, lanes), 1) // per_head + first
    return jnp.where(r == l, 1.0, 0.0).astype(BF)


def step_vectors(raw, rate_row, wk, aux_ref):
    heads, tok = raw.shape
    chunks = tok // CHUNK
    step = jnp.maximum(raw, 0.0) + jnp.log1p(jnp.exp(-jnp.abs(raw)))
    r = lax.broadcasted_iota(jnp.int32, (heads, heads), 0)
    l = lax.broadcasted_iota(jnp.int32, (heads, heads), 1)
    rate = jnp.sum(jnp.where(r == l, rate_row, 0.0), axis=1, keepdims=True)
    logs = -step * jnp.exp(rate)
    parts = split3(logs)
    stacked = jnp.concatenate(
        [p[:, c * CHUNK:(c + 1) * CHUNK] for c in range(chunks) for p in parts], axis=0
    )
    s = lax.broadcasted_iota(jnp.int32, (CHUNK, 2 * CHUNK), 0)
    t = lax.broadcasted_iota(jnp.int32, (CHUNK, 2 * CHUNK), 1)
    tri = jnp.where(jnp.where(t < CHUNK, t - s, s - t + (CHUNK - 1)) >= 0, 1.0, 0.0).astype(BF)
    sums = dot(stacked, tri)
    pre, suf = [], []
    for c in range(chunks):
        base = 3 * heads * c
        total = (
            sums[base:base + heads] + sums[base + heads:base + 2 * heads]
        ) + sums[base + 2 * heads:base + 3 * heads]
        pre.append(total[:, :CHUNK])
        suf.append(total[:, CHUNK:])
    after = jnp.zeros((heads, 1), F32)
    for c in reversed(range(chunks)):
        w = step[:, c * CHUNK:(c + 1) * CHUNK] * jnp.exp(suf[c] + after)
        hi, lo = split2(w)
        wk[:heads, c * CHUNK:(c + 1) * CHUNK] = hi
        wk[heads:, c * CHUNK:(c + 1) * CHUNK] = lo
        after = after + pre[c][:, CHUNK - 1:]
    hi, lo = split2(jnp.broadcast_to(jnp.exp(after), (heads, CHUNK)))
    wk[:heads, tok:] = hi
    wk[heads:, tok:] = lo
    for c in range(chunks):
        aux_ref[c, :heads] = step[:, c * CHUNK:(c + 1) * CHUNK]
        aux_ref[c, heads:2 * heads] = pre[c]
        aux_ref[c, 2 * heads:] = suf[c]


def tail_rows(decays):
    r = lax.broadcasted_iota(jnp.int32, (16, LANES), 0)
    tail = jnp.zeros((16, LANES), F32)
    for k, decay in enumerate(decays):
        hi, lo = split2(decay)
        tail = jnp.where(r == 2 * k, hi.astype(F32), tail)
        tail = jnp.where(r == 2 * k + 1, lo.astype(F32), tail)
    return tail.astype(BF)


def decays_of(msg):
    blocks = (msg.shape[0] - 16) // N
    tail = msg[blocks * N:].astype(F32)
    return [tail[2 * k:2 * k + 1] + tail[2 * k + 1:2 * k + 2] for k in range(blocks)]


def quarter_message(x, b, wk, first_head, msg):
    tok, width = x.shape
    heads2 = wk.shape[0]
    spread = dot(wk[...], pick(heads2, width, heads2 // 2, P_SIZE, first_head), ((0,), (0,)))
    state = dot(b, (x * spread[:tok]).astype(BF), ((0,), (0,)))
    decays = []
    for k in range(width // LANES):
        msg[k * N:(k + 1) * N] = state[:, k * LANES:(k + 1) * LANES].astype(BF)
        decays.append(spread[tok:tok + 1, k * LANES:(k + 1) * LANES])
    msg[msg.shape[0] - 16:] = tail_rows(decays)


def load_quarter(x, x_v, quarter, sem):
    width = x_v.shape[1]
    return pltpu.make_async_copy(
        x.at[:, pl.ds(pl.multiple_of(quarter * width, width), width)], x_v, sem
    )


def give_kernel(raw, rate, x, b, msg1, msg2, msg3, wk, aux, raw_v, rate_v, x_v, b_v, sems):
    mine = lax.axis_index("seq") % 4
    loads = [
        pltpu.make_async_copy(raw, raw_v, sems.at[0]),
        pltpu.make_async_copy(rate, rate_v, sems.at[1]),
        pltpu.make_async_copy(b, b_v, sems.at[2]),
    ] + [load_quarter(x, x_v.at[k - 1], mine ^ k, sems.at[2 + k]) for k in (1, 2, 3)]
    for load in loads:
        load.start()
    loads[0].wait()
    loads[1].wait()
    step_vectors(raw_v[...], rate_v[...], wk, aux)
    for load in loads[2:]:
        load.wait()
    b16 = b_v[...].astype(BF)
    heads = x_v.shape[2] // P_SIZE
    for k, msg in ((1, msg1), (2, msg2), (3, msg3)):
        quarter_message(x_v[k - 1], b16, wk, (mine ^ k) * heads, msg)


def keep_kernel(wk, x, b, msg, x_v, b_v, sems):
    mine = lax.axis_index("seq") % 4
    loads = [load_quarter(x, x_v, mine, sems.at[0]), pltpu.make_async_copy(b, b_v, sems.at[1])]
    for load in loads:
        load.start()
    for load in loads:
        load.wait()
    quarter_message(x_v[...], b_v[...].astype(BF), wk, mine * (x_v.shape[1] // P_SIZE), msg)


HBM = pl.BlockSpec(memory_space=pltpu.HBM)
VMEM = pl.BlockSpec(memory_space=pltpu.VMEM)


def give_states(raw, rate, x, b):
    heads, tok = raw.shape
    lanes = x.shape[1] // 4
    return pl.pallas_call(
        give_kernel,
        in_specs=[HBM] * 4,
        out_shape=[jax.ShapeDtypeStruct((lanes // LANES * N + 16, LANES), BF)] * 3
        + [
            jax.ShapeDtypeStruct((2 * heads, tok + CHUNK), BF),
            jax.ShapeDtypeStruct((tok // CHUNK, 3 * heads, CHUNK), F32),
        ],
        scratch_shapes=[
            pltpu.VMEM((heads, tok), F32),
            pltpu.VMEM((1, heads), F32),
            pltpu.VMEM((3, tok, lanes), F32),
            pltpu.VMEM((tok, N), F32),
            pltpu.SemaphoreType.DMA((6,)),
        ],
        compiler_params=pltpu.CompilerParams(vmem_limit_bytes=WHOLE_VMEM),
        cost_estimate=pl.CostEstimate(flops=4_000_000_000, bytes_accessed=1_500_000, transcendentals=0),
        name="give_states",
    )(raw, rate, x, b)


def keep_states(wk, x, b):
    tok = x.shape[0]
    lanes = x.shape[1] // 4
    return pl.pallas_call(
        keep_kernel,
        in_specs=[VMEM, HBM, HBM],
        out_shape=jax.ShapeDtypeStruct((lanes // LANES * N + 16, LANES), BF),
        scratch_shapes=[
            pltpu.VMEM((tok, lanes), F32),
            pltpu.VMEM((tok, N), F32),
            pltpu.SemaphoreType.DMA((2,)),
        ],
        compiler_params=pltpu.CompilerParams(vmem_limit_bytes=VMEM_LIMIT),
        cost_estimate=pl.CostEstimate(flops=800_000_000, bytes_accessed=1_500_000, transcendentals=0),
        name="keep_states",
    )(wk, x, b)


def link(later, earlier, out):
    ahead, behind = decays_of(later), decays_of(earlier)
    for k, decay in enumerate(ahead):
        rows = slice(k * N, (k + 1) * N)
        out[rows] = (later[rows].astype(F32) + decay * earlier[rows].astype(F32)).astype(BF)
    out[len(ahead) * N:] = tail_rows([p * q for p, q in zip(ahead, behind)])


def is_later(distance):
    return (lax.axis_index("seq") // distance) % 2


def run_kernel(distance, own, come, out):
    later = is_later(distance)

    @pl.when(later == 0)
    def _():
        link(come, own, out)

    @pl.when(later == 1)
    def _():
        link(own, come, out)


def first_ahead_kernel(distance, come, out):
    later = is_later(distance)
    rows = out.shape[0] - 16

    @pl.when(later == 0)
    def _():
        out[:rows] = jnp.zeros((rows, LANES), BF)
        out[rows:] = tail_rows([jnp.ones((1, LANES), F32)] * (rows // N))

    @pl.when(later == 1)
    def _():
        out[...] = come[...]


def ahead_kernel(distance, ahead, come, out):
    later = is_later(distance)

    @pl.when(later == 0)
    def _():
        out[...] = ahead[...]

    @pl.when(later == 1)
    def _():
        link(ahead, come, out)


def by_section(work):
    mine = lax.axis_index("seq") % 4
    for v in range(4):
        pl.when(mine == v)(functools.partial(work, [j ^ v for j in range(4)]))


def join_four_kernel(own, come1, come2, come3, out):
    messages = (own, come1, come2, come3)

    def work(place):
        sections = [messages[p] for p in place]
        decays = [decays_of(section) for section in sections]
        for k in range(len(decays[0])):
            rows = slice(k * N, (k + 1) * N)
            total = sections[0][rows].astype(F32)
            for section, decay in zip(sections[1:], decays[1:]):
                total = section[rows].astype(F32) + decay[k] * total
            out[rows] = total.astype(BF)
        spans = [p * q * r * t for p, q, r, t in zip(*decays)]
        out[len(spans) * N:] = tail_rows(spans)

    by_section(work)


def end_kernel(distance, ahead, last, own, come1, come2, come3, mine, out1, out2, out3):
    messages, outs = (own, come1, come2, come3), (mine, out1, out2, out3)
    weight = is_later(distance).astype(F32)

    def work(place):
        sections, targets = [messages[p] for p in place], [outs[p] for p in place]
        decays = [decays_of(section) for section in sections]
        for k in range(len(decays[0])):
            rows = slice(k * N, (k + 1) * N)
            state = weight * last[rows].astype(F32)
            if ahead is not None:
                state = ahead[rows].astype(F32) + decays_of(ahead)[k] * state
            for j in range(4):
                targets[j][rows] = state.astype(BF)
                if j < 3:
                    state = sections[j][rows].astype(F32) + decays[j][k] * state

    by_section(work)


def scan_call(kernel, operands, shapes, name):
    return pl.pallas_call(
        kernel,
        out_shape=[jax.ShapeDtypeStruct(shape, BF) for shape in shapes],
        compiler_params=pltpu.CompilerParams(vmem_limit_bytes=VMEM_LIMIT),
        cost_estimate=pl.CostEstimate(flops=500_000, bytes_accessed=400_000, transcendentals=0),
        name=name,
    )(*operands)


def incoming_states(gives, keep, count, hold):
    def exchange(value, distance):
        return lax.ppermute(value, "seq", [(s, s ^ distance) for s in range(count)])

    def joined(kernel, *operands):
        return scan_call(kernel, operands, [keep.shape], "join_states")[0]

    come = {k: exchange(gives[k - 1], k) for k in (1, 2, 3)}
    parts = [keep] + [come[k] for k in (1, 2, 3)]
    hold, parts = lax.optimization_barrier((hold, parts))
    run, ahead, distance = joined(join_four_kernel, *parts), None, 4
    got = exchange(run, distance)
    while distance * 2 < count:
        if ahead is None:
            ahead = joined(functools.partial(first_ahead_kernel, distance), got)
        else:
            ahead = joined(functools.partial(ahead_kernel, distance), ahead, got)
        run = joined(functools.partial(run_kernel, distance), run, got)
        distance *= 2
        got = exchange(run, distance)
    operands = [got] + parts
    if ahead is None:
        kernel = functools.partial(end_kernel, distance, None)
    else:
        kernel, operands = functools.partial(end_kernel, distance), [ahead] + operands
    shape = (keep.shape[0] - 16, LANES)
    outs = scan_call(kernel, operands, [shape] * 4, "join_end")
    back = {k: exchange(outs[k], k) for k in (1, 2, 3)}
    return hold, [outs[0]] + [back[k] for k in (1, 2, 3)]


def rows_of(ref, block):
    return ref[pl.ds(pl.multiple_of(block * CHUNK, CHUNK), CHUNK), :]


def within_kernel(far, aux, x_ref, b_ref, c_ref, gate_ref, skip_ref, own_ref, lead_ref):
    channels = x_ref.shape[1]
    heads = aux.shape[1] // 3
    width = 256
    here = width // P_SIZE
    half = lax.axis_index("head") // 2
    half = 1 - half if far else half
    second = half == 1

    def vectors(c):
        return [aux[c, k * heads:(k + 1) * heads] for k in range(3)]

    def put(values):
        return jnp.concatenate([jnp.concatenate(split2(v), axis=0) for v in values], axis=1)

    first, then = vectors(0), vectors(1)
    ends = [v[1][:, CHUNK - 1:] for v in (first, then)]
    early = put(
        [
            jnp.where(second, first[0] * jnp.exp(first[2] + ends[1]), 0.0),
            jnp.where(second, then[0] * jnp.exp(then[2]), 0.0),
        ]
    )
    before = jnp.where(second, ends[0] + ends[1], 0.0)
    r = lax.broadcasted_iota(jnp.int32, (CHUNK, CHUNK), 0)
    l = lax.broadcasted_iota(jnp.int32, (CHUNK, CHUNK), 1)
    duo, trip, lines, scores, rows_b, rows_c, rows_x, rows_g = ([] for _ in range(8))
    for i in range(2):
        block = 2 * half + i
        step, pre, suf = vectors(block)
        duo.append(put((step, step * jnp.exp(suf), jnp.exp(pre), jnp.exp(pre + before))))
        trip.append(jnp.concatenate(split3(pre), axis=0))
        lines.append(pre)
        before = before + pre[:, CHUNK - 1:]
        b, c = rows_of(b_ref, block), rows_of(c_ref, block)
        raw = dot(c, b, ((1,), (1,)), lax.Precision.HIGHEST)
        scores.append(jnp.where(r >= l, raw, 0.0))
        rows_b.append(b.astype(BF))
        rows_c.append(c.astype(BF))
        rows_x.append(rows_of(x_ref, block))
        rows_g.append(rows_of(gate_ref, block))
    early_b = b_ref[:2 * CHUNK].astype(BF)
    gains = jnp.broadcast_to(jnp.concatenate(split3(skip_ref[...]), axis=1), (8, 3 * heads))
    lane = lax.broadcasted_iota(jnp.int32, (CHUNK, LANES), 1)
    for g in range(channels // width):
        at = slice(g * width, (g + 1) * width)
        spread = pick(2 * heads, width, heads, P_SIZE, g * here)
        columns = pick(3 * heads, here * CHUNK, heads, CHUNK, g * here)
        skip = dot(gains, pick(3 * heads, width, heads, P_SIZE, g * here))[:1]
        weights = dot(early, spread, ((0,), (0,)))
        state = dot(early_b, (x_ref[:2 * CHUNK, at] * weights).astype(BF), ((0,), (0,)))
        for i in range(2):
            cut = slice(i * CHUNK, (i + 1) * CHUNK)
            wide = dot(duo[i], spread, ((0,), (0,)))
            x = rows_x[i][:, at]
            stepped = x * wide[:CHUNK]
            lead = wide[2 * CHUNK:3 * CHUNK]
            tall = dot(trip[i], columns, ((0,), (0,)))
            outs = []
            for pair in range(here // 2):
                mixes = []
                for h in (2 * pair, 2 * pair + 1):
                    line = lines[i][g * here + h:g * here + h + 1]
                    gap = tall[:, h * CHUNK:(h + 1) * CHUNK] - line
                    mixes.append((scores[i] * jnp.exp(jnp.minimum(gap, 0.0))).astype(BF))
                both = stepped[:, pair * LANES:(pair + 1) * LANES]
                stacked = jnp.concatenate(
                    [
                        jnp.where(lane < P_SIZE, both, 0.0).astype(BF),
                        jnp.where(lane < P_SIZE, 0.0, both).astype(BF),
                    ],
                    axis=0,
                )
                outs.append(dot(jnp.concatenate(mixes, axis=1), stacked))
            y = jnp.concatenate(outs, axis=1) + skip * x
            y = y + lead * dot(rows_c[i], state.astype(BF))
            v = rows_g[i][:, at].astype(F32)
            silu = v / (1.0 + jnp.exp(-v))
            own_ref[cut, at] = y * silu
            lead_ref[cut, at] = wide[3 * CHUNK:] * silu
            if i == 0:
                weighted = (x * wide[CHUNK:2 * CHUNK]).astype(BF)
                state = state * lead[CHUNK - 1:] + dot(rows_b[i], weighted, ((0,), (0,)))


def within(far, aux, x, b, c, gate, skip):
    channels = x.shape[1]
    return pl.pallas_call(
        functools.partial(within_kernel, far),
        in_specs=[VMEM] * 6,
        out_specs=[VMEM] * 2,
        out_shape=[jax.ShapeDtypeStruct((2 * CHUNK, channels), F32)] * 2,
        compiler_params=pltpu.CompilerParams(vmem_limit_bytes=VMEM_LIMIT),
        cost_estimate=pl.CostEstimate(
            flops=4_000_000_000, bytes_accessed=3_000_000, transcendentals=500_000
        ),
        name="within_far" if far else "within_near",
    )(aux, x, b, c, gate, skip)


def finish_rows(own, lead, c, incoming, gain):
    c = c.astype(BF)
    blocks = incoming.shape[1] // N
    carried = jnp.concatenate(
        [dot(c, incoming[q, k * N:(k + 1) * N]) for q in range(4) for k in range(blocks)], axis=1
    )
    gated = own + lead * carried
    mean = jnp.mean(gated * gated, axis=1, keepdims=True)
    return (gated * lax.rsqrt(mean + 1e-05) * gain).astype(BF)


def finish_block(block, own, lead, c, incoming, gain):
    return finish_rows(
        rows_of(own, block % 2), rows_of(lead, block % 2), rows_of(c, block), incoming, gain[...]
    )


def fill_incoming(quarters, incoming):
    mine = lax.axis_index("seq") % 4
    for k, quarter in enumerate(quarters):
        incoming[mine ^ k] = quarter[...]


def project_both(normed, w, start, columns, theirs, mine, at=0):
    wide = 512
    for k in range(0, columns, wide):
        out = dot(normed[...], w[:, start + k:start + k + wide])
        theirs[:, at + k:at + k + wide] = out[:CHUNK].astype(BF)
        mine[:, k:k + wide] = out[CHUNK:]


def far_kernel(
    columns, own, lead, c, q0, q1, q2, q3, gain, w, theirs, mine, normed, incoming
):
    me = lax.axis_index("head")
    fill_incoming((q0, q1, q2, q3), incoming)
    normed[:CHUNK] = finish_block(me ^ 3, own, lead, c, incoming, gain)
    normed[CHUNK:] = finish_block(me ^ 2, own, lead, c, incoming, gain)
    project_both(normed, w, 0, columns, theirs, mine)


def more_kernel(start, columns, normed, w, theirs, mine):
    project_both(normed, w, start, columns, theirs, mine)


def mixed_kernel(
    start, columns, normed, own, lead, c, q0, q1, q2, q3, gain, w,
    theirs, mine, kept, incoming, given,
):
    me = lax.axis_index("head")
    project_both(normed, w, start, columns, theirs, mine)
    fill_incoming((q0, q1, q2, q3), incoming)
    given[...] = finish_block(me ^ 1, own, lead, c, incoming, gain)
    kept[...] = finish_block(me, own, lead, c, incoming, gain)
    wide = 512
    for k in range(0, w.shape[1], wide):
        theirs[:, columns + k:columns + k + wide] = dot(given[...], w[:, k:k + wide]).astype(BF)


def kept_kernel(columns, kept, come, w, out):
    wide = 512
    for k in range(0, w.shape[1], wide):
        out[:, k:k + wide] = dot(kept[...], w[:, k:k + wide]) + come[
            :, columns + k:columns + k + wide
        ].astype(F32)


def add_kernel(mine, come, out):
    out[...] = (mine[...] + come[:, :out.shape[1]].astype(F32)).astype(BF)


def local_call(kernel, operands, outs, name, scratch=(), flops=0, limit=VMEM_LIMIT):
    return pl.pallas_call(
        kernel,
        in_specs=[VMEM] * len(operands),
        out_specs=[VMEM] * len(outs),
        out_shape=[jax.ShapeDtypeStruct(shape, dtype) for shape, dtype in outs],
        scratch_shapes=list(scratch),
        compiler_params=pltpu.CompilerParams(vmem_limit_bytes=limit),
        cost_estimate=pl.CostEstimate(flops=flops, bytes_accessed=0, transcendentals=0),
        name=name,
    )(*operands)


def pass_kernel(*refs):
    pass


def await_piece(piece, *earlier):
    arrays = [piece, *earlier]
    return pl.pallas_call(
        pass_kernel,
        in_specs=[pl.BlockSpec(memory_space=pl.ANY)] * len(arrays),
        out_specs=[pl.BlockSpec(memory_space=pl.ANY)] * len(arrays),
        out_shape=[jax.ShapeDtypeStruct(v.shape, v.dtype) for v in arrays],
        input_output_aliases={k: k for k in range(len(arrays))},
        compiler_params=pltpu.CompilerParams(vmem_limit_bytes=1024 * 1024),
        cost_estimate=pl.CostEstimate(
            flops=20_000_000_000, bytes_accessed=100_000_000, transcendentals=0
        ),
        name="await_piece",
    )(*arrays)


def early_kernel(kept, first, second, out):
    at = 0
    for piece in (first, second):
        cut = slice(at, at + piece.shape[1])
        out[:, cut] = (kept[:, cut] + piece[...].astype(F32)).astype(BF)
        at += piece.shape[1]


def early_sums(kept, first, second):
    rows = first.shape[0]
    wide = first.shape[1] + second.shape[1]
    return pl.pallas_call(
        early_kernel,
        grid=(1,),
        in_specs=[VMEM] * 3,
        out_specs=pl.BlockSpec((rows, wide), lambda j: (0, 0)),
        out_shape=jax.ShapeDtypeStruct(kept.shape, BF),
        compiler_params=pltpu.CompilerParams(vmem_limit_bytes=VMEM_LIMIT),
        name="early_sums",
    )(kept, first, second)


def last_kernel(kept, third, filled, out, part, sems):
    wide = third.shape[1]
    start = kept.shape[1] - wide
    block = wide // 2
    stores = []
    for k in range(2):
        cut = slice(k * block, (k + 1) * block)
        part[:, cut] = (
            kept[:, start + k * block:start + (k + 1) * block] + third[:, cut].astype(F32)
        ).astype(BF)
        stores.append(
            pltpu.make_async_copy(
                part.at[:, cut], out.at[:, start + k * block:start + (k + 1) * block], sems.at[k]
            )
        )
        stores[k].start()
    for store in stores:
        store.wait()


def last_sums(kept, third, filled):
    return pl.pallas_call(
        last_kernel,
        in_specs=[VMEM, VMEM, pl.BlockSpec(memory_space=pl.ANY)],
        out_specs=pl.BlockSpec(memory_space=pl.ANY),
        out_shape=jax.ShapeDtypeStruct(kept.shape, BF),
        input_output_aliases={2: 0},
        scratch_shapes=[pltpu.VMEM(third.shape, BF), pltpu.SemaphoreType.DMA((2,))],
        compiler_params=pltpu.CompilerParams(vmem_limit_bytes=VMEM_LIMIT),
        name="last_sums",
    )(kept, third, filled)


def per_device(
    seq_count,
    ssm_input,
    gate_input,
    step_raw,
    decay_log,
    state_in,
    state_out,
    skip_gain,
    norm_gain,
    out_weight,
):
    tok = ssm_input.shape[0]
    heads = decay_log.shape[0]
    b = state_in.reshape(tok, N)
    c = state_out.reshape(tok, N)
    *gives, wk, aux = give_states(step_raw.T, decay_log.reshape(1, heads), ssm_input, b)
    keep = keep_states(wk, ssm_input, b)
    inputs = (ssm_input, b, c, gate_input, skip_gain.reshape(1, heads))
    local = within(True, aux, *inputs)
    (own, lead), quarters = incoming_states(gives, keep, seq_count, local)

    near = [(h, h ^ 1) for h in range(4)]
    far = [(h, h ^ 2) for h in range(4)]
    gain = norm_gain.reshape(1, -1)
    channels, dout = out_weight.shape
    rows = CHUNK
    states = pltpu.VMEM((4,) + quarters[0].shape, BF)
    finish = (own, lead, c, *quarters, gain, out_weight)
    (_, one), (start2, two), (start3, three) = PIECES

    def piece_outs(columns, extra=0):
        return [((rows, columns + extra), BF), ((rows, columns), F32)]

    def add(mine, theirs):
        come = lax.ppermute(theirs, "head", near)
        return local_call(add_kernel, (mine, come), [(mine.shape, BF)], "add_pair", limit=1 << 22)[0], come

    theirs, mine, normed = local_call(
        functools.partial(far_kernel, one),
        finish,
        piece_outs(one) + [((2 * rows, channels), BF)],
        "finish_far",
        [states],
        4 * rows * channels * one,
    )
    first, _ = add(mine, theirs)
    aux, first = lax.optimization_barrier((aux, first))
    theirs, mine = local_call(
        functools.partial(more_kernel, start2, two),
        (normed, out_weight),
        piece_outs(two),
        "project_more",
        flops=4 * rows * channels * two,
    )
    second, _ = add(mine, theirs)
    near_own, near_lead = within(False, aux, *inputs)
    normed, second = lax.optimization_barrier((normed, second))
    theirs, mine, kept = local_call(
        functools.partial(mixed_kernel, start3, three),
        (normed, near_own, near_lead) + finish[2:],
        piece_outs(three, dout) + [((rows, channels), BF)],
        "finish_near",
        [states, pltpu.VMEM((rows, channels), BF)],
        2 * rows * channels * (2 * three + dout),
    )
    third, come = add(mine, theirs)
    kept = local_call(
        functools.partial(kept_kernel, three),
        (kept, come, out_weight),
        [((rows, dout), F32)],
        "project_kept",
        flops=2 * rows * channels * dout,
    )[0]
    first = await_piece(lax.ppermute(first, "head", far))[0]
    second, first = await_piece(lax.ppermute(second, "head", far), first)
    filled = early_sums(kept, first, second)
    third, filled = await_piece(lax.ppermute(third, "head", far), filled)
    return last_sums(kept, third, filled)


def solution(mesh):
    in_specs = (
        P("seq", "head"),
        P("seq", "head"),
        P("seq", "head"),
        P("head"),
        P("seq", "head", None),
        P("seq", "head", None),
        P("head"),
        P("head"),
        P("head", None),
    )
    out_specs = P(("seq", "head"), None)
    return jax.shard_map(
        functools.partial(per_device, mesh.shape["seq"]),
        mesh=mesh,
        in_specs=in_specs,
        out_specs=out_specs,
        check_vma=False,
    )
```

```python
import functools

import jax
import jax.numpy as jnp
from jax import lax
from jax.experimental import pallas as pl
from jax.experimental.pallas import tpu as pltpu
from jax.sharding import PartitionSpec as P

P_SIZE = 64
N = 128
CHUNK = 128
LANES = 128
BF = jnp.bfloat16
F32 = jnp.float32
VMEM_LIMIT = 16 * 1024 * 1024
WHOLE_VMEM = 61 * 1024 * 1024 + 512 * 1024
PIECES = ((0, 768), (768, 2304), (3072, 1024))


def dot(a, b, contract=((1,), (0,)), precision=None):
    return lax.dot_general(a, b, (contract, ((), ())), precision=precision, preferred_element_type=F32)


def split2(v):
    hi = v.astype(BF)
    return hi, (v - hi.astype(F32)).astype(BF)


def split3(v):
    hi, rest = v.astype(BF), v
    rest = v - hi.astype(F32)
    mid = rest.astype(BF)
    return hi, mid, (rest - mid.astype(F32)).astype(BF)


def pick(rows, lanes, heads, per_head, first):
    r = lax.broadcasted_iota(jnp.int32, (rows, lanes), 0) % heads
    l = lax.broadcasted_iota(jnp.int32, (rows, lanes), 1) // per_head + first
    return jnp.where(r == l, 1.0, 0.0).astype(BF)


def step_vectors(raw, rate_row, wk, aux_ref):
    heads, tok = raw.shape
    chunks = tok // CHUNK
    step = jnp.maximum(raw, 0.0) + jnp.log1p(jnp.exp(-jnp.abs(raw)))
    r = lax.broadcasted_iota(jnp.int32, (heads, heads), 0)
    l = lax.broadcasted_iota(jnp.int32, (heads, heads), 1)
    rate = jnp.sum(jnp.where(r == l, rate_row, 0.0), axis=1, keepdims=True)
    logs = -step * jnp.exp(rate)
    parts = split3(logs)
    stacked = jnp.concatenate(
        [p[:, c * CHUNK:(c + 1) * CHUNK] for c in range(chunks) for p in parts], axis=0
    )
    s = lax.broadcasted_iota(jnp.int32, (CHUNK, 2 * CHUNK), 0)
    t = lax.broadcasted_iota(jnp.int32, (CHUNK, 2 * CHUNK), 1)
    tri = jnp.where(jnp.where(t < CHUNK, t - s, s - t + (CHUNK - 1)) >= 0, 1.0, 0.0).astype(BF)
    sums = dot(stacked, tri)
    pre, suf = [], []
    for c in range(chunks):
        base = 3 * heads * c
        total = (
            sums[base:base + heads] + sums[base + heads:base + 2 * heads]
        ) + sums[base + 2 * heads:base + 3 * heads]
        pre.append(total[:, :CHUNK])
        suf.append(total[:, CHUNK:])
    after = jnp.zeros((heads, 1), F32)
    for c in reversed(range(chunks)):
        w = step[:, c * CHUNK:(c + 1) * CHUNK] * jnp.exp(suf[c] + after)
        hi, lo = split2(w)
        wk[:heads, c * CHUNK:(c + 1) * CHUNK] = hi
        wk[heads:, c * CHUNK:(c + 1) * CHUNK] = lo
        after = after + pre[c][:, CHUNK - 1:]
    hi, lo = split2(jnp.broadcast_to(jnp.exp(after), (heads, CHUNK)))
    wk[:heads, tok:] = hi
    wk[heads:, tok:] = lo
    for c in range(chunks):
        aux_ref[c, :heads] = step[:, c * CHUNK:(c + 1) * CHUNK]
        aux_ref[c, heads:2 * heads] = pre[c]
        aux_ref[c, 2 * heads:] = suf[c]


def tail_rows(decays):
    r = lax.broadcasted_iota(jnp.int32, (16, LANES), 0)
    tail = jnp.zeros((16, LANES), F32)
    for k, decay in enumerate(decays):
        hi, lo = split2(decay)
        tail = jnp.where(r == 2 * k, hi.astype(F32), tail)
        tail = jnp.where(r == 2 * k + 1, lo.astype(F32), tail)
    return tail.astype(BF)


def decays_of(msg):
    blocks = (msg.shape[0] - 16) // N
    tail = msg[blocks * N:].astype(F32)
    return [tail[2 * k:2 * k + 1] + tail[2 * k + 1:2 * k + 2] for k in range(blocks)]


def quarter_message(x, b, wk, first_head, msg):
    tok, width = x.shape
    heads2 = wk.shape[0]
    spread = dot(wk[...], pick(heads2, width, heads2 // 2, P_SIZE, first_head), ((0,), (0,)))
    state = dot(b, (x * spread[:tok]).astype(BF), ((0,), (0,)))
    decays = []
    for k in range(width // LANES):
        msg[k * N:(k + 1) * N] = state[:, k * LANES:(k + 1) * LANES].astype(BF)
        decays.append(spread[tok:tok + 1, k * LANES:(k + 1) * LANES])
    msg[msg.shape[0] - 16:] = tail_rows(decays)


def load_quarter(x, x_v, quarter, sem):
    width = x_v.shape[1]
    return pltpu.make_async_copy(
        x.at[:, pl.ds(pl.multiple_of(quarter * width, width), width)], x_v, sem
    )


def give_kernel(raw, rate, x, b, msg1, msg2, msg3, wk, aux, raw_v, rate_v, x_v, b_v, sems):
    mine = lax.axis_index("seq") % 4
    loads = [
        pltpu.make_async_copy(raw, raw_v, sems.at[0]),
        pltpu.make_async_copy(rate, rate_v, sems.at[1]),
        pltpu.make_async_copy(b, b_v, sems.at[2]),
    ] + [load_quarter(x, x_v.at[k - 1], mine ^ k, sems.at[2 + k]) for k in (1, 2, 3)]
    for load in loads:
        load.start()
    loads[0].wait()
    loads[1].wait()
    step_vectors(raw_v[...], rate_v[...], wk, aux)
    for load in loads[2:]:
        load.wait()
    b16 = b_v[...].astype(BF)
    heads = x_v.shape[2] // P_SIZE
    for k, msg in ((1, msg1), (2, msg2), (3, msg3)):
        quarter_message(x_v[k - 1], b16, wk, (mine ^ k) * heads, msg)


def keep_kernel(wk, x, b, msg, x_v, b_v, sems):
    mine = lax.axis_index("seq") % 4
    loads = [load_quarter(x, x_v, mine, sems.at[0]), pltpu.make_async_copy(b, b_v, sems.at[1])]
    for load in loads:
        load.start()
    for load in loads:
        load.wait()
    quarter_message(x_v[...], b_v[...].astype(BF), wk, mine * (x_v.shape[1] // P_SIZE), msg)


HBM = pl.BlockSpec(memory_space=pltpu.HBM)
VMEM = pl.BlockSpec(memory_space=pltpu.VMEM)


def give_states(raw, rate, x, b):
    heads, tok = raw.shape
    lanes = x.shape[1] // 4
    return pl.pallas_call(
        give_kernel,
        in_specs=[HBM] * 4,
        out_shape=[jax.ShapeDtypeStruct((lanes // LANES * N + 16, LANES), BF)] * 3
        + [
            jax.ShapeDtypeStruct((2 * heads, tok + CHUNK), BF),
            jax.ShapeDtypeStruct((tok // CHUNK, 3 * heads, CHUNK), F32),
        ],
        scratch_shapes=[
            pltpu.VMEM((heads, tok), F32),
            pltpu.VMEM((1, heads), F32),
            pltpu.VMEM((3, tok, lanes), F32),
            pltpu.VMEM((tok, N), F32),
            pltpu.SemaphoreType.DMA((6,)),
        ],
        compiler_params=pltpu.CompilerParams(vmem_limit_bytes=WHOLE_VMEM),
        cost_estimate=pl.CostEstimate(flops=200_000_000, bytes_accessed=1_500_000, transcendentals=0),
        name="give_states",
    )(raw, rate, x, b)


def keep_states(wk, x, b):
    tok = x.shape[0]
    lanes = x.shape[1] // 4
    return pl.pallas_call(
        keep_kernel,
        in_specs=[VMEM, HBM, HBM],
        out_shape=jax.ShapeDtypeStruct((lanes // LANES * N + 16, LANES), BF),
        scratch_shapes=[
            pltpu.VMEM((tok, lanes), F32),
            pltpu.VMEM((tok, N), F32),
            pltpu.SemaphoreType.DMA((2,)),
        ],
        compiler_params=pltpu.CompilerParams(vmem_limit_bytes=VMEM_LIMIT),
        cost_estimate=pl.CostEstimate(flops=200_000_000, bytes_accessed=1_500_000, transcendentals=0),
        name="keep_states",
    )(wk, x, b)


def link(later, earlier, out):
    ahead, behind = decays_of(later), decays_of(earlier)
    for k, decay in enumerate(ahead):
        rows = slice(k * N, (k + 1) * N)
        out[rows] = (later[rows].astype(F32) + decay * earlier[rows].astype(F32)).astype(BF)
    out[len(ahead) * N:] = tail_rows([p * q for p, q in zip(ahead, behind)])


def is_later(distance):
    return (lax.axis_index("seq") // distance) % 2


def run_kernel(distance, own, come, out):
    later = is_later(distance)

    @pl.when(later == 0)
    def _():
        link(come, own, out)

    @pl.when(later == 1)
    def _():
        link(own, come, out)


def first_ahead_kernel(distance, come, out):
    later = is_later(distance)
    rows = out.shape[0] - 16

    @pl.when(later == 0)
    def _():
        out[:rows] = jnp.zeros((rows, LANES), BF)
        out[rows:] = tail_rows([jnp.ones((1, LANES), F32)] * (rows // N))

    @pl.when(later == 1)
    def _():
        out[...] = come[...]


def ahead_kernel(distance, ahead, come, out):
    later = is_later(distance)

    @pl.when(later == 0)
    def _():
        out[...] = ahead[...]

    @pl.when(later == 1)
    def _():
        link(ahead, come, out)


def by_section(work):
    mine = lax.axis_index("seq") % 4
    for v in range(4):
        pl.when(mine == v)(functools.partial(work, [j ^ v for j in range(4)]))


def join_four_kernel(own, come1, come2, come3, out):
    messages = (own, come1, come2, come3)

    def work(place):
        sections = [messages[p] for p in place]
        decays = [decays_of(section) for section in sections]
        for k in range(len(decays[0])):
            rows = slice(k * N, (k + 1) * N)
            total = sections[0][rows].astype(F32)
            for section, decay in zip(sections[1:], decays[1:]):
                total = section[rows].astype(F32) + decay[k] * total
            out[rows] = total.astype(BF)
        spans = [p * q * r * t for p, q, r, t in zip(*decays)]
        out[len(spans) * N:] = tail_rows(spans)

    by_section(work)


def end_kernel(distance, ahead, last, own, come1, come2, come3, mine, out1, out2, out3):
    messages, outs = (own, come1, come2, come3), (mine, out1, out2, out3)
    weight = is_later(distance).astype(F32)

    def work(place):
        sections, targets = [messages[p] for p in place], [outs[p] for p in place]
        decays = [decays_of(section) for section in sections]
        for k in range(len(decays[0])):
            rows = slice(k * N, (k + 1) * N)
            state = weight * last[rows].astype(F32)
            if ahead is not None:
                state = ahead[rows].astype(F32) + decays_of(ahead)[k] * state
            for j in range(4):
                targets[j][rows] = state.astype(BF)
                if j < 3:
                    state = sections[j][rows].astype(F32) + decays[j][k] * state

    by_section(work)


def scan_call(kernel, operands, shapes, name):
    return pl.pallas_call(
        kernel,
        out_shape=[jax.ShapeDtypeStruct(shape, BF) for shape in shapes],
        compiler_params=pltpu.CompilerParams(vmem_limit_bytes=VMEM_LIMIT),
        cost_estimate=pl.CostEstimate(flops=500_000, bytes_accessed=400_000, transcendentals=0),
        name=name,
    )(*operands)


def incoming_states(gives, keep, count, hold):
    def exchange(value, distance):
        return lax.ppermute(value, "seq", [(s, s ^ distance) for s in range(count)])

    def joined(kernel, *operands):
        return scan_call(kernel, operands, [keep.shape], "join_states")[0]

    parts = [keep] + [exchange(give, k) for k, give in zip((1, 2, 3), gives)]
    run, ahead, distance = joined(join_four_kernel, *parts), None, 4
    got = exchange(run, distance)
    while distance * 2 < count:
        if ahead is None:
            ahead = joined(functools.partial(first_ahead_kernel, distance), got)
        else:
            ahead = joined(functools.partial(ahead_kernel, distance), ahead, got)
        run = joined(functools.partial(run_kernel, distance), run, got)
        distance *= 2
        got = exchange(run, distance)
    hold, got = lax.optimization_barrier((hold, got))
    operands = [got] + parts
    if ahead is None:
        kernel = functools.partial(end_kernel, distance, None)
    else:
        kernel, operands = functools.partial(end_kernel, distance), [ahead] + operands
    shape = (keep.shape[0] - 16, LANES)
    outs = scan_call(kernel, operands, [shape] * 4, "join_end")
    return hold, [outs[0]] + [exchange(out, k) for k, out in zip((1, 2, 3), outs[1:])]


def rows_of(ref, block):
    return ref[pl.ds(pl.multiple_of(block * CHUNK, CHUNK), CHUNK), :]


def within_kernel(far, aux, x_ref, b_ref, c_ref, gate_ref, skip_ref, own_ref, lead_ref):
    channels = x_ref.shape[1]
    heads = aux.shape[1] // 3
    width = 256
    here = width // P_SIZE
    half = lax.axis_index("head") // 2
    half = 1 - half if far else half
    second = half == 1

    def vectors(c):
        return [aux[c, k * heads:(k + 1) * heads] for k in range(3)]

    def put(values):
        return jnp.concatenate([jnp.concatenate(split2(v), axis=0) for v in values], axis=1)

    first, then = vectors(0), vectors(1)
    ends = [v[1][:, CHUNK - 1:] for v in (first, then)]
    early = put(
        [
            jnp.where(second, first[0] * jnp.exp(first[2] + ends[1]), 0.0),
            jnp.where(second, then[0] * jnp.exp(then[2]), 0.0),
        ]
    )
    before = jnp.where(second, ends[0] + ends[1], 0.0)
    r = lax.broadcasted_iota(jnp.int32, (CHUNK, CHUNK), 0)
    l = lax.broadcasted_iota(jnp.int32, (CHUNK, CHUNK), 1)
    duo, trip, lines, scores, rows_b, rows_c, rows_x, rows_g = ([] for _ in range(8))
    for i in range(2):
        block = 2 * half + i
        step, pre, suf = vectors(block)
        duo.append(put((step, step * jnp.exp(suf), jnp.exp(pre), jnp.exp(pre + before))))
        trip.append(jnp.concatenate(split3(pre), axis=0))
        lines.append(pre)
        before = before + pre[:, CHUNK - 1:]
        b, c = rows_of(b_ref, block), rows_of(c_ref, block)
        raw = dot(c, b, ((1,), (1,)), lax.Precision.HIGHEST)
        scores.append(jnp.where(r >= l, raw, 0.0))
        rows_b.append(b.astype(BF))
        rows_c.append(c.astype(BF))
        rows_x.append(rows_of(x_ref, block))
        rows_g.append(rows_of(gate_ref, block))
    early_b = b_ref[:2 * CHUNK].astype(BF)
    gains = jnp.broadcast_to(jnp.concatenate(split3(skip_ref[...]), axis=1), (8, 3 * heads))
    lane = lax.broadcasted_iota(jnp.int32, (CHUNK, LANES), 1)
    for g in range(channels // width):
        at = slice(g * width, (g + 1) * width)
        spread = pick(2 * heads, width, heads, P_SIZE, g * here)
        columns = pick(3 * heads, here * CHUNK, heads, CHUNK, g * here)
        skip = dot(gains, pick(3 * heads, width, heads, P_SIZE, g * here))[:1]
        weights = dot(early, spread, ((0,), (0,)))
        state = dot(early_b, (x_ref[:2 * CHUNK, at] * weights).astype(BF), ((0,), (0,)))
        for i in range(2):
            cut = slice(i * CHUNK, (i + 1) * CHUNK)
            wide = dot(duo[i], spread, ((0,), (0,)))
            x = rows_x[i][:, at]
            stepped = x * wide[:CHUNK]
            lead = wide[2 * CHUNK:3 * CHUNK]
            tall = dot(trip[i], columns, ((0,), (0,)))
            outs = []
            for pair in range(here // 2):
                mixes = []
                for h in (2 * pair, 2 * pair + 1):
                    line = lines[i][g * here + h:g * here + h + 1]
                    gap = tall[:, h * CHUNK:(h + 1) * CHUNK] - line
                    mixes.append((scores[i] * jnp.exp(jnp.minimum(gap, 0.0))).astype(BF))
                both = stepped[:, pair * LANES:(pair + 1) * LANES]
                stacked = jnp.concatenate(
                    [
                        jnp.where(lane < P_SIZE, both, 0.0).astype(BF),
                        jnp.where(lane < P_SIZE, 0.0, both).astype(BF),
                    ],
                    axis=0,
                )
                outs.append(dot(jnp.concatenate(mixes, axis=1), stacked))
            y = jnp.concatenate(outs, axis=1) + skip * x
            y = y + lead * dot(rows_c[i], state.astype(BF))
            v = rows_g[i][:, at].astype(F32)
            silu = v / (1.0 + jnp.exp(-v))
            own_ref[cut, at] = y * silu
            lead_ref[cut, at] = wide[3 * CHUNK:] * silu
            if i == 0:
                weighted = (x * wide[CHUNK:2 * CHUNK]).astype(BF)
                state = state * lead[CHUNK - 1:] + dot(rows_b[i], weighted, ((0,), (0,)))


def within(far, aux, x, b, c, gate, skip):
    channels = x.shape[1]
    return pl.pallas_call(
        functools.partial(within_kernel, far),
        in_specs=[VMEM] * 6,
        out_specs=[VMEM] * 2,
        out_shape=[jax.ShapeDtypeStruct((2 * CHUNK, channels), F32)] * 2,
        compiler_params=pltpu.CompilerParams(vmem_limit_bytes=VMEM_LIMIT),
        cost_estimate=pl.CostEstimate(
            flops=4_000_000_000, bytes_accessed=3_000_000, transcendentals=500_000
        ),
        name="within_far" if far else "within_near",
    )(aux, x, b, c, gate, skip)


def finish_rows(own, lead, c, incoming, gain):
    c = c.astype(BF)
    blocks = incoming.shape[1] // N
    carried = jnp.concatenate(
        [dot(c, incoming[q, k * N:(k + 1) * N]) for q in range(4) for k in range(blocks)], axis=1
    )
    gated = own + lead * carried
    mean = jnp.mean(gated * gated, axis=1, keepdims=True)
    return (gated * lax.rsqrt(mean + 1e-05) * gain).astype(BF)


def finish_block(block, own, lead, c, incoming, gain):
    return finish_rows(
        rows_of(own, block % 2), rows_of(lead, block % 2), rows_of(c, block), incoming, gain[...]
    )


def fill_incoming(quarters, incoming):
    mine = lax.axis_index("seq") % 4
    for k, quarter in enumerate(quarters):
        incoming[mine ^ k] = quarter[...]


def project_both(normed, w, start, columns, theirs, mine, at=0):
    wide = 256
    for k in range(0, columns, wide):
        out = dot(normed[...], w[:, start + k:start + k + wide])
        theirs[:, at + k:at + k + wide] = out[:CHUNK].astype(BF)
        mine[:, k:k + wide] = out[CHUNK:]


def far_kernel(
    columns, own, lead, c, q0, q1, q2, q3, gain, w, theirs, mine, normed, incoming
):
    me = lax.axis_index("head")
    fill_incoming((q0, q1, q2, q3), incoming)
    normed[:CHUNK] = finish_block(me ^ 3, own, lead, c, incoming, gain)
    normed[CHUNK:] = finish_block(me ^ 2, own, lead, c, incoming, gain)
    project_both(normed, w, 0, columns, theirs, mine)


def more_kernel(start, columns, normed, w, theirs, mine):
    project_both(normed, w, start, columns, theirs, mine)


def mixed_kernel(
    start, columns, normed, own, lead, c, q0, q1, q2, q3, gain, w,
    theirs, mine, kept, incoming, given,
):
    me = lax.axis_index("head")
    project_both(normed, w, start, columns, theirs, mine)
    fill_incoming((q0, q1, q2, q3), incoming)
    given[...] = finish_block(me ^ 1, own, lead, c, incoming, gain)
    kept[...] = finish_block(me, own, lead, c, incoming, gain)
    wide = 512
    for k in range(0, w.shape[1], wide):
        theirs[:, columns + k:columns + k + wide] = dot(given[...], w[:, k:k + wide]).astype(BF)


def kept_kernel(columns, kept, come, w, out):
    wide = 512
    for k in range(0, w.shape[1], wide):
        out[:, k:k + wide] = dot(kept[...], w[:, k:k + wide]) + come[
            :, columns + k:columns + k + wide
        ].astype(F32)


def add_kernel(mine, come, out):
    out[...] = (mine[...] + come[:, :out.shape[1]].astype(F32)).astype(BF)


def local_call(kernel, operands, outs, name, scratch=(), flops=0, limit=VMEM_LIMIT):
    return pl.pallas_call(
        kernel,
        in_specs=[VMEM] * len(operands),
        out_specs=[VMEM] * len(outs),
        out_shape=[jax.ShapeDtypeStruct(shape, dtype) for shape, dtype in outs],
        scratch_shapes=list(scratch),
        compiler_params=pltpu.CompilerParams(vmem_limit_bytes=limit),
        cost_estimate=pl.CostEstimate(flops=flops, bytes_accessed=0, transcendentals=0),
        name=name,
    )(*operands)


def pass_kernel(*refs):
    pass


def await_piece(piece, *earlier):
    arrays = [piece, *earlier]
    return pl.pallas_call(
        pass_kernel,
        in_specs=[pl.BlockSpec(memory_space=pl.ANY)] * len(arrays),
        out_specs=[pl.BlockSpec(memory_space=pl.ANY)] * len(arrays),
        out_shape=[jax.ShapeDtypeStruct(v.shape, v.dtype) for v in arrays],
        input_output_aliases={k: k for k in range(len(arrays))},
        compiler_params=pltpu.CompilerParams(vmem_limit_bytes=1024 * 1024),
        cost_estimate=pl.CostEstimate(
            flops=20_000_000_000, bytes_accessed=100_000_000, transcendentals=0
        ),
        name="await_piece",
    )(*arrays)


def early_kernel(kept, first, second, out):
    at = 0
    for piece in (first, second):
        cut = slice(at, at + piece.shape[1])
        out[:, cut] = (kept[:, cut] + piece[...].astype(F32)).astype(BF)
        at += piece.shape[1]


def early_sums(kept, first, second):
    rows = first.shape[0]
    wide = first.shape[1] + second.shape[1]
    return pl.pallas_call(
        early_kernel,
        grid=(1,),
        in_specs=[VMEM] * 3,
        out_specs=pl.BlockSpec((rows, wide), lambda j: (0, 0)),
        out_shape=jax.ShapeDtypeStruct(kept.shape, BF),
        compiler_params=pltpu.CompilerParams(vmem_limit_bytes=VMEM_LIMIT),
        name="early_sums",
    )(kept, first, second)


def last_kernel(kept, third, filled, out, part, sems):
    wide = third.shape[1]
    start = kept.shape[1] - wide
    block = wide // 2
    stores = []
    for k in range(2):
        cut = slice(k * block, (k + 1) * block)
        part[:, cut] = (
            kept[:, start + k * block:start + (k + 1) * block] + third[:, cut].astype(F32)
        ).astype(BF)
        stores.append(
            pltpu.make_async_copy(
                part.at[:, cut], out.at[:, start + k * block:start + (k + 1) * block], sems.at[k]
            )
        )
        stores[k].start()
    for store in stores:
        store.wait()


def last_sums(kept, third, filled):
    return pl.pallas_call(
        last_kernel,
        in_specs=[VMEM, VMEM, pl.BlockSpec(memory_space=pl.ANY)],
        out_specs=pl.BlockSpec(memory_space=pl.ANY),
        out_shape=jax.ShapeDtypeStruct(kept.shape, BF),
        input_output_aliases={2: 0},
        scratch_shapes=[pltpu.VMEM(third.shape, BF), pltpu.SemaphoreType.DMA((2,))],
        compiler_params=pltpu.CompilerParams(vmem_limit_bytes=VMEM_LIMIT),
        name="last_sums",
    )(kept, third, filled)


def per_device(
    seq_count,
    ssm_input,
    gate_input,
    step_raw,
    decay_log,
    state_in,
    state_out,
    skip_gain,
    norm_gain,
    out_weight,
):
    tok = ssm_input.shape[0]
    heads = decay_log.shape[0]
    b = state_in.reshape(tok, N)
    c = state_out.reshape(tok, N)
    *gives, wk, aux = give_states(step_raw.T, decay_log.reshape(1, heads), ssm_input, b)
    keep = keep_states(wk, ssm_input, b)
    inputs = (ssm_input, b, c, gate_input, skip_gain.reshape(1, heads))
    local = within(True, aux, *inputs)
    (own, lead), quarters = incoming_states(gives, keep, seq_count, local)

    near = [(h, h ^ 1) for h in range(4)]
    far = [(h, h ^ 2) for h in range(4)]
    gain = norm_gain.reshape(1, -1)
    channels, dout = out_weight.shape
    rows = CHUNK
    states = pltpu.VMEM((4,) + quarters[0].shape, BF)
    finish = (own, lead, c, *quarters, gain, out_weight)
    (_, one), (start2, two), (start3, three) = PIECES

    def piece_outs(columns, extra=0):
        return [((rows, columns + extra), BF), ((rows, columns), F32)]

    def add(mine, theirs):
        come = lax.ppermute(theirs, "head", near)
        return local_call(add_kernel, (mine, come), [(mine.shape, BF)], "add_pair", limit=1 << 22)[0], come

    theirs, mine, normed = local_call(
        functools.partial(far_kernel, one),
        finish,
        piece_outs(one) + [((2 * rows, channels), BF)],
        "finish_far",
        [states],
        4 * rows * channels * one,
    )
    first, _ = add(mine, theirs)
    aux, first = lax.optimization_barrier((aux, first))
    theirs, mine = local_call(
        functools.partial(more_kernel, start2, two),
        (normed, out_weight),
        piece_outs(two),
        "project_more",
        flops=4 * rows * channels * two,
    )
    second, _ = add(mine, theirs)
    near_own, near_lead = within(False, aux, *inputs)
    normed, second = lax.optimization_barrier((normed, second))
    theirs, mine, kept = local_call(
        functools.partial(mixed_kernel, start3, three),
        (normed, near_own, near_lead) + finish[2:],
        piece_outs(three, dout) + [((rows, channels), BF)],
        "finish_near",
        [states, pltpu.VMEM((rows, channels), BF)],
        2 * rows * channels * (2 * three + dout),
    )
    third, come = add(mine, theirs)
    kept = local_call(
        functools.partial(kept_kernel, three),
        (kept, come, out_weight),
        [((rows, dout), F32)],
        "project_kept",
        flops=2 * rows * channels * dout,
    )[0]
    first = await_piece(lax.ppermute(first, "head", far))[0]
    second, first = await_piece(lax.ppermute(second, "head", far), first)
    filled = early_sums(kept, first, second)
    third, filled = await_piece(lax.ppermute(third, "head", far), filled)
    return last_sums(kept, third, filled)


def solution(mesh):
    in_specs = (
        P("seq", "head"),
        P("seq", "head"),
        P("seq", "head"),
        P("head"),
        P("seq", "head", None),
        P("seq", "head", None),
        P("head"),
        P("head"),
        P("head", None),
    )
    out_specs = P(("seq", "head"), None)
    return jax.shard_map(
        functools.partial(per_device, mesh.shape["seq"]),
        mesh=mesh,
        in_specs=in_specs,
        out_specs=out_specs,
        check_vma=False,
    )
```

```python
import functools

import jax
import jax.numpy as jnp
from jax import lax
from jax.experimental import pallas as pl
from jax.experimental.pallas import tpu as pltpu
from jax.sharding import PartitionSpec as P

P_SIZE = 64
N = 128
CHUNK = 128
LANES = 128
BF = jnp.bfloat16
F32 = jnp.float32
VMEM_LIMIT = 16 * 1024 * 1024
WHOLE_VMEM = 61 * 1024 * 1024 + 512 * 1024
PIECES = ((0, 1024), (1024, 2048), (3072, 1024))


def dot(a, b, contract=((1,), (0,)), precision=None):
    return lax.dot_general(a, b, (contract, ((), ())), precision=precision, preferred_element_type=F32)


def split2(v):
    hi = v.astype(BF)
    return hi, (v - hi.astype(F32)).astype(BF)


def split3(v):
    hi, rest = v.astype(BF), v
    rest = v - hi.astype(F32)
    mid = rest.astype(BF)
    return hi, mid, (rest - mid.astype(F32)).astype(BF)


def pick(rows, lanes, heads, per_head, first):
    r = lax.broadcasted_iota(jnp.int32, (rows, lanes), 0) % heads
    l = lax.broadcasted_iota(jnp.int32, (rows, lanes), 1) // per_head + first
    return jnp.where(r == l, 1.0, 0.0).astype(BF)


def step_vectors(raw, rate_row, wk, aux_ref):
    heads, tok = raw.shape
    chunks = tok // CHUNK
    step = jnp.maximum(raw, 0.0) + jnp.log1p(jnp.exp(-jnp.abs(raw)))
    r = lax.broadcasted_iota(jnp.int32, (heads, heads), 0)
    l = lax.broadcasted_iota(jnp.int32, (heads, heads), 1)
    rate = jnp.sum(jnp.where(r == l, rate_row, 0.0), axis=1, keepdims=True)
    logs = -step * jnp.exp(rate)
    parts = split3(logs)
    stacked = jnp.concatenate(
        [p[:, c * CHUNK:(c + 1) * CHUNK] for c in range(chunks) for p in parts], axis=0
    )
    s = lax.broadcasted_iota(jnp.int32, (CHUNK, 2 * CHUNK), 0)
    t = lax.broadcasted_iota(jnp.int32, (CHUNK, 2 * CHUNK), 1)
    tri = jnp.where(jnp.where(t < CHUNK, t - s, s - t + (CHUNK - 1)) >= 0, 1.0, 0.0).astype(BF)
    sums = dot(stacked, tri)
    pre, suf = [], []
    for c in range(chunks):
        base = 3 * heads * c
        total = (
            sums[base:base + heads] + sums[base + heads:base + 2 * heads]
        ) + sums[base + 2 * heads:base + 3 * heads]
        pre.append(total[:, :CHUNK])
        suf.append(total[:, CHUNK:])
    after = jnp.zeros((heads, 1), F32)
    for c in reversed(range(chunks)):
        w = step[:, c * CHUNK:(c + 1) * CHUNK] * jnp.exp(suf[c] + after)
        hi, lo = split2(w)
        wk[:heads, c * CHUNK:(c + 1) * CHUNK] = hi
        wk[heads:, c * CHUNK:(c + 1) * CHUNK] = lo
        after = after + pre[c][:, CHUNK - 1:]
    hi, lo = split2(jnp.broadcast_to(jnp.exp(after), (heads, CHUNK)))
    wk[:heads, tok:] = hi
    wk[heads:, tok:] = lo
    for c in range(chunks):
        aux_ref[c, :heads] = step[:, c * CHUNK:(c + 1) * CHUNK]
        aux_ref[c, heads:2 * heads] = pre[c]
        aux_ref[c, 2 * heads:] = suf[c]


def tail_rows(decays):
    r = lax.broadcasted_iota(jnp.int32, (16, LANES), 0)
    tail = jnp.zeros((16, LANES), F32)
    for k, decay in enumerate(decays):
        hi, lo = split2(decay)
        tail = jnp.where(r == 2 * k, hi.astype(F32), tail)
        tail = jnp.where(r == 2 * k + 1, lo.astype(F32), tail)
    return tail.astype(BF)


def decays_of(msg):
    blocks = (msg.shape[0] - 16) // N
    tail = msg[blocks * N:].astype(F32)
    return [tail[2 * k:2 * k + 1] + tail[2 * k + 1:2 * k + 2] for k in range(blocks)]


def quarter_message(x, b, wk, first_head, msg):
    tok, width = x.shape
    heads2 = wk.shape[0]
    spread = dot(wk[...], pick(heads2, width, heads2 // 2, P_SIZE, first_head), ((0,), (0,)))
    state = dot(b, (x * spread[:tok]).astype(BF), ((0,), (0,)))
    decays = []
    for k in range(width // LANES):
        msg[k * N:(k + 1) * N] = state[:, k * LANES:(k + 1) * LANES].astype(BF)
        decays.append(spread[tok:tok + 1, k * LANES:(k + 1) * LANES])
    msg[msg.shape[0] - 16:] = tail_rows(decays)


def load_quarter(x, x_v, quarter, sem):
    width = x_v.shape[1]
    return pltpu.make_async_copy(
        x.at[:, pl.ds(pl.multiple_of(quarter * width, width), width)], x_v, sem
    )


def give_kernel(raw, rate, x, b, msg1, msg2, msg3, wk, aux, raw_v, rate_v, x_v, b_v, sems):
    mine = lax.axis_index("seq") % 4
    loads = [
        pltpu.make_async_copy(raw, raw_v, sems.at[0]),
        pltpu.make_async_copy(rate, rate_v, sems.at[1]),
        pltpu.make_async_copy(b, b_v, sems.at[2]),
    ] + [load_quarter(x, x_v.at[k - 1], mine ^ k, sems.at[2 + k]) for k in (1, 2, 3)]
    for load in loads:
        load.start()
    loads[0].wait()
    loads[1].wait()
    step_vectors(raw_v[...], rate_v[...], wk, aux)
    for load in loads[2:]:
        load.wait()
    b16 = b_v[...].astype(BF)
    heads = x_v.shape[2] // P_SIZE
    for k, msg in ((1, msg1), (2, msg2), (3, msg3)):
        quarter_message(x_v[k - 1], b16, wk, (mine ^ k) * heads, msg)


def keep_kernel(wk, x, b, msg, x_v, b_v, sems):
    mine = lax.axis_index("seq") % 4
    loads = [load_quarter(x, x_v, mine, sems.at[0]), pltpu.make_async_copy(b, b_v, sems.at[1])]
    for load in loads:
        load.start()
    for load in loads:
        load.wait()
    quarter_message(x_v[...], b_v[...].astype(BF), wk, mine * (x_v.shape[1] // P_SIZE), msg)


HBM = pl.BlockSpec(memory_space=pltpu.HBM)
VMEM = pl.BlockSpec(memory_space=pltpu.VMEM)


def give_states(raw, rate, x, b):
    heads, tok = raw.shape
    lanes = x.shape[1] // 4
    return pl.pallas_call(
        give_kernel,
        in_specs=[HBM] * 4,
        out_shape=[jax.ShapeDtypeStruct((lanes // LANES * N + 16, LANES), BF)] * 3
        + [
            jax.ShapeDtypeStruct((2 * heads, tok + CHUNK), BF),
            jax.ShapeDtypeStruct((tok // CHUNK, 3 * heads, CHUNK), F32),
        ],
        scratch_shapes=[
            pltpu.VMEM((heads, tok), F32),
            pltpu.VMEM((1, heads), F32),
            pltpu.VMEM((3, tok, lanes), F32),
            pltpu.VMEM((tok, N), F32),
            pltpu.SemaphoreType.DMA((6,)),
        ],
        compiler_params=pltpu.CompilerParams(vmem_limit_bytes=WHOLE_VMEM),
        cost_estimate=pl.CostEstimate(flops=200_000_000, bytes_accessed=1_500_000, transcendentals=0),
        name="give_states",
    )(raw, rate, x, b)


def keep_states(wk, x, b):
    tok = x.shape[0]
    lanes = x.shape[1] // 4
    return pl.pallas_call(
        keep_kernel,
        in_specs=[VMEM, HBM, HBM],
        out_shape=jax.ShapeDtypeStruct((lanes // LANES * N + 16, LANES), BF),
        scratch_shapes=[
            pltpu.VMEM((tok, lanes), F32),
            pltpu.VMEM((tok, N), F32),
            pltpu.SemaphoreType.DMA((2,)),
        ],
        compiler_params=pltpu.CompilerParams(vmem_limit_bytes=VMEM_LIMIT),
        cost_estimate=pl.CostEstimate(flops=200_000_000, bytes_accessed=1_500_000, transcendentals=0),
        name="keep_states",
    )(wk, x, b)


def link(later, earlier, out):
    ahead, behind = decays_of(later), decays_of(earlier)
    for k, decay in enumerate(ahead):
        rows = slice(k * N, (k + 1) * N)
        out[rows] = (later[rows].astype(F32) + decay * earlier[rows].astype(F32)).astype(BF)
    out[len(ahead) * N:] = tail_rows([p * q for p, q in zip(ahead, behind)])


def is_later(distance):
    return (lax.axis_index("seq") // distance) % 2


def run_kernel(distance, own, come, out):
    later = is_later(distance)

    @pl.when(later == 0)
    def _():
        link(come, own, out)

    @pl.when(later == 1)
    def _():
        link(own, come, out)


def first_ahead_kernel(distance, come, out):
    later = is_later(distance)
    rows = out.shape[0] - 16

    @pl.when(later == 0)
    def _():
        out[:rows] = jnp.zeros((rows, LANES), BF)
        out[rows:] = tail_rows([jnp.ones((1, LANES), F32)] * (rows // N))

    @pl.when(later == 1)
    def _():
        out[...] = come[...]


def ahead_kernel(distance, ahead, come, out):
    later = is_later(distance)

    @pl.when(later == 0)
    def _():
        out[...] = ahead[...]

    @pl.when(later == 1)
    def _():
        link(ahead, come, out)


def by_section(work):
    mine = lax.axis_index("seq") % 4
    for v in range(4):
        pl.when(mine == v)(functools.partial(work, [j ^ v for j in range(4)]))


def join_four_kernel(own, come1, come2, come3, out):
    messages = (own, come1, come2, come3)

    def work(place):
        sections = [messages[p] for p in place]
        decays = [decays_of(section) for section in sections]
        for k in range(len(decays[0])):
            rows = slice(k * N, (k + 1) * N)
            total = sections[0][rows].astype(F32)
            for section, decay in zip(sections[1:], decays[1:]):
                total = section[rows].astype(F32) + decay[k] * total
            out[rows] = total.astype(BF)
        spans = [p * q * r * t for p, q, r, t in zip(*decays)]
        out[len(spans) * N:] = tail_rows(spans)

    by_section(work)


def end_kernel(distance, ahead, last, own, come1, come2, come3, mine, out1, out2, out3):
    messages, outs = (own, come1, come2, come3), (mine, out1, out2, out3)
    weight = is_later(distance).astype(F32)

    def work(place):
        sections, targets = [messages[p] for p in place], [outs[p] for p in place]
        decays = [decays_of(section) for section in sections]
        for k in range(len(decays[0])):
            rows = slice(k * N, (k + 1) * N)
            state = weight * last[rows].astype(F32)
            if ahead is not None:
                state = ahead[rows].astype(F32) + decays_of(ahead)[k] * state
            for j in range(4):
                targets[j][rows] = state.astype(BF)
                if j < 3:
                    state = sections[j][rows].astype(F32) + decays[j][k] * state

    by_section(work)


def scan_call(kernel, operands, shapes, name):
    return pl.pallas_call(
        kernel,
        out_shape=[jax.ShapeDtypeStruct(shape, BF) for shape in shapes],
        compiler_params=pltpu.CompilerParams(vmem_limit_bytes=VMEM_LIMIT),
        cost_estimate=pl.CostEstimate(flops=500_000, bytes_accessed=400_000, transcendentals=0),
        name=name,
    )(*operands)


def incoming_states(gives, keep, count, hold):
    def exchange(value, distance):
        return lax.ppermute(value, "seq", [(s, s ^ distance) for s in range(count)])

    def joined(kernel, *operands):
        return scan_call(kernel, operands, [keep.shape], "join_states")[0]

    parts = [keep] + [exchange(give, k) for k, give in zip((1, 2, 3), gives)]
    run, ahead, distance = joined(join_four_kernel, *parts), None, 4
    got = exchange(run, distance)
    while distance * 2 < count:
        if ahead is None:
            ahead = joined(functools.partial(first_ahead_kernel, distance), got)
        else:
            ahead = joined(functools.partial(ahead_kernel, distance), ahead, got)
        run = joined(functools.partial(run_kernel, distance), run, got)
        distance *= 2
        got = exchange(run, distance)
    hold, got = lax.optimization_barrier((hold, got))
    operands = [got] + parts
    if ahead is None:
        kernel = functools.partial(end_kernel, distance, None)
    else:
        kernel, operands = functools.partial(end_kernel, distance), [ahead] + operands
    shape = (keep.shape[0] - 16, LANES)
    outs = scan_call(kernel, operands, [shape] * 4, "join_end")
    return hold, [outs[0]] + [exchange(out, k) for k, out in zip((1, 2, 3), outs[1:])]


def rows_of(ref, block):
    return ref[pl.ds(pl.multiple_of(block * CHUNK, CHUNK), CHUNK), :]


def within_kernel(far, aux, x_ref, b_ref, c_ref, gate_ref, skip_ref, own_ref, lead_ref):
    channels = x_ref.shape[1]
    heads = aux.shape[1] // 3
    width = 256
    here = width // P_SIZE
    half = lax.axis_index("head") // 2
    half = 1 - half if far else half
    second = half == 1

    def vectors(c):
        return [aux[c, k * heads:(k + 1) * heads] for k in range(3)]

    def put(values):
        return jnp.concatenate([jnp.concatenate(split2(v), axis=0) for v in values], axis=1)

    first, then = vectors(0), vectors(1)
    ends = [v[1][:, CHUNK - 1:] for v in (first, then)]
    early = put(
        [
            jnp.where(second, first[0] * jnp.exp(first[2] + ends[1]), 0.0),
            jnp.where(second, then[0] * jnp.exp(then[2]), 0.0),
        ]
    )
    before = jnp.where(second, ends[0] + ends[1], 0.0)
    r = lax.broadcasted_iota(jnp.int32, (CHUNK, CHUNK), 0)
    l = lax.broadcasted_iota(jnp.int32, (CHUNK, CHUNK), 1)
    duo, trip, lines, scores, rows_b, rows_c, rows_x, rows_g = ([] for _ in range(8))
    for i in range(2):
        block = 2 * half + i
        step, pre, suf = vectors(block)
        duo.append(put((step, step * jnp.exp(suf), jnp.exp(pre), jnp.exp(pre + before))))
        trip.append(jnp.concatenate(split3(pre), axis=0))
        lines.append(pre)
        before = before + pre[:, CHUNK - 1:]
        b, c = rows_of(b_ref, block), rows_of(c_ref, block)
        raw = dot(c, b, ((1,), (1,)), lax.Precision.HIGHEST)
        scores.append(jnp.where(r >= l, raw, 0.0))
        rows_b.append(b.astype(BF))
        rows_c.append(c.astype(BF))
        rows_x.append(rows_of(x_ref, block))
        rows_g.append(rows_of(gate_ref, block))
    early_b = b_ref[:2 * CHUNK].astype(BF)
    gains = jnp.broadcast_to(jnp.concatenate(split3(skip_ref[...]), axis=1), (8, 3 * heads))
    lane = lax.broadcasted_iota(jnp.int32, (CHUNK, LANES), 1)
    for g in range(channels // width):
        at = slice(g * width, (g + 1) * width)
        spread = pick(2 * heads, width, heads, P_SIZE, g * here)
        columns = pick(3 * heads, here * CHUNK, heads, CHUNK, g * here)
        skip = dot(gains, pick(3 * heads, width, heads, P_SIZE, g * here))[:1]
        weights = dot(early, spread, ((0,), (0,)))
        state = dot(early_b, (x_ref[:2 * CHUNK, at] * weights).astype(BF), ((0,), (0,)))
        for i in range(2):
            cut = slice(i * CHUNK, (i + 1) * CHUNK)
            wide = dot(duo[i], spread, ((0,), (0,)))
            x = rows_x[i][:, at]
            stepped = x * wide[:CHUNK]
            lead = wide[2 * CHUNK:3 * CHUNK]
            tall = dot(trip[i], columns, ((0,), (0,)))
            outs = []
            for pair in range(here // 2):
                mixes = []
                for h in (2 * pair, 2 * pair + 1):
                    line = lines[i][g * here + h:g * here + h + 1]
                    gap = tall[:, h * CHUNK:(h + 1) * CHUNK] - line
                    mixes.append((scores[i] * jnp.exp(jnp.minimum(gap, 0.0))).astype(BF))
                both = stepped[:, pair * LANES:(pair + 1) * LANES]
                stacked = jnp.concatenate(
                    [
                        jnp.where(lane < P_SIZE, both, 0.0).astype(BF),
                        jnp.where(lane < P_SIZE, 0.0, both).astype(BF),
                    ],
                    axis=0,
                )
                outs.append(dot(jnp.concatenate(mixes, axis=1), stacked))
            y = jnp.concatenate(outs, axis=1) + skip * x
            y = y + lead * dot(rows_c[i], state.astype(BF))
            v = rows_g[i][:, at].astype(F32)
            silu = v / (1.0 + jnp.exp(-v))
            own_ref[cut, at] = y * silu
            lead_ref[cut, at] = wide[3 * CHUNK:] * silu
            if i == 0:
                weighted = (x * wide[CHUNK:2 * CHUNK]).astype(BF)
                state = state * lead[CHUNK - 1:] + dot(rows_b[i], weighted, ((0,), (0,)))


def within(far, aux, x, b, c, gate, skip):
    channels = x.shape[1]
    return pl.pallas_call(
        functools.partial(within_kernel, far),
        in_specs=[VMEM] * 6,
        out_specs=[VMEM] * 2,
        out_shape=[jax.ShapeDtypeStruct((2 * CHUNK, channels), F32)] * 2,
        compiler_params=pltpu.CompilerParams(vmem_limit_bytes=VMEM_LIMIT),
        cost_estimate=pl.CostEstimate(
            flops=4_000_000_000, bytes_accessed=3_000_000, transcendentals=500_000
        ),
        name="within_far" if far else "within_near",
    )(aux, x, b, c, gate, skip)


def finish_rows(own, lead, c, incoming, gain):
    c = c.astype(BF)
    blocks = incoming.shape[1] // N
    carried = jnp.concatenate(
        [dot(c, incoming[q, k * N:(k + 1) * N]) for q in range(4) for k in range(blocks)], axis=1
    )
    gated = own + lead * carried
    mean = jnp.mean(gated * gated, axis=1, keepdims=True)
    return (gated * lax.rsqrt(mean + 1e-05) * gain).astype(BF)


def finish_block(block, own, lead, c, incoming, gain):
    return finish_rows(
        rows_of(own, block % 2), rows_of(lead, block % 2), rows_of(c, block), incoming, gain[...]
    )


def fill_incoming(quarters, incoming):
    mine = lax.axis_index("seq") % 4
    for k, quarter in enumerate(quarters):
        incoming[mine ^ k] = quarter[...]


def project_both(normed, w, start, columns, theirs, mine, at=0):
    wide = 512
    for k in range(0, columns, wide):
        out = dot(normed[...], w[:, start + k:start + k + wide])
        theirs[:, at + k:at + k + wide] = out[:CHUNK].astype(BF)
        mine[:, k:k + wide] = out[CHUNK:]


def far_kernel(
    columns, own, lead, c, q0, q1, q2, q3, gain, w, theirs, mine, normed, incoming
):
    me = lax.axis_index("head")
    fill_incoming((q0, q1, q2, q3), incoming)
    normed[:CHUNK] = finish_block(me ^ 3, own, lead, c, incoming, gain)
    normed[CHUNK:] = finish_block(me ^ 2, own, lead, c, incoming, gain)
    project_both(normed, w, 0, columns, theirs, mine)


def more_kernel(start, columns, normed, w, theirs, mine):
    project_both(normed, w, start, columns, theirs, mine)


def mixed_kernel(
    start, columns, normed, own, lead, c, q0, q1, q2, q3, gain, w,
    theirs, mine, kept, incoming, given,
):
    me = lax.axis_index("head")
    project_both(normed, w, start, columns, theirs, mine)
    fill_incoming((q0, q1, q2, q3), incoming)
    given[...] = finish_block(me ^ 1, own, lead, c, incoming, gain)
    kept[...] = finish_block(me, own, lead, c, incoming, gain)
    wide = 512
    for k in range(0, w.shape[1], wide):
        theirs[:, columns + k:columns + k + wide] = dot(given[...], w[:, k:k + wide]).astype(BF)


def kept_kernel(columns, kept, come, w, out):
    wide = 512
    for k in range(0, w.shape[1], wide):
        out[:, k:k + wide] = dot(kept[...], w[:, k:k + wide]) + come[
            :, columns + k:columns + k + wide
        ].astype(F32)


def add_kernel(mine, come, out):
    out[...] = (mine[...] + come[:, :out.shape[1]].astype(F32)).astype(BF)


def local_call(kernel, operands, outs, name, scratch=(), flops=0, limit=VMEM_LIMIT):
    return pl.pallas_call(
        kernel,
        in_specs=[VMEM] * len(operands),
        out_specs=[VMEM] * len(outs),
        out_shape=[jax.ShapeDtypeStruct(shape, dtype) for shape, dtype in outs],
        scratch_shapes=list(scratch),
        compiler_params=pltpu.CompilerParams(vmem_limit_bytes=limit),
        cost_estimate=pl.CostEstimate(flops=flops, bytes_accessed=0, transcendentals=0),
        name=name,
    )(*operands)


def pass_kernel(*refs):
    pass


def await_piece(piece, *earlier):
    arrays = [piece, *earlier]
    return pl.pallas_call(
        pass_kernel,
        in_specs=[pl.BlockSpec(memory_space=pl.ANY)] * len(arrays),
        out_specs=[pl.BlockSpec(memory_space=pl.ANY)] * len(arrays),
        out_shape=[jax.ShapeDtypeStruct(v.shape, v.dtype) for v in arrays],
        input_output_aliases={k: k for k in range(len(arrays))},
        compiler_params=pltpu.CompilerParams(vmem_limit_bytes=1024 * 1024),
        cost_estimate=pl.CostEstimate(
            flops=20_000_000_000, bytes_accessed=100_000_000, transcendentals=0
        ),
        name="await_piece",
    )(*arrays)


def early_kernel(kept, first, second, out):
    at = 0
    for piece in (first, second):
        cut = slice(at, at + piece.shape[1])
        out[:, cut] = (kept[:, cut] + piece[...].astype(F32)).astype(BF)
        at += piece.shape[1]


def early_sums(kept, first, second):
    rows = first.shape[0]
    wide = first.shape[1] + second.shape[1]
    return pl.pallas_call(
        early_kernel,
        grid=(1,),
        in_specs=[VMEM] * 3,
        out_specs=pl.BlockSpec((rows, wide), lambda j: (0, 0)),
        out_shape=jax.ShapeDtypeStruct(kept.shape, BF),
        compiler_params=pltpu.CompilerParams(vmem_limit_bytes=VMEM_LIMIT),
        name="early_sums",
    )(kept, first, second)


def last_kernel(kept, third, filled, out, part, sems):
    wide = third.shape[1]
    start = kept.shape[1] - wide
    block = wide // 2
    stores = []
    for k in range(2):
        cut = slice(k * block, (k + 1) * block)
        part[:, cut] = (
            kept[:, start + k * block:start + (k + 1) * block] + third[:, cut].astype(F32)
        ).astype(BF)
        stores.append(
            pltpu.make_async_copy(
                part.at[:, cut], out.at[:, start + k * block:start + (k + 1) * block], sems.at[k]
            )
        )
        stores[k].start()
    for store in stores:
        store.wait()


def last_sums(kept, third, filled):
    return pl.pallas_call(
        last_kernel,
        in_specs=[VMEM, VMEM, pl.BlockSpec(memory_space=pl.ANY)],
        out_specs=pl.BlockSpec(memory_space=pl.ANY),
        out_shape=jax.ShapeDtypeStruct(kept.shape, BF),
        input_output_aliases={2: 0},
        scratch_shapes=[pltpu.VMEM(third.shape, BF), pltpu.SemaphoreType.DMA((2,))],
        compiler_params=pltpu.CompilerParams(vmem_limit_bytes=VMEM_LIMIT),
        name="last_sums",
    )(kept, third, filled)


def per_device(
    seq_count,
    ssm_input,
    gate_input,
    step_raw,
    decay_log,
    state_in,
    state_out,
    skip_gain,
    norm_gain,
    out_weight,
):
    tok = ssm_input.shape[0]
    heads = decay_log.shape[0]
    b = state_in.reshape(tok, N)
    c = state_out.reshape(tok, N)
    *gives, wk, aux = give_states(step_raw.T, decay_log.reshape(1, heads), ssm_input, b)
    keep = keep_states(wk, ssm_input, b)
    inputs = (ssm_input, b, c, gate_input, skip_gain.reshape(1, heads))
    local = within(True, aux, *inputs)
    (own, lead), quarters = incoming_states(gives, keep, seq_count, local)

    near = [(h, h ^ 1) for h in range(4)]
    far = [(h, h ^ 2) for h in range(4)]
    gain = norm_gain.reshape(1, -1)
    channels, dout = out_weight.shape
    rows = CHUNK
    states = pltpu.VMEM((4,) + quarters[0].shape, BF)
    finish = (own, lead, c, *quarters, gain, out_weight)
    (_, one), (start2, two), (start3, three) = PIECES

    def piece_outs(columns, extra=0):
        return [((rows, columns + extra), BF), ((rows, columns), F32)]

    def add(mine, theirs):
        come = lax.ppermute(theirs, "head", near)
        return local_call(add_kernel, (mine, come), [(mine.shape, BF)], "add_pair", limit=1 << 22)[0], come

    theirs, mine, normed = local_call(
        functools.partial(far_kernel, one),
        finish,
        piece_outs(one) + [((2 * rows, channels), BF)],
        "finish_far",
        [states],
        4 * rows * channels * one,
    )
    first, _ = add(mine, theirs)
    aux, first = lax.optimization_barrier((aux, first))
    theirs, mine = local_call(
        functools.partial(more_kernel, start2, two),
        (normed, out_weight),
        piece_outs(two),
        "project_more",
        flops=4 * rows * channels * two,
    )
    second, _ = add(mine, theirs)
    near_own, near_lead = within(False, aux, *inputs)
    normed, second = lax.optimization_barrier((normed, second))
    theirs, mine, kept = local_call(
        functools.partial(mixed_kernel, start3, three),
        (normed, near_own, near_lead) + finish[2:],
        piece_outs(three, dout) + [((rows, channels), BF)],
        "finish_near",
        [states, pltpu.VMEM((rows, channels), BF)],
        2 * rows * channels * (2 * three + dout),
    )
    third, come = add(mine, theirs)
    kept = local_call(
        functools.partial(kept_kernel, three),
        (kept, come, out_weight),
        [((rows, dout), F32)],
        "project_kept",
        flops=2 * rows * channels * dout,
    )[0]
    first = await_piece(lax.ppermute(first, "head", far))[0]
    second, first = await_piece(lax.ppermute(second, "head", far), first)
    filled = early_sums(kept, first, second)
    third, filled = await_piece(lax.ppermute(third, "head", far), filled)
    return last_sums(kept, third, filled)


def solution(mesh):
    in_specs = (
        P("seq", "head"),
        P("seq", "head"),
        P("seq", "head"),
        P("head"),
        P("seq", "head", None),
        P("seq", "head", None),
        P("head"),
        P("head"),
        P("head", None),
    )
    out_specs = P(("seq", "head"), None)
    return jax.shard_map(
        functools.partial(per_device, mesh.shape["seq"]),
        mesh=mesh,
        in_specs=in_specs,
        out_specs=out_specs,
        check_vma=False,
    )
```

```python
import functools

import jax
import jax.numpy as jnp
from jax import lax
from jax.experimental import pallas as pl
from jax.experimental.pallas import tpu as pltpu
from jax.sharding import PartitionSpec as P

P_SIZE = 64
N = 128
CHUNK = 128
LANES = 128
BF = jnp.bfloat16
F32 = jnp.float32
VMEM_LIMIT = 16 * 1024 * 1024
WHOLE_VMEM = 61 * 1024 * 1024 + 512 * 1024
PIECES = ((0, 1024), (1024, 1536), (2560, 1536))


def dot(a, b, contract=((1,), (0,)), precision=None):
    return lax.dot_general(a, b, (contract, ((), ())), precision=precision, preferred_element_type=F32)


def split2(v):
    hi = v.astype(BF)
    return hi, (v - hi.astype(F32)).astype(BF)


def split3(v):
    hi, rest = v.astype(BF), v
    rest = v - hi.astype(F32)
    mid = rest.astype(BF)
    return hi, mid, (rest - mid.astype(F32)).astype(BF)


def pick(rows, lanes, heads, per_head, first):
    r = lax.broadcasted_iota(jnp.int32, (rows, lanes), 0) % heads
    l = lax.broadcasted_iota(jnp.int32, (rows, lanes), 1) // per_head + first
    return jnp.where(r == l, 1.0, 0.0).astype(BF)


def step_vectors(raw, rate_row, wk, aux_ref):
    heads, tok = raw.shape
    chunks = tok // CHUNK
    step = jnp.maximum(raw, 0.0) + jnp.log1p(jnp.exp(-jnp.abs(raw)))
    r = lax.broadcasted_iota(jnp.int32, (heads, heads), 0)
    l = lax.broadcasted_iota(jnp.int32, (heads, heads), 1)
    rate = jnp.sum(jnp.where(r == l, rate_row, 0.0), axis=1, keepdims=True)
    logs = -step * jnp.exp(rate)
    parts = split3(logs)
    stacked = jnp.concatenate(
        [p[:, c * CHUNK:(c + 1) * CHUNK] for c in range(chunks) for p in parts], axis=0
    )
    s = lax.broadcasted_iota(jnp.int32, (CHUNK, 2 * CHUNK), 0)
    t = lax.broadcasted_iota(jnp.int32, (CHUNK, 2 * CHUNK), 1)
    tri = jnp.where(jnp.where(t < CHUNK, t - s, s - t + (CHUNK - 1)) >= 0, 1.0, 0.0).astype(BF)
    sums = dot(stacked, tri)
    pre, suf = [], []
    for c in range(chunks):
        base = 3 * heads * c
        total = (
            sums[base:base + heads] + sums[base + heads:base + 2 * heads]
        ) + sums[base + 2 * heads:base + 3 * heads]
        pre.append(total[:, :CHUNK])
        suf.append(total[:, CHUNK:])
    after = jnp.zeros((heads, 1), F32)
    for c in reversed(range(chunks)):
        w = step[:, c * CHUNK:(c + 1) * CHUNK] * jnp.exp(suf[c] + after)
        hi, lo = split2(w)
        wk[:heads, c * CHUNK:(c + 1) * CHUNK] = hi
        wk[heads:, c * CHUNK:(c + 1) * CHUNK] = lo
        after = after + pre[c][:, CHUNK - 1:]
    hi, lo = split2(jnp.broadcast_to(jnp.exp(after), (heads, CHUNK)))
    wk[:heads, tok:] = hi
    wk[heads:, tok:] = lo
    for c in range(chunks):
        aux_ref[c, :heads] = step[:, c * CHUNK:(c + 1) * CHUNK]
        aux_ref[c, heads:2 * heads] = pre[c]
        aux_ref[c, 2 * heads:] = suf[c]


def tail_rows(decays):
    r = lax.broadcasted_iota(jnp.int32, (16, LANES), 0)
    tail = jnp.zeros((16, LANES), F32)
    for k, decay in enumerate(decays):
        hi, lo = split2(decay)
        tail = jnp.where(r == 2 * k, hi.astype(F32), tail)
        tail = jnp.where(r == 2 * k + 1, lo.astype(F32), tail)
    return tail.astype(BF)


def decays_of(msg):
    blocks = (msg.shape[0] - 16) // N
    tail = msg[blocks * N:].astype(F32)
    return [tail[2 * k:2 * k + 1] + tail[2 * k + 1:2 * k + 2] for k in range(blocks)]


def quarter_message(x, b, wk, first_head, msg):
    tok, width = x.shape
    heads2 = wk.shape[0]
    spread = dot(wk[...], pick(heads2, width, heads2 // 2, P_SIZE, first_head), ((0,), (0,)))
    state = dot(b, (x * spread[:tok]).astype(BF), ((0,), (0,)))
    decays = []
    for k in range(width // LANES):
        msg[k * N:(k + 1) * N] = state[:, k * LANES:(k + 1) * LANES].astype(BF)
        decays.append(spread[tok:tok + 1, k * LANES:(k + 1) * LANES])
    msg[msg.shape[0] - 16:] = tail_rows(decays)


def load_quarter(x, x_v, quarter, sem):
    width = x_v.shape[1]
    return pltpu.make_async_copy(
        x.at[:, pl.ds(pl.multiple_of(quarter * width, width), width)], x_v, sem
    )


def give_kernel(raw, rate, x, b, msg1, msg2, msg3, wk, aux, raw_v, rate_v, x_v, b_v, sems):
    mine = lax.axis_index("seq") % 4
    loads = [
        pltpu.make_async_copy(raw, raw_v, sems.at[0]),
        pltpu.make_async_copy(rate, rate_v, sems.at[1]),
        pltpu.make_async_copy(b, b_v, sems.at[2]),
    ] + [load_quarter(x, x_v.at[k - 1], mine ^ k, sems.at[2 + k]) for k in (1, 2, 3)]
    for load in loads:
        load.start()
    loads[0].wait()
    loads[1].wait()
    step_vectors(raw_v[...], rate_v[...], wk, aux)
    loads[2].wait()
    b16 = b_v[...].astype(BF)
    heads = x_v.shape[2] // P_SIZE
    for k, msg in ((1, msg1), (2, msg2), (3, msg3)):
        loads[2 + k].wait()
        quarter_message(x_v[k - 1], b16, wk, (mine ^ k) * heads, msg)


def keep_kernel(wk, x, b, msg, x_v, b_v, sems):
    mine = lax.axis_index("seq") % 4
    loads = [load_quarter(x, x_v, mine, sems.at[0]), pltpu.make_async_copy(b, b_v, sems.at[1])]
    for load in loads:
        load.start()
    for load in loads:
        load.wait()
    quarter_message(x_v[...], b_v[...].astype(BF), wk, mine * (x_v.shape[1] // P_SIZE), msg)


HBM = pl.BlockSpec(memory_space=pltpu.HBM)
VMEM = pl.BlockSpec(memory_space=pltpu.VMEM)


def give_states(raw, rate, x, b):
    heads, tok = raw.shape
    lanes = x.shape[1] // 4
    return pl.pallas_call(
        give_kernel,
        in_specs=[HBM] * 4,
        out_shape=[jax.ShapeDtypeStruct((lanes // LANES * N + 16, LANES), BF)] * 3
        + [
            jax.ShapeDtypeStruct((2 * heads, tok + CHUNK), BF),
            jax.ShapeDtypeStruct((tok // CHUNK, 3 * heads, CHUNK), F32),
        ],
        scratch_shapes=[
            pltpu.VMEM((heads, tok), F32),
            pltpu.VMEM((1, heads), F32),
            pltpu.VMEM((3, tok, lanes), F32),
            pltpu.VMEM((tok, N), F32),
            pltpu.SemaphoreType.DMA((6,)),
        ],
        compiler_params=pltpu.CompilerParams(vmem_limit_bytes=WHOLE_VMEM),
        cost_estimate=pl.CostEstimate(flops=200_000_000, bytes_accessed=1_500_000, transcendentals=0),
        name="give_states",
    )(raw, rate, x, b)


def keep_states(wk, x, b):
    tok = x.shape[0]
    lanes = x.shape[1] // 4
    return pl.pallas_call(
        keep_kernel,
        in_specs=[VMEM, HBM, HBM],
        out_shape=jax.ShapeDtypeStruct((lanes // LANES * N + 16, LANES), BF),
        scratch_shapes=[
            pltpu.VMEM((tok, lanes), F32),
            pltpu.VMEM((tok, N), F32),
            pltpu.SemaphoreType.DMA((2,)),
        ],
        compiler_params=pltpu.CompilerParams(vmem_limit_bytes=VMEM_LIMIT),
        cost_estimate=pl.CostEstimate(flops=200_000_000, bytes_accessed=1_500_000, transcendentals=0),
        name="keep_states",
    )(wk, x, b)


def link(later, earlier, out):
    ahead, behind = decays_of(later), decays_of(earlier)
    for k, decay in enumerate(ahead):
        rows = slice(k * N, (k + 1) * N)
        out[rows] = (later[rows].astype(F32) + decay * earlier[rows].astype(F32)).astype(BF)
    out[len(ahead) * N:] = tail_rows([p * q for p, q in zip(ahead, behind)])


def is_later(distance):
    return (lax.axis_index("seq") // distance) % 2


def run_kernel(distance, own, come, out):
    later = is_later(distance)

    @pl.when(later == 0)
    def _():
        link(come, own, out)

    @pl.when(later == 1)
    def _():
        link(own, come, out)


def first_ahead_kernel(distance, come, out):
    later = is_later(distance)
    rows = out.shape[0] - 16

    @pl.when(later == 0)
    def _():
        out[:rows] = jnp.zeros((rows, LANES), BF)
        out[rows:] = tail_rows([jnp.ones((1, LANES), F32)] * (rows // N))

    @pl.when(later == 1)
    def _():
        out[...] = come[...]


def ahead_kernel(distance, ahead, come, out):
    later = is_later(distance)

    @pl.when(later == 0)
    def _():
        out[...] = ahead[...]

    @pl.when(later == 1)
    def _():
        link(ahead, come, out)


def by_section(work):
    mine = lax.axis_index("seq") % 4
    for v in range(4):
        pl.when(mine == v)(functools.partial(work, [j ^ v for j in range(4)]))


def join_four_kernel(own, come1, come2, come3, out):
    messages = (own, come1, come2, come3)

    def work(place):
        sections = [messages[p] for p in place]
        decays = [decays_of(section) for section in sections]
        for k in range(len(decays[0])):
            rows = slice(k * N, (k + 1) * N)
            total = sections[0][rows].astype(F32)
            for section, decay in zip(sections[1:], decays[1:]):
                total = section[rows].astype(F32) + decay[k] * total
            out[rows] = total.astype(BF)
        spans = [p * q * r * t for p, q, r, t in zip(*decays)]
        out[len(spans) * N:] = tail_rows(spans)

    by_section(work)


def end_kernel(distance, ahead, last, own, come1, come2, come3, mine, out1, out2, out3):
    messages, outs = (own, come1, come2, come3), (mine, out1, out2, out3)
    weight = is_later(distance).astype(F32)

    def work(place):
        sections, targets = [messages[p] for p in place], [outs[p] for p in place]
        decays = [decays_of(section) for section in sections]
        for k in range(len(decays[0])):
            rows = slice(k * N, (k + 1) * N)
            state = weight * last[rows].astype(F32)
            if ahead is not None:
                state = ahead[rows].astype(F32) + decays_of(ahead)[k] * state
            for j in range(4):
                targets[j][rows] = state.astype(BF)
                if j < 3:
                    state = sections[j][rows].astype(F32) + decays[j][k] * state

    by_section(work)


def scan_call(kernel, operands, shapes, name):
    return pl.pallas_call(
        kernel,
        out_shape=[jax.ShapeDtypeStruct(shape, BF) for shape in shapes],
        compiler_params=pltpu.CompilerParams(vmem_limit_bytes=VMEM_LIMIT),
        cost_estimate=pl.CostEstimate(flops=500_000, bytes_accessed=400_000, transcendentals=0),
        name=name,
    )(*operands)


def incoming_states(gives, keep, count, hold):
    def exchange(value, distance):
        return lax.ppermute(value, "seq", [(s, s ^ distance) for s in range(count)])

    def joined(kernel, *operands):
        return scan_call(kernel, operands, [keep.shape], "join_states")[0]

    parts = [keep] + [exchange(give, k) for k, give in zip((1, 2, 3), gives)]
    run, ahead, distance = joined(join_four_kernel, *parts), None, 4
    got = exchange(run, distance)
    while distance * 2 < count:
        if ahead is None:
            ahead = joined(functools.partial(first_ahead_kernel, distance), got)
        else:
            ahead = joined(functools.partial(ahead_kernel, distance), ahead, got)
        run = joined(functools.partial(run_kernel, distance), run, got)
        distance *= 2
        got = exchange(run, distance)
    hold, got = lax.optimization_barrier((hold, got))
    operands = [got] + parts
    if ahead is None:
        kernel = functools.partial(end_kernel, distance, None)
    else:
        kernel, operands = functools.partial(end_kernel, distance), [ahead] + operands
    shape = (keep.shape[0] - 16, LANES)
    outs = scan_call(kernel, operands, [shape] * 4, "join_end")
    return hold, [outs[0]] + [exchange(out, k) for k, out in zip((1, 2, 3), outs[1:])]


def rows_of(ref, block):
    return ref[pl.ds(pl.multiple_of(block * CHUNK, CHUNK), CHUNK), :]


def within_kernel(far, aux, x_ref, b_ref, c_ref, gate_ref, skip_ref, own_ref, lead_ref):
    channels = x_ref.shape[1]
    heads = aux.shape[1] // 3
    width = 256
    here = width // P_SIZE
    half = lax.axis_index("head") // 2
    half = 1 - half if far else half
    second = half == 1

    def vectors(c):
        return [aux[c, k * heads:(k + 1) * heads] for k in range(3)]

    def put(values):
        return jnp.concatenate([jnp.concatenate(split2(v), axis=0) for v in values], axis=1)

    first, then = vectors(0), vectors(1)
    ends = [v[1][:, CHUNK - 1:] for v in (first, then)]
    early = put(
        [
            jnp.where(second, first[0] * jnp.exp(first[2] + ends[1]), 0.0),
            jnp.where(second, then[0] * jnp.exp(then[2]), 0.0),
        ]
    )
    before = jnp.where(second, ends[0] + ends[1], 0.0)
    r = lax.broadcasted_iota(jnp.int32, (CHUNK, CHUNK), 0)
    l = lax.broadcasted_iota(jnp.int32, (CHUNK, CHUNK), 1)
    duo, trip, lines, scores, rows_b, rows_c, rows_x, rows_g = ([] for _ in range(8))
    for i in range(2):
        block = 2 * half + i
        step, pre, suf = vectors(block)
        duo.append(put((step, step * jnp.exp(suf), jnp.exp(pre), jnp.exp(pre + before))))
        trip.append(jnp.concatenate(split3(pre), axis=0))
        lines.append(pre)
        before = before + pre[:, CHUNK - 1:]
        b, c = rows_of(b_ref, block), rows_of(c_ref, block)
        (ch, cl), (bh, bl) = split2(c), split2(b)
        raw = dot(
            jnp.concatenate([ch, ch, cl], axis=1), jnp.concatenate([bh, bl, bh], axis=1), ((1,), (1,))
        )
        scores.append(jnp.where(r >= l, raw, 0.0))
        rows_b.append(b.astype(BF))
        rows_c.append(c.astype(BF))
        rows_x.append(rows_of(x_ref, block))
        rows_g.append(rows_of(gate_ref, block))
    early_b = b_ref[:2 * CHUNK].astype(BF)
    gains = jnp.broadcast_to(jnp.concatenate(split3(skip_ref[...]), axis=1), (8, 3 * heads))
    lane = lax.broadcasted_iota(jnp.int32, (CHUNK, LANES), 1)
    for g in range(channels // width):
        at = slice(g * width, (g + 1) * width)
        spread = pick(2 * heads, width, heads, P_SIZE, g * here)
        columns = pick(3 * heads, here * CHUNK, heads, CHUNK, g * here)
        skip = dot(gains, pick(3 * heads, width, heads, P_SIZE, g * here))[:1]
        weights = dot(early, spread, ((0,), (0,)))
        state = dot(early_b, (x_ref[:2 * CHUNK, at] * weights).astype(BF), ((0,), (0,)))
        for i in range(2):
            cut = slice(i * CHUNK, (i + 1) * CHUNK)
            wide = dot(duo[i], spread, ((0,), (0,)))
            x = rows_x[i][:, at]
            stepped = x * wide[:CHUNK]
            lead = wide[2 * CHUNK:3 * CHUNK]
            tall = dot(trip[i], columns, ((0,), (0,)))
            outs = []
            for pair in range(here // 2):
                mixes = []
                for h in (2 * pair, 2 * pair + 1):
                    line = lines[i][g * here + h:g * here + h + 1]
                    gap = tall[:, h * CHUNK:(h + 1) * CHUNK] - line
                    mixes.append((scores[i] * jnp.exp(jnp.minimum(gap, 0.0))).astype(BF))
                both = stepped[:, pair * LANES:(pair + 1) * LANES]
                stacked = jnp.concatenate(
                    [
                        jnp.where(lane < P_SIZE, both, 0.0).astype(BF),
                        jnp.where(lane < P_SIZE, 0.0, both).astype(BF),
                    ],
                    axis=0,
                )
                outs.append(dot(jnp.concatenate(mixes, axis=1), stacked))
            y = jnp.concatenate(outs, axis=1) + skip * x
            y = y + lead * dot(rows_c[i], state.astype(BF))
            v = rows_g[i][:, at].astype(F32)
            silu = v / (1.0 + jnp.exp(-v))
            own_ref[cut, at] = y * silu
            lead_ref[cut, at] = wide[3 * CHUNK:] * silu
            if i == 0:
                weighted = (x * wide[CHUNK:2 * CHUNK]).astype(BF)
                state = state * lead[CHUNK - 1:] + dot(rows_b[i], weighted, ((0,), (0,)))


def within(far, aux, x, b, c, gate, skip):
    channels = x.shape[1]
    return pl.pallas_call(
        functools.partial(within_kernel, far),
        in_specs=[VMEM] * 6,
        out_specs=[VMEM] * 2,
        out_shape=[jax.ShapeDtypeStruct((2 * CHUNK, channels), F32)] * 2,
        compiler_params=pltpu.CompilerParams(vmem_limit_bytes=VMEM_LIMIT),
        cost_estimate=pl.CostEstimate(
            flops=4_000_000_000, bytes_accessed=3_000_000, transcendentals=500_000
        ),
        name="within_far" if far else "within_near",
    )(aux, x, b, c, gate, skip)


def finish_rows(own, lead, c, incoming, gain):
    c = c.astype(BF)
    blocks = incoming.shape[1] // N
    carried = jnp.concatenate(
        [dot(c, incoming[q, k * N:(k + 1) * N]) for q in range(4) for k in range(blocks)], axis=1
    )
    gated = own + lead * carried
    mean = jnp.mean(gated * gated, axis=1, keepdims=True)
    return (gated * lax.rsqrt(mean + 1e-05) * gain).astype(BF)


def finish_block(block, own, lead, c, incoming, gain):
    return finish_rows(
        rows_of(own, block % 2), rows_of(lead, block % 2), rows_of(c, block), incoming, gain[...]
    )


def fill_incoming(quarters, incoming):
    mine = lax.axis_index("seq") % 4
    for k, quarter in enumerate(quarters):
        incoming[mine ^ k] = quarter[...]


def project_both(normed, w, start, columns, theirs, mine, at=0):
    wide = 512
    for k in range(0, columns, wide):
        out = dot(normed[...], w[:, start + k:start + k + wide])
        theirs[:, at + k:at + k + wide] = out[:CHUNK].astype(BF)
        mine[:, k:k + wide] = out[CHUNK:]


def far_kernel(
    columns, own, lead, c, q0, q1, q2, q3, gain, w, theirs, mine, normed, incoming
):
    me = lax.axis_index("head")
    fill_incoming((q0, q1, q2, q3), incoming)
    normed[:CHUNK] = finish_block(me ^ 3, own, lead, c, incoming, gain)
    normed[CHUNK:] = finish_block(me ^ 2, own, lead, c, incoming, gain)
    project_both(normed, w, 0, columns, theirs, mine)


def more_kernel(start, columns, normed, w, theirs, mine):
    project_both(normed, w, start, columns, theirs, mine)


def mixed_kernel(
    start, columns, normed, own, lead, c, q0, q1, q2, q3, gain, w,
    theirs, mine, kept, incoming, given,
):
    me = lax.axis_index("head")
    project_both(normed, w, start, columns, theirs, mine)
    fill_incoming((q0, q1, q2, q3), incoming)
    given[...] = finish_block(me ^ 1, own, lead, c, incoming, gain)
    kept[...] = finish_block(me, own, lead, c, incoming, gain)
    wide = 512
    for k in range(0, w.shape[1], wide):
        theirs[:, columns + k:columns + k + wide] = dot(given[...], w[:, k:k + wide]).astype(BF)


def kept_kernel(columns, kept, come, w, out):
    wide = 512
    for k in range(0, w.shape[1], wide):
        out[:, k:k + wide] = dot(kept[...], w[:, k:k + wide]) + come[
            :, columns + k:columns + k + wide
        ].astype(F32)


def add_kernel(mine, come, out):
    out[...] = (mine[...] + come[:, :out.shape[1]].astype(F32)).astype(BF)


def local_call(kernel, operands, outs, name, scratch=(), flops=0, limit=VMEM_LIMIT):
    return pl.pallas_call(
        kernel,
        in_specs=[VMEM] * len(operands),
        out_specs=[VMEM] * len(outs),
        out_shape=[jax.ShapeDtypeStruct(shape, dtype) for shape, dtype in outs],
        scratch_shapes=list(scratch),
        compiler_params=pltpu.CompilerParams(vmem_limit_bytes=limit),
        cost_estimate=pl.CostEstimate(flops=flops, bytes_accessed=0, transcendentals=0),
        name=name,
    )(*operands)


def pass_kernel(*refs):
    pass


def await_piece(piece, *earlier):
    arrays = [piece, *earlier]
    return pl.pallas_call(
        pass_kernel,
        in_specs=[pl.BlockSpec(memory_space=pl.ANY)] * len(arrays),
        out_specs=[pl.BlockSpec(memory_space=pl.ANY)] * len(arrays),
        out_shape=[jax.ShapeDtypeStruct(v.shape, v.dtype) for v in arrays],
        input_output_aliases={k: k for k in range(len(arrays))},
        compiler_params=pltpu.CompilerParams(vmem_limit_bytes=1024 * 1024),
        cost_estimate=pl.CostEstimate(
            flops=20_000_000_000, bytes_accessed=100_000_000, transcendentals=0
        ),
        name="await_piece",
    )(*arrays)


def early_kernel(kept, first, second, out):
    at = 0
    for piece in (first, second):
        cut = slice(at, at + piece.shape[1])
        out[:, cut] = (kept[:, cut] + piece[...].astype(F32)).astype(BF)
        at += piece.shape[1]


def early_sums(kept, first, second):
    rows = first.shape[0]
    wide = first.shape[1] + second.shape[1]
    return pl.pallas_call(
        early_kernel,
        grid=(1,),
        in_specs=[VMEM] * 3,
        out_specs=pl.BlockSpec((rows, wide), lambda j: (0, 0)),
        out_shape=jax.ShapeDtypeStruct(kept.shape, BF),
        compiler_params=pltpu.CompilerParams(vmem_limit_bytes=VMEM_LIMIT),
        name="early_sums",
    )(kept, first, second)


def last_kernel(kept, third, filled, out, part, sems):
    wide = third.shape[1]
    start = kept.shape[1] - wide
    block = wide // 2
    stores = []
    for k in range(2):
        cut = slice(k * block, (k + 1) * block)
        part[:, cut] = (
            kept[:, start + k * block:start + (k + 1) * block] + third[:, cut].astype(F32)
        ).astype(BF)
        stores.append(
            pltpu.make_async_copy(
                part.at[:, cut], out.at[:, start + k * block:start + (k + 1) * block], sems.at[k]
            )
        )
        stores[k].start()
    for store in stores:
        store.wait()


def last_sums(kept, third, filled):
    return pl.pallas_call(
        last_kernel,
        in_specs=[VMEM, VMEM, pl.BlockSpec(memory_space=pl.ANY)],
        out_specs=pl.BlockSpec(memory_space=pl.ANY),
        out_shape=jax.ShapeDtypeStruct(kept.shape, BF),
        input_output_aliases={2: 0},
        scratch_shapes=[pltpu.VMEM(third.shape, BF), pltpu.SemaphoreType.DMA((2,))],
        compiler_params=pltpu.CompilerParams(vmem_limit_bytes=VMEM_LIMIT),
        name="last_sums",
    )(kept, third, filled)


def per_device(
    seq_count,
    ssm_input,
    gate_input,
    step_raw,
    decay_log,
    state_in,
    state_out,
    skip_gain,
    norm_gain,
    out_weight,
):
    tok = ssm_input.shape[0]
    heads = decay_log.shape[0]
    b = state_in.reshape(tok, N)
    c = state_out.reshape(tok, N)
    *gives, wk, aux = give_states(step_raw.T, decay_log.reshape(1, heads), ssm_input, b)
    keep = keep_states(wk, ssm_input, b)
    inputs = (ssm_input, b, c, gate_input, skip_gain.reshape(1, heads))
    local = within(True, aux, *inputs)
    (own, lead), quarters = incoming_states(gives, keep, seq_count, local)

    near = [(h, h ^ 1) for h in range(4)]
    far = [(h, h ^ 2) for h in range(4)]
    gain = norm_gain.reshape(1, -1)
    channels, dout = out_weight.shape
    rows = CHUNK
    states = pltpu.VMEM((4,) + quarters[0].shape, BF)
    finish = (own, lead, c, *quarters, gain, out_weight)
    (_, one), (start2, two), (start3, three) = PIECES

    def piece_outs(columns, extra=0):
        return [((rows, columns + extra), BF), ((rows, columns), F32)]

    def add(mine, theirs):
        come = lax.ppermute(theirs, "head", near)
        return local_call(add_kernel, (mine, come), [(mine.shape, BF)], "add_pair", limit=1 << 22)[0], come

    theirs, mine, normed = local_call(
        functools.partial(far_kernel, one),
        finish,
        piece_outs(one) + [((2 * rows, channels), BF)],
        "finish_far",
        [states],
        4 * rows * channels * one,
    )
    first, _ = add(mine, theirs)
    aux, first = lax.optimization_barrier((aux, first))
    theirs, mine = local_call(
        functools.partial(more_kernel, start2, two),
        (normed, out_weight),
        piece_outs(two),
        "project_more",
        flops=4 * rows * channels * two,
    )
    second, _ = add(mine, theirs)
    near_own, near_lead = within(False, aux, *inputs)
    normed, second = lax.optimization_barrier((normed, second))
    theirs, mine, kept = local_call(
        functools.partial(mixed_kernel, start3, three),
        (normed, near_own, near_lead) + finish[2:],
        piece_outs(three, dout) + [((rows, channels), BF)],
        "finish_near",
        [states, pltpu.VMEM((rows, channels), BF)],
        2 * rows * channels * (2 * three + dout),
    )
    third, come = add(mine, theirs)
    kept = local_call(
        functools.partial(kept_kernel, three),
        (kept, come, out_weight),
        [((rows, dout), F32)],
        "project_kept",
        flops=2 * rows * channels * dout,
    )[0]
    first = await_piece(lax.ppermute(first, "head", far))[0]
    second, first = await_piece(lax.ppermute(second, "head", far), first)
    filled = early_sums(kept, first, second)
    third, filled = await_piece(lax.ppermute(third, "head", far), filled)
    return last_sums(kept, third, filled)


def solution(mesh):
    in_specs = (
        P("seq", "head"),
        P("seq", "head"),
        P("seq", "head"),
        P("head"),
        P("seq", "head", None),
        P("seq", "head", None),
        P("head"),
        P("head"),
        P("head", None),
    )
    out_specs = P(("seq", "head"), None)
    return jax.shard_map(
        functools.partial(per_device, mesh.shape["seq"]),
        mesh=mesh,
        in_specs=in_specs,
        out_specs=out_specs,
        check_vma=False,
    )
```

```python
import functools

import jax
import jax.numpy as jnp
from jax import lax
from jax.experimental import pallas as pl
from jax.experimental.pallas import tpu as pltpu
from jax.sharding import PartitionSpec as P

P_SIZE = 64
N = 128
CHUNK = 128
LANES = 128
BF = jnp.bfloat16
F32 = jnp.float32
VMEM_LIMIT = 16 * 1024 * 1024
WHOLE_VMEM = 61 * 1024 * 1024 + 512 * 1024
PIECES = ((0, 1024), (1024, 1536), (2560, 1536))


def dot(a, b, contract=((1,), (0,)), precision=None):
    return lax.dot_general(a, b, (contract, ((), ())), precision=precision, preferred_element_type=F32)


def split2(v):
    hi = v.astype(BF)
    return hi, (v - hi.astype(F32)).astype(BF)


def split3(v):
    hi, rest = v.astype(BF), v
    rest = v - hi.astype(F32)
    mid = rest.astype(BF)
    return hi, mid, (rest - mid.astype(F32)).astype(BF)


def pick(rows, lanes, heads, per_head, first):
    r = lax.broadcasted_iota(jnp.int32, (rows, lanes), 0) % heads
    l = lax.broadcasted_iota(jnp.int32, (rows, lanes), 1) // per_head + first
    return jnp.where(r == l, 1.0, 0.0).astype(BF)


def step_vectors(raw, rate_row, wk, aux_ref):
    heads, tok = raw.shape
    chunks = tok // CHUNK
    step = jnp.maximum(raw, 0.0) + jnp.log1p(jnp.exp(-jnp.abs(raw)))
    r = lax.broadcasted_iota(jnp.int32, (heads, heads), 0)
    l = lax.broadcasted_iota(jnp.int32, (heads, heads), 1)
    rate = jnp.sum(jnp.where(r == l, rate_row, 0.0), axis=1, keepdims=True)
    logs = -step * jnp.exp(rate)
    parts = split3(logs)
    stacked = jnp.concatenate(
        [p[:, c * CHUNK:(c + 1) * CHUNK] for c in range(chunks) for p in parts], axis=0
    )
    s = lax.broadcasted_iota(jnp.int32, (CHUNK, 2 * CHUNK), 0)
    t = lax.broadcasted_iota(jnp.int32, (CHUNK, 2 * CHUNK), 1)
    tri = jnp.where(jnp.where(t < CHUNK, t - s, s - t + (CHUNK - 1)) >= 0, 1.0, 0.0).astype(BF)
    sums = dot(stacked, tri)
    pre, suf = [], []
    for c in range(chunks):
        base = 3 * heads * c
        total = (
            sums[base:base + heads] + sums[base + heads:base + 2 * heads]
        ) + sums[base + 2 * heads:base + 3 * heads]
        pre.append(total[:, :CHUNK])
        suf.append(total[:, CHUNK:])
    after = jnp.zeros((heads, 1), F32)
    for c in reversed(range(chunks)):
        w = step[:, c * CHUNK:(c + 1) * CHUNK] * jnp.exp(suf[c] + after)
        hi, lo = split2(w)
        wk[:heads, c * CHUNK:(c + 1) * CHUNK] = hi
        wk[heads:, c * CHUNK:(c + 1) * CHUNK] = lo
        after = after + pre[c][:, CHUNK - 1:]
    hi, lo = split2(jnp.broadcast_to(jnp.exp(after), (heads, CHUNK)))
    wk[:heads, tok:] = hi
    wk[heads:, tok:] = lo
    for c in range(chunks):
        aux_ref[c, :heads] = step[:, c * CHUNK:(c + 1) * CHUNK]
        aux_ref[c, heads:2 * heads] = pre[c]
        aux_ref[c, 2 * heads:] = suf[c]


def tail_rows(decays):
    r = lax.broadcasted_iota(jnp.int32, (16, LANES), 0)
    tail = jnp.zeros((16, LANES), F32)
    for k, decay in enumerate(decays):
        hi, lo = split2(decay)
        tail = jnp.where(r == 2 * k, hi.astype(F32), tail)
        tail = jnp.where(r == 2 * k + 1, lo.astype(F32), tail)
    return tail.astype(BF)


def decays_of(msg):
    blocks = (msg.shape[0] - 16) // N
    tail = msg[blocks * N:].astype(F32)
    return [tail[2 * k:2 * k + 1] + tail[2 * k + 1:2 * k + 2] for k in range(blocks)]


def quarter_message(x, b, wk, first_head, msg):
    tok, width = x.shape
    heads2 = wk.shape[0]
    spread = dot(wk[...], pick(heads2, width, heads2 // 2, P_SIZE, first_head), ((0,), (0,)))
    state = dot(b, (x * spread[:tok]).astype(BF), ((0,), (0,)))
    decays = []
    for k in range(width // LANES):
        msg[k * N:(k + 1) * N] = state[:, k * LANES:(k + 1) * LANES].astype(BF)
        decays.append(spread[tok:tok + 1, k * LANES:(k + 1) * LANES])
    msg[msg.shape[0] - 16:] = tail_rows(decays)


def load_quarter(x, x_v, quarter, sem):
    width = x_v.shape[1]
    return pltpu.make_async_copy(
        x.at[:, pl.ds(pl.multiple_of(quarter * width, width), width)], x_v, sem
    )


def give_kernel(raw, rate, x, b, msg1, msg2, msg3, wk, aux, raw_v, rate_v, x_v, b_v, sems):
    mine = lax.axis_index("seq") % 4
    loads = [
        pltpu.make_async_copy(raw, raw_v, sems.at[0]),
        pltpu.make_async_copy(rate, rate_v, sems.at[1]),
        pltpu.make_async_copy(b, b_v, sems.at[2]),
    ] + [load_quarter(x, x_v.at[k - 1], mine ^ k, sems.at[2 + k]) for k in (1, 2, 3)]
    for load in loads:
        load.start()
    loads[0].wait()
    loads[1].wait()
    step_vectors(raw_v[...], rate_v[...], wk, aux)
    loads[2].wait()
    b16 = b_v[...].astype(BF)
    heads = x_v.shape[2] // P_SIZE
    for k, msg in ((1, msg1), (2, msg2), (3, msg3)):
        loads[2 + k].wait()
        quarter_message(x_v[k - 1], b16, wk, (mine ^ k) * heads, msg)


def keep_kernel(wk, x, b, msg, x_v, b_v, sems):
    mine = lax.axis_index("seq") % 4
    loads = [load_quarter(x, x_v, mine, sems.at[0]), pltpu.make_async_copy(b, b_v, sems.at[1])]
    for load in loads:
        load.start()
    for load in loads:
        load.wait()
    quarter_message(x_v[...], b_v[...].astype(BF), wk, mine * (x_v.shape[1] // P_SIZE), msg)


HBM = pl.BlockSpec(memory_space=pltpu.HBM)
VMEM = pl.BlockSpec(memory_space=pltpu.VMEM)


def give_states(raw, rate, x, b):
    heads, tok = raw.shape
    lanes = x.shape[1] // 4
    return pl.pallas_call(
        give_kernel,
        in_specs=[HBM] * 4,
        out_shape=[jax.ShapeDtypeStruct((lanes // LANES * N + 16, LANES), BF)] * 3
        + [
            jax.ShapeDtypeStruct((2 * heads, tok + CHUNK), BF),
            jax.ShapeDtypeStruct((tok // CHUNK, 3 * heads, CHUNK), F32),
        ],
        scratch_shapes=[
            pltpu.VMEM((heads, tok), F32),
            pltpu.VMEM((1, heads), F32),
            pltpu.VMEM((3, tok, lanes), F32),
            pltpu.VMEM((tok, N), F32),
            pltpu.SemaphoreType.DMA((6,)),
        ],
        compiler_params=pltpu.CompilerParams(vmem_limit_bytes=WHOLE_VMEM),
        cost_estimate=pl.CostEstimate(flops=200_000_000, bytes_accessed=1_500_000, transcendentals=0),
        name="give_states",
    )(raw, rate, x, b)


def keep_states(wk, x, b):
    tok = x.shape[0]
    lanes = x.shape[1] // 4
    return pl.pallas_call(
        keep_kernel,
        in_specs=[VMEM, HBM, HBM],
        out_shape=jax.ShapeDtypeStruct((lanes // LANES * N + 16, LANES), BF),
        scratch_shapes=[
            pltpu.VMEM((tok, lanes), F32),
            pltpu.VMEM((tok, N), F32),
            pltpu.SemaphoreType.DMA((2,)),
        ],
        compiler_params=pltpu.CompilerParams(vmem_limit_bytes=VMEM_LIMIT),
        cost_estimate=pl.CostEstimate(flops=200_000_000, bytes_accessed=1_500_000, transcendentals=0),
        name="keep_states",
    )(wk, x, b)


def link(later, earlier, out):
    ahead, behind = decays_of(later), decays_of(earlier)
    for k, decay in enumerate(ahead):
        rows = slice(k * N, (k + 1) * N)
        out[rows] = (later[rows].astype(F32) + decay * earlier[rows].astype(F32)).astype(BF)
    out[len(ahead) * N:] = tail_rows([p * q for p, q in zip(ahead, behind)])


def is_later(distance):
    return (lax.axis_index("seq") // distance) % 2


def run_kernel(distance, own, come, out):
    later = is_later(distance)

    @pl.when(later == 0)
    def _():
        link(come, own, out)

    @pl.when(later == 1)
    def _():
        link(own, come, out)


def first_ahead_kernel(distance, come, out):
    later = is_later(distance)
    rows = out.shape[0] - 16

    @pl.when(later == 0)
    def _():
        out[:rows] = jnp.zeros((rows, LANES), BF)
        out[rows:] = tail_rows([jnp.ones((1, LANES), F32)] * (rows // N))

    @pl.when(later == 1)
    def _():
        out[...] = come[...]


def ahead_kernel(distance, ahead, come, out):
    later = is_later(distance)

    @pl.when(later == 0)
    def _():
        out[...] = ahead[...]

    @pl.when(later == 1)
    def _():
        link(ahead, come, out)


def by_section(work):
    mine = lax.axis_index("seq") % 4
    for v in range(4):
        pl.when(mine == v)(functools.partial(work, [j ^ v for j in range(4)]))


def join_four_kernel(own, come1, come2, come3, out):
    messages = (own, come1, come2, come3)

    def work(place):
        sections = [messages[p] for p in place]
        decays = [decays_of(section) for section in sections]
        for k in range(len(decays[0])):
            rows = slice(k * N, (k + 1) * N)
            total = sections[0][rows].astype(F32)
            for section, decay in zip(sections[1:], decays[1:]):
                total = section[rows].astype(F32) + decay[k] * total
            out[rows] = total.astype(BF)
        spans = [p * q * r * t for p, q, r, t in zip(*decays)]
        out[len(spans) * N:] = tail_rows(spans)

    by_section(work)


def end_kernel(distance, ahead, last, own, come1, come2, come3, mine, out1, out2, out3):
    messages, outs = (own, come1, come2, come3), (mine, out1, out2, out3)
    weight = is_later(distance).astype(F32)

    def work(place):
        sections, targets = [messages[p] for p in place], [outs[p] for p in place]
        decays = [decays_of(section) for section in sections]
        for k in range(len(decays[0])):
            rows = slice(k * N, (k + 1) * N)
            state = weight * last[rows].astype(F32)
            if ahead is not None:
                state = ahead[rows].astype(F32) + decays_of(ahead)[k] * state
            for j in range(4):
                targets[j][rows] = state.astype(BF)
                if j < 3:
                    state = sections[j][rows].astype(F32) + decays[j][k] * state

    by_section(work)


def scan_call(kernel, operands, shapes, name):
    return pl.pallas_call(
        kernel,
        out_shape=[jax.ShapeDtypeStruct(shape, BF) for shape in shapes],
        compiler_params=pltpu.CompilerParams(vmem_limit_bytes=VMEM_LIMIT),
        cost_estimate=pl.CostEstimate(flops=500_000, bytes_accessed=400_000, transcendentals=0),
        name=name,
    )(*operands)


def incoming_states(gives, keep, count, hold):
    def exchange(value, distance):
        return lax.ppermute(value, "seq", [(s, s ^ distance) for s in range(count)])

    def joined(kernel, *operands):
        return scan_call(kernel, operands, [keep.shape], "join_states")[0]

    parts = [keep] + [exchange(give, k) for k, give in zip((1, 2, 3), gives)]
    run, ahead, distance = joined(join_four_kernel, *parts), None, 4
    got = exchange(run, distance)
    while distance * 2 < count:
        if ahead is None:
            ahead = joined(functools.partial(first_ahead_kernel, distance), got)
        else:
            ahead = joined(functools.partial(ahead_kernel, distance), ahead, got)
        run = joined(functools.partial(run_kernel, distance), run, got)
        distance *= 2
        got = exchange(run, distance)
    operands = [got] + parts
    if ahead is None:
        kernel = functools.partial(end_kernel, distance, None)
    else:
        kernel, operands = functools.partial(end_kernel, distance), [ahead] + operands
    shape = (keep.shape[0] - 16, LANES)
    outs = scan_call(kernel, operands, [shape] * 4, "join_end")
    return hold, [outs[0]] + [exchange(out, k) for k, out in zip((1, 2, 3), outs[1:])]


def rows_of(ref, block):
    return ref[pl.ds(pl.multiple_of(block * CHUNK, CHUNK), CHUNK), :]


def within_kernel(far, aux, x_ref, b_ref, c_ref, gate_ref, skip_ref, own_ref, lead_ref):
    channels = x_ref.shape[1]
    heads = aux.shape[1] // 3
    width = 256
    here = width // P_SIZE
    half = lax.axis_index("head") // 2
    half = 1 - half if far else half
    second = half == 1

    def vectors(c):
        return [aux[c, k * heads:(k + 1) * heads] for k in range(3)]

    def put(values):
        return jnp.concatenate([jnp.concatenate(split2(v), axis=0) for v in values], axis=1)

    first, then = vectors(0), vectors(1)
    ends = [v[1][:, CHUNK - 1:] for v in (first, then)]
    early = put(
        [
            jnp.where(second, first[0] * jnp.exp(first[2] + ends[1]), 0.0),
            jnp.where(second, then[0] * jnp.exp(then[2]), 0.0),
        ]
    )
    before = jnp.where(second, ends[0] + ends[1], 0.0)
    r = lax.broadcasted_iota(jnp.int32, (CHUNK, CHUNK), 0)
    l = lax.broadcasted_iota(jnp.int32, (CHUNK, CHUNK), 1)
    duo, trip, lines, scores, rows_b, rows_c, rows_x, rows_g = ([] for _ in range(8))
    for i in range(2):
        block = 2 * half + i
        step, pre, suf = vectors(block)
        duo.append(put((step, step * jnp.exp(suf), jnp.exp(pre), jnp.exp(pre + before))))
        trip.append(jnp.concatenate(split3(pre), axis=0))
        lines.append(pre)
        before = before + pre[:, CHUNK - 1:]
        b, c = rows_of(b_ref, block), rows_of(c_ref, block)
        (ch, cl), (bh, bl) = split2(c), split2(b)
        raw = dot(
            jnp.concatenate([ch, ch, cl], axis=1), jnp.concatenate([bh, bl, bh], axis=1), ((1,), (1,))
        )
        scores.append(jnp.where(r >= l, raw, 0.0))
        rows_b.append(b.astype(BF))
        rows_c.append(c.astype(BF))
        rows_x.append(rows_of(x_ref, block))
        rows_g.append(rows_of(gate_ref, block))
    early_b = b_ref[:2 * CHUNK].astype(BF)
    gains = jnp.broadcast_to(jnp.concatenate(split3(skip_ref[...]), axis=1), (8, 3 * heads))
    lane = lax.broadcasted_iota(jnp.int32, (CHUNK, LANES), 1)
    for g in range(channels // width):
        at = slice(g * width, (g + 1) * width)
        spread = pick(2 * heads, width, heads, P_SIZE, g * here)
        columns = pick(3 * heads, here * CHUNK, heads, CHUNK, g * here)
        skip = dot(gains, pick(3 * heads, width, heads, P_SIZE, g * here))[:1]
        weights = dot(early, spread, ((0,), (0,)))
        state = dot(early_b, (x_ref[:2 * CHUNK, at] * weights).astype(BF), ((0,), (0,)))
        for i in range(2):
            cut = slice(i * CHUNK, (i + 1) * CHUNK)
            wide = dot(duo[i], spread, ((0,), (0,)))
            x = rows_x[i][:, at]
            stepped = x * wide[:CHUNK]
            lead = wide[2 * CHUNK:3 * CHUNK]
            tall = dot(trip[i], columns, ((0,), (0,)))
            outs = []
            for pair in range(here // 2):
                mixes = []
                for h in (2 * pair, 2 * pair + 1):
                    line = lines[i][g * here + h:g * here + h + 1]
                    gap = tall[:, h * CHUNK:(h + 1) * CHUNK] - line
                    mixes.append((scores[i] * jnp.exp(jnp.minimum(gap, 0.0))).astype(BF))
                both = stepped[:, pair * LANES:(pair + 1) * LANES]
                stacked = jnp.concatenate(
                    [
                        jnp.where(lane < P_SIZE, both, 0.0).astype(BF),
                        jnp.where(lane < P_SIZE, 0.0, both).astype(BF),
                    ],
                    axis=0,
                )
                outs.append(dot(jnp.concatenate(mixes, axis=1), stacked))
            y = jnp.concatenate(outs, axis=1) + skip * x
            y = y + lead * dot(rows_c[i], state.astype(BF))
            v = rows_g[i][:, at].astype(F32)
            silu = v / (1.0 + jnp.exp(-v))
            own_ref[cut, at] = y * silu
            lead_ref[cut, at] = wide[3 * CHUNK:] * silu
            if i == 0:
                weighted = (x * wide[CHUNK:2 * CHUNK]).astype(BF)
                state = state * lead[CHUNK - 1:] + dot(rows_b[i], weighted, ((0,), (0,)))


def within(far, aux, x, b, c, gate, skip):
    channels = x.shape[1]
    return pl.pallas_call(
        functools.partial(within_kernel, far),
        in_specs=[VMEM] * 6,
        out_specs=[VMEM] * 2,
        out_shape=[jax.ShapeDtypeStruct((2 * CHUNK, channels), F32)] * 2,
        compiler_params=pltpu.CompilerParams(vmem_limit_bytes=VMEM_LIMIT),
        cost_estimate=pl.CostEstimate(
            flops=4_000_000_000, bytes_accessed=3_000_000, transcendentals=500_000
        ),
        name="within_far" if far else "within_near",
    )(aux, x, b, c, gate, skip)


def finish_rows(own, lead, c, incoming, gain):
    c = c.astype(BF)
    blocks = incoming.shape[1] // N
    carried = jnp.concatenate(
        [dot(c, incoming[q, k * N:(k + 1) * N]) for q in range(4) for k in range(blocks)], axis=1
    )
    gated = own + lead * carried
    mean = jnp.mean(gated * gated, axis=1, keepdims=True)
    return (gated * lax.rsqrt(mean + 1e-05) * gain).astype(BF)


def finish_block(block, own, lead, c, incoming, gain):
    return finish_rows(
        rows_of(own, block % 2), rows_of(lead, block % 2), rows_of(c, block), incoming, gain[...]
    )


def fill_incoming(quarters, incoming):
    mine = lax.axis_index("seq") % 4
    for k, quarter in enumerate(quarters):
        incoming[mine ^ k] = quarter[...]


def project_both(normed, w, start, columns, theirs, mine, at=0):
    wide = 512
    for k in range(0, columns, wide):
        out = dot(normed[...], w[:, start + k:start + k + wide])
        theirs[:, at + k:at + k + wide] = out[:CHUNK].astype(BF)
        mine[:, k:k + wide] = out[CHUNK:]


def far_kernel(
    columns, own, lead, c, q0, q1, q2, q3, gain, w, theirs, mine, normed, incoming
):
    me = lax.axis_index("head")
    fill_incoming((q0, q1, q2, q3), incoming)
    normed[:CHUNK] = finish_block(me ^ 3, own, lead, c, incoming, gain)
    normed[CHUNK:] = finish_block(me ^ 2, own, lead, c, incoming, gain)
    project_both(normed, w, 0, columns, theirs, mine)


def more_kernel(start, columns, normed, w, theirs, mine):
    project_both(normed, w, start, columns, theirs, mine)


def mixed_kernel(
    start, columns, normed, own, lead, c, q0, q1, q2, q3, gain, w,
    theirs, mine, kept, incoming, given,
):
    me = lax.axis_index("head")
    project_both(normed, w, start, columns, theirs, mine)
    fill_incoming((q0, q1, q2, q3), incoming)
    given[...] = finish_block(me ^ 1, own, lead, c, incoming, gain)
    kept[...] = finish_block(me, own, lead, c, incoming, gain)
    wide = 512
    for k in range(0, w.shape[1], wide):
        theirs[:, columns + k:columns + k + wide] = dot(given[...], w[:, k:k + wide]).astype(BF)


def kept_kernel(columns, kept, come, w, out):
    wide = 512
    for k in range(0, w.shape[1], wide):
        out[:, k:k + wide] = dot(kept[...], w[:, k:k + wide]) + come[
            :, columns + k:columns + k + wide
        ].astype(F32)


def add_kernel(mine, come, out):
    out[...] = (mine[...] + come[:, :out.shape[1]].astype(F32)).astype(BF)


def local_call(kernel, operands, outs, name, scratch=(), flops=0, limit=VMEM_LIMIT):
    return pl.pallas_call(
        kernel,
        in_specs=[VMEM] * len(operands),
        out_specs=[VMEM] * len(outs),
        out_shape=[jax.ShapeDtypeStruct(shape, dtype) for shape, dtype in outs],
        scratch_shapes=list(scratch),
        compiler_params=pltpu.CompilerParams(vmem_limit_bytes=limit),
        cost_estimate=pl.CostEstimate(flops=flops, bytes_accessed=0, transcendentals=0),
        name=name,
    )(*operands)


def pass_kernel(*refs):
    pass


def await_piece(piece, *earlier):
    arrays = [piece, *earlier]
    return pl.pallas_call(
        pass_kernel,
        in_specs=[pl.BlockSpec(memory_space=pl.ANY)] * len(arrays),
        out_specs=[pl.BlockSpec(memory_space=pl.ANY)] * len(arrays),
        out_shape=[jax.ShapeDtypeStruct(v.shape, v.dtype) for v in arrays],
        input_output_aliases={k: k for k in range(len(arrays))},
        compiler_params=pltpu.CompilerParams(vmem_limit_bytes=1024 * 1024),
        cost_estimate=pl.CostEstimate(
            flops=20_000_000_000, bytes_accessed=100_000_000, transcendentals=0
        ),
        name="await_piece",
    )(*arrays)


def early_kernel(kept, first, second, out):
    at = 0
    for piece in (first, second):
        cut = slice(at, at + piece.shape[1])
        out[:, cut] = (kept[:, cut] + piece[...].astype(F32)).astype(BF)
        at += piece.shape[1]


def early_sums(kept, first, second):
    rows = first.shape[0]
    wide = first.shape[1] + second.shape[1]
    return pl.pallas_call(
        early_kernel,
        grid=(1,),
        in_specs=[VMEM] * 3,
        out_specs=pl.BlockSpec((rows, wide), lambda j: (0, 0)),
        out_shape=jax.ShapeDtypeStruct(kept.shape, BF),
        compiler_params=pltpu.CompilerParams(vmem_limit_bytes=VMEM_LIMIT),
        name="early_sums",
    )(kept, first, second)


def last_kernel(kept, third, filled, out, part, sems):
    wide = third.shape[1]
    start = kept.shape[1] - wide
    block = wide // 2
    stores = []
    for k in range(2):
        cut = slice(k * block, (k + 1) * block)
        part[:, cut] = (
            kept[:, start + k * block:start + (k + 1) * block] + third[:, cut].astype(F32)
        ).astype(BF)
        stores.append(
            pltpu.make_async_copy(
                part.at[:, cut], out.at[:, start + k * block:start + (k + 1) * block], sems.at[k]
            )
        )
        stores[k].start()
    for store in stores:
        store.wait()


def last_sums(kept, third, filled):
    return pl.pallas_call(
        last_kernel,
        in_specs=[VMEM, VMEM, pl.BlockSpec(memory_space=pl.ANY)],
        out_specs=pl.BlockSpec(memory_space=pl.ANY),
        out_shape=jax.ShapeDtypeStruct(kept.shape, BF),
        input_output_aliases={2: 0},
        scratch_shapes=[pltpu.VMEM(third.shape, BF), pltpu.SemaphoreType.DMA((2,))],
        compiler_params=pltpu.CompilerParams(vmem_limit_bytes=VMEM_LIMIT),
        name="last_sums",
    )(kept, third, filled)


def per_device(
    seq_count,
    ssm_input,
    gate_input,
    step_raw,
    decay_log,
    state_in,
    state_out,
    skip_gain,
    norm_gain,
    out_weight,
):
    tok = ssm_input.shape[0]
    heads = decay_log.shape[0]
    b = state_in.reshape(tok, N)
    c = state_out.reshape(tok, N)
    *gives, wk, aux = give_states(step_raw.T, decay_log.reshape(1, heads), ssm_input, b)
    keep = keep_states(wk, ssm_input, b)
    inputs = (ssm_input, b, c, gate_input, skip_gain.reshape(1, heads))
    local = within(True, aux, *inputs)
    (own, lead), quarters = incoming_states(gives, keep, seq_count, local)

    near = [(h, h ^ 1) for h in range(4)]
    far = [(h, h ^ 2) for h in range(4)]
    gain = norm_gain.reshape(1, -1)
    channels, dout = out_weight.shape
    rows = CHUNK
    states = pltpu.VMEM((4,) + quarters[0].shape, BF)
    finish = (own, lead, c, *quarters, gain, out_weight)
    (_, one), (start2, two), (start3, three) = PIECES

    def piece_outs(columns, extra=0):
        return [((rows, columns + extra), BF), ((rows, columns), F32)]

    def add(mine, theirs):
        come = lax.ppermute(theirs, "head", near)
        return local_call(add_kernel, (mine, come), [(mine.shape, BF)], "add_pair", limit=1 << 22)[0], come

    theirs, mine, normed = local_call(
        functools.partial(far_kernel, one),
        finish,
        piece_outs(one) + [((2 * rows, channels), BF)],
        "finish_far",
        [states],
        4 * rows * channels * one,
    )
    first, _ = add(mine, theirs)
    aux, first = lax.optimization_barrier((aux, first))
    theirs, mine = local_call(
        functools.partial(more_kernel, start2, two),
        (normed, out_weight),
        piece_outs(two),
        "project_more",
        flops=4 * rows * channels * two,
    )
    second, _ = add(mine, theirs)
    near_own, near_lead = within(False, aux, *inputs)
    normed, second = lax.optimization_barrier((normed, second))
    theirs, mine, kept = local_call(
        functools.partial(mixed_kernel, start3, three),
        (normed, near_own, near_lead) + finish[2:],
        piece_outs(three, dout) + [((rows, channels), BF)],
        "finish_near",
        [states, pltpu.VMEM((rows, channels), BF)],
        2 * rows * channels * (2 * three + dout),
    )
    third, come = add(mine, theirs)
    kept = local_call(
        functools.partial(kept_kernel, three),
        (kept, come, out_weight),
        [((rows, dout), F32)],
        "project_kept",
        flops=2 * rows * channels * dout,
    )[0]
    first = await_piece(lax.ppermute(first, "head", far))[0]
    second, first = await_piece(lax.ppermute(second, "head", far), first)
    filled = early_sums(kept, first, second)
    third, filled = await_piece(lax.ppermute(third, "head", far), filled)
    return last_sums(kept, third, filled)


def solution(mesh):
    in_specs = (
        P("seq", "head"),
        P("seq", "head"),
        P("seq", "head"),
        P("head"),
        P("seq", "head", None),
        P("seq", "head", None),
        P("head"),
        P("head"),
        P("head", None),
    )
    out_specs = P(("seq", "head"), None)
    return jax.shard_map(
        functools.partial(per_device, mesh.shape["seq"]),
        mesh=mesh,
        in_specs=in_specs,
        out_specs=out_specs,
        check_vma=False,
    )
```
